32 devices in a mesh: dp: 16 (over z, y, x), tensor: 2 (over core).
Axes of the slice: x: 2, y: 2, z: 4, core: 2. Of those that a mesh axis runs over, the one named last changes fastest.
Arguments:
- inputs: bfloat16 [3, 16384, 1024], P(None, ('dp', 'tensor')), may hold values from -6 to 6
- gain_attn: bfloat16 [1024], P('dp'), may hold values from 0.5 to 1.5
- gain_mlp: bfloat16 [1024], P('dp'), may hold values from 0.5 to 1.5
- w_query: bfloat16 [1024, 256], P('dp', 'tensor'), may hold values from -0.1875 to 0.1875
- w_key: bfloat16 [1024, 256], P('dp', 'tensor'), may hold values from -0.1875 to 0.1875
- w_value: bfloat16 [1024, 1024], P('dp', 'tensor'), may hold values from -0.1875 to 0.1875
- w_out: bfloat16 [1024, 1024], P('tensor', 'dp'), may hold values from -3 to 3
- w_gate: bfloat16 [1024, 2752], P('dp', 'tensor'), may hold values from -0.1875 to 0.1875
- w_up: bfloat16 [1024, 2752], P('dp', 'tensor'), may hold values from -0.1875 to 0.1875
- w_down: bfloat16 [2752, 1024], P('tensor', 'dp'), may hold values from -0.109375 to 0.109375
- out_grad: bfloat16 [3, 16384, 1024], P(None, ('dp', 'tensor')), may hold values from -6 to 6
- lengths: int32 [3, 16, 8], P(None, 'dp'), may hold values from 1 to 512, 1024 in all within a row
Outputs:
- mixed_out: bfloat16 [3, 16384, 1024], P(None, ('dp', 'tensor'))
- input_grad: float32 [3, 16384, 1024], P(None, ('dp', 'tensor'))
- grad_gain_attn: float32 [1024], P('dp')
- grad_gain_mlp: float32 [1024], P('dp')
- grad_query: float32 [1024, 256], P('dp', 'tensor')
- grad_key: float32 [1024, 256], P('dp', 'tensor')
- grad_value: float32 [1024, 1024], P('dp', 'tensor')
- grad_out: float32 [1024, 1024], P('tensor', 'dp')
- grad_gate: float32 [1024, 2752], P('dp', 'tensor')
- grad_up: float32 [1024, 2752], P('dp', 'tensor')
- grad_down: float32 [2752, 1024], P('tensor', 'dp')
The draws below stay inside these ranges and needn't reach their ends.
Inputs may be any that keep to these rules, and one draw needn't show every extreme that they name: Each group's 8 lengths sum to 1024, and the longest is exactly 512.
All inputs are finite; a program needn't handle non-finite values.
Results may differ from the reference program's by a relative error of at most 0.025.
Values may be sent and summed in bfloat16 or wider, within the bound.
A program may use at most 320 MiB of HBM per device.

```python
import math
import jax
import jax.numpy as jnp
import numpy as np
from jax import lax

D = 1024
HEADS = 16
FEAT = 16
VD = 64
FF = 2752
TOK_DEV = 1024
MB = 3
DOCS = 8
BLK = 512
MOST = 512
TOKENS = 16384
N_DP = 16


def block_scale(own_key, extent, cuts, low, largest):
    gain = 1.0
    for axis_at, parts in cuts:
        steps = jax.random.uniform(jax.random.fold_in(jax.random.fold_in(own_key, 6), axis_at), (parts,), jnp.float32, low / len(cuts), largest / len(cuts))
        gain = gain * jnp.repeat(jnp.exp(steps), extent[axis_at] // parts).reshape((-1,) + (1,) * (len(extent) - 1 - axis_at))
    return gain


def profile(number_of, total, most, lean):
    portions = [(1 << 20) // math.isqrt(grade ** lean) + 1 for grade in range(2, number_of + 1)]
    rest, given = total - most - (number_of - 1), [1] * (number_of - 1)
    while rest > 0:
        candidates = [i for i in range(number_of - 1) if given[i] < most]
        pool, budget = sum([portions[i] for i in candidates]), rest
        for i in candidates:
            more = min(most - given[i], max(1, budget * portions[i] // pool), rest)
            given[i] = given[i] + more
            rest = rest - more
    return np.array([most] + given)


def uneven_parts(stream_key, amount, total, most, skew):
    if amount == 2:
        one = jax.random.randint(stream_key, (), max(1, total - most), min(most, total - 1) + 1)
        return jnp.stack([one, total - one])
    tallies = jnp.asarray(profile(amount, total, most, skew), jnp.int32)
    pairs = (amount - 1) // 2
    source_of, receiver = tallies[1:1 + 2 * pairs:2], tallies[2:2 + 2 * pairs:2]
    slack = jnp.minimum(source_of - 1, most - receiver)
    shifted = jax.random.randint(jax.random.fold_in(stream_key, 1), (pairs,), 0, 1 << 20) % (slack + 1)
    tallies = tallies.at[1:1 + 2 * pairs:2].set(source_of - shifted).at[2:2 + 2 * pairs:2].set(receiver + shifted)
    return tallies[jax.random.permutation(jax.random.fold_in(stream_key, 2), amount)]


def gaussian(own_key, extent, scale, limit, cuts=(), kind=jnp.bfloat16):
    level = block_scale(own_key, extent, cuts, -0.22, 0.18) if cuts else 1.0
    values = jax.random.normal(own_key, extent, jnp.float32) * scale * level
    return jnp.minimum(jnp.maximum(values, -limit), limit).astype(kind)


def setup_inputs(seed: int = 0) -> dict:
    streams_of = jax.random.split(jax.random.key(seed), 13)
    return {
        "inputs": gaussian(streams_of[0], (MB, TOKENS, D), 1.0, 6.0, ((1, 32),)),
        "gain_attn": jnp.clip(1.0 + 0.1 * jax.random.normal(streams_of[1], (D,), jnp.float32), 0.5, 1.5).astype(jnp.bfloat16),
        "gain_mlp": jnp.clip(1.0 + 0.1 * jax.random.normal(streams_of[2], (D,), jnp.float32), 0.5, 1.5).astype(jnp.bfloat16),
        "w_query": gaussian(streams_of[3], (D, HEADS * FEAT), D ** -0.5, 0.1875, ((0, 16), (1, 2))),
        "w_key": gaussian(streams_of[4], (D, HEADS * FEAT), D ** -0.5, 0.1875, ((0, 16), (1, 2))),
        "w_value": gaussian(streams_of[5], (D, HEADS * VD), D ** -0.5, 0.1875, ((0, 16), (1, 2))),
        "w_out": gaussian(streams_of[6], (HEADS * VD, D), (max(4 * HEADS * VD // TOK_DEV, 1)) ** -0.5, 3.0, ((0, 2), (1, 16))),
        "w_gate": gaussian(streams_of[7], (D, FF), D ** -0.5, 0.1875, ((0, 16), (1, 2))),
        "w_up": gaussian(streams_of[8], (D, FF), D ** -0.5, 0.1875, ((0, 16), (1, 2))),
        "w_down": gaussian(streams_of[9], (FF, D), FF ** -0.5, 0.109375, ((0, 2), (1, 16))),
        "out_grad": gaussian(streams_of[10], (MB, TOKENS, D), 1.0, 6.0, ((1, 32),)),
        "lengths": jax.vmap(lambda own: uneven_parts(own, DOCS, TOK_DEV, MOST, 2))(jax.random.split(streams_of[11], MB * N_DP)).reshape((MB, N_DP, DOCS)).astype(jnp.int32),
    }


EXACT = lax.Precision.HIGHEST

@jax.custom_vjp
def low(v):
    return lax.optimization_barrier(v.astype(jnp.bfloat16)).astype(jnp.float32)

@jax.custom_vjp
def low_back(v):
    return v

def low_keep(v):
    return (low(v), None)

def low_pass(kept, grad):
    return (grad,)

def back_keep(v):
    return (v, None)

def back_low(kept, grad):
    return (low(grad),)
low.defvjp(low_keep, low_pass)
low_back.defvjp(back_keep, back_low)

def product(left, right):
    return jnp.dot(left, right, precision=EXACT, preferred_element_type=jnp.float32)

def root_norm(values):
    return values * lax.rsqrt(lax.optimization_barrier(jnp.mean(values * values, axis=-1, keepdims=True)) + 1e-05)

def taylor(halved):
    feature_dim = halved.shape[-1]
    upper_idx, lower_idx = np.triu_indices(feature_dim)
    pick_upper = jnp.asarray(np.eye(feature_dim)[:, upper_idx], jnp.float32)
    pick_lower = jnp.asarray(np.eye(feature_dim)[:, lower_idx], jnp.float32)
    factors = jnp.asarray(np.where(upper_idx == lower_idx, math.sqrt(0.5), 1.0), jnp.float32)
    first_pick = jnp.einsum('rhf,fp->rhp', halved, pick_upper, precision=EXACT)
    second_pick = jnp.einsum('rhf,fp->rhp', halved, pick_lower, precision=EXACT)
    ones_col = jnp.ones(halved.shape[:-1] + (1,), jnp.float32)
    return jnp.concatenate([ones_col, halved, first_pick * second_pick * factors], axis=-1)

def attend_block(carry_in, block_in):
    kv_state, totals, previous = carry_in
    queries, keys_in, values_in, doc_ids = block_in
    half_q = 0.5 * queries
    half_k = 0.5 * keys_in
    scores = jnp.einsum('rhf,chf->hrc', half_q, half_k, precision=EXACT)
    places = jnp.arange(doc_ids.shape[0], dtype=jnp.int32)
    allowed = (doc_ids[:, None] == doc_ids[None, :]) & (places[None, :] <= places[:, None])
    weights = jnp.where(allowed[None], 1.0 + scores + 0.5 * scores * scores, 0.0)
    feat_q = taylor(half_q)
    feat_k = taylor(half_k)
    carried_in = (doc_ids == previous).astype(jnp.float32)
    numerator = jnp.einsum('hrc,chv->rhv', weights, values_in, precision=EXACT) + carried_in[:, None, None] * jnp.einsum('rhf,hfv->rhv', feat_q, kv_state, precision=EXACT)
    denominator = lax.optimization_barrier(jnp.sum(weights, axis=2)).T + carried_in[:, None] * jnp.einsum('rhf,hf->rh', feat_q, totals, precision=EXACT)
    mixed_rows = numerator / denominator[:, :, None]
    final_doc = doc_ids[-1].astype(jnp.int32)
    staying = (doc_ids == final_doc).astype(jnp.float32)[:, None, None] * feat_k
    joined = (final_doc == previous).astype(jnp.float32)
    kv_state = jnp.einsum('rhf,rhv->hfv', staying, values_in, precision=EXACT) + joined * kv_state
    totals = lax.optimization_barrier(jnp.sum(staying, axis=0)) + joined * totals
    return ((kv_state, totals, final_doc), mixed_rows)

def attend(queries, keys_in, values_in, doc_ids):
    row_total, head_count, feature_dim = queries.shape
    value_dim = values_in.shape[2]
    block_count = row_total // BLK
    feature_total = 1 + feature_dim + feature_dim * (feature_dim + 1) // 2
    initial = (jnp.zeros((head_count, feature_total, value_dim), jnp.float32), jnp.zeros((head_count, feature_total), jnp.float32), jnp.array(-1, jnp.int32))
    pieces = (queries.reshape(block_count, BLK, head_count, feature_dim), keys_in.reshape(block_count, BLK, head_count, feature_dim), values_in.reshape(block_count, BLK, head_count, value_dim), doc_ids.reshape(block_count, BLK))
    last_carry, mixed_rows = lax.scan(jax.checkpoint(attend_block), initial, pieces)
    return mixed_rows.reshape(row_total, head_count * value_dim)

def document_ids(lengths_row, row_total):
    doc_ends = jnp.cumsum(lengths_row).astype(jnp.int32)
    places = jnp.arange(row_total, dtype=jnp.int32)
    return lax.optimization_barrier(jnp.sum((places[:, None] >= doc_ends[None, :]).astype(jnp.int32), axis=1)).astype(jnp.int32)

def layer(values, gain_attn, gain_mlp, w_query, w_key, w_value, w_out, w_gate, w_up, w_down, doc_ids):
    row_total = values.shape[0]
    normed_in = low(root_norm(values) * gain_attn)
    queries = low(low_back(product(normed_in, w_query))).reshape(row_total, HEADS, FEAT)
    keys_in = low(low_back(product(normed_in, w_key))).reshape(row_total, HEADS, FEAT)
    values_in = low(low_back(product(normed_in, w_value))).reshape(row_total, HEADS, VD)
    mixed_rows = low(low_back(attend(queries, keys_in, values_in, doc_ids)))
    residual = values + low_back(product(mixed_rows, w_out))
    normed_mid = low(root_norm(residual) * gain_mlp)
    gate_pre = low_back(product(normed_mid, w_gate))
    up_pre = low_back(product(normed_mid, w_up))
    hidden = low(jax.nn.silu(gate_pre) * up_pre)
    return residual + product(hidden, w_down)

def reference(inputs, gain_attn, gain_mlp, w_query, w_key, w_value, w_out, w_gate, w_up, w_down, out_grad, lengths):
    parameters = tuple((p.astype(jnp.float32) for p in (gain_attn, gain_mlp, w_query, w_key, w_value, w_out, w_gate, w_up, w_down)))
    groups = inputs.reshape(MB * N_DP, TOK_DEV, D)
    cotangents = out_grad.reshape(MB * N_DP, TOK_DEV, D)
    group_lengths = lengths.reshape(MB * N_DP, DOCS)

    def step_group(summed, item_in):
        group_rows, group_cot, group_len = item_in
        doc_ids = document_ids(group_len, TOK_DEV)

        def forward(values, *weights_in):
            return layer(values, *weights_in, doc_ids)
        layer_out, pullback = jax.vjp(forward, group_rows.astype(jnp.float32), *parameters)
        gradients = pullback(group_cot.astype(jnp.float32))
        summed = tuple((a + b for a, b in zip(summed, gradients[1:])))
        return (summed, (layer_out.astype(jnp.bfloat16), gradients[0]))
    zero_sums = tuple((jnp.zeros_like(p) for p in parameters))
    summed, (layer_outs, input_grads) = lax.scan(step_group, zero_sums, (groups, cotangents, group_lengths))
    return (layer_outs.reshape(MB, TOKENS, D), input_grads.reshape(MB, TOKENS, D), summed[0], summed[1], summed[2], summed[3], summed[4], summed[5], summed[6], summed[7], summed[8])
```

```python
import functools
import math

import jax
import jax.numpy as jnp
import numpy as np
from jax import lax
from jax.experimental import pallas as pl
from jax.experimental.pallas import tpu as pltpu
from jax.sharding import PartitionSpec as P

FEAT = 16
VD = 64
BLK = 512


EXACT = lax.Precision.HIGHEST


def taylor(halved):
    feature_dim = halved.shape[-1]
    upper_idx, lower_idx = np.triu_indices(feature_dim)
    flat_index = jnp.asarray(upper_idx * feature_dim + lower_idx, jnp.int32)
    factors = jnp.asarray(np.where(upper_idx == lower_idx, math.sqrt(0.5), 1.0), jnp.float32)
    outer = (halved[..., :, None] * halved[..., None, :]).reshape(
        halved.shape[:-1] + (feature_dim * feature_dim,)
    )
    second = jnp.take(outer, flat_index, axis=-1) * factors
    ones_col = jnp.ones(halved.shape[:-1] + (1,), jnp.float32)
    return jnp.concatenate([ones_col, halved, second], axis=-1)


def attend_block(carry_in, block_in):
    kv_state, totals, previous = carry_in
    queries, keys_in, values_in, doc_ids = block_in
    half_q = 0.5 * queries
    half_k = 0.5 * keys_in
    scores = jnp.einsum("rhf,chf->hrc", half_q, half_k, preferred_element_type=jnp.float32)
    places = jnp.arange(doc_ids.shape[0], dtype=jnp.int32)
    allowed = (doc_ids[:, None] == doc_ids[None, :]) & (places[None, :] <= places[:, None])
    weights = jnp.where(allowed[None], 1.0 + scores + 0.5 * scores * scores, 0.0)
    feat_q = taylor(half_q)
    feat_k = taylor(half_k)
    carried_in = (doc_ids == previous).astype(jnp.float32)
    numerator = jnp.einsum("hrc,chv->rhv", weights, values_in, precision=EXACT) + carried_in[
        :, None, None
    ] * jnp.einsum("rhf,hfv->rhv", feat_q, kv_state, precision=EXACT)
    denominator = jnp.sum(weights, axis=2).T + carried_in[:, None] * jnp.einsum(
        "rhf,hf->rh", feat_q, totals, precision=EXACT
    )
    mixed_rows = numerator / denominator[:, :, None]
    final_doc = doc_ids[-1]
    staying = (doc_ids == final_doc).astype(jnp.float32)[:, None, None] * feat_k
    joined = (final_doc == previous).astype(jnp.float32)
    kv_state = jnp.einsum("rhf,rhv->hfv", staying, values_in, precision=EXACT) + joined * kv_state
    totals = jnp.sum(staying, axis=0) + joined * totals
    return ((kv_state, totals, final_doc), mixed_rows)


def attend(queries, keys_in, values_in, doc_ids):
    row_total, head_count, feature_dim = queries.shape
    value_dim = values_in.shape[2]
    block_count = row_total // BLK
    feature_total = 1 + feature_dim + feature_dim * (feature_dim + 1) // 2
    initial = (
        jnp.zeros((head_count, feature_total, value_dim), jnp.float32),
        jnp.zeros((head_count, feature_total), jnp.float32),
        jnp.array(-1, jnp.int32),
    )
    pieces = (
        queries.reshape(block_count, BLK, head_count, feature_dim),
        keys_in.reshape(block_count, BLK, head_count, feature_dim),
        values_in.reshape(block_count, BLK, head_count, value_dim),
        doc_ids.reshape(block_count, BLK),
    )
    last_carry, mixed_rows = lax.scan(jax.checkpoint(attend_block), initial, pieces)
    return mixed_rows.reshape(row_total, head_count * value_dim)


def document_ids(lengths_row, row_total):
    doc_ends = jnp.cumsum(lengths_row)
    places = jnp.arange(row_total, dtype=jnp.int32)
    return jnp.sum((places[:, None] >= doc_ends[None, :]).astype(jnp.int32), axis=1)


def rows_product(left, right):
    return lax.dot_general(
        left, right, (((0,), (0,)), ((), ())), preferred_element_type=jnp.float32
    )


def back_product(left, right):
    return lax.dot_general(
        left, right, (((1,), (1,)), ((), ())), preferred_element_type=jnp.float32
    )


def norm_back(grad_normed, normed, inverse, gain_full):
    scaled = grad_normed * gain_full
    return inverse * (scaled - normed * jnp.mean(scaled * normed, axis=-1, keepdims=True))


def row_slice(matrix, first_row, row_count):
    return lax.dynamic_slice_in_dim(matrix, first_row, row_count, 0)


def inverse_root(values):
    return lax.rsqrt(jnp.mean(values * values, axis=-1, keepdims=True) + 1e-05)


def fetch_weights(gain_attn, gain_mlp, w_query, w_key, w_value, w_out, w_gate, w_up, w_down):
    row_parts = (
        lax.all_gather(w_query, "dp", axis=0, tiled=True),
        lax.all_gather(w_key, "dp", axis=0, tiled=True),
        lax.all_gather(w_value, "dp", axis=0, tiled=True),
        lax.all_gather(w_gate, "dp", axis=0, tiled=True),
        lax.all_gather(w_up, "dp", axis=0, tiled=True),
        lax.all_gather(gain_attn, "dp", axis=0, tiled=True),
        lax.all_gather(gain_mlp, "dp", axis=0, tiled=True),
    )
    col_parts = (
        lax.all_gather(w_out, "dp", axis=1, tiled=True),
        lax.all_gather(w_down, "dp", axis=1, tiled=True),
    )
    return tuple(row_parts) + tuple(col_parts)


def plain_body(
    inputs,
    gain_attn,
    gain_mlp,
    w_query,
    w_key,
    w_value,
    w_out,
    w_gate,
    w_up,
    w_down,
    out_grad,
    lengths,
):
    micro_count = inputs.shape[0]
    shard_rows = inputs.shape[1]
    model_dim = inputs.shape[2]
    group_rows = shard_rows * lax.axis_size("tensor")
    local_heads = w_query.shape[1] // FEAT
    grad_query_sum = jnp.zeros((model_dim, w_query.shape[1]), jnp.float32)
    grad_key_sum = jnp.zeros((model_dim, w_key.shape[1]), jnp.float32)
    grad_value_sum = jnp.zeros((model_dim, w_value.shape[1]), jnp.float32)
    grad_gate_sum = jnp.zeros((model_dim, w_gate.shape[1]), jnp.float32)
    grad_up_sum = jnp.zeros((model_dim, w_up.shape[1]), jnp.float32)
    grad_out_sum = jnp.zeros((w_out.shape[0], model_dim), jnp.float32)
    grad_down_sum = jnp.zeros((w_down.shape[0], model_dim), jnp.float32)
    gain_attn_sum = jnp.zeros((model_dim,), jnp.float32)
    gain_mlp_sum = jnp.zeros((model_dim,), jnp.float32)
    outputs = []
    input_grads = []
    for micro_step in range(micro_count):
        (
            full_query,
            full_key,
            full_value,
            full_gate,
            full_up,
            full_gain_attn,
            full_gain_mlp,
            full_out,
            full_down,
        ) = fetch_weights(gain_attn, gain_mlp, w_query, w_key, w_value, w_out, w_gate, w_up, w_down)
        gain_in = full_gain_attn.astype(jnp.float32)
        gain_mid = full_gain_mlp.astype(jnp.float32)
        doc_ids = document_ids(lengths[micro_step, 0], group_rows)
        values = inputs[micro_step].astype(jnp.float32)
        inverse_in = inverse_root(values)
        normed_in = values * inverse_in
        gathered_in = lax.all_gather(
            (normed_in * gain_in).astype(jnp.bfloat16), "tensor", axis=0, tiled=True
        )
        query_low = jnp.dot(gathered_in, full_query, preferred_element_type=jnp.float32).astype(
            jnp.bfloat16
        )
        key_low = jnp.dot(gathered_in, full_key, preferred_element_type=jnp.float32).astype(
            jnp.bfloat16
        )
        value_low = jnp.dot(gathered_in, full_value, preferred_element_type=jnp.float32).astype(
            jnp.bfloat16
        )
        query_full = query_low.astype(jnp.float32).reshape(group_rows, local_heads, FEAT)
        key_full = key_low.astype(jnp.float32).reshape(group_rows, local_heads, FEAT)
        value_full = value_low.astype(jnp.float32).reshape(group_rows, local_heads, VD)

        def local_attend(query_arg, key_arg, value_arg):
            return attend(query_arg, key_arg, value_arg, doc_ids)

        mixed_full, pullback = jax.vjp(local_attend, query_full, key_full, value_full)
        mixed_low = mixed_full.astype(jnp.bfloat16)
        residual = values + lax.psum_scatter(
            jnp.dot(
                row_slice(mixed_low, jnp.int32(0), shard_rows * lax.axis_size("tensor")),
                full_out,
                preferred_element_type=jnp.float32,
            ),
            "tensor",
            scatter_dimension=0,
            tiled=True,
        )
        inverse_mid = inverse_root(residual)
        normed_mid = residual * inverse_mid
        gathered_mid = lax.all_gather(
            (normed_mid * gain_mid).astype(jnp.bfloat16), "tensor", axis=0, tiled=True
        )
        gate_pre = jnp.dot(gathered_mid, full_gate, preferred_element_type=jnp.float32)
        up_pre = jnp.dot(gathered_mid, full_up, preferred_element_type=jnp.float32)
        sigmoid_gate = jax.nn.sigmoid(gate_pre)
        silu_gate = gate_pre * sigmoid_gate
        hidden = (silu_gate * up_pre).astype(jnp.bfloat16)
        mlp_part = lax.psum_scatter(
            jnp.dot(
                row_slice(hidden, jnp.int32(0), shard_rows * lax.axis_size("tensor")),
                full_down,
                preferred_element_type=jnp.float32,
            ).astype(jnp.bfloat16),
            "tensor",
            scatter_dimension=0,
            tiled=True,
        ).astype(jnp.float32)
        outputs.append((residual + mlp_part).astype(jnp.bfloat16))
        cotangent = out_grad[micro_step]
        gathered_grad = lax.all_gather(cotangent, "tensor", axis=0, tiled=True)
        grad_down_sum += rows_product(hidden, gathered_grad)
        grad_hidden = back_product(gathered_grad, full_down)
        grad_gate_low = (
            grad_hidden * up_pre * sigmoid_gate * (1.0 + gate_pre * (1.0 - sigmoid_gate))
        ).astype(jnp.bfloat16)
        grad_up_low = (grad_hidden * silu_gate).astype(jnp.bfloat16)
        grad_gate_sum += rows_product(gathered_mid, grad_gate_low)
        grad_up_sum += rows_product(gathered_mid, grad_up_low)
        first_row = jnp.int32(0)
        grad_mid = lax.psum_scatter(
            back_product(
                row_slice(grad_gate_low, first_row, shard_rows * lax.axis_size("tensor")), full_gate
            )
            + back_product(
                row_slice(grad_up_low, first_row, shard_rows * lax.axis_size("tensor")), full_up
            ),
            "tensor",
            scatter_dimension=0,
            tiled=True,
        )
        gain_mlp_sum += jnp.sum(grad_mid * normed_mid, axis=0)
        grad_resid = cotangent.astype(jnp.float32) + norm_back(
            grad_mid, normed_mid, inverse_mid, gain_mid
        )
        gathered_resid = lax.all_gather(
            grad_resid.astype(jnp.bfloat16), "tensor", axis=0, tiled=True
        )
        grad_out_sum += rows_product(mixed_low, gathered_resid)
        grad_mixed = back_product(gathered_resid, full_out).astype(jnp.bfloat16).astype(jnp.float32)
        grad_query_full, grad_key_full, grad_value_full = pullback(grad_mixed)
        grad_query_low = grad_query_full.reshape(group_rows, -1).astype(jnp.bfloat16)
        grad_key_low = grad_key_full.reshape(group_rows, -1).astype(jnp.bfloat16)
        grad_value_low = grad_value_full.reshape(group_rows, -1).astype(jnp.bfloat16)
        grad_query_sum += rows_product(gathered_in, grad_query_low)
        grad_key_sum += rows_product(gathered_in, grad_key_low)
        grad_value_sum += rows_product(gathered_in, grad_value_low)
        attn_first_row = jnp.int32(0)
        grad_in = lax.psum_scatter(
            (
                back_product(
                    row_slice(grad_query_low, attn_first_row, shard_rows * lax.axis_size("tensor")),
                    full_query,
                )
                + back_product(
                    row_slice(grad_key_low, attn_first_row, shard_rows * lax.axis_size("tensor")),
                    full_key,
                )
                + back_product(
                    row_slice(grad_value_low, attn_first_row, shard_rows * lax.axis_size("tensor")),
                    full_value,
                )
            ).astype(jnp.bfloat16),
            "tensor",
            scatter_dimension=0,
            tiled=True,
        ).astype(jnp.float32)
        gain_attn_sum += jnp.sum(grad_in * normed_in, axis=0)
        input_grads.append(grad_resid + norm_back(grad_in, normed_in, inverse_in, gain_in))
    row_grads = (
        lax.psum_scatter(
            grad_query_sum.astype(jnp.bfloat16), "dp", scatter_dimension=0, tiled=True
        ).astype(jnp.float32),
        lax.psum_scatter(
            grad_key_sum.astype(jnp.bfloat16), "dp", scatter_dimension=0, tiled=True
        ).astype(jnp.float32),
        lax.psum_scatter(
            grad_value_sum.astype(jnp.bfloat16), "dp", scatter_dimension=0, tiled=True
        ).astype(jnp.float32),
        lax.psum_scatter(
            grad_gate_sum.astype(jnp.bfloat16), "dp", scatter_dimension=0, tiled=True
        ).astype(jnp.float32),
        lax.psum_scatter(
            grad_up_sum.astype(jnp.bfloat16), "dp", scatter_dimension=0, tiled=True
        ).astype(jnp.float32),
        lax.psum_scatter(
            gain_attn_sum.astype(jnp.bfloat16), "dp", scatter_dimension=0, tiled=True
        ).astype(jnp.float32),
        lax.psum_scatter(
            gain_mlp_sum.astype(jnp.bfloat16), "dp", scatter_dimension=0, tiled=True
        ).astype(jnp.float32),
    )
    col_grads = (
        lax.psum_scatter(
            grad_out_sum.astype(jnp.bfloat16), "dp", scatter_dimension=1, tiled=True
        ).astype(jnp.float32),
        lax.psum_scatter(
            grad_down_sum.astype(jnp.bfloat16), "dp", scatter_dimension=1, tiled=True
        ).astype(jnp.float32),
    )
    gain_grads = lax.psum((row_grads[5], row_grads[6]), "tensor")
    return (
        jnp.stack(outputs, 0),
        jnp.stack(input_grads, 0),
        gain_grads[0],
        gain_grads[1],
        row_grads[0],
        row_grads[1],
        row_grads[2],
        col_grads[0],
        row_grads[3],
        row_grads[4],
        col_grads[1],
    )


F32 = jnp.float32
BF16 = jnp.bfloat16
NN = (((1,), (0,)), ((), ()))
NT = (((1,), (1,)), ((), ()))
TN = (((0,), (0,)), ((), ()))
TILE = 256
SPAN = 2
CHUNK = 512
VMEM_BYTES = 60 << 20


def mm(left, right, dims=NN):
    return lax.dot_general(left, right, dims, preferred_element_type=F32)


def params():
    return pltpu.CompilerParams(vmem_limit_bytes=VMEM_BYTES)


def anywhere():
    return pl.BlockSpec(memory_space=pl.ANY)


def exchange(value, bit):
    count = lax.axis_size("dp")
    return lax.ppermute(value, "dp", [(i, i ^ bit) for i in range(count)])


def swap(value):
    return lax.ppermute(value, "tensor", [(0, 1), (1, 0)])


def gather_slab(slab):
    half = slab.shape[0] // 2
    far = lax.axis_size("dp") // 4
    line = [slab] + [exchange(slab, 4 * k) for k in range(1, far)]
    upper = jnp.stack([s[:half] for s in line])
    lower = jnp.stack([s[half:] for s in line])
    upper_y = exchange(upper, 2)
    lower_x = exchange(lower, 1)
    upper_x = exchange(upper, 1)
    lower_y = exchange(lower, 2)
    return (upper, lower, upper_x, lower_x, upper_y, lower_y, exchange(upper_y, 1), exchange(lower_x, 2))


def place_slab(pieces, dest, sems):
    me = lax.axis_index("dp")
    far, half = pieces[0].shape[0], pieces[0].shape[1]
    copies = []
    for index, piece in enumerate(pieces):
        for k in range(far):
            row = (me ^ (4 * k + index // 2)) * (2 * half) + (index % 2) * half
            copies.append(
                pltpu.make_async_copy(
                    piece.at[k], dest.at[pl.ds(pl.multiple_of(row, half), half)], sems.at[index, k]
                )
            )
    for copy in copies:
        copy.start()
    for copy in copies:
        copy.wait()


def grad_shapes(rows, columns):
    far = lax.axis_size("dp") // 4
    half = rows // lax.axis_size("dp") // 2
    return [jax.ShapeDtypeStruct((far, 2 * half, columns), BF16)] + [
        jax.ShapeDtypeStruct((far, half, columns), BF16)
    ] * 6


def grad_specs(shapes):
    return [pl.BlockSpec(s.shape, lambda *_: (0, 0, 0)) for s in shapes]


def split_grads(total, outs):
    me = lax.axis_index("dp")
    far, rows = outs[0].shape[0], outs[0].shape[1]
    half = rows // 2
    for k in range(far):
        for xy in range(4):
            row = pl.multiple_of((me ^ (4 * k + xy)) * rows, rows)
            if xy == 0:
                outs[0][k] = total[pl.ds(row, rows)].astype(BF16)
            else:
                outs[2 * xy - 1][k] = total[pl.ds(row, half)].astype(BF16)
                outs[2 * xy][k] = total[pl.ds(pl.multiple_of(row + half, half), half)].astype(BF16)


def add(*terms):
    total = terms[0].astype(F32)
    for term in terms[1:]:
        total = total + term.astype(F32)
    return total


def scatter_grads(pieces):
    own, x_up, x_low, y_up, y_low, d_up, d_low = pieces
    half = x_up.shape[1]
    got_y_up = exchange(d_up, 1)
    got_x_low = exchange(d_low, 2)
    got_x_up = exchange(x_up, 1)
    got_y_low = exchange(y_low, 2)
    from_y_up = exchange(add(y_up, got_y_up).astype(BF16), 2)
    from_x_low = exchange(add(x_low, got_x_low).astype(BF16), 1)
    sums = []
    for k in range(own.shape[0]):
        top = add(own[k, :half], got_x_up[k], from_y_up[k])
        low = add(own[k, half:], from_x_low[k], got_y_low[k])
        sums.append(jnp.concatenate([top, low], 0))
    arrived = [exchange(sums[k].astype(BF16), 4 * k) for k in range(1, own.shape[0])]
    return add(sums[0], *arrived)


def dma_sems(far):
    return pltpu.SemaphoreType.DMA((8, far))


def own_block(width, micro, rows):
    return pl.BlockSpec((1, rows, width), lambda i, c: (jnp.maximum(i - micro, 0), 0, 0))


def other_block(width, micro, rows):
    return pl.BlockSpec((1, rows, width), lambda i, c: (jnp.minimum(i, micro - 1), 0, 0))


def group_block(width, micro, rows, column=0):
    def place(i, c):
        return (lax.rem(i, micro), jnp.where(i < micro, 1 - c[0], c[0]), column)

    return pl.BlockSpec((1, rows, width), place)


def rows_kernel(kernel, name, core, micro, in_specs, out_specs, out_shape, scratch, operands):
    return pl.pallas_call(
        kernel,
        grid_spec=pltpu.PrefetchScalarGridSpec(
            num_scalar_prefetch=1,
            grid=(2 * micro,),
            in_specs=in_specs,
            out_specs=out_specs,
            scratch_shapes=scratch,
        ),
        out_shape=out_shape,
        compiler_params=params(),
        name=name,
    )(core, *operands)


def pick(is_other, other_ref, own_ref):
    return jnp.where(is_other, other_ref[0], own_ref[0])


def put(is_other, other_ref, own_ref, value):
    @pl.when(is_other)
    def _():
        other_ref[0] = value

    @pl.when(jnp.logical_not(is_other))
    def _():
        own_ref[0] = value


def spread_gains(slab, column):
    dim = slab.shape[0]
    blocks = lax.axis_size("dp")
    each = dim // blocks
    lane_block = lax.broadcasted_iota(jnp.int32, (blocks, dim), 1) // each
    block = lax.broadcasted_iota(jnp.int32, (blocks, dim), 0)
    rows = []
    for which in range(2):
        picked = jnp.concatenate(
            [slab[each * b : each * b + 16, column : column + 128].astype(F32)[which : which + 1] for b in range(blocks)], 0
        )
        tiled = jnp.concatenate([picked] * (dim // 128), 1)
        rows.append(jnp.sum(jnp.where(lane_block == block, tiled, 0.0), axis=0, keepdims=True))
    return jnp.concatenate(rows + [jnp.zeros((6, dim), F32)], 0)


def project_kernel(micro, core, own, other, *refs):
    pieces, (h_out, qkv_out, gain_out, slab, sems) = refs[:8], refs[8:]
    i = pl.program_id(0)
    columns = qkv_out.shape[2]

    @pl.when(i == 0)
    def _():
        place_slab(pieces, slab, sems)
        gain_out[...] = spread_gains(slab, columns)

    x = pick(i < micro, other, own).astype(F32)
    inverse = lax.rsqrt(jnp.mean(x * x, axis=-1, keepdims=True) + 1e-05)
    h = (x * inverse * gain_out[0:1]).astype(BF16)
    h_out[0] = h
    qkv_out[0] = mm(h, slab[:, :columns]).astype(BF16)


def project(core, x_own, x_other, pieces, columns):
    micro, rows, dim = x_own.shape
    return rows_kernel(
        functools.partial(project_kernel, micro),
        "project",
        core,
        micro,
        [own_block(dim, micro, rows), other_block(dim, micro, rows)] + [anywhere()] * 8,
        [
            group_block(dim, micro, rows),
            group_block(columns, micro, rows),
            pl.BlockSpec((8, dim), lambda i, c: (0, 0)),
        ],
        [
            jax.ShapeDtypeStruct((micro, 2 * rows, dim), BF16),
            jax.ShapeDtypeStruct((micro, 2 * rows, columns), BF16),
            jax.ShapeDtypeStruct((8, dim), F32),
        ],
        [pltpu.VMEM((dim, pieces[0].shape[2]), BF16), dma_sems(pieces[0].shape[0])],
        (x_own, x_other, *pieces),
    )


def first_lane(lane):
    return (lane == 0).astype(F32).astype(BF16)


def attend_kernel(q_ref, k_ref, v_ref, start_ref, mix_ref, inv_ref, keys, mask, queries, values):
    pair = pl.program_id(1)
    group = q_ref.shape[1]
    tiles = group // TILE
    lane = lax.broadcasted_iota(jnp.int32, (group, 128), 1)

    @pl.when(pair == 0)
    def _():
        keys[:, :128] = k_ref[0]
        keys[:, 128:] = first_lane(lane)
        for i in range(tiles):
            j = max(0, i - SPAN)
            wide = (i - j + 1) * TILE
            column = lax.broadcasted_iota(jnp.int32, (TILE, wide), 1) + j * TILE
            row = lax.broadcasted_iota(jnp.int32, (TILE, wide), 0) + i * TILE
            allowed = (column <= row) & (column >= start_ref[0, i * TILE : (i + 1) * TILE, :])
            mask[i * TILE : (i + 1) * TILE, :wide] = jnp.where(allowed, 1.0, 0.0)

    query = q_ref[0].astype(F32)
    value = v_ref[0].astype(F32)
    for side in range(2):
        queries[side, :, :128] = jnp.where(lane // FEAT == 2 * pair + side, query * 0.25, 0.0).astype(BF16)
        queries[side, :, 128:] = first_lane(lane)
        mine = lane // VD == side
        values[side, :, :128] = jnp.where(mine, value, 0.0).astype(BF16)
        values[side, :, 128:] = mine.astype(F32).astype(BF16)
    for i in range(tiles):
        j = max(0, i - SPAN)
        wide = (i - j + 1) * TILE
        here = slice(i * TILE, (i + 1) * TILE)
        total = None
        for side in range(2):
            t = mm(queries[side, here], keys[j * TILE : (i + 1) * TILE], NT)
            weights = ((t * t + 1.0) * mask[here, :wide]).astype(BF16)
            part = mm(weights, values[side, j * TILE : (i + 1) * TILE])
            total = part if total is None else total + part
        inverse = 1.0 / total[:, 128:]
        mix_ref[0, here, :] = (total[:, :128] * inverse).astype(BF16)
        inv_ref[0, here, :] = inverse


def lanes_at(group, column):
    return pl.BlockSpec((1, group, 128), lambda m, p: (m, 0, column))


def lanes_of_pair(group, first):
    return pl.BlockSpec((1, group, 128), lambda m, p: (m, 0, first + p))


def attend_all(qkv, starts):
    micro, group, columns = qkv.shape
    wide = columns - 256
    pair = lanes_of_pair(group, 0)
    return pl.pallas_call(
        attend_kernel,
        grid=(micro, wide // 128),
        in_specs=[
            lanes_at(group, 0),
            lanes_at(group, 1),
            lanes_of_pair(group, 2),
            pl.BlockSpec((1, group, 1), lambda m, p: (m, 0, 0)),
        ],
        out_specs=[pair, pair],
        out_shape=[
            jax.ShapeDtypeStruct((micro, group, wide), BF16),
            jax.ShapeDtypeStruct((micro, group, wide), F32),
        ],
        scratch_shapes=[
            pltpu.VMEM((group, 256), BF16),
            pltpu.VMEM((group, TILE * (SPAN + 1)), F32),
            pltpu.VMEM((2, group, 256), BF16),
            pltpu.VMEM((2, group, 256), BF16),
        ],
        compiler_params=params(),
        name="attend",
    )(qkv, qkv, qkv, starts)


def attend_back_kernel(
    q_ref, k_ref, v_ref, mix_ref, inv_ref, dmix_ref, start_ref, dq_ref, dk_ref, dv_ref,
    keys, keys_t, mask, queries, values, douts, scaled_q, scaled_d, dk_sum, dq_t, scale,
):
    pair = pl.program_id(1)
    group = q_ref.shape[1]
    tiles = group // TILE
    lane = lax.broadcasted_iota(jnp.int32, (group, 128), 1)

    @pl.when(pair == 0)
    def _():
        keys[:, :128] = k_ref[0]
        keys[:, 128:] = first_lane(lane)
        keys_t[...] = k_ref[0].astype(F32).T.astype(BF16)
        for j in range(tiles):
            i = min(tiles, j + SPAN + 1)
            wide = (i - j) * TILE
            column = lax.broadcasted_iota(jnp.int32, (TILE, wide), 0) + j * TILE
            row = lax.broadcasted_iota(jnp.int32, (TILE, wide), 1) + j * TILE
            allowed = (column <= row) & (column >= start_ref[0, :, j * TILE : i * TILE])
            mask[j * TILE : (j + 1) * TILE, :wide] = jnp.where(allowed, 1.0, 0.0)
        dk_sum[...] = jnp.zeros_like(dk_sum)
        scale[...] = jnp.zeros_like(scale)

    query = q_ref[0].astype(F32)
    dmix = dmix_ref[0].astype(F32)
    inverse = inv_ref[0]
    values[:, :128] = v_ref[0]
    values[:, 128:] = (lane < 2).astype(F32).astype(BF16)
    product = dmix * mix_ref[0].astype(F32)
    for side in range(2):
        mine = lane // VD == side
        head = lane // FEAT == 2 * pair + side
        masked = jnp.where(head, query, 0.0)
        queries[side, :, :128] = (masked * 0.25).astype(BF16)
        queries[side, :, 128:] = first_lane(lane)
        delta = jnp.sum(jnp.where(mine, product, 0.0), axis=1, keepdims=True)
        coarse = delta.astype(BF16).astype(F32)
        douts[side, :, :128] = jnp.where(mine, dmix, 0.0).astype(BF16)
        douts[side, :, 128:] = jnp.where(lane == 0, -coarse, jnp.where(lane == 1, coarse - delta, 0.0)).astype(BF16)
        half_inverse = inverse[:, VD * side : VD * side + 1] * 0.5
        scaled_q[side] = (masked * half_inverse).astype(BF16)
        scaled_d[side] = jnp.where(mine, dmix * inverse, 0.0).astype(BF16)
        scale[...] += jnp.where(head, half_inverse, 0.0)
    for j in range(tiles):
        i = min(tiles, j + SPAN + 1)
        here = slice(j * TILE, (j + 1) * TILE)
        below = slice(j * TILE, i * TILE)
        allowed = mask[here, : (i - j) * TILE]
        dv = None
        dk = None
        for side in range(2):
            t = mm(keys[here], queries[side, below], NT)
            slope = mm(values[here], douts[side, below], NT)
            masked_t = t * allowed
            d_t = (slope * masked_t).astype(BF16)
            weights = (t * masked_t + allowed).astype(BF16)
            dv_part = mm(weights, scaled_d[side, below])
            dk_part = mm(d_t, scaled_q[side, below])
            dv = dv_part if dv is None else dv + dv_part
            dk = dk_part if dk is None else dk + dk_part
            rows = pl.ds(pl.multiple_of((2 * pair + side) * FEAT, FEAT), FEAT)
            dq_part = mm(keys_t[rows, here], d_t)
            for r in range(j, i):
                piece = dq_part[:, (r - j) * TILE : (r - j + 1) * TILE]
                if j == max(0, r - SPAN):
                    dq_t[rows, r * TILE : (r + 1) * TILE] = piece
                else:
                    dq_t[rows, r * TILE : (r + 1) * TILE] += piece
        dv_ref[0, here, :] = dv.astype(BF16)
        dk_sum[here] += dk

    @pl.when(pair == pl.num_programs(1) - 1)
    def _():
        dk_ref[0] = dk_sum[...].astype(BF16)
        dq_ref[0] = (dq_t[...].T * scale[...]).astype(BF16)


def attend_back(qkv, mix, inverse, dmix, starts):
    micro, group, columns = qkv.shape
    wide = columns - 256
    pair = lanes_of_pair(group, 0)
    narrow = jax.ShapeDtypeStruct((micro, group, 128), BF16)
    return pl.pallas_call(
        attend_back_kernel,
        grid=(micro, wide // 128),
        in_specs=[
            lanes_at(group, 0),
            lanes_at(group, 1),
            lanes_of_pair(group, 2),
            pair,
            pair,
            pair,
            pl.BlockSpec((1, 1, group), lambda m, p: (m, 0, 0)),
        ],
        out_specs=[lanes_at(group, 0), lanes_at(group, 0), pair],
        out_shape=[narrow, narrow, jax.ShapeDtypeStruct((micro, group, wide), BF16)],
        scratch_shapes=[
            pltpu.VMEM((group, 256), BF16),
            pltpu.VMEM((128, group), BF16),
            pltpu.VMEM((group, TILE * (SPAN + 1)), F32),
            pltpu.VMEM((2, group, 256), BF16),
            pltpu.VMEM((group, 256), BF16),
            pltpu.VMEM((2, group, 256), BF16),
            pltpu.VMEM((2, group, 128), BF16),
            pltpu.VMEM((2, group, 128), BF16),
            pltpu.VMEM((group, 128), F32),
            pltpu.VMEM((128, group), F32),
            pltpu.VMEM((group, 128), F32),
        ],
        compiler_params=params(),
        name="attend_back",
    )(qkv, qkv, qkv, mix, inverse, dmix, starts)


def out_kernel(micro, core, mix, *refs):
    pieces, (own, other, slab, sems) = refs[:8], refs[8:]
    i = pl.program_id(0)

    @pl.when(i == 0)
    def _():
        place_slab(pieces, slab, sems)

    put(i < micro, other, own, mm(mix[0], slab[...], NT).astype(BF16))


def out_project(core, mix, pieces):
    micro, group, wide = mix.shape
    rows = group // 2
    far, half, columns = pieces[0].shape
    dim = far * half * 8
    shape = jax.ShapeDtypeStruct((micro, rows, dim), BF16)
    return rows_kernel(
        functools.partial(out_kernel, micro),
        "out_project",
        core,
        micro,
        [group_block(wide, micro, rows)] + [anywhere()] * 8,
        [own_block(dim, micro, rows), other_block(dim, micro, rows)],
        [shape, shape],
        [pltpu.VMEM((dim, columns), BF16), dma_sems(far)],
        (mix, *pieces),
    )


def mid_kernel(x, own, got, gains, resid_out, h_out):
    resid = x[0].astype(F32) + own[0].astype(F32) + got[0].astype(F32)
    inverse = lax.rsqrt(jnp.mean(resid * resid, axis=-1, keepdims=True) + 1e-05)
    resid_out[0] = resid.astype(BF16)
    h_out[0] = (resid * inverse * gains[1:2]).astype(BF16)


def local_call(kernel, name, arrays, gains, out_types):
    micro, rows, dim = arrays[0].shape
    tile = min(rows, 256)
    block = pl.BlockSpec((1, tile, dim), lambda m, t: (m, t, 0))
    return pl.pallas_call(
        kernel,
        grid=(micro, rows // tile),
        in_specs=[block] * len(arrays) + [pl.BlockSpec((8, dim), lambda m, t: (0, 0))],
        out_specs=[block] * len(out_types),
        out_shape=[jax.ShapeDtypeStruct((micro, rows, dim), t) for t in out_types],
        compiler_params=params(),
        name=name,
    )(*arrays, gains)


def feed_kernel(micro, width, first, core, h_own, h_other, g_own, g_other, *refs):
    if first:
        before = None
    else:
        before, refs = refs[:4], refs[4:]
    pieces, refs = refs[:8], refs[8:]
    out_own, out_other, dm_own, dm_other = refs[:4]
    grads, (slab, total, hidden_s, dgu_s, sems) = refs[4:11], refs[11:]
    i = pl.program_id(0)
    is_other = i < micro

    @pl.when(i == 0)
    def _():
        place_slab(pieces, slab, sems)
        total[...] = jnp.zeros_like(total)

    w_gu = slab[:, : 2 * width]
    w_down = slab[:, 2 * width :]
    h = pick(is_other, h_other, h_own)
    g = pick(is_other, g_other, g_own)
    gate_up = mm(h, w_gu)
    d_hidden = mm(g, w_down)
    gate = gate_up[:, :width]
    up = gate_up[:, width:]
    sigmoid = 0.5 * jnp.tanh(0.5 * gate) + 0.5
    silu = gate * sigmoid
    hidden_s[...] = (silu * up).astype(BF16)
    dgu_s[:, :width] = (d_hidden * up * (sigmoid + silu * (1.0 - sigmoid))).astype(BF16)
    dgu_s[:, width:] = (d_hidden * silu).astype(BF16)
    out = mm(hidden_s[...], w_down, NT)
    dm = mm(dgu_s[...], w_gu, NT)
    if not first:
        out = out + pick(is_other, before[1], before[0]).astype(F32)
        dm = dm + pick(is_other, before[3], before[2]).astype(F32)
    put(is_other, out_other, out_own, out.astype(BF16))
    put(is_other, dm_other, dm_own, dm.astype(BF16))
    total[:, : 2 * width] += mm(h, dgu_s[...], TN)
    total[:, 2 * width :] += mm(g, hidden_s[...], TN)

    @pl.when(i == 2 * micro - 1)
    def _():
        split_grads(total, grads)


def feed(core, h_own, h_other, g_own, g_other, before, pieces):
    micro, rows, dim = h_own.shape
    far, half, columns = pieces[0].shape
    own = own_block(dim, micro, rows)
    other = other_block(dim, micro, rows)
    shape = jax.ShapeDtypeStruct((micro, rows, dim), BF16)
    grads = grad_shapes(dim, columns)
    first = before is None
    results = rows_kernel(
        functools.partial(feed_kernel, micro, columns // 3, first),
        "feed",
        core,
        micro,
        [own, other, own, other] + ([] if first else [own, other, own, other]) + [anywhere()] * 8,
        [own, other, own, other] + grad_specs(grads),
        [shape] * 4 + grads,
        [
            pltpu.VMEM((dim, columns), BF16),
            pltpu.VMEM((dim, columns), F32),
            pltpu.VMEM((rows, columns // 3), BF16),
            pltpu.VMEM((rows, 2 * (columns // 3)), BF16),
            dma_sems(far),
        ],
        (h_own, h_other, g_own, g_other) + (() if first else tuple(before)) + tuple(pieces),
    )
    return results[:4], results[4:]


def back_mid_kernel(resid, own, got, g, gains, d_out):
    res = resid[0].astype(F32)
    inverse = lax.rsqrt(jnp.mean(res * res, axis=-1, keepdims=True) + 1e-05)
    normed = res * inverse
    scaled = (own[0].astype(F32) + got[0].astype(F32)) * gains[1:2]
    slope = inverse * (scaled - normed * jnp.mean(scaled * normed, axis=-1, keepdims=True))
    d_out[0] = (g[0].astype(F32) + slope).astype(BF16)


def back_in_kernel(x, own, got, d, gains, grad_out):
    values = x[0].astype(F32)
    inverse = lax.rsqrt(jnp.mean(values * values, axis=-1, keepdims=True) + 1e-05)
    normed = values * inverse
    scaled = (own[0].astype(F32) + got[0].astype(F32)) * gains[0:1]
    slope = inverse * (scaled - normed * jnp.mean(scaled * normed, axis=-1, keepdims=True))
    grad_out[0] = d[0].astype(F32) + slope


def back_out_kernel(micro, core, d_own, d_other, mix, *refs):
    pieces, dmix, grads, (slab, total, sems) = refs[:8], refs[8], refs[9:16], refs[16:]
    i = pl.program_id(0)

    @pl.when(i == 0)
    def _():
        place_slab(pieces, slab, sems)
        total[...] = jnp.zeros_like(total)

    d = pick(i < micro, d_other, d_own)
    dmix[0] = mm(d, slab[...]).astype(BF16)
    total[...] += mm(d, mix[0], TN)

    @pl.when(i == 2 * micro - 1)
    def _():
        split_grads(total, grads)


def back_out(core, d_own, d_other, mix, pieces):
    micro, rows, dim = d_own.shape
    far, half, columns = pieces[0].shape
    grads = grad_shapes(dim, columns)
    results = rows_kernel(
        functools.partial(back_out_kernel, micro),
        "back_out",
        core,
        micro,
        [own_block(dim, micro, rows), other_block(dim, micro, rows), group_block(columns, micro, rows)]
        + [anywhere()] * 8,
        [group_block(columns, micro, rows)] + grad_specs(grads),
        [jax.ShapeDtypeStruct((micro, 2 * rows, columns), BF16)] + grads,
        [pltpu.VMEM((dim, columns), BF16), pltpu.VMEM((dim, columns), F32), dma_sems(far)],
        (d_own, d_other, mix, *pieces),
    )
    return results[0], results[1:]


def grad_qkv_kernel(micro, core, h, dq, dk, dv, *refs):
    grads, total = refs[:7], refs[7]
    i = pl.program_id(0)

    @pl.when(i == 0)
    def _():
        total[...] = jnp.zeros_like(total)

    total[...] += mm(h[0], jnp.concatenate([dq[0], dk[0], dv[0]], 1), TN)

    @pl.when(i == 2 * micro - 1)
    def _():
        split_grads(total, grads)


def grad_qkv(core, h, dq, dk, dv):
    micro, group, dim = h.shape
    rows = group // 2
    widths = [dq.shape[2], dk.shape[2], dv.shape[2]]
    grads = grad_shapes(dim, sum(widths))
    return rows_kernel(
        functools.partial(grad_qkv_kernel, micro),
        "grad_qkv",
        core,
        micro,
        [group_block(w, micro, rows) for w in [dim] + widths],
        grad_specs(grads),
        grads,
        [pltpu.VMEM((dim, sum(widths)), F32)],
        (h, dq, dk, dv),
    )


def back_in_project_kernel(micro, core, dq, dk, dv, *refs):
    pieces, (own, other, slab, sems) = refs[:8], refs[8:]
    i = pl.program_id(0)

    @pl.when(i == 0)
    def _():
        place_slab(pieces, slab, sems)

    d = jnp.concatenate([dq[0], dk[0], dv[0]], 1)
    put(i < micro, other, own, mm(d, slab[:, : d.shape[1]], NT).astype(BF16))


def back_in_project(core, dq, dk, dv, pieces):
    micro, group, _ = dq.shape
    rows = group // 2
    far, half, columns = pieces[0].shape
    dim = far * half * 8
    shape = jax.ShapeDtypeStruct((micro, rows, dim), BF16)
    return rows_kernel(
        functools.partial(back_in_project_kernel, micro),
        "back_in_project",
        core,
        micro,
        [group_block(a.shape[2], micro, rows) for a in (dq, dk, dv)] + [anywhere()] * 8,
        [own_block(dim, micro, rows), other_block(dim, micro, rows)],
        [shape, shape],
        [pltpu.VMEM((dim, columns), BF16), dma_sems(far)],
        (dq, dk, dv, *pieces),
    )


def fused_body(
    inputs, gain_attn, gain_mlp, w_query, w_key, w_value, w_out, w_gate, w_up, w_down, out_grad, lengths
):
    micro, rows, dim = inputs.shape
    group = rows * lax.axis_size("tensor")
    core = lax.axis_index("tensor").astype(jnp.int32).reshape(1)
    each = w_query.shape[0]
    units = w_gate.shape[1]

    gain_rows = jnp.stack([gain_attn, gain_mlp])
    gain_part = jnp.pad(jnp.concatenate([gain_rows, gain_rows], 1), ((0, each - 2), (0, 0)))
    slab_in = jnp.concatenate([w_query, w_key, w_value, gain_part], 1)
    widths_in = (w_query.shape[1], w_key.shape[1], w_value.shape[1])
    slab_out = w_out.T
    down_t = w_down.T
    padded = -(-units // 128) * 128
    edges = [(at, min(at + CHUNK, padded)) for at in range(0, padded, CHUNK)]
    slabs = []
    for low, high in edges:
        parts = [a[:, low : min(high, units)] for a in (w_gate, w_up, down_t)]
        slabs.append(jnp.concatenate([jnp.pad(a, ((0, 0), (0, high - low - a.shape[1]))) for a in parts], 1))

    ends = jnp.cumsum(lengths[:, 0], axis=-1)
    places = jnp.arange(group, dtype=jnp.int32)
    starts = jnp.max(jnp.where(places[None, :, None] >= ends[:, None, :], ends[:, None, :], 0), axis=-1)

    x_other = swap(inputs)
    pieces_in = gather_slab(slab_in)
    g_other = swap(out_grad)
    pieces_out = gather_slab(slab_out)
    pieces_feed = [gather_slab(s) for s in slabs]

    h_in, qkv, gains = project(core, inputs, x_other, pieces_in, sum(widths_in))
    mix, inverse = attend_all(qkv, starts.reshape(micro, group, 1))
    part_own, part_other = out_project(core, mix, pieces_out)
    resid, h_own = local_call(mid_kernel, "mid", [inputs, part_own, swap(part_other)], gains, [BF16, BF16])
    h_other = swap(h_own)

    sums = None
    feed_grads = []
    for pieces in pieces_feed:
        sums, grads = feed(core, h_own, h_other, out_grad, g_other, sums, pieces)
        feed_grads.append(scatter_grads(grads))
    out_own, out_other, dm_own, dm_other = sums
    (d_own,) = local_call(back_mid_kernel, "back_mid", [resid, dm_own, swap(dm_other), out_grad], gains, [BF16])
    mixed_out = add(resid, out_own, swap(out_other)).astype(BF16)
    dmix, grads = back_out(core, d_own, swap(d_own), mix, pieces_out)
    grad_out_t = scatter_grads(grads)
    dq, dk, dv = attend_back(qkv, mix, inverse, dmix, starts.reshape(micro, 1, group))
    grad_in = scatter_grads(grad_qkv(core, h_in, dq, dk, dv))
    din_own, din_other = back_in_project(core, dq, dk, dv, pieces_in)
    (input_grad,) = local_call(
        back_in_kernel, "back_in", [inputs, din_own, swap(din_other), d_own], gains, [F32]
    )

    def columns_of(at):
        kept = []
        for (low, high), grad in zip(edges, feed_grads):
            kept.append(grad[:, at * (high - low) : at * (high - low) + min(high, units) - low])
        return jnp.concatenate(kept, 1)

    grad_gate, grad_up, grad_down_t = columns_of(0), columns_of(1), columns_of(2)
    from_in = jnp.sum(slab_in[:, : sum(widths_in)].astype(F32) * grad_in, axis=1)
    from_mid = jnp.sum(w_gate.astype(F32) * grad_gate + w_up.astype(F32) * grad_up, axis=1)
    both = jnp.stack([from_in / gain_attn.astype(F32), from_mid / gain_mlp.astype(F32)])
    both = both + swap(both)
    at_key = widths_in[0]
    at_value = widths_in[0] + widths_in[1]
    return (
        mixed_out,
        input_grad,
        both[0],
        both[1],
        grad_in[:, :at_key],
        grad_in[:, at_key:at_value],
        grad_in[:, at_value:],
        grad_out_t.T,
        grad_gate,
        grad_up,
        grad_down_t.T,
    )


def solution(mesh):
    in_specs = (
        P(None, ("dp", "tensor"), None),
        P("dp"),
        P("dp"),
        P("dp", "tensor"),
        P("dp", "tensor"),
        P("dp", "tensor"),
        P("tensor", "dp"),
        P("dp", "tensor"),
        P("dp", "tensor"),
        P("tensor", "dp"),
        P(None, ("dp", "tensor"), None),
        P(None, "dp", None),
    )
    out_specs = (
        P(None, ("dp", "tensor"), None),
        P(None, ("dp", "tensor"), None),
        P("dp"),
        P("dp"),
        P("dp", "tensor"),
        P("dp", "tensor"),
        P("dp", "tensor"),
        P("tensor", "dp"),
        P("dp", "tensor"),
        P("dp", "tensor"),
        P("tensor", "dp"),
    )
    fits = mesh.shape["tensor"] == 2 and mesh.shape["dp"] % 4 == 0
    chosen = fused_body if fits else plain_body
    return jax.shard_map(chosen, mesh=mesh, in_specs=in_specs, out_specs=out_specs, check_vma=False)
```

```python
import functools
import math

import jax
import jax.numpy as jnp
import numpy as np
from jax import lax
from jax.experimental import pallas as pl
from jax.experimental.pallas import tpu as pltpu
from jax.sharding import PartitionSpec as P

FEAT = 16
VD = 64
BLK = 512


EXACT = lax.Precision.HIGHEST


def taylor(halved):
    feature_dim = halved.shape[-1]
    upper_idx, lower_idx = np.triu_indices(feature_dim)
    flat_index = jnp.asarray(upper_idx * feature_dim + lower_idx, jnp.int32)
    factors = jnp.asarray(np.where(upper_idx == lower_idx, math.sqrt(0.5), 1.0), jnp.float32)
    outer = (halved[..., :, None] * halved[..., None, :]).reshape(
        halved.shape[:-1] + (feature_dim * feature_dim,)
    )
    second = jnp.take(outer, flat_index, axis=-1) * factors
    ones_col = jnp.ones(halved.shape[:-1] + (1,), jnp.float32)
    return jnp.concatenate([ones_col, halved, second], axis=-1)


def attend_block(carry_in, block_in):
    kv_state, totals, previous = carry_in
    queries, keys_in, values_in, doc_ids = block_in
    half_q = 0.5 * queries
    half_k = 0.5 * keys_in
    scores = jnp.einsum("rhf,chf->hrc", half_q, half_k, preferred_element_type=jnp.float32)
    places = jnp.arange(doc_ids.shape[0], dtype=jnp.int32)
    allowed = (doc_ids[:, None] == doc_ids[None, :]) & (places[None, :] <= places[:, None])
    weights = jnp.where(allowed[None], 1.0 + scores + 0.5 * scores * scores, 0.0)
    feat_q = taylor(half_q)
    feat_k = taylor(half_k)
    carried_in = (doc_ids == previous).astype(jnp.float32)
    numerator = jnp.einsum("hrc,chv->rhv", weights, values_in, precision=EXACT) + carried_in[
        :, None, None
    ] * jnp.einsum("rhf,hfv->rhv", feat_q, kv_state, precision=EXACT)
    denominator = jnp.sum(weights, axis=2).T + carried_in[:, None] * jnp.einsum(
        "rhf,hf->rh", feat_q, totals, precision=EXACT
    )
    mixed_rows = numerator / denominator[:, :, None]
    final_doc = doc_ids[-1]
    staying = (doc_ids == final_doc).astype(jnp.float32)[:, None, None] * feat_k
    joined = (final_doc == previous).astype(jnp.float32)
    kv_state = jnp.einsum("rhf,rhv->hfv", staying, values_in, precision=EXACT) + joined * kv_state
    totals = jnp.sum(staying, axis=0) + joined * totals
    return ((kv_state, totals, final_doc), mixed_rows)


def attend(queries, keys_in, values_in, doc_ids):
    row_total, head_count, feature_dim = queries.shape
    value_dim = values_in.shape[2]
    block_count = row_total // BLK
    feature_total = 1 + feature_dim + feature_dim * (feature_dim + 1) // 2
    initial = (
        jnp.zeros((head_count, feature_total, value_dim), jnp.float32),
        jnp.zeros((head_count, feature_total), jnp.float32),
        jnp.array(-1, jnp.int32),
    )
    pieces = (
        queries.reshape(block_count, BLK, head_count, feature_dim),
        keys_in.reshape(block_count, BLK, head_count, feature_dim),
        values_in.reshape(block_count, BLK, head_count, value_dim),
        doc_ids.reshape(block_count, BLK),
    )
    last_carry, mixed_rows = lax.scan(jax.checkpoint(attend_block), initial, pieces)
    return mixed_rows.reshape(row_total, head_count * value_dim)


def document_ids(lengths_row, row_total):
    doc_ends = jnp.cumsum(lengths_row)
    places = jnp.arange(row_total, dtype=jnp.int32)
    return jnp.sum((places[:, None] >= doc_ends[None, :]).astype(jnp.int32), axis=1)


def rows_product(left, right):
    return lax.dot_general(
        left, right, (((0,), (0,)), ((), ())), preferred_element_type=jnp.float32
    )


def back_product(left, right):
    return lax.dot_general(
        left, right, (((1,), (1,)), ((), ())), preferred_element_type=jnp.float32
    )


def norm_back(grad_normed, normed, inverse, gain_full):
    scaled = grad_normed * gain_full
    return inverse * (scaled - normed * jnp.mean(scaled * normed, axis=-1, keepdims=True))


def row_slice(matrix, first_row, row_count):
    return lax.dynamic_slice_in_dim(matrix, first_row, row_count, 0)


def inverse_root(values):
    return lax.rsqrt(jnp.mean(values * values, axis=-1, keepdims=True) + 1e-05)


def fetch_weights(gain_attn, gain_mlp, w_query, w_key, w_value, w_out, w_gate, w_up, w_down):
    row_parts = (
        lax.all_gather(w_query, "dp", axis=0, tiled=True),
        lax.all_gather(w_key, "dp", axis=0, tiled=True),
        lax.all_gather(w_value, "dp", axis=0, tiled=True),
        lax.all_gather(w_gate, "dp", axis=0, tiled=True),
        lax.all_gather(w_up, "dp", axis=0, tiled=True),
        lax.all_gather(gain_attn, "dp", axis=0, tiled=True),
        lax.all_gather(gain_mlp, "dp", axis=0, tiled=True),
    )
    col_parts = (
        lax.all_gather(w_out, "dp", axis=1, tiled=True),
        lax.all_gather(w_down, "dp", axis=1, tiled=True),
    )
    return tuple(row_parts) + tuple(col_parts)


def plain_body(
    inputs,
    gain_attn,
    gain_mlp,
    w_query,
    w_key,
    w_value,
    w_out,
    w_gate,
    w_up,
    w_down,
    out_grad,
    lengths,
):
    micro_count = inputs.shape[0]
    shard_rows = inputs.shape[1]
    model_dim = inputs.shape[2]
    group_rows = shard_rows * lax.axis_size("tensor")
    local_heads = w_query.shape[1] // FEAT
    grad_query_sum = jnp.zeros((model_dim, w_query.shape[1]), jnp.float32)
    grad_key_sum = jnp.zeros((model_dim, w_key.shape[1]), jnp.float32)
    grad_value_sum = jnp.zeros((model_dim, w_value.shape[1]), jnp.float32)
    grad_gate_sum = jnp.zeros((model_dim, w_gate.shape[1]), jnp.float32)
    grad_up_sum = jnp.zeros((model_dim, w_up.shape[1]), jnp.float32)
    grad_out_sum = jnp.zeros((w_out.shape[0], model_dim), jnp.float32)
    grad_down_sum = jnp.zeros((w_down.shape[0], model_dim), jnp.float32)
    gain_attn_sum = jnp.zeros((model_dim,), jnp.float32)
    gain_mlp_sum = jnp.zeros((model_dim,), jnp.float32)
    outputs = []
    input_grads = []
    for micro_step in range(micro_count):
        (
            full_query,
            full_key,
            full_value,
            full_gate,
            full_up,
            full_gain_attn,
            full_gain_mlp,
            full_out,
            full_down,
        ) = fetch_weights(gain_attn, gain_mlp, w_query, w_key, w_value, w_out, w_gate, w_up, w_down)
        gain_in = full_gain_attn.astype(jnp.float32)
        gain_mid = full_gain_mlp.astype(jnp.float32)
        doc_ids = document_ids(lengths[micro_step, 0], group_rows)
        values = inputs[micro_step].astype(jnp.float32)
        inverse_in = inverse_root(values)
        normed_in = values * inverse_in
        gathered_in = lax.all_gather(
            (normed_in * gain_in).astype(jnp.bfloat16), "tensor", axis=0, tiled=True
        )
        query_low = jnp.dot(gathered_in, full_query, preferred_element_type=jnp.float32).astype(
            jnp.bfloat16
        )
        key_low = jnp.dot(gathered_in, full_key, preferred_element_type=jnp.float32).astype(
            jnp.bfloat16
        )
        value_low = jnp.dot(gathered_in, full_value, preferred_element_type=jnp.float32).astype(
            jnp.bfloat16
        )
        query_full = query_low.astype(jnp.float32).reshape(group_rows, local_heads, FEAT)
        key_full = key_low.astype(jnp.float32).reshape(group_rows, local_heads, FEAT)
        value_full = value_low.astype(jnp.float32).reshape(group_rows, local_heads, VD)

        def local_attend(query_arg, key_arg, value_arg):
            return attend(query_arg, key_arg, value_arg, doc_ids)

        mixed_full, pullback = jax.vjp(local_attend, query_full, key_full, value_full)
        mixed_low = mixed_full.astype(jnp.bfloat16)
        residual = values + lax.psum_scatter(
            jnp.dot(
                row_slice(mixed_low, jnp.int32(0), shard_rows * lax.axis_size("tensor")),
                full_out,
                preferred_element_type=jnp.float32,
            ),
            "tensor",
            scatter_dimension=0,
            tiled=True,
        )
        inverse_mid = inverse_root(residual)
        normed_mid = residual * inverse_mid
        gathered_mid = lax.all_gather(
            (normed_mid * gain_mid).astype(jnp.bfloat16), "tensor", axis=0, tiled=True
        )
        gate_pre = jnp.dot(gathered_mid, full_gate, preferred_element_type=jnp.float32)
        up_pre = jnp.dot(gathered_mid, full_up, preferred_element_type=jnp.float32)
        sigmoid_gate = jax.nn.sigmoid(gate_pre)
        silu_gate = gate_pre * sigmoid_gate
        hidden = (silu_gate * up_pre).astype(jnp.bfloat16)
        mlp_part = lax.psum_scatter(
            jnp.dot(
                row_slice(hidden, jnp.int32(0), shard_rows * lax.axis_size("tensor")),
                full_down,
                preferred_element_type=jnp.float32,
            ).astype(jnp.bfloat16),
            "tensor",
            scatter_dimension=0,
            tiled=True,
        ).astype(jnp.float32)
        outputs.append((residual + mlp_part).astype(jnp.bfloat16))
        cotangent = out_grad[micro_step]
        gathered_grad = lax.all_gather(cotangent, "tensor", axis=0, tiled=True)
        grad_down_sum += rows_product(hidden, gathered_grad)
        grad_hidden = back_product(gathered_grad, full_down)
        grad_gate_low = (
            grad_hidden * up_pre * sigmoid_gate * (1.0 + gate_pre * (1.0 - sigmoid_gate))
        ).astype(jnp.bfloat16)
        grad_up_low = (grad_hidden * silu_gate).astype(jnp.bfloat16)
        grad_gate_sum += rows_product(gathered_mid, grad_gate_low)
        grad_up_sum += rows_product(gathered_mid, grad_up_low)
        first_row = jnp.int32(0)
        grad_mid = lax.psum_scatter(
            back_product(
                row_slice(grad_gate_low, first_row, shard_rows * lax.axis_size("tensor")), full_gate
            )
            + back_product(
                row_slice(grad_up_low, first_row, shard_rows * lax.axis_size("tensor")), full_up
            ),
            "tensor",
            scatter_dimension=0,
            tiled=True,
        )
        gain_mlp_sum += jnp.sum(grad_mid * normed_mid, axis=0)
        grad_resid = cotangent.astype(jnp.float32) + norm_back(
            grad_mid, normed_mid, inverse_mid, gain_mid
        )
        gathered_resid = lax.all_gather(
            grad_resid.astype(jnp.bfloat16), "tensor", axis=0, tiled=True
        )
        grad_out_sum += rows_product(mixed_low, gathered_resid)
        grad_mixed = back_product(gathered_resid, full_out).astype(jnp.bfloat16).astype(jnp.float32)
        grad_query_full, grad_key_full, grad_value_full = pullback(grad_mixed)
        grad_query_low = grad_query_full.reshape(group_rows, -1).astype(jnp.bfloat16)
        grad_key_low = grad_key_full.reshape(group_rows, -1).astype(jnp.bfloat16)
        grad_value_low = grad_value_full.reshape(group_rows, -1).astype(jnp.bfloat16)
        grad_query_sum += rows_product(gathered_in, grad_query_low)
        grad_key_sum += rows_product(gathered_in, grad_key_low)
        grad_value_sum += rows_product(gathered_in, grad_value_low)
        attn_first_row = jnp.int32(0)
        grad_in = lax.psum_scatter(
            (
                back_product(
                    row_slice(grad_query_low, attn_first_row, shard_rows * lax.axis_size("tensor")),
                    full_query,
                )
                + back_product(
                    row_slice(grad_key_low, attn_first_row, shard_rows * lax.axis_size("tensor")),
                    full_key,
                )
                + back_product(
                    row_slice(grad_value_low, attn_first_row, shard_rows * lax.axis_size("tensor")),
                    full_value,
                )
            ).astype(jnp.bfloat16),
            "tensor",
            scatter_dimension=0,
            tiled=True,
        ).astype(jnp.float32)
        gain_attn_sum += jnp.sum(grad_in * normed_in, axis=0)
        input_grads.append(grad_resid + norm_back(grad_in, normed_in, inverse_in, gain_in))
    row_grads = (
        lax.psum_scatter(
            grad_query_sum.astype(jnp.bfloat16), "dp", scatter_dimension=0, tiled=True
        ).astype(jnp.float32),
        lax.psum_scatter(
            grad_key_sum.astype(jnp.bfloat16), "dp", scatter_dimension=0, tiled=True
        ).astype(jnp.float32),
        lax.psum_scatter(
            grad_value_sum.astype(jnp.bfloat16), "dp", scatter_dimension=0, tiled=True
        ).astype(jnp.float32),
        lax.psum_scatter(
            grad_gate_sum.astype(jnp.bfloat16), "dp", scatter_dimension=0, tiled=True
        ).astype(jnp.float32),
        lax.psum_scatter(
            grad_up_sum.astype(jnp.bfloat16), "dp", scatter_dimension=0, tiled=True
        ).astype(jnp.float32),
        lax.psum_scatter(
            gain_attn_sum.astype(jnp.bfloat16), "dp", scatter_dimension=0, tiled=True
        ).astype(jnp.float32),
        lax.psum_scatter(
            gain_mlp_sum.astype(jnp.bfloat16), "dp", scatter_dimension=0, tiled=True
        ).astype(jnp.float32),
    )
    col_grads = (
        lax.psum_scatter(
            grad_out_sum.astype(jnp.bfloat16), "dp", scatter_dimension=1, tiled=True
        ).astype(jnp.float32),
        lax.psum_scatter(
            grad_down_sum.astype(jnp.bfloat16), "dp", scatter_dimension=1, tiled=True
        ).astype(jnp.float32),
    )
    gain_grads = lax.psum((row_grads[5], row_grads[6]), "tensor")
    return (
        jnp.stack(outputs, 0),
        jnp.stack(input_grads, 0),
        gain_grads[0],
        gain_grads[1],
        row_grads[0],
        row_grads[1],
        row_grads[2],
        col_grads[0],
        row_grads[3],
        row_grads[4],
        col_grads[1],
    )


F32 = jnp.float32
BF16 = jnp.bfloat16
NN = (((1,), (0,)), ((), ()))
NT = (((1,), (1,)), ((), ()))
TN = (((0,), (0,)), ((), ()))
TILE = 256
SPAN = 2
CHUNK = 512
VMEM_BYTES = 62 << 20
MESH = pl.DeviceIdType.MESH


def mm(left, right, dims=NN):
    return lax.dot_general(left, right, dims, preferred_element_type=F32)


def params(number=None):
    if number is None:
        return pltpu.CompilerParams(vmem_limit_bytes=VMEM_BYTES)
    return pltpu.CompilerParams(vmem_limit_bytes=VMEM_BYTES, collective_id=number, has_side_effects=True)


def anywhere():
    return pl.BlockSpec(memory_space=pl.ANY)


def once(shape):
    return pl.BlockSpec(shape, lambda *_: (0,) * len(shape), pipeline_mode=pl.Buffered(1))


def far_count():
    return lax.axis_size("dp") // 4


def dp_peer(bits):
    return {"dp": lax.axis_index("dp") ^ bits}


def sibling():
    return {"tensor": 1 - lax.axis_index("tensor")}


def dp_peers():
    return [dp_peer(1), dp_peer(2)] + [dp_peer(4 * k) for k in range(1, far_count())]


def greet(peers):
    barrier = pltpu.get_barrier_semaphore()
    for peer in peers:
        pl.semaphore_signal(barrier, inc=1, device_id=peer, device_id_type=MESH)
    pl.semaphore_wait(barrier, len(peers))


def remote(source, target, send, recv, peer):
    return pltpu.make_async_remote_copy(
        src_ref=source, dst_ref=target, send_sem=send, recv_sem=recv, device_id=peer, device_id_type=MESH
    )


def gather_sems():
    count = 7 * far_count() - 1
    return [pltpu.SemaphoreType.DMA((count,)), pltpu.SemaphoreType.DMA((count,)), pltpu.SemaphoreType.DMA]


class Gather:
    def __init__(self, source, whole, send, recv, local):
        self.source, self.whole, self.send, self.recv, self.local = source, whole, send, recv, local
        self.me = lax.axis_index("dp")
        self.far = far_count()
        self.each = whole.shape[0] // lax.axis_size("dp")
        self.half = self.each // 2

    def block(self, bits):
        start = pl.multiple_of((self.me ^ bits) * self.each, self.each)
        return self.whole.at[pl.ds(start, self.each)]

    def piece(self, bits, part):
        start = pl.multiple_of((self.me ^ bits) * self.each + part * self.half, self.half)
        return self.whole.at[pl.ds(start, self.half)]


    def along(self, k):
        return k - 1, self.source, self.block(0), 4 * k, self.block(4 * k)

    def first(self, k, part, bit):
        index = self.far - 1 + 4 * k + 2 * part + bit - 1
        if k == 0:
            source = self.source.at[pl.ds(part * self.half, self.half)]
        else:
            source = self.piece(4 * k, part)
        return index, source, self.piece(4 * k, part), bit, self.piece(4 * k + bit, part)

    def second(self, k, part):
        index = 5 * self.far - 1 + 2 * k + part
        source = self.piece(4 * k + 2 - part, part)
        return index, source, source, 1 + part, self.piece(4 * k + 3, part)

    def outgoing(self, transfer):
        index, source, target, bits, _ = transfer
        return remote(source, target, self.send.at[index], self.recv.at[index], dp_peer(bits))

    def start(self, transfer):
        self.outgoing(transfer).start()

    def sent(self, transfer):
        self.outgoing(transfer).wait_send()

    def arrived(self, transfer):
        index, _, _, bits, landing = transfer
        remote(landing, landing, self.send.at[index], self.recv.at[index], dp_peer(bits)).wait_recv()

    def kept(self):
        return pltpu.make_async_copy(self.source, self.block(0), self.local)

    def pass_on(self, k):
        for part, bit in ((0, 2), (1, 1), (0, 1), (1, 2)):
            self.start(self.first(k, part, bit))

    def begin(self):
        self.kept().start()
        for k in range(1, self.far):
            self.start(self.along(k))
        self.pass_on(0)

    def spread(self, k):
        self.arrived(self.along(k))
        self.pass_on(k)

    def turn(self, k):
        self.arrived(self.first(k, 0, 2))
        self.start(self.second(k, 0))
        self.arrived(self.first(k, 1, 1))
        self.start(self.second(k, 1))

    def finish(self):
        for k in range(self.far):
            self.arrived(self.first(k, 0, 1))
            self.arrived(self.first(k, 1, 2))
            for part in range(2):
                self.arrived(self.second(k, part))
        for k in range(1, self.far):
            self.sent(self.along(k))
        for k in range(self.far):
            for part in range(2):
                for bit in (1, 2):
                    self.sent(self.first(k, part, bit))
                self.sent(self.second(k, part))
        self.kept().wait()

    def schedule(self, spreads, turns):
        steps = {0: [self.begin]}
        for k, at in enumerate(spreads):
            steps.setdefault(at, []).append(functools.partial(self.spread, k + 1))
        for k, at in enumerate(turns):
            steps.setdefault(at, []).append(functools.partial(self.turn, k))
        return steps


def run_schedule(step, steps):
    for at in sorted(steps):

        @pl.when(step == at)
        def _(actions=steps[at]):
            for action in actions:
                action()


def scatter_scratch(columns, dim):
    far = far_count()
    half = dim // lax.axis_size("dp") // 2
    part = pltpu.VMEM((far, half, columns), BF16)
    return [part] * 8 + [
        pltpu.VMEM((far, 2, half, columns), BF16),
        pltpu.VMEM((far - 1, 2, half, columns), BF16),
        pltpu.SemaphoreType.DMA((5 + far,)),
        pltpu.SemaphoreType.DMA((5 + far,)),
        pltpu.SemaphoreType.DMA((3,)),
    ]


SCATTER_REFS = 13


class Scatter:
    def __init__(self, grads, out, refs):
        (
            self.mine_y, self.mine_x, self.got_dy, self.got_dx, self.got_x, self.got_y, self.got_y2, self.got_x2,
            self.mine, self.got_far, self.send, self.recv, self.local,
        ) = refs
        self.grads, self.out = grads, out
        me = lax.axis_index("dp")
        self.far = far_count()
        self.low, self.high = lax.rem(me, 4), lax.div(me, 4)

    def copy(self, index, source, target, bits):
        return remote(source, target, self.send.at[index], self.recv.at[index], dp_peer(bits))

    def from_grads(self):
        g, low = self.grads, self.low
        return [
            self.copy(0, g.at[:, low ^ 3, 0], self.got_dy, 1),
            self.copy(1, g.at[:, low ^ 3, 1], self.got_dx, 2),
            self.copy(2, g.at[:, low ^ 1, 0], self.got_x, 1),
            self.copy(3, g.at[:, low ^ 2, 1], self.got_y, 2),
        ]

    def added(self):
        return [self.copy(4, self.mine_y, self.got_y2, 2), self.copy(5, self.mine_x, self.got_x2, 1)]

    def along(self):
        return [
            self.copy(5 + k, self.mine.at[self.high ^ k], self.got_far.at[k - 1], 4 * k) for k in range(1, self.far)
        ]

    def loads(self):
        g, low = self.grads, self.low
        return [
            pltpu.make_async_copy(g.at[:, low ^ 2, 0], self.mine_y, self.local.at[0]),
            pltpu.make_async_copy(g.at[:, low ^ 1, 1], self.mine_x, self.local.at[1]),
            pltpu.make_async_copy(g.at[:, low], self.mine, self.local.at[2]),
        ]

    def begin(self):
        for copy in self.from_grads() + self.loads():
            copy.start()

    def second(self):
        loads, got, added = self.loads(), self.from_grads(), self.added()
        loads[0].wait()
        got[0].wait_recv()
        self.mine_y[...] = add(self.mine_y[...], self.got_dy[...]).astype(BF16)
        added[0].start()
        loads[1].wait()
        got[1].wait_recv()
        self.mine_x[...] = add(self.mine_x[...], self.got_dx[...]).astype(BF16)
        added[1].start()

    def third(self):
        got, added = self.from_grads(), self.added()
        self.loads()[2].wait()
        got[2].wait_recv()
        added[0].wait_recv()
        self.mine[:, 0] = add(self.mine[:, 0], self.got_x[...], self.got_y2[...]).astype(BF16)
        got[3].wait_recv()
        added[1].wait_recv()
        self.mine[:, 1] = add(self.mine[:, 1], self.got_y[...], self.got_x2[...]).astype(BF16)
        for copy in self.along():
            copy.start()

    def finish(self):
        for copy in self.along():
            copy.wait_recv()
        self.out[...] = add(self.mine[self.high], *[self.got_far[k] for k in range(self.far - 1)])
        for copy in self.from_grads() + self.added() + self.along():
            copy.wait_send()


def scatter_out(columns, dim):
    half = dim // lax.axis_size("dp") // 2
    return jax.ShapeDtypeStruct((2, half, columns), F32), once((2, half, columns))


def grad_shape(dim, columns):
    return jax.ShapeDtypeStruct((far_count(), 4, 2, dim // lax.axis_size("dp") // 2, columns), BF16)


def add(*terms):
    total = terms[0].astype(F32)
    for term in terms[1:]:
        total = total + term.astype(F32)
    return total


def own_block(width, micro, rows, first=0):
    return pl.BlockSpec((1, rows, width), lambda i: (jnp.clip(i - micro - first, 0, micro - 1), 0, 0))


def other_block(width, micro, rows, first=0):
    return pl.BlockSpec((1, rows, width), lambda i: (jnp.clip(i - first, 0, micro - 1), 0, 0))


def group_place(i, micro):
    core = lax.axis_index("tensor")
    return lax.rem(i, micro), jnp.where(lax.rem(i, 2 * micro) < micro, 1 - core, core), 0


def group_block(width, micro, rows):
    return pl.BlockSpec((1, rows, width), lambda i: group_place(i, micro))


def call(kernel, name, number, steps, in_specs, out_specs, out_shape, scratch, operands):
    return pl.pallas_call(
        kernel,
        grid=steps if isinstance(steps, tuple) else (steps,),
        in_specs=in_specs,
        out_specs=out_specs,
        out_shape=out_shape,
        scratch_shapes=scratch,
        compiler_params=params(number),
        name=name,
    )(*operands)


def pick(is_other, other_ref, own_ref):
    return jnp.where(is_other, other_ref[0], own_ref[0])


def put(is_other, other_ref, own_ref, value):
    @pl.when(is_other)
    def _():
        other_ref[0] = value

    @pl.when(jnp.logical_not(is_other))
    def _():
        own_ref[0] = value


def spread_gains(slab, column):
    dim = slab.shape[0]
    blocks = lax.axis_size("dp")
    each = dim // blocks
    lane_block = lax.broadcasted_iota(jnp.int32, (blocks, dim), 1) // each
    block = lax.broadcasted_iota(jnp.int32, (blocks, dim), 0)
    rows = []
    for which in range(2):
        picked = jnp.concatenate(
            [slab[each * b : each * b + 16, column : column + 128].astype(F32)[which : which + 1] for b in range(blocks)], 0
        )
        tiled = jnp.concatenate([picked] * (dim // 128), 1)
        rows.append(jnp.sum(jnp.where(lane_block == block, tiled, 0.0), axis=0, keepdims=True))
    return jnp.concatenate(rows + [jnp.zeros((6, dim), F32)], 0)


def project_kernel(micro, own, inputs, slab_own, h_out, qkv_out, gain_out, slab_out, slab, other, *sems):
    swap_send, swap_recv, kept = sems[:3]
    i = pl.program_id(0)
    columns = qkv_out.shape[2]
    swap = remote(inputs, other, swap_send, swap_recv, sibling())
    keep = pltpu.make_async_copy(slab, slab_out, kept)

    @pl.when(i == 0)
    def _():
        greet(dp_peers() + [sibling()])
        gather = Gather(slab_own, slab, *sems[3:])
        gather.begin()
        swap.start()
        for k in range(1, gather.far):
            gather.spread(k)
        for k in range(gather.far):
            gather.turn(k)
        gather.finish()
        keep.start()
        swap.wait()
        gain_out[...] = spread_gains(slab, columns)

    x = jnp.where(i < micro, other[lax.rem(i, micro)], own[0]).astype(F32)
    inverse = lax.rsqrt(jnp.mean(x * x, axis=-1, keepdims=True) + 1e-05)
    h = (x * inverse * gain_out[0:1]).astype(BF16)
    h_out[0] = h
    qkv_out[0] = mm(h, slab[:, :columns]).astype(BF16)

    @pl.when(i == 2 * micro - 1)
    def _():
        keep.wait()


def project(inputs, slab, columns):
    micro, rows, dim = inputs.shape
    dma = pltpu.SemaphoreType.DMA
    return call(
        functools.partial(project_kernel, micro),
        "project",
        1,
        2 * micro,
        [own_block(dim, micro, rows), anywhere(), anywhere()],
        [group_block(dim, micro, rows), group_block(columns, micro, rows), once((8, dim)), anywhere()],
        [
            jax.ShapeDtypeStruct((micro, 2 * rows, dim), BF16),
            jax.ShapeDtypeStruct((micro, 2 * rows, columns), BF16),
            jax.ShapeDtypeStruct((8, dim), F32),
            jax.ShapeDtypeStruct((dim, slab.shape[1]), BF16),
        ],
        [pltpu.VMEM((dim, slab.shape[1]), BF16), pltpu.VMEM((micro, rows, dim), BF16), dma, dma, dma] + gather_sems(),
        (inputs, inputs, slab),
    )


def first_lane(lane):
    return (lane == 0).astype(F32).astype(BF16)


def attend_kernel(
    q_ref, k_ref, v_ref, start_ref, grad_own, slab_own, mix_ref, inv_ref, grad_other, slab_whole,
    keys, mask, queries, values, *sems,
):
    pair = pl.program_id(1)
    step = pl.program_id(0) * pl.num_programs(1) + pair
    group = q_ref.shape[1]
    tiles = group // TILE
    lane = lax.broadcasted_iota(jnp.int32, (group, 128), 1)
    swap = remote(grad_own, grad_other, sems[0], sems[1], sibling())
    gather = Gather(slab_own, slab_whole, *sems[2:])

    @pl.when(step == 0)
    def _():
        greet(dp_peers() + [sibling()])
        swap.start()

    run_schedule(step, gather.schedule((3, 6, 8), (4, 7, 9, 10)))

    @pl.when(pair == 0)
    def _():
        keys[:, :128] = k_ref[0]
        keys[:, 128:] = first_lane(lane)
        for i in range(tiles):
            j = max(0, i - SPAN)
            wide = (i - j + 1) * TILE
            column = lax.broadcasted_iota(jnp.int32, (TILE, wide), 1) + j * TILE
            row = lax.broadcasted_iota(jnp.int32, (TILE, wide), 0) + i * TILE
            allowed = (column <= row) & (column >= start_ref[0, i * TILE : (i + 1) * TILE, :])
            mask[i * TILE : (i + 1) * TILE, :wide] = jnp.where(allowed, 1.0, 0.0)

    query = q_ref[0].astype(F32)
    value = v_ref[0].astype(F32)
    for side in range(2):
        queries[side, :, :128] = jnp.where(lane // FEAT == 2 * pair + side, query * 0.25, 0.0).astype(BF16)
        queries[side, :, 128:] = first_lane(lane)
        mine = lane // VD == side
        values[side, :, :128] = jnp.where(mine, value, 0.0).astype(BF16)
        values[side, :, 128:] = mine.astype(F32).astype(BF16)
    for i in range(tiles):
        j = max(0, i - SPAN)
        wide = (i - j + 1) * TILE
        here = slice(i * TILE, (i + 1) * TILE)
        total = None
        for side in range(2):
            t = mm(queries[side, here], keys[j * TILE : (i + 1) * TILE], NT)
            weights = ((t * t + 1.0) * mask[here, :wide]).astype(BF16)
            part = mm(weights, values[side, j * TILE : (i + 1) * TILE])
            total = part if total is None else total + part
        inverse = 1.0 / total[:, 128:]
        mix_ref[0, here, :] = (total[:, :128] * inverse).astype(BF16)
        inv_ref[0, here, :] = inverse

    @pl.when(step == pl.num_programs(0) * pl.num_programs(1) - 1)
    def _():
        gather.finish()
        swap.wait()


def lanes_at(group, column):
    return pl.BlockSpec((1, group, 128), lambda m, p: (m, 0, column))


def lanes_of_pair(group, first):
    return pl.BlockSpec((1, group, 128), lambda m, p: (m, 0, first + p))


def attend_all(qkv, starts, out_grad, slab):
    micro, group, columns = qkv.shape
    dim = out_grad.shape[2]
    wide = columns - 256
    pair = lanes_of_pair(group, 0)
    dma = pltpu.SemaphoreType.DMA
    return call(
        attend_kernel,
        "attend",
        2,
        (micro, wide // 128),
        [
            lanes_at(group, 0),
            lanes_at(group, 1),
            lanes_of_pair(group, 2),
            pl.BlockSpec((1, group, 1), lambda m, p: (m, 0, 0)),
            anywhere(),
            anywhere(),
        ],
        [pair, pair, anywhere(), anywhere()],
        [
            jax.ShapeDtypeStruct((micro, group, wide), BF16),
            jax.ShapeDtypeStruct((micro, group, wide), F32),
            jax.ShapeDtypeStruct(out_grad.shape, BF16),
            jax.ShapeDtypeStruct((dim, slab.shape[1]), BF16),
        ],
        [
            pltpu.VMEM((group, 256), BF16),
            pltpu.VMEM((group, TILE * (SPAN + 1)), F32),
            pltpu.VMEM((2, group, 256), BF16),
            pltpu.VMEM((2, group, 256), BF16),
            dma,
            dma,
        ]
        + gather_sems(),
        (qkv, qkv, qkv, starts, out_grad, slab),
    )


def attend_back_kernel(
    widths, q_ref, k_ref, v_ref, mix_ref, inv_ref, dmix_ref, start_ref, grads_a, grads_b,
    dq_ref, dk_ref, dv_ref, out_a, out_b,
    keys, keys_t, mask, queries, values, douts, scaled_q, scaled_d, dk_sum, dq_t, scale, *refs,
):
    pair = pl.program_id(1)
    step = pl.program_id(0) * pl.num_programs(1) + pair
    group = q_ref.shape[1]
    tiles = group // TILE
    lane = lax.broadcasted_iota(jnp.int32, (group, 128), 1)
    one = Scatter(grads_a, out_a, refs[:SCATTER_REFS])
    two = Scatter(grads_b, out_b, refs[SCATTER_REFS:])

    @pl.when(step == 0)
    def _():
        greet(dp_peers())

    run_schedule(
        step, {0: [one.begin, two.begin], 5: [one.second], 6: [two.second], 8: [one.third], 9: [two.third]}
    )

    @pl.when(pair == 0)
    def _():
        keys[:, :128] = k_ref[0]
        keys[:, 128:] = first_lane(lane)
        keys_t[...] = k_ref[0].astype(F32).T.astype(BF16)
        for j in range(tiles):
            i = min(tiles, j + SPAN + 1)
            wide = (i - j) * TILE
            column = lax.broadcasted_iota(jnp.int32, (TILE, wide), 0) + j * TILE
            row = lax.broadcasted_iota(jnp.int32, (TILE, wide), 1) + j * TILE
            allowed = (column <= row) & (column >= start_ref[0, :, j * TILE : i * TILE])
            mask[j * TILE : (j + 1) * TILE, :wide] = jnp.where(allowed, 1.0, 0.0)
        dk_sum[...] = jnp.zeros_like(dk_sum)
        scale[...] = jnp.zeros_like(scale)

    query = q_ref[0].astype(F32)
    dmix = dmix_ref[0].astype(F32)
    inverse = inv_ref[0]
    values[:, :128] = v_ref[0]
    values[:, 128:] = (lane < 2).astype(F32).astype(BF16)
    product = dmix * mix_ref[0].astype(F32)
    for side in range(2):
        mine = lane // VD == side
        head = lane // FEAT == 2 * pair + side
        masked = jnp.where(head, query, 0.0)
        queries[side, :, :128] = (masked * 0.25).astype(BF16)
        queries[side, :, 128:] = first_lane(lane)
        delta = jnp.sum(jnp.where(mine, product, 0.0), axis=1, keepdims=True)
        coarse = delta.astype(BF16).astype(F32)
        douts[side, :, :128] = jnp.where(mine, dmix, 0.0).astype(BF16)
        douts[side, :, 128:] = jnp.where(lane == 0, -coarse, jnp.where(lane == 1, coarse - delta, 0.0)).astype(BF16)
        half_inverse = inverse[:, VD * side : VD * side + 1] * 0.5
        scaled_q[side] = (masked * half_inverse).astype(BF16)
        scaled_d[side] = jnp.where(mine, dmix * inverse, 0.0).astype(BF16)
        scale[...] += jnp.where(head, half_inverse, 0.0)
    for j in range(tiles):
        i = min(tiles, j + SPAN + 1)
        here = slice(j * TILE, (j + 1) * TILE)
        below = slice(j * TILE, i * TILE)
        allowed = mask[here, : (i - j) * TILE]
        dv = None
        dk = None
        for side in range(2):
            t = mm(keys[here], queries[side, below], NT)
            slope = mm(values[here], douts[side, below], NT)
            masked_t = t * allowed
            d_t = (slope * masked_t).astype(BF16)
            weights = (t * masked_t + allowed).astype(BF16)
            dv_part = mm(weights, scaled_d[side, below])
            dk_part = mm(d_t, scaled_q[side, below])
            dv = dv_part if dv is None else dv + dv_part
            dk = dk_part if dk is None else dk + dk_part
            rows = pl.ds(pl.multiple_of((2 * pair + side) * FEAT, FEAT), FEAT)
            dq_part = mm(keys_t[rows, here], d_t)
            for r in range(j, i):
                piece = dq_part[:, (r - j) * TILE : (r - j + 1) * TILE]
                if j == max(0, r - SPAN):
                    dq_t[rows, r * TILE : (r + 1) * TILE] = piece
                else:
                    dq_t[rows, r * TILE : (r + 1) * TILE] += piece
        dv_ref[0, here, :] = dv.astype(BF16)
        dk_sum[here] += dk

    @pl.when(pair == pl.num_programs(1) - 1)
    def _():
        dk_ref[0] = dk_sum[...].astype(BF16)
        dq_ref[0] = (dq_t[...].T * scale[...]).astype(BF16)

    @pl.when(step == pl.num_programs(0) * pl.num_programs(1) - 1)
    def _():
        one.finish()
        two.finish()


def attend_back(qkv, mix, inverse, dmix, starts, grads_a, grads_b):
    micro, group, columns = qkv.shape
    wide = columns - 256
    pair = lanes_of_pair(group, 0)
    narrow = jax.ShapeDtypeStruct((micro, group, 128), BF16)
    dim = grads_a.shape[3] * 2 * lax.axis_size("dp")
    outs = [scatter_out(g.shape[4], dim) for g in (grads_a, grads_b)]
    return call(
        functools.partial(attend_back_kernel, None),
        "attend_back",
        8,
        (micro, wide // 128),
        [
            lanes_at(group, 0),
            lanes_at(group, 1),
            lanes_of_pair(group, 2),
            pair,
            pair,
            pair,
            pl.BlockSpec((1, 1, group), lambda m, p: (m, 0, 0)),
            anywhere(),
            anywhere(),
        ],
        [lanes_at(group, 0), lanes_at(group, 0), pair] + [o[1] for o in outs],
        [narrow, narrow, jax.ShapeDtypeStruct((micro, group, wide), BF16)] + [o[0] for o in outs],
        [
            pltpu.VMEM((group, 256), BF16),
            pltpu.VMEM((128, group), BF16),
            pltpu.VMEM((group, TILE * (SPAN + 1)), F32),
            pltpu.VMEM((2, group, 256), BF16),
            pltpu.VMEM((group, 256), BF16),
            pltpu.VMEM((2, group, 256), BF16),
            pltpu.VMEM((2, group, 128), BF16),
            pltpu.VMEM((2, group, 128), BF16),
            pltpu.VMEM((group, 128), F32),
            pltpu.VMEM((128, group), F32),
            pltpu.VMEM((group, 128), F32),
        ]
        + scatter_scratch(grads_a.shape[4], dim)
        + scatter_scratch(grads_b.shape[4], dim),
        (qkv, qkv, qkv, mix, inverse, dmix, starts, grads_a, grads_b),
    )


def out_kernel(micro, mix, x, weights, gains, resid_out, h_out, h_other, sent, got, h_sent, send, recv):
    i = pl.program_id(0)
    m = lax.rem(i, micro)

    @pl.when(i == 0)
    def _():
        greet([sibling()])

    part = mm(mix[0], weights[...], NT)
    swap = remote(sent.at[m], got.at[m], send.at[m], recv.at[m], sibling())
    swap_h = remote(h_sent.at[m], h_other.at[m], send.at[micro + m], recv.at[micro + m], sibling())

    @pl.when(i < micro)
    def _():
        sent[m] = part.astype(BF16)
        swap.start()

    @pl.when(i >= micro)
    def _():
        swap.wait_recv()
        resid = x[0].astype(F32) + part + got[m].astype(F32)
        inverse = lax.rsqrt(jnp.mean(resid * resid, axis=-1, keepdims=True) + 1e-05)
        resid_out[0] = resid.astype(BF16)
        h = (resid * inverse * gains[1:2]).astype(BF16)
        h_out[0] = h
        h_sent[m] = h
        swap_h.start()

    @pl.when(i == 2 * micro - 1)
    def _():
        for k in range(micro):
            remote(sent.at[k], got.at[k], send.at[k], recv.at[k], sibling()).wait_send()
            remote(h_sent.at[k], h_other.at[k], send.at[micro + k], recv.at[micro + k], sibling()).wait()


def out_project(mix, x, slab, gains, columns):
    micro, rows, dim = x.shape
    wide = mix.shape[2]
    own = own_block(dim, micro, rows)
    shape = jax.ShapeDtypeStruct((micro, rows, dim), BF16)
    buffer = pltpu.VMEM((micro, rows, dim), BF16)
    sems = pltpu.SemaphoreType.DMA((2 * micro,))
    return call(
        functools.partial(out_kernel, micro),
        "out_project",
        3,
        2 * micro,
        [group_block(wide, micro, rows), own, once((dim, columns)), once((8, dim))],
        [own, own, anywhere()],
        [shape, shape, shape],
        [buffer, buffer, buffer, sems, sems],
        (mix, x, slab, gains),
    )


def feed_kernel(micro, width, column, first, has_next, has_last, h_own, h_other, g_own, g_other, weights, *refs):
    before, refs = (None, refs) if first else (refs[:4], refs[4:])
    if has_next:
        slab_next, refs = refs[0], refs[1:]
    if has_last:
        grads_last, refs = refs[0], refs[1:]
    (out_own, out_other, dm_own, dm_other, grads), refs = refs[:5], refs[5:]
    if has_next:
        whole_next, refs = refs[0], refs[1:]
    if has_last:
        grad_out, refs = refs[0], refs[1:]
    (slab, total, hidden_s, dgu_s, rounded, sem, out_sem), refs = refs[:7], refs[7:]
    i = pl.program_id(0)
    is_other = i < micro
    last = 2 * micro - 1
    load = pltpu.make_async_copy(weights.at[:, pl.ds(column, 3 * width)], slab, sem)
    steps = {}
    ends = []
    if has_next:
        gather = Gather(slab_next, whole_next, *refs[:3])
        refs = refs[3:]
        steps = gather.schedule((1, 2, 3), (2, 3, 4, 5))
        ends.append(gather.finish)
    if has_last:
        scatter = Scatter(grads_last, grad_out, refs)
        for at, action in ((0, scatter.begin), (3, scatter.second), (4, scatter.third)):
            steps.setdefault(at, []).append(action)
        ends.append(scatter.finish)

    @pl.when(i == 0)
    def _():
        load.start()
        greet(dp_peers())

    run_schedule(i, steps)

    @pl.when(i == 0)
    def _():
        total[...] = jnp.zeros_like(total)
        load.wait()

    w_gu = slab[:, : 2 * width]
    w_down = slab[:, 2 * width :]
    h = pick(is_other, h_other, h_own)
    g = pick(is_other, g_other, g_own)
    gate_up = mm(h, w_gu)
    d_hidden = mm(g, w_down)
    gate = gate_up[:, :width]
    up = gate_up[:, width:]
    sigmoid = 0.5 * jnp.tanh(0.5 * gate) + 0.5
    silu = gate * sigmoid
    hidden_s[...] = (silu * up).astype(BF16)
    dgu_s[:, :width] = (d_hidden * up * (sigmoid + silu * (1.0 - sigmoid))).astype(BF16)
    dgu_s[:, width:] = (d_hidden * silu).astype(BF16)
    out = mm(hidden_s[...], w_down, NT)
    dm = mm(dgu_s[...], w_gu, NT)
    if not first:
        out = out + pick(is_other, before[1], before[0]).astype(F32)
        dm = dm + pick(is_other, before[3], before[2]).astype(F32)
    put(is_other, out_other, out_own, out.astype(BF16))
    put(is_other, dm_other, dm_own, dm.astype(BF16))
    total[:, : 2 * width] += mm(h, dgu_s[...], TN)
    total[:, 2 * width :] += mm(g, hidden_s[...], TN)

    @pl.when(i == last)
    def _():
        rounded[...] = total[...].astype(BF16).reshape(rounded.shape)
        write = pltpu.make_async_copy(rounded, grads, out_sem)
        write.start()
        for end in ends:
            end()
        write.wait()


def feed(number, h_own, h_other, g_own, g_other, weights, column, width, before, slab_next, grads_last):
    micro, rows, dim = h_own.shape
    columns = 3 * width
    own = own_block(dim, micro, rows)
    other = other_block(dim, micro, rows)
    shape = jax.ShapeDtypeStruct((micro, rows, dim), BF16)
    grads = grad_shape(dim, columns)
    first = before is None
    has_next, has_last = slab_next is not None, grads_last is not None
    in_specs = [own, other, own, other, anywhere()] + ([] if first else [own, other, own, other])
    operands = [h_own, h_other, g_own, g_other, weights] + ([] if first else list(before))
    out_specs = [own, other, own, other, anywhere()]
    out_shape = [shape] * 4 + [grads]
    scratch = [
        pltpu.VMEM((dim, columns), BF16),
        pltpu.VMEM((dim, columns), F32),
        pltpu.VMEM((rows, width), BF16),
        pltpu.VMEM((rows, 2 * width), BF16),
        pltpu.VMEM(grads.shape, BF16),
        pltpu.SemaphoreType.DMA,
        pltpu.SemaphoreType.DMA,
    ]
    if has_next:
        in_specs.append(anywhere())
        operands.append(slab_next)
        out_specs.append(anywhere())
        out_shape.append(jax.ShapeDtypeStruct((dim, slab_next.shape[1]), BF16))
        scratch += gather_sems()
    if has_last:
        in_specs.append(anywhere())
        operands.append(grads_last)
        result = scatter_out(grads_last.shape[4], dim)
        out_specs.append(result[1])
        out_shape.append(result[0])
        scratch += scatter_scratch(grads_last.shape[4], dim)
    results = call(
        functools.partial(feed_kernel, micro, width, column, first, has_next, has_last),
        "feed",
        number,
        2 * micro,
        in_specs,
        out_specs,
        out_shape,
        scratch,
        operands,
    )
    rest = list(results[5:])
    whole_next = rest.pop(0) if has_next else None
    grad_last = rest.pop(0) if has_last else None
    return results[:4], results[4], whole_next, grad_last


def norm_slope(values, scaled):
    inverse = lax.rsqrt(jnp.mean(values * values, axis=-1, keepdims=True) + 1e-05)
    normed = values * inverse
    return inverse * (scaled - normed * jnp.mean(scaled * normed, axis=-1, keepdims=True))


def back_mid_kernel(
    micro, resid, out_own, dm_own, g_own, out_other, dm_other, mix, weights, gains,
    mixed_out, d_out, dmix, grads, got_out, got_dm, both, total, rounded, send, recv, out_sem,
):
    i = pl.program_id(0)
    m = lax.rem(i, micro)

    def swaps(k):
        return [
            remote(dm_other.at[k], got_dm.at[k], send.at[k], recv.at[k], sibling()),
            remote(out_other.at[k], got_out.at[k], send.at[micro + k], recv.at[micro + k], sibling()),
        ]

    def swap_d(k):
        return remote(both.at[k], both.at[micro + k], send.at[2 * micro + k], recv.at[2 * micro + k], sibling())

    @pl.when(i == 0)
    def _():
        greet([sibling()])
        for k in range(micro):
            for swap in swaps(k):
                swap.start()
        total[...] = jnp.zeros_like(total)

    @pl.when(i < micro)
    def _():
        for swap in swaps(m):
            swap.wait_recv()
        values = resid[0].astype(F32)
        mixed_out[0] = (values + out_own[0].astype(F32) + got_out[m].astype(F32)).astype(BF16)
        scaled = (dm_own[0].astype(F32) + got_dm[m].astype(F32)) * gains[1:2]
        d = (g_own[0].astype(F32) + norm_slope(values, scaled)).astype(BF16)
        d_out[0] = d
        both[m] = d
        swap_d(m).start()

    @pl.when(i >= 2 * micro)
    def _():
        swap_d(m).wait_recv()

    @pl.when(i >= micro)
    def _():
        d = both[i - micro]
        dmix[0] = mm(d, weights[...]).astype(BF16)
        total[...] += mm(d, mix[0], TN)

    @pl.when(i == 3 * micro - 1)
    def _():
        rounded[...] = total[...].astype(BF16).reshape(rounded.shape)
        write = pltpu.make_async_copy(rounded, grads, out_sem)
        write.start()
        for k in range(micro):
            for swap in swaps(k):
                swap.wait_send()
            swap_d(k).wait_send()
        write.wait()


def back_mid(resid, sums, out_grad, mix, slab, gains, columns):
    micro, rows, dim = resid.shape
    out_own, out_other, dm_own, dm_other = sums
    own = pl.BlockSpec((1, rows, dim), lambda i: (jnp.minimum(i, micro - 1), 0, 0))

    def place(i):
        core = lax.axis_index("tensor")
        return lax.rem(jnp.maximum(i - micro, 0), micro), jnp.where(i < 2 * micro, core, 1 - core), 0

    at_group = pl.BlockSpec((1, rows, columns), place)
    shape = jax.ShapeDtypeStruct((micro, rows, dim), BF16)
    grads = grad_shape(dim, columns)
    buffer = pltpu.VMEM((micro, rows, dim), BF16)
    sems = pltpu.SemaphoreType.DMA((3 * micro,))
    return call(
        functools.partial(back_mid_kernel, micro),
        "back_mid",
        7,
        3 * micro,
        [own] * 4 + [anywhere(), anywhere(), at_group, once((dim, columns)), once((8, dim))],
        [own, own, at_group, anywhere()],
        [shape, shape, jax.ShapeDtypeStruct((micro, 2 * rows, columns), BF16), grads],
        [
            buffer,
            buffer,
            pltpu.VMEM((2 * micro, rows, dim), BF16),
            pltpu.VMEM((dim, columns), F32),
            pltpu.VMEM(grads.shape, BF16),
            sems,
            sems,
            pltpu.SemaphoreType.DMA,
        ],
        (resid, out_own, dm_own, out_grad, out_other, dm_other, mix, slab, gains),
    )


def back_in_kernel(
    micro, h, dq, dk, dv, x, d_own, weights, gains, input_grad, grads_own, grads, total, sent, got, send, recv, out_sem,
    rounded, *refs,
):
    i = pl.program_id(0)
    m = lax.rem(i, micro)
    scatter = Scatter(grads, grads_own, refs)

    def swap(k):
        return remote(sent.at[k], got.at[k], send.at[k], recv.at[k], sibling())

    @pl.when(i == 0)
    def _():
        greet(dp_peers() + [sibling()])
        total[...] = jnp.zeros_like(total)

    d = jnp.concatenate([dq[0], dk[0], dv[0]], 1)

    @pl.when(i < 2 * micro)
    def _():
        total[...] += mm(h[0], d, TN)

    @pl.when(i == 2 * micro - 1)
    def _():
        rounded[...] = total[...].astype(BF16).reshape(rounded.shape)
        write = pltpu.make_async_copy(rounded, grads, out_sem)
        write.start()
        write.wait()
        scatter.begin()

    run_schedule(i, {3 * micro: [scatter.second], 4 * micro - 2: [scatter.third]})

    @pl.when(i >= 2 * micro)
    def _():
        part = mm(d, weights[:, : d.shape[1]], NT)

        @pl.when(i < 3 * micro)
        def _():
            sent[m] = part.astype(BF16)
            swap(m).start()

        @pl.when(i >= 3 * micro)
        def _():
            swap(m).wait_recv()
            scaled = (part + got[m].astype(F32)) * gains[0:1]
            input_grad[0] = (d_own[0].astype(F32) + norm_slope(x[0].astype(F32), scaled)).astype(BF16)

    @pl.when(i == 4 * micro - 1)
    def _():
        for k in range(micro):
            swap(k).wait_send()
        scatter.finish()


def back_in(h, dq, dk, dv, x, d_own, slab, gains):
    micro, rows, dim = x.shape
    widths = [a.shape[2] for a in (dq, dk, dv)]
    columns = sum(widths)
    own = own_block(dim, micro, rows, 2 * micro)
    grads = grad_shape(dim, columns)
    result = scatter_out(columns, dim)
    buffer = pltpu.VMEM((micro, rows, dim), BF16)
    sems = pltpu.SemaphoreType.DMA((micro,))

    def h_place(i):
        return group_place(jnp.minimum(i, 2 * micro - 1), micro)

    return call(
        functools.partial(back_in_kernel, micro),
        "back_in",
        9,
        4 * micro,
        [pl.BlockSpec((1, rows, dim), h_place)]
        + [group_block(w, micro, rows) for w in widths]
        + [own, own, once(slab.shape), once((8, dim))],
        [own, result[1], anywhere()],
        [jax.ShapeDtypeStruct((micro, rows, dim), BF16), result[0], grads],
        [
            pltpu.VMEM((dim, columns), F32),
            buffer,
            buffer,
            sems,
            sems,
            pltpu.SemaphoreType.DMA,
            pltpu.VMEM(grads.shape, BF16),
        ]
        + scatter_scratch(columns, dim),
        (h, dq, dk, dv, x, d_own, slab, gains),
    )


def fused_body(
    inputs, gain_attn, gain_mlp, w_query, w_key, w_value, w_out, w_gate, w_up, w_down, out_grad, lengths
):
    micro, rows, dim = inputs.shape
    group = rows * lax.axis_size("tensor")
    each = w_query.shape[0]
    units = w_gate.shape[1]

    gain_rows = jnp.stack([gain_attn, gain_mlp])
    gain_part = jnp.pad(jnp.concatenate([gain_rows, gain_rows], 1), ((0, each - 2), (0, 0)))
    slab_in = jnp.concatenate([w_query, w_key, w_value, gain_part], 1)
    widths_in = (w_query.shape[1], w_key.shape[1], w_value.shape[1])
    out_columns = w_out.shape[0]
    down_t = w_down.T
    padded = -(-units // 128) * 128
    edges = [(max(at - CHUNK, 0), at) for at in range(padded, 0, -CHUNK)][::-1]
    slabs = []
    for low, high in edges:
        parts = [a[:, low : min(high, units)] for a in (w_gate, w_up, down_t)]
        slabs.append([jnp.pad(a, ((0, 0), (0, high - low - a.shape[1]))) for a in parts])
    slabs[0] = [w_out.T] + slabs[0]
    slabs = [jnp.concatenate(s, 1) for s in slabs]

    ends = jnp.cumsum(lengths[:, 0], axis=-1)
    places = jnp.arange(group, dtype=jnp.int32)
    starts = jnp.max(jnp.where(places[None, :, None] >= ends[:, None, :], ends[:, None, :], 0), axis=-1)

    h_in, qkv, gains, whole_in = project(inputs, slab_in, sum(widths_in))
    mix, inverse, g_other, whole_out = attend_all(qkv, starts.reshape(micro, group, 1), out_grad, slabs[0])
    resid, h_own, h_other = out_project(mix, inputs, whole_out, gains, out_columns)

    sums = None
    grads_last = None
    whole, column = whole_out, out_columns
    feed_grads = []
    for at, (low, high) in enumerate(edges):
        slab_next = slabs[at + 1] if at + 1 < len(edges) else None
        sums, grads, whole, done = feed(
            4 + at, h_own, h_other, out_grad, g_other, whole, column, high - low, sums, slab_next, grads_last
        )
        if done is not None:
            feed_grads.append(done)
        grads_last, column = grads, 0
    mixed_out, d_own, dmix, grads_out = back_mid(resid, sums, out_grad, mix, whole_out, gains, out_columns)
    dq, dk, dv, done, grad_out_t = attend_back(
        qkv, mix, inverse, dmix, starts.reshape(micro, 1, group), grads_last, grads_out
    )
    feed_grads.append(done)
    input_grad, grad_in, _ = back_in(h_in, dq, dk, dv, inputs, d_own, whole_in, gains)
    feed_grads = [g.reshape(each, g.shape[2]) for g in feed_grads]
    grad_out_t = grad_out_t.reshape(each, out_columns)
    grad_in = grad_in.reshape(each, grad_in.shape[2])

    def columns_of(at):
        kept = []
        for (low, high), grad in zip(edges, feed_grads):
            kept.append(grad[:, at * (high - low) : at * (high - low) + min(high, units) - low])
        return jnp.concatenate(kept, 1)

    grad_gate, grad_up, grad_down_t = columns_of(0), columns_of(1), columns_of(2)
    from_in = jnp.sum(slab_in[:, : sum(widths_in)].astype(F32) * grad_in, axis=1)
    from_mid = jnp.sum(w_gate.astype(F32) * grad_gate + w_up.astype(F32) * grad_up, axis=1)
    both = jnp.stack([from_in / gain_attn.astype(F32), from_mid / gain_mlp.astype(F32)])
    both = both + lax.ppermute(both, "tensor", [(0, 1), (1, 0)])
    at_key = widths_in[0]
    at_value = widths_in[0] + widths_in[1]
    return (
        mixed_out,
        input_grad.astype(F32),
        both[0],
        both[1],
        grad_in[:, :at_key],
        grad_in[:, at_key:at_value],
        grad_in[:, at_value:],
        grad_out_t.T,
        grad_gate,
        grad_up,
        grad_down_t.T,
    )


def solution(mesh):
    in_specs = (
        P(None, ("dp", "tensor"), None),
        P("dp"),
        P("dp"),
        P("dp", "tensor"),
        P("dp", "tensor"),
        P("dp", "tensor"),
        P("tensor", "dp"),
        P("dp", "tensor"),
        P("dp", "tensor"),
        P("tensor", "dp"),
        P(None, ("dp", "tensor"), None),
        P(None, "dp", None),
    )
    out_specs = (
        P(None, ("dp", "tensor"), None),
        P(None, ("dp", "tensor"), None),
        P("dp"),
        P("dp"),
        P("dp", "tensor"),
        P("dp", "tensor"),
        P("dp", "tensor"),
        P("tensor", "dp"),
        P("dp", "tensor"),
        P("dp", "tensor"),
        P("tensor", "dp"),
    )
    fits = mesh.shape["tensor"] == 2 and mesh.shape["dp"] % 4 == 0
    chosen = fused_body if fits else plain_body
    return jax.shard_map(chosen, mesh=mesh, in_specs=in_specs, out_specs=out_specs, check_vma=False)
```

```python
import functools
import math

import jax
import jax.numpy as jnp
import numpy as np
from jax import lax
from jax.experimental import pallas as pl
from jax.experimental.pallas import tpu as pltpu
from jax.sharding import PartitionSpec as P

FEAT = 16
VD = 64
BLK = 512


EXACT = lax.Precision.HIGHEST


def taylor(halved):
    feature_dim = halved.shape[-1]
    upper_idx, lower_idx = np.triu_indices(feature_dim)
    flat_index = jnp.asarray(upper_idx * feature_dim + lower_idx, jnp.int32)
    factors = jnp.asarray(np.where(upper_idx == lower_idx, math.sqrt(0.5), 1.0), jnp.float32)
    outer = (halved[..., :, None] * halved[..., None, :]).reshape(
        halved.shape[:-1] + (feature_dim * feature_dim,)
    )
    second = jnp.take(outer, flat_index, axis=-1) * factors
    ones_col = jnp.ones(halved.shape[:-1] + (1,), jnp.float32)
    return jnp.concatenate([ones_col, halved, second], axis=-1)


def attend_block(carry_in, block_in):
    kv_state, totals, previous = carry_in
    queries, keys_in, values_in, doc_ids = block_in
    half_q = 0.5 * queries
    half_k = 0.5 * keys_in
    scores = jnp.einsum("rhf,chf->hrc", half_q, half_k, preferred_element_type=jnp.float32)
    places = jnp.arange(doc_ids.shape[0], dtype=jnp.int32)
    allowed = (doc_ids[:, None] == doc_ids[None, :]) & (places[None, :] <= places[:, None])
    weights = jnp.where(allowed[None], 1.0 + scores + 0.5 * scores * scores, 0.0)
    feat_q = taylor(half_q)
    feat_k = taylor(half_k)
    carried_in = (doc_ids == previous).astype(jnp.float32)
    numerator = jnp.einsum("hrc,chv->rhv", weights, values_in, precision=EXACT) + carried_in[
        :, None, None
    ] * jnp.einsum("rhf,hfv->rhv", feat_q, kv_state, precision=EXACT)
    denominator = jnp.sum(weights, axis=2).T + carried_in[:, None] * jnp.einsum(
        "rhf,hf->rh", feat_q, totals, precision=EXACT
    )
    mixed_rows = numerator / denominator[:, :, None]
    final_doc = doc_ids[-1]
    staying = (doc_ids == final_doc).astype(jnp.float32)[:, None, None] * feat_k
    joined = (final_doc == previous).astype(jnp.float32)
    kv_state = jnp.einsum("rhf,rhv->hfv", staying, values_in, precision=EXACT) + joined * kv_state
    totals = jnp.sum(staying, axis=0) + joined * totals
    return ((kv_state, totals, final_doc), mixed_rows)


def attend(queries, keys_in, values_in, doc_ids):
    row_total, head_count, feature_dim = queries.shape
    value_dim = values_in.shape[2]
    block_count = row_total // BLK
    feature_total = 1 + feature_dim + feature_dim * (feature_dim + 1) // 2
    initial = (
        jnp.zeros((head_count, feature_total, value_dim), jnp.float32),
        jnp.zeros((head_count, feature_total), jnp.float32),
        jnp.array(-1, jnp.int32),
    )
    pieces = (
        queries.reshape(block_count, BLK, head_count, feature_dim),
        keys_in.reshape(block_count, BLK, head_count, feature_dim),
        values_in.reshape(block_count, BLK, head_count, value_dim),
        doc_ids.reshape(block_count, BLK),
    )
    last_carry, mixed_rows = lax.scan(jax.checkpoint(attend_block), initial, pieces)
    return mixed_rows.reshape(row_total, head_count * value_dim)


def document_ids(lengths_row, row_total):
    doc_ends = jnp.cumsum(lengths_row)
    places = jnp.arange(row_total, dtype=jnp.int32)
    return jnp.sum((places[:, None] >= doc_ends[None, :]).astype(jnp.int32), axis=1)


def rows_product(left, right):
    return lax.dot_general(
        left, right, (((0,), (0,)), ((), ())), preferred_element_type=jnp.float32
    )


def back_product(left, right):
    return lax.dot_general(
        left, right, (((1,), (1,)), ((), ())), preferred_element_type=jnp.float32
    )


def norm_back(grad_normed, normed, inverse, gain_full):
    scaled = grad_normed * gain_full
    return inverse * (scaled - normed * jnp.mean(scaled * normed, axis=-1, keepdims=True))


def row_slice(matrix, first_row, row_count):
    return lax.dynamic_slice_in_dim(matrix, first_row, row_count, 0)


def inverse_root(values):
    return lax.rsqrt(jnp.mean(values * values, axis=-1, keepdims=True) + 1e-05)


def fetch_weights(gain_attn, gain_mlp, w_query, w_key, w_value, w_out, w_gate, w_up, w_down):
    row_parts = (
        lax.all_gather(w_query, "dp", axis=0, tiled=True),
        lax.all_gather(w_key, "dp", axis=0, tiled=True),
        lax.all_gather(w_value, "dp", axis=0, tiled=True),
        lax.all_gather(w_gate, "dp", axis=0, tiled=True),
        lax.all_gather(w_up, "dp", axis=0, tiled=True),
        lax.all_gather(gain_attn, "dp", axis=0, tiled=True),
        lax.all_gather(gain_mlp, "dp", axis=0, tiled=True),
    )
    col_parts = (
        lax.all_gather(w_out, "dp", axis=1, tiled=True),
        lax.all_gather(w_down, "dp", axis=1, tiled=True),
    )
    return tuple(row_parts) + tuple(col_parts)


def plain_body(
    inputs,
    gain_attn,
    gain_mlp,
    w_query,
    w_key,
    w_value,
    w_out,
    w_gate,
    w_up,
    w_down,
    out_grad,
    lengths,
):
    micro_count = inputs.shape[0]
    shard_rows = inputs.shape[1]
    model_dim = inputs.shape[2]
    group_rows = shard_rows * lax.axis_size("tensor")
    local_heads = w_query.shape[1] // FEAT
    grad_query_sum = jnp.zeros((model_dim, w_query.shape[1]), jnp.float32)
    grad_key_sum = jnp.zeros((model_dim, w_key.shape[1]), jnp.float32)
    grad_value_sum = jnp.zeros((model_dim, w_value.shape[1]), jnp.float32)
    grad_gate_sum = jnp.zeros((model_dim, w_gate.shape[1]), jnp.float32)
    grad_up_sum = jnp.zeros((model_dim, w_up.shape[1]), jnp.float32)
    grad_out_sum = jnp.zeros((w_out.shape[0], model_dim), jnp.float32)
    grad_down_sum = jnp.zeros((w_down.shape[0], model_dim), jnp.float32)
    gain_attn_sum = jnp.zeros((model_dim,), jnp.float32)
    gain_mlp_sum = jnp.zeros((model_dim,), jnp.float32)
    outputs = []
    input_grads = []
    for micro_step in range(micro_count):
        (
            full_query,
            full_key,
            full_value,
            full_gate,
            full_up,
            full_gain_attn,
            full_gain_mlp,
            full_out,
            full_down,
        ) = fetch_weights(gain_attn, gain_mlp, w_query, w_key, w_value, w_out, w_gate, w_up, w_down)
        gain_in = full_gain_attn.astype(jnp.float32)
        gain_mid = full_gain_mlp.astype(jnp.float32)
        doc_ids = document_ids(lengths[micro_step, 0], group_rows)
        values = inputs[micro_step].astype(jnp.float32)
        inverse_in = inverse_root(values)
        normed_in = values * inverse_in
        gathered_in = lax.all_gather(
            (normed_in * gain_in).astype(jnp.bfloat16), "tensor", axis=0, tiled=True
        )
        query_low = jnp.dot(gathered_in, full_query, preferred_element_type=jnp.float32).astype(
            jnp.bfloat16
        )
        key_low = jnp.dot(gathered_in, full_key, preferred_element_type=jnp.float32).astype(
            jnp.bfloat16
        )
        value_low = jnp.dot(gathered_in, full_value, preferred_element_type=jnp.float32).astype(
            jnp.bfloat16
        )
        query_full = query_low.astype(jnp.float32).reshape(group_rows, local_heads, FEAT)
        key_full = key_low.astype(jnp.float32).reshape(group_rows, local_heads, FEAT)
        value_full = value_low.astype(jnp.float32).reshape(group_rows, local_heads, VD)

        def local_attend(query_arg, key_arg, value_arg):
            return attend(query_arg, key_arg, value_arg, doc_ids)

        mixed_full, pullback = jax.vjp(local_attend, query_full, key_full, value_full)
        mixed_low = mixed_full.astype(jnp.bfloat16)
        residual = values + lax.psum_scatter(
            jnp.dot(
                row_slice(mixed_low, jnp.int32(0), shard_rows * lax.axis_size("tensor")),
                full_out,
                preferred_element_type=jnp.float32,
            ),
            "tensor",
            scatter_dimension=0,
            tiled=True,
        )
        inverse_mid = inverse_root(residual)
        normed_mid = residual * inverse_mid
        gathered_mid = lax.all_gather(
            (normed_mid * gain_mid).astype(jnp.bfloat16), "tensor", axis=0, tiled=True
        )
        gate_pre = jnp.dot(gathered_mid, full_gate, preferred_element_type=jnp.float32)
        up_pre = jnp.dot(gathered_mid, full_up, preferred_element_type=jnp.float32)
        sigmoid_gate = jax.nn.sigmoid(gate_pre)
        silu_gate = gate_pre * sigmoid_gate
        hidden = (silu_gate * up_pre).astype(jnp.bfloat16)
        mlp_part = lax.psum_scatter(
            jnp.dot(
                row_slice(hidden, jnp.int32(0), shard_rows * lax.axis_size("tensor")),
                full_down,
                preferred_element_type=jnp.float32,
            ).astype(jnp.bfloat16),
            "tensor",
            scatter_dimension=0,
            tiled=True,
        ).astype(jnp.float32)
        outputs.append((residual + mlp_part).astype(jnp.bfloat16))
        cotangent = out_grad[micro_step]
        gathered_grad = lax.all_gather(cotangent, "tensor", axis=0, tiled=True)
        grad_down_sum += rows_product(hidden, gathered_grad)
        grad_hidden = back_product(gathered_grad, full_down)
        grad_gate_low = (
            grad_hidden * up_pre * sigmoid_gate * (1.0 + gate_pre * (1.0 - sigmoid_gate))
        ).astype(jnp.bfloat16)
        grad_up_low = (grad_hidden * silu_gate).astype(jnp.bfloat16)
        grad_gate_sum += rows_product(gathered_mid, grad_gate_low)
        grad_up_sum += rows_product(gathered_mid, grad_up_low)
        first_row = jnp.int32(0)
        grad_mid = lax.psum_scatter(
            back_product(
                row_slice(grad_gate_low, first_row, shard_rows * lax.axis_size("tensor")), full_gate
            )
            + back_product(
                row_slice(grad_up_low, first_row, shard_rows * lax.axis_size("tensor")), full_up
            ),
            "tensor",
            scatter_dimension=0,
            tiled=True,
        )
        gain_mlp_sum += jnp.sum(grad_mid * normed_mid, axis=0)
        grad_resid = cotangent.astype(jnp.float32) + norm_back(
            grad_mid, normed_mid, inverse_mid, gain_mid
        )
        gathered_resid = lax.all_gather(
            grad_resid.astype(jnp.bfloat16), "tensor", axis=0, tiled=True
        )
        grad_out_sum += rows_product(mixed_low, gathered_resid)
        grad_mixed = back_product(gathered_resid, full_out).astype(jnp.bfloat16).astype(jnp.float32)
        grad_query_full, grad_key_full, grad_value_full = pullback(grad_mixed)
        grad_query_low = grad_query_full.reshape(group_rows, -1).astype(jnp.bfloat16)
        grad_key_low = grad_key_full.reshape(group_rows, -1).astype(jnp.bfloat16)
        grad_value_low = grad_value_full.reshape(group_rows, -1).astype(jnp.bfloat16)
        grad_query_sum += rows_product(gathered_in, grad_query_low)
        grad_key_sum += rows_product(gathered_in, grad_key_low)
        grad_value_sum += rows_product(gathered_in, grad_value_low)
        attn_first_row = jnp.int32(0)
        grad_in = lax.psum_scatter(
            (
                back_product(
                    row_slice(grad_query_low, attn_first_row, shard_rows * lax.axis_size("tensor")),
                    full_query,
                )
                + back_product(
                    row_slice(grad_key_low, attn_first_row, shard_rows * lax.axis_size("tensor")),
                    full_key,
                )
                + back_product(
                    row_slice(grad_value_low, attn_first_row, shard_rows * lax.axis_size("tensor")),
                    full_value,
                )
            ).astype(jnp.bfloat16),
            "tensor",
            scatter_dimension=0,
            tiled=True,
        ).astype(jnp.float32)
        gain_attn_sum += jnp.sum(grad_in * normed_in, axis=0)
        input_grads.append(grad_resid + norm_back(grad_in, normed_in, inverse_in, gain_in))
    row_grads = (
        lax.psum_scatter(
            grad_query_sum.astype(jnp.bfloat16), "dp", scatter_dimension=0, tiled=True
        ).astype(jnp.float32),
        lax.psum_scatter(
            grad_key_sum.astype(jnp.bfloat16), "dp", scatter_dimension=0, tiled=True
        ).astype(jnp.float32),
        lax.psum_scatter(
            grad_value_sum.astype(jnp.bfloat16), "dp", scatter_dimension=0, tiled=True
        ).astype(jnp.float32),
        lax.psum_scatter(
            grad_gate_sum.astype(jnp.bfloat16), "dp", scatter_dimension=0, tiled=True
        ).astype(jnp.float32),
        lax.psum_scatter(
            grad_up_sum.astype(jnp.bfloat16), "dp", scatter_dimension=0, tiled=True
        ).astype(jnp.float32),
        lax.psum_scatter(
            gain_attn_sum.astype(jnp.bfloat16), "dp", scatter_dimension=0, tiled=True
        ).astype(jnp.float32),
        lax.psum_scatter(
            gain_mlp_sum.astype(jnp.bfloat16), "dp", scatter_dimension=0, tiled=True
        ).astype(jnp.float32),
    )
    col_grads = (
        lax.psum_scatter(
            grad_out_sum.astype(jnp.bfloat16), "dp", scatter_dimension=1, tiled=True
        ).astype(jnp.float32),
        lax.psum_scatter(
            grad_down_sum.astype(jnp.bfloat16), "dp", scatter_dimension=1, tiled=True
        ).astype(jnp.float32),
    )
    gain_grads = lax.psum((row_grads[5], row_grads[6]), "tensor")
    return (
        jnp.stack(outputs, 0),
        jnp.stack(input_grads, 0),
        gain_grads[0],
        gain_grads[1],
        row_grads[0],
        row_grads[1],
        row_grads[2],
        col_grads[0],
        row_grads[3],
        row_grads[4],
        col_grads[1],
    )


F32 = jnp.float32
BF16 = jnp.bfloat16
NN = (((1,), (0,)), ((), ()))
NT = (((1,), (1,)), ((), ()))
TN = (((0,), (0,)), ((), ()))
TILE = 256
SPAN = 2
CHUNK = 512
UNIT = 1536
EARLY = 640
JOBS = ((), ((0, 768), (0, 384), (1, 768)), ((1, 384),), ((1, 384), (2, 768), (2, 768)))
RATE = 0.019
VMEM_BYTES = 62 << 20
MESH = pl.DeviceIdType.MESH


def mm(left, right, dims=NN):
    return lax.dot_general(left, right, dims, preferred_element_type=F32)


def params(number=None):
    if number is None:
        return pltpu.CompilerParams(vmem_limit_bytes=VMEM_BYTES)
    return pltpu.CompilerParams(vmem_limit_bytes=VMEM_BYTES, collective_id=number, has_side_effects=True)


def anywhere():
    return pl.BlockSpec(memory_space=pl.ANY)


def once(shape):
    return pl.BlockSpec(shape, lambda *_: (0,) * len(shape), pipeline_mode=pl.Buffered(1))


def far_count():
    return lax.axis_size("dp") // 4


def dp_peer(bits):
    return {"dp": lax.axis_index("dp") ^ bits}


def sibling():
    return {"tensor": 1 - lax.axis_index("tensor")}


def dp_peers():
    return [dp_peer(1), dp_peer(2)] + [dp_peer(4 * k) for k in range(1, far_count())]


def greet(peers):
    barrier = pltpu.get_barrier_semaphore()
    for peer in peers:
        pl.semaphore_signal(barrier, inc=1, device_id=peer, device_id_type=MESH)
    pl.semaphore_wait(barrier, len(peers))


def remote(source, target, send, recv, peer):
    return pltpu.make_async_remote_copy(
        src_ref=source, dst_ref=target, send_sem=send, recv_sem=recv, device_id=peer, device_id_type=MESH
    )


def gather_sems():
    count = 7 * far_count() - 1
    return [pltpu.SemaphoreType.DMA((count,)), pltpu.SemaphoreType.DMA((count,)), pltpu.SemaphoreType.DMA]


class Gather:
    def __init__(self, source, whole, send, recv, local=None):
        self.source, self.whole, self.send, self.recv, self.local = source, whole, send, recv, local
        self.me = lax.axis_index("dp")
        self.far = far_count()
        self.each = whole.shape[0] // lax.axis_size("dp")
        self.half = self.each // 2

    def block(self, bits):
        start = pl.multiple_of((self.me ^ bits) * self.each, self.each)
        return self.whole.at[pl.ds(start, self.each)]

    def piece(self, bits, part):
        start = pl.multiple_of((self.me ^ bits) * self.each + part * self.half, self.half)
        return self.whole.at[pl.ds(start, self.half)]


    def along(self, k):
        return k - 1, self.source, self.block(0), 4 * k, self.block(4 * k)

    def first(self, k, part, bit):
        index = self.far - 1 + 4 * k + 2 * part + bit - 1
        if k == 0:
            source = self.source.at[pl.ds(part * self.half, self.half)]
        else:
            source = self.piece(4 * k, part)
        return index, source, self.piece(4 * k, part), bit, self.piece(4 * k + bit, part)

    def second(self, k, part):
        index = 5 * self.far - 1 + 2 * k + part
        source = self.piece(4 * k + 2 - part, part)
        return index, source, source, 1 + part, self.piece(4 * k + 3, part)

    def outgoing(self, transfer):
        index, source, target, bits, _ = transfer
        return remote(source, target, self.send.at[index], self.recv.at[index], dp_peer(bits))

    def start(self, transfer):
        self.outgoing(transfer).start()

    def sent(self, transfer):
        self.outgoing(transfer).wait_send()

    def arrived(self, transfer):
        index, _, _, bits, landing = transfer
        remote(landing, landing, self.send.at[index], self.recv.at[index], dp_peer(bits)).wait_recv()

    def kept(self):
        return pltpu.make_async_copy(self.source, self.block(0), self.local)

    def pass_on(self, k):
        for part, bit in ((0, 2), (1, 1), (0, 1), (1, 2)):
            self.start(self.first(k, part, bit))

    def begin(self):
        if self.local is not None:
            self.kept().start()
        for k in range(1, self.far):
            self.start(self.along(k))
        self.pass_on(0)

    def spread(self, k):
        self.arrived(self.along(k))
        self.pass_on(k)

    def turn(self, k):
        self.arrived(self.first(k, 0, 2))
        self.start(self.second(k, 0))
        self.arrived(self.first(k, 1, 1))
        self.start(self.second(k, 1))

    def finish(self):
        for k in range(self.far):
            self.arrived(self.first(k, 0, 1))
            self.arrived(self.first(k, 1, 2))
            for part in range(2):
                self.arrived(self.second(k, part))
        for k in range(1, self.far):
            self.sent(self.along(k))
        for k in range(self.far):
            for part in range(2):
                for bit in (1, 2):
                    self.sent(self.first(k, part, bit))
                self.sent(self.second(k, part))
        if self.local is not None:
            self.kept().wait()

    def plan(self, start):
        along = RATE * self.whole.shape[1]
        far = 2 * along / 3
        events = [(start, self.begin)]
        for k in range(1, self.far):
            at = start + 3.0 + far * (0.4 + 0.6 * k / (self.far - 1))
            events.append((at, functools.partial(self.spread, k)))
        for k in range(self.far):
            at = start + 6.0 + far * (0.4 + 0.6 * k / (self.far - 1)) + along / 4
            events.append((at, functools.partial(self.turn, k)))
        return events


class Plan:

    def __init__(self, step, steps, places, step_us):
        self.step, self.steps, self.places, self.step_us = step, steps, places, step_us
        self.events = {}
        self.ends = []

    def add(self, events, end):
        for time, action in events:
            index = min(int(time * self.places / self.step_us), self.steps * self.places - 1)
            self.events.setdefault(divmod(index, self.places), []).append((time, action))
        self.ends.append(end)

    def at(self, place):
        for key in sorted(self.events):
            if key[1] == place:

                @pl.when(self.step == key[0])
                def _(actions=sorted(self.events[key], key=lambda event: event[0])):
                    for _, action in actions:
                        action()

    def finish(self):
        for end in self.ends:
            end()


def add_gathers(plan, jobs, refs, start=0.0):
    for at, (source, whole, first, target, width) in enumerate(jobs):
        gather = Gather(
            source.at[:, pl.ds(first, width)], whole.at[:, pl.ds(target, width)], *refs[3 * at : 3 * at + 3]
        )
        plan.add(gather.plan(start), gather.finish)
        start += RATE * width


def pieces_of(width, most):
    return [(at, min(most, width - at)) for at in range(0, width, most)]


def scatter_scratch(columns, dim):
    far = far_count()
    half = dim // lax.axis_size("dp") // 2
    part = pltpu.VMEM((far, half, columns), BF16)
    return [part] * 8 + [
        pltpu.VMEM((far, 2, half, columns), BF16),
        pltpu.VMEM((far - 1, 2, half, columns), BF16),
        pltpu.SemaphoreType.DMA((5 + far,)),
        pltpu.SemaphoreType.DMA((5 + far,)),
        pltpu.SemaphoreType.DMA((3,)),
    ]


SCATTER_REFS = 13


class Scatter:
    def __init__(self, grads, first, out, refs):
        (
            self.mine_y, self.mine_x, self.got_dy, self.got_dx, self.got_x, self.got_y, self.got_y2, self.got_x2,
            self.mine, self.got_far, self.send, self.recv, self.local,
        ) = refs
        self.grads, self.out = grads, out
        self.columns = pl.ds(first, self.mine.shape[3])
        me = lax.axis_index("dp")
        self.far = far_count()
        self.low, self.high = lax.rem(me, 4), lax.div(me, 4)

    def copy(self, index, source, target, bits):
        return remote(source, target, self.send.at[index], self.recv.at[index], dp_peer(bits))

    def share(self, bits, part):
        return self.grads.at[:, self.low ^ bits, part, :, self.columns]

    def from_grads(self):
        return [
            self.copy(0, self.share(3, 0), self.got_dy, 1),
            self.copy(1, self.share(3, 1), self.got_dx, 2),
            self.copy(2, self.share(1, 0), self.got_x, 1),
            self.copy(3, self.share(2, 1), self.got_y, 2),
        ]

    def added(self):
        return [self.copy(4, self.mine_y, self.got_y2, 2), self.copy(5, self.mine_x, self.got_x2, 1)]

    def along(self):
        return [
            self.copy(5 + k, self.mine.at[self.high ^ k], self.got_far.at[k - 1], 4 * k) for k in range(1, self.far)
        ]

    def loads(self):
        own = self.grads.at[:, self.low, :, :, self.columns]
        return [
            pltpu.make_async_copy(self.share(2, 0), self.mine_y, self.local.at[0]),
            pltpu.make_async_copy(self.share(1, 1), self.mine_x, self.local.at[1]),
            pltpu.make_async_copy(own, self.mine, self.local.at[2]),
        ]

    def begin(self):
        for copy in self.from_grads() + self.loads():
            copy.start()

    def second(self):
        loads, got, added = self.loads(), self.from_grads(), self.added()
        loads[0].wait()
        got[0].wait_recv()
        self.mine_y[...] = add(self.mine_y[...], self.got_dy[...]).astype(BF16)
        added[0].start()
        loads[1].wait()
        got[1].wait_recv()
        self.mine_x[...] = add(self.mine_x[...], self.got_dx[...]).astype(BF16)
        added[1].start()

    def third(self):
        got, added = self.from_grads(), self.added()
        self.loads()[2].wait()
        got[2].wait_recv()
        added[0].wait_recv()
        self.mine[:, 0] = add(self.mine[:, 0], self.got_x[...], self.got_y2[...]).astype(BF16)
        got[3].wait_recv()
        added[1].wait_recv()
        self.mine[:, 1] = add(self.mine[:, 1], self.got_y[...], self.got_x2[...]).astype(BF16)
        for copy in self.along():
            copy.start()

    def finish(self):
        for copy in self.along():
            copy.wait_recv()
        self.out[...] = add(self.mine[self.high], *[self.got_far[k] for k in range(self.far - 1)])
        for copy in self.from_grads() + self.added() + self.along():
            copy.wait_send()


    def plan(self, start):
        along = RATE * self.mine.shape[3]
        times = (start, start + 4 + 2 * along / 3, start + 8 + along)
        return list(zip(times, (self.begin, self.second, self.third)))


def scatters_scratch(jobs, dim):
    scratch = []
    for _, width in jobs:
        scratch += scatter_scratch(width, dim)
    return scratch


def scatter_outs(jobs, dim):
    half = dim // lax.axis_size("dp") // 2
    shapes = [jax.ShapeDtypeStruct((2, half, width), F32) for _, width in jobs]
    return shapes, [once(shape.shape) for shape in shapes]


def add_scatters(plan, jobs, sources, outs, refs, start=0.0):
    for at, (first, width) in enumerate(jobs):
        scatter = Scatter(sources[at], first, outs[at], refs[SCATTER_REFS * at : SCATTER_REFS * (at + 1)])
        plan.add(scatter.plan(start), scatter.finish)
        start += RATE * width


def grad_shape(dim, columns):
    return jax.ShapeDtypeStruct((far_count(), 4, 2, dim // lax.axis_size("dp") // 2, columns), BF16)


def add(*terms):
    total = terms[0].astype(F32)
    for term in terms[1:]:
        total = total + term.astype(F32)
    return total


def call(kernel, name, number, steps, in_specs, out_specs, out_shape, scratch, operands):
    return pl.pallas_call(
        kernel,
        grid=steps if isinstance(steps, tuple) else (steps,),
        in_specs=in_specs,
        out_specs=out_specs,
        out_shape=out_shape,
        scratch_shapes=scratch,
        compiler_params=params(number),
        name=name,
    )(*operands)


def spread_gains(slab, column):
    dim = slab.shape[0]
    blocks = lax.axis_size("dp")
    each = dim // blocks
    lane_block = lax.broadcasted_iota(jnp.int32, (blocks, dim), 1) // each
    block = lax.broadcasted_iota(jnp.int32, (blocks, dim), 0)
    rows = []
    for which in range(2):
        picked = jnp.concatenate(
            [slab[each * b : each * b + 16, column : column + 128].astype(F32)[which : which + 1] for b in range(blocks)], 0
        )
        tiled = jnp.concatenate([picked] * (dim // 128), 1)
        rows.append(jnp.sum(jnp.where(lane_block == block, tiled, 0.0), axis=0, keepdims=True))
    return jnp.concatenate(rows + [jnp.zeros((6, dim), F32)], 0)


def part_block(width, per, rows, lag=0, last=None):
    def place(i):
        i = i - lag if last is None else jnp.clip(i - lag, 0, last)
        return lax.div(i, per), lax.rem(i, per), 0

    return pl.BlockSpec((1, rows, width), place)


def core_block(width, per, rows, other, last=None):
    def place(i):
        if last is not None:
            i = jnp.minimum(i, last)
        core = lax.axis_index("tensor")
        return lax.div(i, per), (1 - core if other else core) * per + lax.rem(i, per), 0

    return pl.BlockSpec((1, rows, width), place)


def root_mean(values):
    return lax.rsqrt(jnp.mean(values * values, axis=-1, keepdims=True) + 1e-05)


def norm_slope(values, scaled):
    inverse = root_mean(values)
    normed = values * inverse
    return inverse * (scaled - normed * jnp.mean(scaled * normed, axis=-1, keepdims=True))


def half_sems(count):
    return [pltpu.SemaphoreType.DMA((count,)), pltpu.SemaphoreType.DMA((count,))]


def chunk_slices(width):
    return [(at, min(256, width - at)) for at in range(0, width, 256)]


def build_slabs(edges, gate, up, down_t, out_t, slabs):
    at = out_t.shape[1]
    slabs[:, :at] = out_t[...]
    units = gate.shape[1]

    def place(ref, low, high):
        nonlocal at
        end = min(high, units)
        slabs[:, at : at + end - low] = ref[:, low:end]
        if end < high:
            slabs[:, at + end - low : at + high - low] = jnp.zeros((slabs.shape[0], high - end), BF16)
        at += high - low

    for low, high in edges:
        for start, width in chunk_slices(high - low):
            place(gate, low + start, low + start + width)
            place(up, low + start, low + start + width)
        place(down_t, low, high)


def project_kernel(
    edges, inputs, w_query, w_key, w_value, gain_attn, gain_mlp, gate, up, down_t, out_t,
    h_out, qkv_out, gain_out, whole_in, slabs, x_own, x_other, h_all, qkv_all, slab, gain_slab,
    local, swap_send, swap_recv, *sems,
):
    micro, rows, _ = x_own.shape
    each = w_query.shape[0]
    core = lax.axis_index("tensor")
    parts = 2 * micro

    def load(m):
        return pltpu.make_async_copy(inputs.at[m], x_own.at[m], local.at[m])

    def swap(m):
        return remote(inputs.at[m], x_other.at[m], swap_send.at[m], swap_recv.at[m], sibling())

    def place(t):
        first = pl.multiple_of((core if t < micro else 1 - core) * rows, rows)
        return t % micro, pl.ds(first, rows)

    def store_h(t):
        return pltpu.make_async_copy(h_all.at[t], h_out.at[place(t)], local.at[micro + t])

    def store_qkv(t):
        return pltpu.make_async_copy(qkv_all.at[t], qkv_out.at[place(t)], local.at[micro + parts + t])

    def keep():
        return pltpu.make_async_copy(slab, whole_in, local.at[micro + 2 * parts])

    def norm(t):
        x = (x_own if t < micro else x_other)[t % micro].astype(F32)
        h_all[t] = (x * root_mean(x) * gain_out[0:1]).astype(BF16)
        store_h(t).start()

    for m in range(micro):
        load(m).start()
    mine = pl.ds(pl.multiple_of(lax.axis_index("dp") * each, each), each)
    at = 0
    for ref in (w_query, w_key, w_value):
        slab[mine, at : at + ref.shape[1]] = ref[...]
        at += ref.shape[1]
    both = jnp.concatenate([gain_attn[...], gain_mlp[...]], 0).astype(F32)
    both = jnp.concatenate([both, both], 1)
    gain_slab[mine] = jnp.concatenate([both, jnp.zeros((each - 2, both.shape[1]), F32)], 0).astype(BF16)
    greet(dp_peers() + [sibling()])
    gains = Gather(gain_slab.at[mine], gain_slab, *sems[:2])
    weights = Gather(slab.at[mine], slab, *sems[2:])
    gains.begin()
    weights.begin()
    for m in range(micro):
        swap(m).start()
    build_slabs(edges, gate, up, down_t, out_t, slabs)
    for k in range(1, gains.far):
        gains.spread(k)
    for k in range(gains.far):
        gains.turn(k)
    gains.finish()
    gain_out[...] = spread_gains(gain_slab, 0)
    duties = [functools.partial(weights.spread, k) for k in range(1, weights.far)]
    duties += [functools.partial(weights.turn, k) for k in range(weights.far)]
    for t in range(parts):
        if t < micro:
            load(t).wait()
        else:
            swap(t - micro).wait()
        norm(t)
        if duties:
            duties.pop(0)()
    for duty in duties:
        duty()
    weights.finish()
    keep().start()
    for t in range(parts):
        qkv_all[t] = mm(h_all[t], slab[...]).astype(BF16)
        store_qkv(t).start()
    for t in range(parts):
        store_h(t).wait()
        store_qkv(t).wait()
    keep().wait()


def project(edges, inputs, w_query, w_key, w_value, gain_attn, gain_mlp, w_gate, w_up, down_t, out_t):
    micro, rows, dim = inputs.shape
    each = w_query.shape[0]
    columns = w_query.shape[1] + w_key.shape[1] + w_value.shape[1]
    all_columns = out_t.shape[1] + 3 * edges[-1][1]
    locals_ = (w_query, w_key, w_value, gain_attn, gain_mlp, w_gate, w_up, down_t, out_t)
    return call(
        functools.partial(project_kernel, edges),
        "project",
        1,
        1,
        [anywhere()] + [once(a.shape) for a in locals_],
        [anywhere(), anywhere(), once((8, dim)), anywhere(), once((each, all_columns))],
        [
            jax.ShapeDtypeStruct((micro, 2 * rows, dim), BF16),
            jax.ShapeDtypeStruct((micro, 2 * rows, columns), BF16),
            jax.ShapeDtypeStruct((8, dim), F32),
            jax.ShapeDtypeStruct((dim, columns), BF16),
            jax.ShapeDtypeStruct((each, all_columns), BF16),
        ],
        [
            pltpu.VMEM((micro, rows, dim), BF16),
            pltpu.VMEM((micro, rows, dim), BF16),
            pltpu.VMEM((2 * micro, rows, dim), BF16),
            pltpu.VMEM((2 * micro, rows, columns), BF16),
            pltpu.VMEM((dim, columns), BF16),
            pltpu.VMEM((dim, 128), BF16),
            pltpu.SemaphoreType.DMA((5 * micro + 1,)),
        ]
        + half_sems(micro)
        + gather_sems()[:2]
        + gather_sems()[:2],
        (inputs, *locals_),
    )


def fill_mask(mask, lengths, micro_step):
    tiles = mask.shape[0]
    row = lax.broadcasted_iota(jnp.int32, (tiles * TILE, TILE), 0)
    start = jnp.zeros_like(row)
    end = 0
    for d in range(lengths.shape[1]):
        end = end + lengths[micro_step, d]
        start = jnp.where(row >= end, end, start)
    lane = lax.broadcasted_iota(jnp.int32, (tiles * TILE, TILE), 1)
    for j in range(tiles):
        i = min(tiles, j + SPAN + 1)
        tall = (i - j) * TILE
        below = slice(j * TILE, i * TILE)
        column = lane[:tall] + j * TILE
        allowed = (column <= row[below]) & (column >= start[below])
        mask[j, :tall, :] = jnp.where(allowed, 1.0, 0.0)


def add_rows(total, j, tiles, value):
    end = min(tiles, j + SPAN + 1)
    begun = min(tiles, j + SPAN) if j else 0
    if begun > j:
        total[j * TILE : begun * TILE] += value[: (begun - j) * TILE]
    if end > max(begun, j):
        start = max(begun, j)
        total[start * TILE : end * TILE] = value[(start - j) * TILE :]


def attend_kernel(
    jobs, lengths, qkv, grad_own, slabs, mix_ref, inv_ref, grad_other, whole_out, unit, mask, queries, values, total, *sems
):
    m = pl.program_id(0)
    group = qkv.shape[1]
    tiles = group // TILE
    pairs = mix_ref.shape[2] // 128
    lane = lax.broadcasted_iota(jnp.int32, (group, 128), 1)
    zero = jnp.zeros((), BF16)

    def swap():
        return remote(grad_own, grad_other, sems[0], sems[1], sibling())

    plan = Plan(m, lengths.shape[0], pairs, 8.0)
    plan.add([(0.0, lambda: swap().start())], lambda: swap().wait())
    add_gathers(plan, [(slabs, (whole_out, unit)[w], *job) for w, *job in jobs], sems[2:])

    @pl.when(m == 0)
    def _():
        greet(dp_peers() + [sibling()])

    fill_mask(mask, lengths, m)
    query = qkv[0, :, :128] * jnp.asarray(0.25, BF16)
    for pair in range(pairs):
        at = 256 + 128 * pair
        now = pair % 2
        for side in range(2):
            mine = lane // VD == side
            queries[now, side] = jnp.where(lane // FEAT == 2 * pair + side, query, zero)
            values[now, side, :, :128] = jnp.where(mine, qkv[0, :, at : at + 128], zero)
            values[now, side, :, 128:] = mine.astype(F32).astype(BF16)
        for j in range(tiles):
            if j == 0:
                plan.at(pair)
            i = min(tiles, j + SPAN + 1)
            tall = (i - j) * TILE
            here, below = slice(j * TILE, (j + 1) * TILE), slice(j * TILE, i * TILE)
            scores = mm(queries[now, :, below].reshape(2 * tall, 128), qkv[0, here, 128:256], NT)
            allowed = mask[j, :tall]
            weights = []
            for side in range(2):
                t = scores[side * tall : (side + 1) * tall] + 1.0
                weights.append(((t * t + 1.0) * allowed).astype(BF16))
            part = mm(jnp.concatenate(weights, 1), values[now, :, here].reshape(2 * TILE, 256))
            add_rows(total.at[now], j, tiles, part)
        inverse = 1.0 / total[now, :, 128:]
        mix_ref[0, :, 128 * pair : 128 * (pair + 1)] = (total[now, :, :128] * inverse).astype(BF16)
        turned = inverse.T
        inv_ref[0, pair, 0:1] = turned[0:1]
        inv_ref[0, pair, 1:2] = turned[VD : VD + 1]

    @pl.when(m == pl.num_programs(0) - 1)
    def _():
        plan.finish()


def whole_group(width, group):
    return pl.BlockSpec((1, group, width), lambda m: (m, 0, 0))


def lengths_spec(lengths):
    return pl.BlockSpec(lengths.shape, lambda *_: (0, 0), memory_space=pltpu.SMEM)


def attend_all(qkv, lengths, out_grad, slabs, out_columns, jobs):
    micro, group, columns = qkv.shape
    dim = out_grad.shape[2]
    wide = columns - 256
    dma = pltpu.SemaphoreType.DMA
    unit = sum(job[3] for job in jobs if job[0])
    return call(
        functools.partial(attend_kernel, jobs),
        "attend",
        2,
        micro,
        [lengths_spec(lengths), whole_group(columns, group), anywhere(), anywhere()],
        [
            whole_group(wide, group),
            pl.BlockSpec((1, wide // 128, 8, group), lambda m: (m, 0, 0, 0)),
            anywhere(),
            anywhere(),
            anywhere(),
        ],
        [
            jax.ShapeDtypeStruct((micro, group, wide), BF16),
            jax.ShapeDtypeStruct((micro, wide // 128, 8, group), F32),
            jax.ShapeDtypeStruct(out_grad.shape, BF16),
            jax.ShapeDtypeStruct((dim, out_columns), BF16),
            jax.ShapeDtypeStruct((dim, unit), BF16),
        ],
        [
            pltpu.VMEM((group // TILE, TILE * (SPAN + 1), TILE), F32),
            pltpu.VMEM((2, 2, group, 128), BF16),
            pltpu.VMEM((2, 2, group, 256), BF16),
            pltpu.VMEM((2, group, 256), F32),
            dma,
            dma,
        ]
        + gather_sems() * len(jobs),
        (lengths, qkv, out_grad, slabs),
    )


def attend_back_kernel(jobs, lengths, qkv, mix_ref, inv_ref, dmix_ref, *refs):
    sources, refs = refs[: len(jobs)], refs[len(jobs) :]
    dqkv, refs = refs[0], refs[1:]
    outs, refs = refs[: len(jobs)], refs[len(jobs) :]
    (mask, queries, queries_t, keys, douts, douts_t, deltas, dv_t, dk_t, dq), refs = refs[:10], refs[10:]
    m = pl.program_id(0)
    group = qkv.shape[1]
    tiles = group // TILE
    pairs = mix_ref.shape[2] // 128
    lane = lax.broadcasted_iota(jnp.int32, (group, 128), 1)
    zero = jnp.zeros((), BF16)
    plan = Plan(m, lengths.shape[0], pairs, 15.2)
    add_scatters(plan, jobs, sources, outs, refs)

    @pl.when(m == 0)
    def _():
        greet(dp_peers())

    fill_mask(mask, lengths, m)
    queries_t[...] = (qkv[0, :, :128].astype(F32) * 0.5).T.astype(BF16)
    query = qkv[0, :, :128] * jnp.asarray(0.25, BF16)
    key = qkv[0, :, 128:256] * jnp.asarray(0.5, BF16)
    for pair in range(pairs):
        now = pair % 2
        lanes = slice(128 * pair, 128 * (pair + 1))
        value = slice(256 + 128 * pair, 384 + 128 * pair)
        inverse = jnp.concatenate(
            [jnp.broadcast_to(inv_ref[0, pair, s : s + 1, :], (VD, group)) for s in range(2)], 0
        ).T
        dout_low = (dmix_ref[0, :, lanes].astype(F32) * inverse).astype(BF16)
        dout = dout_low.astype(F32)
        douts_t[now] = dout.T.astype(BF16)
        product = dout * mix_ref[0, :, lanes].astype(F32)
        for side in range(2):
            mine = lane // VD == side
            head = lane // FEAT == 2 * pair + side
            queries[now, side] = jnp.where(head, query, zero)
            keys[now, side] = jnp.where(head, key, zero)
            douts[now, side] = jnp.where(mine, dout_low, zero)
            delta = jnp.sum(jnp.where(mine, product, 0.0), axis=1, keepdims=True)
            deltas[now, side] = jnp.broadcast_to(delta, (group, 128))
        for j in range(tiles):
            if j == 0:
                plan.at(pair)
            i = min(tiles, j + SPAN + 1)
            tall = (i - j) * TILE
            here, below = slice(j * TILE, (j + 1) * TILE), slice(j * TILE, i * TILE)
            scores = mm(queries[now, :, below].reshape(2 * tall, 128), qkv[0, here, 128:256], NT)
            slopes = mm(douts[now, :, below].reshape(2 * tall, 128), qkv[0, here, value], NT)
            allowed = mask[j, :tall]
            d_scores = []
            for side in range(2):
                t = scores[side * tall : (side + 1) * tall] + 1.0
                masked = t * allowed
                delta = jnp.concatenate([deltas[now, side, below]] * (TILE // 128), 1)
                d_score = ((slopes[side * tall : (side + 1) * tall] - delta) * masked).astype(BF16)
                weights = (t * masked + allowed).astype(BF16)
                mine = slice(VD * side, VD * (side + 1))
                head = slice((2 * pair + side) * FEAT, (2 * pair + side + 1) * FEAT)
                dv_t[now, mine, here] = mm(douts_t[now, mine, below], weights)
                dk_t[head, here] = mm(queries_t[head, below], d_score)
                d_scores.append(d_score)
            part = mm(jnp.concatenate(d_scores, 1), keys[now, :, here].reshape(2 * TILE, 128))
            if pair:
                dq[below] += part
            else:
                add_rows(dq, j, tiles, part)
        dqkv[0, :, value] = dv_t[now].T.astype(BF16)
    dqkv[0, :, 128:256] = dk_t[...].T.astype(BF16)
    dqkv[0, :, :128] = dq[...].astype(BF16)

    @pl.when(m == pl.num_programs(0) - 1)
    def _():
        plan.finish()


def attend_back(qkv, mix, inverse, dmix, lengths, sources, jobs):
    micro, group, columns = qkv.shape
    wide = columns - 256
    dim = sources[0].shape[3] * 2 * lax.axis_size("dp")
    shapes, specs = scatter_outs(jobs, dim)
    pair_rows = pltpu.VMEM((2, 2, group, 128), BF16)
    return call(
        functools.partial(attend_back_kernel, jobs),
        "attend_back",
        8,
        micro,
        [
            lengths_spec(lengths),
            whole_group(columns, group),
            whole_group(wide, group),
            pl.BlockSpec((1, wide // 128, 8, group), lambda m: (m, 0, 0, 0)),
            whole_group(wide, group),
        ]
        + [anywhere()] * len(jobs),
        [whole_group(columns, group)] + specs,
        [jax.ShapeDtypeStruct((micro, group, columns), BF16)] + shapes,
        [
            pltpu.VMEM((group // TILE, TILE * (SPAN + 1), TILE), F32),
            pair_rows,
            pltpu.VMEM((128, group), BF16),
            pair_rows,
            pair_rows,
            pltpu.VMEM((2, 128, group), BF16),
            pltpu.VMEM((2, 2, group, 128), F32),
            pltpu.VMEM((2, 128, group), F32),
            pltpu.VMEM((128, group), F32),
            pltpu.VMEM((group, 128), F32),
        ]
        + scatters_scratch(jobs, dim),
        (lengths, qkv, mix, inverse, dmix, *sources),
    )


def out_kernel(
    jobs, mix_own, mix_other, x, weights, gains, slabs, resid_out, h_out, h_other, unit,
    parts, sent, got, h_sent, send, recv, *sems,
):
    i = pl.program_id(0)
    count, rows = got.shape[0], got.shape[1]
    per = h_other.shape[1] // rows
    plan = Plan(i, 2 * count, 1, 0.95)
    add_gathers(plan, [(slabs, unit, *job) for job in jobs], sems)

    def swap(k):
        return remote(sent.at[k], got.at[k], send.at[k], recv.at[k], sibling())

    def swap_h(k):
        place = h_other.at[lax.div(k, per), pl.ds(pl.multiple_of(lax.rem(k, per) * rows, rows), rows)]
        return remote(h_sent.at[k], place, send.at[count + k], recv.at[count + k], sibling())

    @pl.when(i == 0)
    def _():
        greet(dp_peers() + [sibling()])

    plan.at(0)

    @pl.when(i < count)
    def _():
        both = jnp.concatenate([mix_other[0], mix_own[0]], 0)
        part = mm(both, weights[...], NT)
        sent[i] = part[:rows].astype(BF16)
        parts[i] = part[rows:]
        swap(i).start()

    @pl.when(i >= count)
    def _():
        k = i - count
        swap(k).wait_recv()
        resid = x[0].astype(F32) + parts[k] + got[k].astype(F32)
        resid_out[0] = resid.astype(BF16)
        h = (resid * root_mean(resid) * gains[1:2]).astype(BF16)
        h_out[0] = h
        h_sent[k] = h
        swap_h(k).start()

    @pl.when(i == 2 * count - 1)
    def _():
        plan.finish()
        for k in range(count):
            swap(k).wait_send()
            swap_h(k).wait()


def out_project(mix, x, weights, gains, slabs, jobs, rows=256):
    micro, own_rows, dim = x.shape
    wide = mix.shape[2]
    per = own_rows // rows
    count = micro * per
    late = part_block(dim, per, rows, count, count - 1)
    shape = jax.ShapeDtypeStruct((micro, own_rows, dim), BF16)
    buffer = pltpu.VMEM((count, rows, dim), BF16)
    return call(
        functools.partial(out_kernel, jobs),
        "out_project",
        3,
        2 * count,
        [
            core_block(wide, per, rows, False, count - 1),
            core_block(wide, per, rows, True, count - 1),
            late,
            once(weights.shape),
            once((8, dim)),
            anywhere(),
        ],
        [late, late, anywhere(), anywhere()],
        [shape, shape, shape, jax.ShapeDtypeStruct((dim, sum(job[2] for job in jobs)), BF16)],
        [pltpu.VMEM((count, rows, dim), F32), buffer, buffer, buffer]
        + half_sems(2 * count)
        + gather_sems() * len(jobs),
        (mix, mix, x, weights, gains, slabs),
    )


FEED_US = 6.8


def feed_kernel(steps, width, loads, first, last, gathers, scatters, h_own, h_other, g_own, g_other, *refs):
    def take(number):
        nonlocal refs
        taken, refs = refs[:number], refs[number:]
        return taken

    weights = take(len(loads))
    before = None if first else take(4)
    slabs = take(1)[0] if gathers else None
    sources = take(len(scatters))
    if last:
        resid, g_late, resid_end, g_end, gains, mixed_out, d_out, d_other = take(8)
    else:
        out_own, out_other, dm_own, dm_other = take(4)
    grads = take(1)[0]
    unit = take(1)[0] if gathers else None
    outs = take(len(scatters))
    slab, total, h, g, hidden_s, dgu_s, rounded, load_sems, out_sem = take(9)
    i = pl.program_id(0)
    rows = h_own.shape[1]
    plan = Plan(i, steps, 1, FEED_US * width / 512)
    add_gathers(plan, [(slabs, unit, *job) for job in gathers], take(3 * len(gathers)))
    busy = sum(RATE * job[2] for job in gathers)
    add_scatters(plan, scatters, sources, outs, take(SCATTER_REFS * len(scatters)), busy)
    if last:
        dm_sent, dm_got, out_sent, out_got, dm_kept, out_kept, d_sent, mixed_s, send, recv, local = take(11)
        per = d_other.shape[1] // rows

        def place(ref, k):
            return ref.at[lax.div(k, per), pl.ds(pl.multiple_of(lax.rem(k, per) * rows, rows), rows)]

        def swaps(k):
            return [
                remote(dm_sent.at[k], dm_got.at[k + 1], send.at[3 * k], recv.at[3 * k], sibling()),
                remote(out_sent.at[k], out_got.at[k + 1], send.at[3 * k + 1], recv.at[3 * k + 1], sibling()),
            ]

        def results(k):
            return [
                remote(d_sent.at[k + 1], place(d_other, k), send.at[3 * k + 2], recv.at[3 * k + 2], sibling()),
                pltpu.make_async_copy(d_sent.at[k + 1], place(d_out, k), local.at[2 * k]),
                pltpu.make_async_copy(mixed_s.at[k + 1], place(mixed_out, k), local.at[2 * k + 1]),
            ]

        def finish_part(slot, resid, g_late):
            values = resid[0].astype(F32)
            mixed_s[slot] = add(values, out_kept[lax.rem(slot, 2)], out_got[slot]).astype(BF16)
            scaled = add(dm_kept[lax.rem(slot, 2)], dm_got[slot]) * gains[1:2]
            d_sent[slot] = (g_late[0].astype(F32) + norm_slope(values, scaled)).astype(BF16)

    def copies():
        made = []
        for at, (ref, (source, target, columns)) in enumerate(zip(weights, loads)):
            cut = ref.at[:, pl.ds(source, columns)]
            made.append(pltpu.make_async_copy(cut, slab.at[:, pl.ds(target, columns)], load_sems.at[at]))
        return made

    @pl.when(i == 0)
    def _():
        for copy in copies():
            copy.start()
        if last:
            zeros = jnp.zeros(dm_kept.shape[1:], BF16)
            for ref in (dm_got, out_got, dm_kept, out_kept):
                ref[0] = zeros
        greet(dp_peers() + ([sibling()] if last else []))

    plan.at(0)

    @pl.when(i == 0)
    def _():
        total[...] = jnp.zeros_like(total)
        for copy in copies():
            copy.wait()

    h[:rows], h[rows:] = h_other[0], h_own[0]
    g[:rows], g[rows:] = g_other[0], g_own[0]
    half = jnp.asarray(0.5, BF16)
    one = jnp.asarray(1.0, BF16)
    for at, wide in chunk_slices(width):
        both = slice(2 * at, 2 * (at + wide))
        gate_up = mm(h[...], slab[:, both]).astype(BF16)
        d_hidden = mm(g[...], slab[:, 2 * width + at : 2 * width + at + wide]).astype(BF16)
        gate, up = gate_up[:, :wide], gate_up[:, wide:]
        sigmoid = half * jnp.tanh(half * gate) + half
        silu = gate * sigmoid
        hidden_s[:, at : at + wide] = silu * up
        d_gate = d_hidden * up * (sigmoid + silu * (one - sigmoid))
        dgu_s[:, both] = jnp.concatenate([d_gate, d_hidden * silu], 1)
    dim = slab.shape[0]
    for at in range(0, dim, 512):
        cut = slice(at, at + 512)
        out = mm(hidden_s[...], slab[cut, 2 * width :], NT)
        dm = mm(dgu_s[...], slab[cut, : 2 * width], NT)
        parts_now = []
        for at_before, value in enumerate((out[rows:], out[:rows], dm[rows:], dm[:rows])):
            if not first:
                value = value + before[at_before][0, :, cut].astype(F32)
            parts_now.append(value.astype(BF16))
        if last:
            out_sent[i, :, cut], dm_sent[i, :, cut] = parts_now[1], parts_now[3]
            kept = lax.rem(i + 1, 2)
            out_kept[kept, :, cut], dm_kept[kept, :, cut] = parts_now[0], parts_now[2]
        else:
            out_own[0, :, cut], out_other[0, :, cut] = parts_now[0], parts_now[1]
            dm_own[0, :, cut], dm_other[0, :, cut] = parts_now[2], parts_now[3]
    if last:
        for swap in swaps(i):
            swap.start()

        @pl.when(i > 0)
        def _():
            for swap in swaps(i - 1):
                swap.wait_recv()

        finish_part(i, resid, g_late)
    total[:, : 2 * width] += mm(h[...], dgu_s[...], TN)
    total[:, 2 * width :] += mm(g[...], hidden_s[...], TN)
    if last:

        @pl.when(i > 0)
        def _():
            for copy in results(i - 1):
                copy.start()

    @pl.when(i == steps - 1)
    def _():
        rounded[...] = total[...].astype(BF16).reshape(rounded.shape)
        write = pltpu.make_async_copy(rounded, grads, out_sem)
        write.start()
        if last:
            for swap in swaps(steps - 1):
                swap.wait_recv()
            finish_part(steps, resid_end, g_end)
            for copy in results(steps - 1):
                copy.start()
        plan.finish()
        if last:
            for k in range(steps):
                for copy in swaps(k):
                    copy.wait_send()
                for copy in results(k):
                    copy.wait()
        write.wait()


def feed(number, rows_in, loads, width, before, slabs, gathers, sources, scatters, last=None, rows=256):
    micro, own_rows, dim = rows_in[0].shape
    columns = 3 * width
    per = own_rows // rows
    steps = micro * per
    part = part_block(dim, per, rows)
    shape = jax.ShapeDtypeStruct((micro, own_rows, dim), BF16)
    grads = grad_shape(dim, columns)
    first = before is None
    in_specs = [part] * 4 + [anywhere()] * len(loads)
    operands = list(rows_in) + [load[0] for load in loads]
    scratch = [
        pltpu.VMEM((dim, columns), BF16),
        pltpu.VMEM((dim, columns), F32),
        pltpu.VMEM((2 * rows, dim), BF16),
        pltpu.VMEM((2 * rows, dim), BF16),
        pltpu.VMEM((2 * rows, width), BF16),
        pltpu.VMEM((2 * rows, 2 * width), BF16),
        pltpu.VMEM(grads.shape, BF16),
        pltpu.SemaphoreType.DMA((len(loads),)),
        pltpu.SemaphoreType.DMA,
    ]
    if not first:
        in_specs += [part] * 4
        operands += list(before)
    if gathers:
        in_specs.append(anywhere())
        operands.append(slabs)
    in_specs += [anywhere()] * len(scatters)
    operands += sources
    if last:
        resid, gains = last
        late = part_block(dim, per, rows, 1, steps - 1)
        end = pl.BlockSpec((1, rows, dim), lambda i: (micro - 1, per - 1, 0), pipeline_mode=pl.Buffered(1))
        in_specs += [late, late, end, end, once((8, dim))]
        operands += [resid, rows_in[2], resid, rows_in[2], gains]
        out_specs, out_shape = [anywhere()] * 4, [shape] * 3 + [grads]
    else:
        out_specs, out_shape = [part] * 4 + [anywhere()], [shape] * 4 + [grads]
    plain = len(out_shape)
    if gathers:
        out_specs.append(anywhere())
        out_shape.append(jax.ShapeDtypeStruct((dim, sum(job[2] for job in gathers)), BF16))
        scratch += gather_sems() * len(gathers)
    if scatters:
        shapes, specs = scatter_outs(scatters, dim)
        out_specs += specs
        out_shape += shapes
        scratch += scatters_scratch(scatters, dim)
    if last:
        plain_slots, late_slots = pltpu.VMEM((steps, rows, dim), BF16), pltpu.VMEM((steps + 1, rows, dim), BF16)
        two_slots = pltpu.VMEM((2, rows, dim), BF16)
        scratch += [plain_slots, late_slots] * 2 + [two_slots] * 2 + [late_slots] * 2 + half_sems(3 * steps)
        scratch.append(pltpu.SemaphoreType.DMA((2 * steps,)))
    results = call(
        functools.partial(
            feed_kernel, steps, width, [load[1:] for load in loads], first, last is not None, gathers, scatters
        ),
        "feed",
        number,
        steps,
        in_specs,
        out_specs,
        out_shape,
        scratch,
        operands,
    )
    rest = list(results[plain:])
    unit = rest.pop(0) if gathers else None
    return results[: plain - 1], results[plain - 1], unit, rest


def back_out_kernel(micro, jobs, d_own, d_other, mix, weights, *refs):
    sources, refs = refs[: len(jobs)], refs[len(jobs) :]
    (dmix, grads), refs = refs[:2], refs[2:]
    outs, refs = refs[: len(jobs)], refs[len(jobs) :]
    (d, total, rounded, out_sem), refs = refs[:4], refs[4:]
    i = pl.program_id(0)
    rows = d_own.shape[1]
    plan = Plan(i, micro, 1, 4.5)
    add_scatters(plan, jobs, sources, outs, refs)

    @pl.when(i == 0)
    def _():
        greet(dp_peers())
        total[...] = jnp.zeros_like(total)

    plan.at(0)
    core = lax.axis_index("tensor")
    d[pl.ds(pl.multiple_of(core * rows, rows), rows)] = d_own[0]
    d[pl.ds(pl.multiple_of((1 - core) * rows, rows), rows)] = d_other[0]
    dmix[0] = mm(d[...], weights[...]).astype(BF16)
    total[...] += mm(d[...], mix[0], TN)

    @pl.when(i == pl.num_programs(0) - 1)
    def _():
        rounded[...] = total[...].astype(BF16).reshape(rounded.shape)
        write = pltpu.make_async_copy(rounded, grads, out_sem)
        write.start()
        plan.finish()
        write.wait()


def back_out(d_own, d_other, mix, weights, sources, jobs):
    micro, rows, dim = d_own.shape
    columns = mix.shape[2]
    part = pl.BlockSpec((1, rows, dim), lambda i: (i, 0, 0))
    grads = grad_shape(dim, columns)
    shapes, specs = scatter_outs(jobs, dim)
    return call(
        functools.partial(back_out_kernel, micro, jobs),
        "back_out",
        7,
        micro,
        [part, part, whole_group(columns, 2 * rows), once(weights.shape)] + [anywhere()] * len(jobs),
        [whole_group(columns, 2 * rows), anywhere()] + specs,
        [jax.ShapeDtypeStruct((micro, 2 * rows, columns), BF16), grads] + shapes,
        [
            pltpu.VMEM((2 * rows, dim), BF16),
            pltpu.VMEM((dim, columns), F32),
            pltpu.VMEM(grads.shape, BF16),
            pltpu.SemaphoreType.DMA,
        ]
        + scatters_scratch(jobs, dim),
        (d_own, d_other, mix, weights, *sources),
    )


def back_in_kernel(
    micro, feed_jobs, out_jobs, in_jobs, h, dqkv_all, dqkv, x, d_own, weights, gains, grads_last,
    w_query, w_key, w_value, slabs, *refs,
):
    jobs = out_jobs + in_jobs
    feed_count = sum(len(chunk) for chunk in feed_jobs)
    feed_grads, refs = refs[:feed_count], refs[feed_count:]
    (input_grad, gain_sums, grads), refs = refs[:3], refs[3:]
    outs, refs = refs[: len(jobs)], refs[len(jobs) :]
    (total, sent, got, send, recv, out_sem, rounded, sums, sums_got, sums_sems), refs = refs[:10], refs[10:]
    i = pl.program_id(0)
    m = lax.rem(i, micro)
    plan = Plan(i, 3 * micro, 1, 2.4)
    split = SCATTER_REFS * len(out_jobs)
    add_scatters(plan, out_jobs, [grads_last] * len(out_jobs), outs, refs[:split])
    outs = outs[len(out_jobs) :]
    add_scatters(plan, in_jobs, [grads] * len(in_jobs), outs, refs[split:], 2.4 * micro)

    def swap(k):
        return remote(sent.at[k], got.at[k], send.at[k], recv.at[k], sibling())

    def swap_sums():
        return remote(sums, sums_got, sums_sems.at[0], sums_sems.at[1], sibling())

    @pl.when(i == 0)
    def _():
        greet(dp_peers() + [sibling()])
        total[...] = jnp.zeros_like(total)

    @pl.when(i < micro)
    def _():
        total[...] += mm(h[0], dqkv_all[0], TN)

    @pl.when(i == micro - 1)
    def _():
        rounded[...] = total[...].astype(BF16).reshape(rounded.shape)
        write = pltpu.make_async_copy(rounded, grads, out_sem)
        write.start()
        write.wait()

    plan.at(0)

    @pl.when(i >= micro)
    def _():
        part = mm(dqkv[0], weights[...], NT)

        @pl.when(i < 2 * micro)
        def _():
            sent[m] = part.astype(BF16)
            swap(m).start()

        @pl.when(i >= 2 * micro)
        def _():
            swap(m).wait_recv()
            scaled = (part + got[m].astype(F32)) * gains[0:1]
            input_grad[0] = (d_own[0].astype(F32) + norm_slope(x[0].astype(F32), scaled)).astype(BF16)

    @pl.when(i == 3 * micro - 1)
    def _():
        each = slabs.shape[0]
        sizes = [sum(wide for _, wide in chunk) for chunk in feed_jobs]
        at = slabs.shape[1] - sum(sizes)
        index = 0
        mid = jnp.zeros((each, 128), F32)
        for size, chunk in zip(sizes, feed_jobs):
            for first, wide in chunk:
                value = feed_grads[index][...].reshape(each, wide)
                for column in range(0, wide, 128):
                    if first + column < 2 * (size // 3):
                        lanes = slice(at + first + column, at + first + column + 128)
                        mid = mid + value[:, column : column + 128] * slabs[:, lanes].astype(F32)
                index += 1
            at += size
        sums[1] = mid
        plan.finish()
        near = jnp.zeros((each, 128), F32)
        at = 0
        columns = [out[...].reshape(each, out.shape[2]) for out in outs]
        columns = jnp.concatenate(columns, 1) if len(columns) > 1 else columns[0]
        for ref in (w_query, w_key, w_value):
            for column in range(0, ref.shape[1], 128):
                near = near + columns[:, at : at + 128] * ref[:, column : column + 128].astype(F32)
                at += 128
        sums[0] = near
        swap_sums().start()
        for k in range(micro):
            swap(k).wait_send()
        swap_sums().wait()
        gain_sums[...] = sums[...] + sums_got[...]


def back_in(h, dqkv, x, d_own, weights, gains, grads_last, w_in, slabs, feed_grads, feed_jobs, out_jobs, in_jobs):
    jobs = out_jobs + in_jobs
    micro, rows, dim = x.shape
    columns = dqkv.shape[2]
    each = slabs.shape[0]
    own = pl.BlockSpec((1, rows, dim), lambda i: (jnp.maximum(i - 2 * micro, 0), 0, 0))
    grads = grad_shape(dim, columns)
    shapes, specs = scatter_outs(jobs, dim)
    buffer = pltpu.VMEM((micro, rows, dim), BF16)
    sums = jax.ShapeDtypeStruct((2, each, 128), F32)

    def all_place(i):
        return jnp.minimum(i, micro - 1), 0, 0

    def place(i):
        core = lax.axis_index("tensor")
        k = jnp.maximum(i - micro, 0)
        return lax.rem(k, micro), jnp.where(k < micro, 1 - core, core), 0

    locals_ = list(w_in) + [slabs] + list(feed_grads)
    return call(
        functools.partial(back_in_kernel, micro, feed_jobs, out_jobs, in_jobs),
        "back_in",
        9,
        3 * micro,
        [
            pl.BlockSpec((1, 2 * rows, dim), all_place),
            pl.BlockSpec((1, 2 * rows, columns), all_place),
            pl.BlockSpec((1, rows, columns), place),
            own,
            own,
            once(weights.shape),
            once((8, dim)),
            anywhere(),
        ]
        + [once(a.shape) for a in locals_],
        [own, once(sums.shape), anywhere()] + specs,
        [jax.ShapeDtypeStruct((micro, rows, dim), BF16), sums, grads] + shapes,
        [pltpu.VMEM((dim, columns), F32), buffer, buffer]
        + half_sems(micro)
        + [
            pltpu.SemaphoreType.DMA,
            pltpu.VMEM(grads.shape, BF16),
            pltpu.VMEM(sums.shape, F32),
            pltpu.VMEM(sums.shape, F32),
            pltpu.SemaphoreType.DMA((2,)),
        ]
        + scatters_scratch(jobs, dim),
        (h, dqkv, dqkv, x, d_own, weights, gains, grads_last, *locals_),
    )


def finish_kernel(edges, counts, grad_in, mixed, gain_attn, gain_mlp, gain_sums, *refs):
    feed_grads, refs = refs[: counts[0]], refs[counts[0] :]
    out_grads, refs = refs[: counts[1]], refs[counts[1] :]
    in_grads, refs = refs[: counts[2]], refs[counts[2] :]
    mixed_out, grad_out, attn_out, mlp_out, q_out, k_out, v_out, out_t, gate_out, up_out, down_t = refs
    each, units = gate_out.shape
    grad_out[...] = grad_in[...].astype(F32)
    mixed_out[...] = mixed[...]

    def blocks(pieces):
        found = []
        for piece in pieces:
            for at in range(0, piece.shape[2], 128):
                found.append((piece, at))
        return found

    def copy_to(ref, at, block):
        piece, column = block
        wide = min(128, ref.shape[1] - at)
        ref[:, at : at + wide] = piece[:, :, column : column + wide].reshape(each, wide)

    @pl.when(pl.program_id(0) == 0)
    def _():
        turned = [gain_sums[k].T for k in range(2)]
        for value, gain, ref in zip(turned, (gain_attn, gain_mlp), (attn_out, mlp_out)):
            ref[...] = jnp.sum(value, axis=0, keepdims=True) / gain[...].astype(F32)
        queue = blocks(in_grads)
        for ref in (q_out, k_out, v_out):
            for at in range(0, ref.shape[1], 128):
                copy_to(ref, at, queue.pop(0))
        for at, block in zip(range(0, out_t.shape[1], 128), blocks(out_grads)):
            copy_to(out_t, at, block)
        queue = blocks(feed_grads)
        for low, high in edges:
            for start, width in chunk_slices(high - low):
                for ref in (gate_out, up_out):
                    for at in range(low + start, low + start + width, 128):
                        copy_to(ref, at, queue.pop(0))
            for at in range(low, high, 128):
                copy_to(down_t, at, queue.pop(0))


def finish(edges, grad_in, mixed, gain_attn, gain_mlp, gain_sums, feed_grads, out_grads, in_grads, widths, units):
    micro, rows, dim = mixed.shape
    each = gain_sums.shape[1]
    tile = min(rows, 256)
    block = pl.BlockSpec((1, tile, dim), lambda m, t: (m, t, 0))
    small = [gain_attn, gain_mlp, gain_sums, *feed_grads, *out_grads, *in_grads]
    shapes = [jax.ShapeDtypeStruct((1, each), F32)] * 2
    shapes += [jax.ShapeDtypeStruct((each, w), F32) for w in widths + [units] * 3]
    counts = (len(feed_grads), len(out_grads), len(in_grads))
    return call(
        functools.partial(finish_kernel, edges, counts),
        "finish",
        None,
        (micro, rows // tile),
        [block, block] + [once(a.shape) for a in small],
        [block, block] + [once(s.shape) for s in shapes],
        [jax.ShapeDtypeStruct(mixed.shape, BF16), jax.ShapeDtypeStruct(mixed.shape, F32)] + shapes,
        [],
        (grad_in, mixed, *small),
    )


def fused_body(
    inputs, gain_attn, gain_mlp, w_query, w_key, w_value, w_out, w_gate, w_up, w_down, out_grad, lengths
):
    micro, rows, dim = inputs.shape
    units = w_gate.shape[1]
    out_columns = w_out.shape[0]
    lengths = lengths[:, 0]
    gains = gain_attn.reshape(1, -1), gain_mlp.reshape(1, -1)
    w_in = (w_query, w_key, w_value)
    padded = -(-units // 128) * 128
    edges = [(max(at - CHUNK, 0), at) for at in range(padded, 0, -CHUNK)][::-1]
    wide = [3 * (high - low) for low, high in edges]

    h_in, qkv, gain_full, whole_in, slabs = project(edges, inputs, *w_in, *gains, w_gate, w_up, w_down.T, w_out.T)

    begin = [out_columns, out_columns + wide[0], out_columns + wide[0] + wide[1]]
    early = min(EARLY, wide[0])
    mix, inverse, g_other, whole_out, unit_0 = attend_all(
        qkv, lengths, out_grad, slabs, out_columns, [(0, 0, 0, out_columns), (1, begin[0], 0, early)]
    )
    resid, h_own, h_other, unit_1 = out_project(
        mix, inputs, whole_out, gain_full, slabs, [(begin[0] + early, 0, wide[0] - early)]
    )

    def in_pieces(first, width):
        return [(first + at, at, most) for at, most in pieces_of(width, UNIT)]

    feed_jobs, at = [[], [], []], []
    for kernel in JOBS:
        at.append([])
        for chunk, width in kernel:
            first = sum(w for _, w in feed_jobs[chunk])
            feed_jobs[chunk].append((first, width))
            at[-1].append((chunk, (first, width)))

    def parts(number):
        return [grads_of[chunk] for chunk, _ in at[number]], [job for _, job in at[number]]

    rows_in = (h_own, h_other, out_grad, g_other)
    grads_of = [None] * 3
    loads = [(unit_0, 0, 0, early), (unit_1, 0, early, wide[0] - early)]
    sums, grads_of[0], unit, _ = feed(4, rows_in, loads, wide[0] // 3, None, slabs, in_pieces(begin[1], wide[1]), [], [])
    loads = [(unit, 0, 0, wide[1])]
    sums, grads_of[1], unit, done = feed(
        5, rows_in, loads, wide[1] // 3, sums, slabs, in_pieces(begin[2], wide[2]), *parts(0)
    )
    feed_grads = list(done)
    loads = [(unit, 0, 0, wide[2])]
    (mixed_out, d_own, d_other), grads_of[2], _, done = feed(
        6, rows_in, loads, wide[2] // 3, sums, None, [], *parts(1), (resid, gain_full)
    )
    feed_grads += done
    dmix, grads_out, *done = back_out(d_own, d_other, mix, whole_out, *parts(2))
    feed_grads += done
    dqkv, *done = attend_back(qkv, mix, inverse, dmix, lengths, *parts(3))
    feed_grads += done
    out_jobs, in_jobs = pieces_of(out_columns, 512), pieces_of(qkv.shape[2], 384)
    input_grad, gain_sums, _, *done = back_in(
        h_in, dqkv, inputs, d_own, whole_in, gain_full, grads_out, w_in, slabs, feed_grads, feed_jobs, out_jobs, in_jobs
    )
    out_grads, in_grads = done[: len(out_jobs)], done[len(out_jobs) :]
    widths = [w.shape[1] for w in w_in] + [out_columns]
    mixed_out, input_grad, attn_grad, mlp_grad, grad_query, grad_key, grad_value, out_t, gate, up, down_t = finish(
        edges, input_grad, mixed_out, *gains, gain_sums, feed_grads, out_grads, in_grads, widths, units
    )
    return (
        mixed_out,
        input_grad,
        attn_grad[0],
        mlp_grad[0],
        grad_query,
        grad_key,
        grad_value,
        out_t.T,
        gate,
        up,
        down_t.T,
    )


def solution(mesh):
    in_specs = (
        P(None, ("dp", "tensor"), None),
        P("dp"),
        P("dp"),
        P("dp", "tensor"),
        P("dp", "tensor"),
        P("dp", "tensor"),
        P("tensor", "dp"),
        P("dp", "tensor"),
        P("dp", "tensor"),
        P("tensor", "dp"),
        P(None, ("dp", "tensor"), None),
        P(None, "dp", None),
    )
    out_specs = (
        P(None, ("dp", "tensor"), None),
        P(None, ("dp", "tensor"), None),
        P("dp"),
        P("dp"),
        P("dp", "tensor"),
        P("dp", "tensor"),
        P("dp", "tensor"),
        P("tensor", "dp"),
        P("dp", "tensor"),
        P("dp", "tensor"),
        P("tensor", "dp"),
    )
    fits = mesh.shape["tensor"] == 2 and mesh.shape["dp"] % 4 == 0
    chosen = fused_body if fits else plain_body
    return jax.shard_map(chosen, mesh=mesh, in_specs=in_specs, out_specs=out_specs, check_vma=False)
```

```python
import functools
import math

import jax
import jax.numpy as jnp
import numpy as np
from jax import lax
from jax.experimental import pallas as pl
from jax.experimental.pallas import tpu as pltpu
from jax.sharding import PartitionSpec as P

FEAT = 16
VD = 64
BLK = 512


EXACT = lax.Precision.HIGHEST


def taylor(halved):
    feature_dim = halved.shape[-1]
    upper_idx, lower_idx = np.triu_indices(feature_dim)
    flat_index = jnp.asarray(upper_idx * feature_dim + lower_idx, jnp.int32)
    factors = jnp.asarray(np.where(upper_idx == lower_idx, math.sqrt(0.5), 1.0), jnp.float32)
    outer = (halved[..., :, None] * halved[..., None, :]).reshape(
        halved.shape[:-1] + (feature_dim * feature_dim,)
    )
    second = jnp.take(outer, flat_index, axis=-1) * factors
    ones_col = jnp.ones(halved.shape[:-1] + (1,), jnp.float32)
    return jnp.concatenate([ones_col, halved, second], axis=-1)


def attend_block(carry_in, block_in):
    kv_state, totals, previous = carry_in
    queries, keys_in, values_in, doc_ids = block_in
    half_q = 0.5 * queries
    half_k = 0.5 * keys_in
    scores = jnp.einsum("rhf,chf->hrc", half_q, half_k, preferred_element_type=jnp.float32)
    places = jnp.arange(doc_ids.shape[0], dtype=jnp.int32)
    allowed = (doc_ids[:, None] == doc_ids[None, :]) & (places[None, :] <= places[:, None])
    weights = jnp.where(allowed[None], 1.0 + scores + 0.5 * scores * scores, 0.0)
    feat_q = taylor(half_q)
    feat_k = taylor(half_k)
    carried_in = (doc_ids == previous).astype(jnp.float32)
    numerator = jnp.einsum("hrc,chv->rhv", weights, values_in, precision=EXACT) + carried_in[
        :, None, None
    ] * jnp.einsum("rhf,hfv->rhv", feat_q, kv_state, precision=EXACT)
    denominator = jnp.sum(weights, axis=2).T + carried_in[:, None] * jnp.einsum(
        "rhf,hf->rh", feat_q, totals, precision=EXACT
    )
    mixed_rows = numerator / denominator[:, :, None]
    final_doc = doc_ids[-1]
    staying = (doc_ids == final_doc).astype(jnp.float32)[:, None, None] * feat_k
    joined = (final_doc == previous).astype(jnp.float32)
    kv_state = jnp.einsum("rhf,rhv->hfv", staying, values_in, precision=EXACT) + joined * kv_state
    totals = jnp.sum(staying, axis=0) + joined * totals
    return ((kv_state, totals, final_doc), mixed_rows)


def attend(queries, keys_in, values_in, doc_ids):
    row_total, head_count, feature_dim = queries.shape
    value_dim = values_in.shape[2]
    block_count = row_total // BLK
    feature_total = 1 + feature_dim + feature_dim * (feature_dim + 1) // 2
    initial = (
        jnp.zeros((head_count, feature_total, value_dim), jnp.float32),
        jnp.zeros((head_count, feature_total), jnp.float32),
        jnp.array(-1, jnp.int32),
    )
    pieces = (
        queries.reshape(block_count, BLK, head_count, feature_dim),
        keys_in.reshape(block_count, BLK, head_count, feature_dim),
        values_in.reshape(block_count, BLK, head_count, value_dim),
        doc_ids.reshape(block_count, BLK),
    )
    last_carry, mixed_rows = lax.scan(jax.checkpoint(attend_block), initial, pieces)
    return mixed_rows.reshape(row_total, head_count * value_dim)


def document_ids(lengths_row, row_total):
    doc_ends = jnp.cumsum(lengths_row)
    places = jnp.arange(row_total, dtype=jnp.int32)
    return jnp.sum((places[:, None] >= doc_ends[None, :]).astype(jnp.int32), axis=1)


def rows_product(left, right):
    return lax.dot_general(
        left, right, (((0,), (0,)), ((), ())), preferred_element_type=jnp.float32
    )


def back_product(left, right):
    return lax.dot_general(
        left, right, (((1,), (1,)), ((), ())), preferred_element_type=jnp.float32
    )


def norm_back(grad_normed, normed, inverse, gain_full):
    scaled = grad_normed * gain_full
    return inverse * (scaled - normed * jnp.mean(scaled * normed, axis=-1, keepdims=True))


def row_slice(matrix, first_row, row_count):
    return lax.dynamic_slice_in_dim(matrix, first_row, row_count, 0)


def inverse_root(values):
    return lax.rsqrt(jnp.mean(values * values, axis=-1, keepdims=True) + 1e-05)


def fetch_weights(gain_attn, gain_mlp, w_query, w_key, w_value, w_out, w_gate, w_up, w_down):
    row_parts = (
        lax.all_gather(w_query, "dp", axis=0, tiled=True),
        lax.all_gather(w_key, "dp", axis=0, tiled=True),
        lax.all_gather(w_value, "dp", axis=0, tiled=True),
        lax.all_gather(w_gate, "dp", axis=0, tiled=True),
        lax.all_gather(w_up, "dp", axis=0, tiled=True),
        lax.all_gather(gain_attn, "dp", axis=0, tiled=True),
        lax.all_gather(gain_mlp, "dp", axis=0, tiled=True),
    )
    col_parts = (
        lax.all_gather(w_out, "dp", axis=1, tiled=True),
        lax.all_gather(w_down, "dp", axis=1, tiled=True),
    )
    return tuple(row_parts) + tuple(col_parts)


def plain_body(
    inputs,
    gain_attn,
    gain_mlp,
    w_query,
    w_key,
    w_value,
    w_out,
    w_gate,
    w_up,
    w_down,
    out_grad,
    lengths,
):
    micro_count = inputs.shape[0]
    shard_rows = inputs.shape[1]
    model_dim = inputs.shape[2]
    group_rows = shard_rows * lax.axis_size("tensor")
    local_heads = w_query.shape[1] // FEAT
    grad_query_sum = jnp.zeros((model_dim, w_query.shape[1]), jnp.float32)
    grad_key_sum = jnp.zeros((model_dim, w_key.shape[1]), jnp.float32)
    grad_value_sum = jnp.zeros((model_dim, w_value.shape[1]), jnp.float32)
    grad_gate_sum = jnp.zeros((model_dim, w_gate.shape[1]), jnp.float32)
    grad_up_sum = jnp.zeros((model_dim, w_up.shape[1]), jnp.float32)
    grad_out_sum = jnp.zeros((w_out.shape[0], model_dim), jnp.float32)
    grad_down_sum = jnp.zeros((w_down.shape[0], model_dim), jnp.float32)
    gain_attn_sum = jnp.zeros((model_dim,), jnp.float32)
    gain_mlp_sum = jnp.zeros((model_dim,), jnp.float32)
    outputs = []
    input_grads = []
    for micro_step in range(micro_count):
        (
            full_query,
            full_key,
            full_value,
            full_gate,
            full_up,
            full_gain_attn,
            full_gain_mlp,
            full_out,
            full_down,
        ) = fetch_weights(gain_attn, gain_mlp, w_query, w_key, w_value, w_out, w_gate, w_up, w_down)
        gain_in = full_gain_attn.astype(jnp.float32)
        gain_mid = full_gain_mlp.astype(jnp.float32)
        doc_ids = document_ids(lengths[micro_step, 0], group_rows)
        values = inputs[micro_step].astype(jnp.float32)
        inverse_in = inverse_root(values)
        normed_in = values * inverse_in
        gathered_in = lax.all_gather(
            (normed_in * gain_in).astype(jnp.bfloat16), "tensor", axis=0, tiled=True
        )
        query_low = jnp.dot(gathered_in, full_query, preferred_element_type=jnp.float32).astype(
            jnp.bfloat16
        )
        key_low = jnp.dot(gathered_in, full_key, preferred_element_type=jnp.float32).astype(
            jnp.bfloat16
        )
        value_low = jnp.dot(gathered_in, full_value, preferred_element_type=jnp.float32).astype(
            jnp.bfloat16
        )
        query_full = query_low.astype(jnp.float32).reshape(group_rows, local_heads, FEAT)
        key_full = key_low.astype(jnp.float32).reshape(group_rows, local_heads, FEAT)
        value_full = value_low.astype(jnp.float32).reshape(group_rows, local_heads, VD)

        def local_attend(query_arg, key_arg, value_arg):
            return attend(query_arg, key_arg, value_arg, doc_ids)

        mixed_full, pullback = jax.vjp(local_attend, query_full, key_full, value_full)
        mixed_low = mixed_full.astype(jnp.bfloat16)
        residual = values + lax.psum_scatter(
            jnp.dot(
                row_slice(mixed_low, jnp.int32(0), shard_rows * lax.axis_size("tensor")),
                full_out,
                preferred_element_type=jnp.float32,
            ),
            "tensor",
            scatter_dimension=0,
            tiled=True,
        )
        inverse_mid = inverse_root(residual)
        normed_mid = residual * inverse_mid
        gathered_mid = lax.all_gather(
            (normed_mid * gain_mid).astype(jnp.bfloat16), "tensor", axis=0, tiled=True
        )
        gate_pre = jnp.dot(gathered_mid, full_gate, preferred_element_type=jnp.float32)
        up_pre = jnp.dot(gathered_mid, full_up, preferred_element_type=jnp.float32)
        sigmoid_gate = jax.nn.sigmoid(gate_pre)
        silu_gate = gate_pre * sigmoid_gate
        hidden = (silu_gate * up_pre).astype(jnp.bfloat16)
        mlp_part = lax.psum_scatter(
            jnp.dot(
                row_slice(hidden, jnp.int32(0), shard_rows * lax.axis_size("tensor")),
                full_down,
                preferred_element_type=jnp.float32,
            ).astype(jnp.bfloat16),
            "tensor",
            scatter_dimension=0,
            tiled=True,
        ).astype(jnp.float32)
        outputs.append((residual + mlp_part).astype(jnp.bfloat16))
        cotangent = out_grad[micro_step]
        gathered_grad = lax.all_gather(cotangent, "tensor", axis=0, tiled=True)
        grad_down_sum += rows_product(hidden, gathered_grad)
        grad_hidden = back_product(gathered_grad, full_down)
        grad_gate_low = (
            grad_hidden * up_pre * sigmoid_gate * (1.0 + gate_pre * (1.0 - sigmoid_gate))
        ).astype(jnp.bfloat16)
        grad_up_low = (grad_hidden * silu_gate).astype(jnp.bfloat16)
        grad_gate_sum += rows_product(gathered_mid, grad_gate_low)
        grad_up_sum += rows_product(gathered_mid, grad_up_low)
        first_row = jnp.int32(0)
        grad_mid = lax.psum_scatter(
            back_product(
                row_slice(grad_gate_low, first_row, shard_rows * lax.axis_size("tensor")), full_gate
            )
            + back_product(
                row_slice(grad_up_low, first_row, shard_rows * lax.axis_size("tensor")), full_up
            ),
            "tensor",
            scatter_dimension=0,
            tiled=True,
        )
        gain_mlp_sum += jnp.sum(grad_mid * normed_mid, axis=0)
        grad_resid = cotangent.astype(jnp.float32) + norm_back(
            grad_mid, normed_mid, inverse_mid, gain_mid
        )
        gathered_resid = lax.all_gather(
            grad_resid.astype(jnp.bfloat16), "tensor", axis=0, tiled=True
        )
        grad_out_sum += rows_product(mixed_low, gathered_resid)
        grad_mixed = back_product(gathered_resid, full_out).astype(jnp.bfloat16).astype(jnp.float32)
        grad_query_full, grad_key_full, grad_value_full = pullback(grad_mixed)
        grad_query_low = grad_query_full.reshape(group_rows, -1).astype(jnp.bfloat16)
        grad_key_low = grad_key_full.reshape(group_rows, -1).astype(jnp.bfloat16)
        grad_value_low = grad_value_full.reshape(group_rows, -1).astype(jnp.bfloat16)
        grad_query_sum += rows_product(gathered_in, grad_query_low)
        grad_key_sum += rows_product(gathered_in, grad_key_low)
        grad_value_sum += rows_product(gathered_in, grad_value_low)
        attn_first_row = jnp.int32(0)
        grad_in = lax.psum_scatter(
            (
                back_product(
                    row_slice(grad_query_low, attn_first_row, shard_rows * lax.axis_size("tensor")),
                    full_query,
                )
                + back_product(
                    row_slice(grad_key_low, attn_first_row, shard_rows * lax.axis_size("tensor")),
                    full_key,
                )
                + back_product(
                    row_slice(grad_value_low, attn_first_row, shard_rows * lax.axis_size("tensor")),
                    full_value,
                )
            ).astype(jnp.bfloat16),
            "tensor",
            scatter_dimension=0,
            tiled=True,
        ).astype(jnp.float32)
        gain_attn_sum += jnp.sum(grad_in * normed_in, axis=0)
        input_grads.append(grad_resid + norm_back(grad_in, normed_in, inverse_in, gain_in))
    row_grads = (
        lax.psum_scatter(
            grad_query_sum.astype(jnp.bfloat16), "dp", scatter_dimension=0, tiled=True
        ).astype(jnp.float32),
        lax.psum_scatter(
            grad_key_sum.astype(jnp.bfloat16), "dp", scatter_dimension=0, tiled=True
        ).astype(jnp.float32),
        lax.psum_scatter(
            grad_value_sum.astype(jnp.bfloat16), "dp", scatter_dimension=0, tiled=True
        ).astype(jnp.float32),
        lax.psum_scatter(
            grad_gate_sum.astype(jnp.bfloat16), "dp", scatter_dimension=0, tiled=True
        ).astype(jnp.float32),
        lax.psum_scatter(
            grad_up_sum.astype(jnp.bfloat16), "dp", scatter_dimension=0, tiled=True
        ).astype(jnp.float32),
        lax.psum_scatter(
            gain_attn_sum.astype(jnp.bfloat16), "dp", scatter_dimension=0, tiled=True
        ).astype(jnp.float32),
        lax.psum_scatter(
            gain_mlp_sum.astype(jnp.bfloat16), "dp", scatter_dimension=0, tiled=True
        ).astype(jnp.float32),
    )
    col_grads = (
        lax.psum_scatter(
            grad_out_sum.astype(jnp.bfloat16), "dp", scatter_dimension=1, tiled=True
        ).astype(jnp.float32),
        lax.psum_scatter(
            grad_down_sum.astype(jnp.bfloat16), "dp", scatter_dimension=1, tiled=True
        ).astype(jnp.float32),
    )
    gain_grads = lax.psum((row_grads[5], row_grads[6]), "tensor")
    return (
        jnp.stack(outputs, 0),
        jnp.stack(input_grads, 0),
        gain_grads[0],
        gain_grads[1],
        row_grads[0],
        row_grads[1],
        row_grads[2],
        col_grads[0],
        row_grads[3],
        row_grads[4],
        col_grads[1],
    )


F32 = jnp.float32
BF16 = jnp.bfloat16
NN = (((1,), (0,)), ((), ()))
NT = (((1,), (1,)), ((), ()))
TN = (((0,), (0,)), ((), ()))
TILE = 256
SPAN = 2
CHUNK = 512
EARLY = 640
JOBS = (((0, 768), (0, 384), (1, 768)), ((1, 768), (2, 768), (2, 384), (2, 384)))
RATE = 0.019
VMEM_BYTES = 62 << 20
MESH = pl.DeviceIdType.MESH


def mm(left, right, dims=NN):
    return lax.dot_general(left, right, dims, preferred_element_type=F32)


def params(number=None):
    if number is None:
        return pltpu.CompilerParams(vmem_limit_bytes=VMEM_BYTES)
    return pltpu.CompilerParams(vmem_limit_bytes=VMEM_BYTES, collective_id=number, has_side_effects=True)


def anywhere():
    return pl.BlockSpec(memory_space=pl.ANY)


def once(shape):
    return pl.BlockSpec(shape, lambda *_: (0,) * len(shape), pipeline_mode=pl.Buffered(1))


def far_count():
    return lax.axis_size("dp") // 4


def dp_peer(bits):
    return {"dp": lax.axis_index("dp") ^ bits}


def sibling():
    return {"tensor": 1 - lax.axis_index("tensor")}


def dp_peers():
    return [dp_peer(1), dp_peer(2)] + [dp_peer(4 * k) for k in range(1, far_count())]


def greet(peers):
    barrier = pltpu.get_barrier_semaphore()
    for peer in peers:
        pl.semaphore_signal(barrier, inc=1, device_id=peer, device_id_type=MESH)
    pl.semaphore_wait(barrier, len(peers))


def remote(source, target, send, recv, peer):
    return pltpu.make_async_remote_copy(
        src_ref=source, dst_ref=target, send_sem=send, recv_sem=recv, device_id=peer, device_id_type=MESH
    )


def gather_sems():
    count = 7 * far_count() - 1
    return [pltpu.SemaphoreType.DMA((count,)), pltpu.SemaphoreType.DMA((count,)), pltpu.SemaphoreType.DMA]


class Gather:

    def __init__(self, source, whole, send, recv, local=None, near=None):
        self.source, self.whole, self.send, self.recv, self.local = source, whole, send, recv, local
        self.near = near
        self.me = lax.axis_index("dp")
        self.far = far_count()
        self.each = whole.shape[0] // lax.axis_size("dp")
        self.half = self.each // 2

    def block(self, bits):
        start = pl.multiple_of((self.me ^ bits) * self.each, self.each)
        return self.whole.at[pl.ds(start, self.each)]

    def piece(self, bits, part):
        start = pl.multiple_of((self.me ^ bits) * self.each + part * self.half, self.half)
        return self.whole.at[pl.ds(start, self.half)]


    def along(self, k):
        return k - 1, self.source, self.block(0), 4 * k, self.block(4 * k)

    def first(self, k, part, bit):
        index = self.far - 1 + 4 * k + 2 * part + bit - 1
        if self.near is not None:
            source = near_block(self.near, k, part * self.half, self.half)
        elif k == 0:
            source = self.source.at[pl.ds(part * self.half, self.half)]
        else:
            source = self.piece(4 * k, part)
        return index, source, self.piece(4 * k, part), bit, self.piece(4 * k + bit, part)

    def second(self, k, part):
        index = 5 * self.far - 1 + 2 * k + part
        source = self.piece(4 * k + 2 - part, part)
        return index, source, source, 1 + part, self.piece(4 * k + 3, part)

    def outgoing(self, transfer):
        index, source, target, bits, _ = transfer
        return remote(source, target, self.send.at[index], self.recv.at[index], dp_peer(bits))

    def start(self, transfer):
        self.outgoing(transfer).start()

    def sent(self, transfer):
        self.outgoing(transfer).wait_send()

    def arrived(self, transfer):
        index, _, _, bits, landing = transfer
        remote(landing, landing, self.send.at[index], self.recv.at[index], dp_peer(bits)).wait_recv()

    def kept(self):
        if self.near is None:
            return [pltpu.make_async_copy(self.source, self.block(0), self.local)]
        sems = [self.local] + [self.recv.at[k - 1] for k in range(1, self.far)]
        return [
            pltpu.make_async_copy(near_block(self.near, k, 0, self.each), self.block(4 * k), sems[k])
            for k in range(self.far)
        ]

    def pass_on(self, k):
        for part, bit in ((0, 2), (1, 1), (0, 1), (1, 2)):
            self.start(self.first(k, part, bit))

    def begin_far(self):
        if self.local is not None:
            for copy in self.kept():
                copy.start()
        if self.near is None:
            for k in range(1, self.far):
                self.start(self.along(k))

    def begin(self):
        self.begin_far()
        self.pass_on(0)

    def spread(self, k):
        if self.near is None:
            self.arrived(self.along(k))
        self.pass_on(k)

    def turn(self, k):
        self.arrived(self.first(k, 0, 2))
        self.start(self.second(k, 0))
        self.arrived(self.first(k, 1, 1))
        self.start(self.second(k, 1))

    def finish(self):
        for k in range(self.far):
            self.arrived(self.first(k, 0, 1))
            self.arrived(self.first(k, 1, 2))
            for part in range(2):
                self.arrived(self.second(k, part))
        if self.near is None:
            for k in range(1, self.far):
                self.sent(self.along(k))
        for k in range(self.far):
            for part in range(2):
                for bit in (1, 2):
                    self.sent(self.first(k, part, bit))
                self.sent(self.second(k, part))
        if self.local is not None:
            for copy in self.kept():
                copy.wait()

    def plan(self, start):
        along = RATE * self.whole.shape[1]
        far = 2 * along / 3
        events = [(start, self.begin)]
        for k in range(1, self.far):
            at = start + 1.0 + far * (0.4 + 0.6 * k / (self.far - 1))
            events.append((at, functools.partial(self.spread, k)))
        for k in range(self.far):
            at = start + 2.0 + far * (0.4 + 0.6 * k / (self.far - 1)) + along / 4
            events.append((at, functools.partial(self.turn, k)))
        return events


    def plan_near(self, far_start, start):
        along = RATE * self.whole.shape[1]
        events = [(far_start, self.begin_far)]
        events += [(start, functools.partial(self.pass_on, 0))]
        events += [(start + 0.001 * k, functools.partial(self.spread, k)) for k in range(1, self.far)]
        for k in range(self.far):
            events.append((start + 2.0 + along * (k + 1) / 6, functools.partial(self.turn, k)))
        return events


def near_block(near, k, first, rows):
    each = near.shape[0] // far_count()
    start = (lax.div(lax.axis_index("dp"), 4) ^ k) * each + first
    return near.at[pl.ds(pl.multiple_of(start, rows), rows)]


class NearGather:

    def __init__(self, source, near, send, recv, local):
        self.source, self.near, self.send, self.recv, self.local = source, near, send, recv, local
        self.each = source.shape[0]

    def copies(self):
        mine = near_block(self.near, 0, 0, self.each)
        made = [pltpu.make_async_copy(self.source, mine, self.local)]
        for k in range(1, far_count()):
            made.append(remote(self.source, mine, self.send.at[k - 1], self.recv.at[k - 1], dp_peer(4 * k)))
        return made

    def begin(self):
        for copy in self.copies():
            copy.start()

    def finish(self):
        for k in range(1, far_count()):
            landing = near_block(self.near, k, 0, self.each)
            remote(landing, landing, self.send.at[k - 1], self.recv.at[k - 1], dp_peer(4 * k)).wait_recv()
        for copy in self.copies()[1:]:
            copy.wait_send()
        self.copies()[0].wait()


class Plan:

    def __init__(self, step, steps, places, step_us, clock=None):
        self.step, self.steps, self.places = step, steps, places
        self.clock = clock or [at * step_us / places for at in range(steps * places)]
        self.events = {}
        self.tail = []
        self.ends = []

    def add(self, events, end, latest=None, earliest=0):
        for at, (time, action) in enumerate(events):
            index = sum(tick < time for tick in self.clock) if at else sum(tick <= time for tick in self.clock) - 1
            index = max(index, earliest)
            if latest is not None:
                index = min(index, latest)
            if index < self.steps * self.places:
                self.events.setdefault(divmod(index, self.places), []).append((time, action))
            else:
                self.tail.append((time, action))
        self.ends.append(end)

    def put(self, step, time, action):
        self.events.setdefault((step, 0), []).append((time, action))

    def at(self, place):
        for key in sorted(self.events):
            if key[1] == place:

                @pl.when(self.step == key[0])
                def _(actions=sorted(self.events[key], key=lambda event: event[0])):
                    for _, action in actions:
                        action()

    def finish(self):
        for _, action in sorted(self.tail, key=lambda event: event[0]):
            action()
        for end in self.ends:
            end()


def add_gathers(plan, jobs, refs, start=0.0):
    for at, (source, whole, first, target, width) in enumerate(jobs):
        gather = Gather(
            source.at[:, pl.ds(first, width)], whole.at[:, pl.ds(target, width)], *refs[3 * at : 3 * at + 3]
        )
        plan.add(gather.plan(start), gather.finish)
        start += RATE * width


def pieces_of(width, most):
    return [(at, min(most, width - at)) for at in range(0, width, most)]


def scatter_scratch(columns, dim):
    far = far_count()
    half = dim // lax.axis_size("dp") // 2
    part = pltpu.VMEM((far, half, columns), BF16)
    return [part] * 8 + [
        pltpu.VMEM((far, 2, half, columns), BF16),
        pltpu.VMEM((far - 1, 2, half, columns), BF16),
        pltpu.SemaphoreType.DMA((5 + far,)),
        pltpu.SemaphoreType.DMA((5 + far,)),
        pltpu.SemaphoreType.DMA((3,)),
    ]


SCATTER_REFS = 13


class Scatter:
    def __init__(self, grads, first, out, refs):
        (
            self.mine_y, self.mine_x, self.got_dy, self.got_dx, self.got_x, self.got_y, self.got_y2, self.got_x2,
            self.mine, self.got_far, self.send, self.recv, self.local,
        ) = refs
        self.grads, self.out = grads, out
        self.columns = pl.ds(first, self.mine.shape[3])
        me = lax.axis_index("dp")
        self.far = far_count()
        self.low, self.high = lax.rem(me, 4), lax.div(me, 4)

    def copy(self, index, source, target, bits):
        return remote(source, target, self.send.at[index], self.recv.at[index], dp_peer(bits))

    def share(self, bits, part):
        return self.grads.at[:, self.low ^ bits, part, :, self.columns]

    def from_grads(self):
        return [
            self.copy(0, self.share(3, 0), self.got_dy, 1),
            self.copy(1, self.share(3, 1), self.got_dx, 2),
            self.copy(2, self.share(1, 0), self.got_x, 1),
            self.copy(3, self.share(2, 1), self.got_y, 2),
        ]

    def added(self):
        return [self.copy(4, self.mine_y, self.got_y2, 2), self.copy(5, self.mine_x, self.got_x2, 1)]

    def along(self):
        return [
            self.copy(5 + k, self.mine.at[self.high ^ k], self.got_far.at[k - 1], 4 * k) for k in range(1, self.far)
        ]

    def loads(self):
        own = self.grads.at[:, self.low, :, :, self.columns]
        return [
            pltpu.make_async_copy(self.share(2, 0), self.mine_y, self.local.at[0]),
            pltpu.make_async_copy(self.share(1, 1), self.mine_x, self.local.at[1]),
            pltpu.make_async_copy(own, self.mine, self.local.at[2]),
        ]

    def begin(self):
        for copy in self.from_grads() + self.loads():
            copy.start()

    def second(self):
        loads, got, added = self.loads(), self.from_grads(), self.added()
        loads[0].wait()
        got[0].wait_recv()
        self.mine_y[...] = add(self.mine_y[...], self.got_dy[...]).astype(BF16)
        added[0].start()
        loads[1].wait()
        got[1].wait_recv()
        self.mine_x[...] = add(self.mine_x[...], self.got_dx[...]).astype(BF16)
        added[1].start()

    def third(self):
        got, added = self.from_grads(), self.added()
        self.loads()[2].wait()
        got[2].wait_recv()
        added[0].wait_recv()
        self.mine[:, 0] = add(self.mine[:, 0], self.got_x[...], self.got_y2[...]).astype(BF16)
        got[3].wait_recv()
        added[1].wait_recv()
        self.mine[:, 1] = add(self.mine[:, 1], self.got_y[...], self.got_x2[...]).astype(BF16)
        for copy in self.along():
            copy.start()

    def finish(self):
        for copy in self.along():
            copy.wait_recv()
        self.out[...] = add(self.mine[self.high], *[self.got_far[k] for k in range(self.far - 1)])
        for copy in self.from_grads() + self.added() + self.along():
            copy.wait_send()


    def plan(self, start):
        along = RATE * self.mine.shape[3]
        times = (start, start + 1.5 + 2 * along / 3, start + 3 + along)
        return list(zip(times, (self.begin, self.second, self.third)))


def scatters_scratch(jobs, dim):
    scratch = []
    for _, width in jobs:
        scratch += scatter_scratch(width, dim)
    return scratch


def scatter_outs(jobs, dim):
    half = dim // lax.axis_size("dp") // 2
    shapes = [jax.ShapeDtypeStruct((2, half, width), F32) for _, width in jobs]
    return shapes, [once(shape.shape) for shape in shapes]


def add_scatters(plan, jobs, sources, outs, refs, start=0.0):
    for at, (first, width) in enumerate(jobs):
        scatter = Scatter(sources[at], first, outs[at], refs[SCATTER_REFS * at : SCATTER_REFS * (at + 1)])
        plan.add(scatter.plan(start), scatter.finish)
        start += RATE * width


def grad_shape(dim, columns):
    return jax.ShapeDtypeStruct((far_count(), 4, 2, dim // lax.axis_size("dp") // 2, columns), BF16)


def add(*terms):
    total = terms[0].astype(F32)
    for term in terms[1:]:
        total = total + term.astype(F32)
    return total


def call(kernel, name, number, steps, in_specs, out_specs, out_shape, scratch, operands):
    return pl.pallas_call(
        kernel,
        grid=steps if isinstance(steps, tuple) else (steps,),
        in_specs=in_specs,
        out_specs=out_specs,
        out_shape=out_shape,
        scratch_shapes=scratch,
        compiler_params=params(number),
        name=name,
    )(*operands)


def spread_gains(slab, column):
    dim = slab.shape[0]
    blocks = lax.axis_size("dp")
    each = dim // blocks
    lane_block = lax.broadcasted_iota(jnp.int32, (blocks, dim), 1) // each
    block = lax.broadcasted_iota(jnp.int32, (blocks, dim), 0)
    rows = []
    for which in range(2):
        picked = jnp.concatenate(
            [slab[each * b : each * b + 16, column : column + 128].astype(F32)[which : which + 1] for b in range(blocks)], 0
        )
        tiled = jnp.concatenate([picked] * (dim // 128), 1)
        rows.append(jnp.sum(jnp.where(lane_block == block, tiled, 0.0), axis=0, keepdims=True))
    return jnp.concatenate(rows + [jnp.zeros((6, dim), F32)], 0)


def part_block(width, per, rows, lag=0, last=None):
    def place(i):
        i = i - lag if last is None else jnp.clip(i - lag, 0, last)
        return lax.div(i, per), lax.rem(i, per), 0

    return pl.BlockSpec((1, rows, width), place)


def core_block(width, per, rows, other, last=None):
    def place(i):
        if last is not None:
            i = jnp.minimum(i, last)
        core = lax.axis_index("tensor")
        return lax.div(i, per), (1 - core if other else core) * per + lax.rem(i, per), 0

    return pl.BlockSpec((1, rows, width), place)


def root_mean(values):
    return lax.rsqrt(jnp.mean(values * values, axis=-1, keepdims=True) + 1e-05)


def norm_slope(values, scaled):
    inverse = root_mean(values)
    normed = values * inverse
    return inverse * (scaled - normed * jnp.mean(scaled * normed, axis=-1, keepdims=True))


def half_sems(count):
    return [pltpu.SemaphoreType.DMA((count,)), pltpu.SemaphoreType.DMA((count,))]


def chunk_slices(width):
    return [(at, min(256, width - at)) for at in range(0, width, 256)]


def build_slabs(edges, gate, up, down_t, out_t, slabs):
    at = out_t.shape[1]
    slabs[:, :at] = out_t[...]
    units = gate.shape[1]

    def place(ref, low, high):
        nonlocal at
        end = min(high, units)
        slabs[:, at : at + end - low] = ref[:, low:end]
        if end < high:
            slabs[:, at + end - low : at + high - low] = jnp.zeros((slabs.shape[0], high - end), BF16)
        at += high - low

    for low, high in edges:
        for start, width in chunk_slices(high - low):
            place(gate, low + start, low + start + width)
            place(up, low + start, low + start + width)
        place(down_t, low, high)


def project_kernel(
    edges, inputs, w_query, w_key, w_value, gain_attn, gain_mlp, gate, up, down_t, out_t,
    h_out, qkv_out, gain_out, whole_in, slabs, x_own, x_other, h_all, qkv_all, slab, gain_slab,
    local, swap_send, swap_recv, *sems,
):
    micro, rows, _ = x_own.shape
    each = w_query.shape[0]
    core = lax.axis_index("tensor")
    parts = 2 * micro

    def load(m):
        return pltpu.make_async_copy(inputs.at[m], x_own.at[m], local.at[m])

    def swap(m):
        return remote(inputs.at[m], x_other.at[m], swap_send.at[m], swap_recv.at[m], sibling())

    def place(t):
        first = pl.multiple_of((core if t < micro else 1 - core) * rows, rows)
        return t % micro, pl.ds(first, rows)

    def store_h(t):
        return pltpu.make_async_copy(h_all.at[t], h_out.at[place(t)], local.at[micro + t])

    def store_qkv(t):
        return pltpu.make_async_copy(qkv_all.at[t], qkv_out.at[place(t)], local.at[micro + parts + t])

    def keep():
        return pltpu.make_async_copy(slab, whole_in, local.at[micro + 2 * parts])

    def norm(t):
        x = (x_own if t < micro else x_other)[t % micro].astype(F32)
        h_all[t] = (x * root_mean(x) * gain_out[0:1]).astype(BF16)
        store_h(t).start()

    for m in range(micro):
        load(m).start()
    mine = pl.ds(pl.multiple_of(lax.axis_index("dp") * each, each), each)
    at = 0
    for ref in (w_query, w_key, w_value):
        slab[mine, at : at + ref.shape[1]] = ref[...]
        at += ref.shape[1]
    both = jnp.concatenate([gain_attn[...], gain_mlp[...]], 0).astype(F32)
    both = jnp.concatenate([both, both], 1)
    gain_slab[mine] = jnp.concatenate([both, jnp.zeros((each - 2, both.shape[1]), F32)], 0).astype(BF16)
    greet(dp_peers() + [sibling()])
    gains = Gather(gain_slab.at[mine], gain_slab, *sems[:2])
    weights = Gather(slab.at[mine], slab, *sems[2:])
    gains.begin()
    weights.begin()
    for m in range(micro):
        swap(m).start()
    build_slabs(edges, gate, up, down_t, out_t, slabs)
    for k in range(1, gains.far):
        gains.spread(k)
    for k in range(gains.far):
        gains.turn(k)
    gains.finish()
    gain_out[...] = spread_gains(gain_slab, 0)
    duties = [functools.partial(weights.spread, k) for k in range(1, weights.far)]
    duties += [functools.partial(weights.turn, k) for k in range(weights.far)]
    for t in range(parts):
        if t < micro:
            load(t).wait()
        else:
            swap(t - micro).wait()
        norm(t)
        if duties:
            duties.pop(0)()
    for duty in duties:
        duty()
    weights.finish()
    keep().start()
    for t in range(parts):
        qkv_all[t] = mm(h_all[t], slab[...]).astype(BF16)
        store_qkv(t).start()
    for t in range(parts):
        store_h(t).wait()
        store_qkv(t).wait()
    keep().wait()


def project(edges, inputs, w_query, w_key, w_value, gain_attn, gain_mlp, w_gate, w_up, down_t, out_t):
    micro, rows, dim = inputs.shape
    each = w_query.shape[0]
    columns = w_query.shape[1] + w_key.shape[1] + w_value.shape[1]
    all_columns = out_t.shape[1] + 3 * edges[-1][1]
    locals_ = (w_query, w_key, w_value, gain_attn, gain_mlp, w_gate, w_up, down_t, out_t)
    return call(
        functools.partial(project_kernel, edges),
        "project",
        1,
        1,
        [anywhere()] + [once(a.shape) for a in locals_],
        [anywhere(), anywhere(), once((8, dim)), anywhere(), once((each, all_columns))],
        [
            jax.ShapeDtypeStruct((micro, 2 * rows, dim), BF16),
            jax.ShapeDtypeStruct((micro, 2 * rows, columns), BF16),
            jax.ShapeDtypeStruct((8, dim), F32),
            jax.ShapeDtypeStruct((dim, columns), BF16),
            jax.ShapeDtypeStruct((each, all_columns), BF16),
        ],
        [
            pltpu.VMEM((micro, rows, dim), BF16),
            pltpu.VMEM((micro, rows, dim), BF16),
            pltpu.VMEM((2 * micro, rows, dim), BF16),
            pltpu.VMEM((2 * micro, rows, columns), BF16),
            pltpu.VMEM((dim, columns), BF16),
            pltpu.VMEM((dim, 128), BF16),
            pltpu.SemaphoreType.DMA((5 * micro + 1,)),
        ]
        + half_sems(micro)
        + gather_sems()[:2]
        + gather_sems()[:2],
        (inputs, *locals_),
    )


def fill_mask(mask, lengths, micro_step):
    tiles = mask.shape[0]
    row = lax.broadcasted_iota(jnp.int32, (tiles * TILE, TILE), 0)
    start = jnp.zeros_like(row)
    end = 0
    for d in range(lengths.shape[1]):
        end = end + lengths[micro_step, d]
        start = jnp.where(row >= end, end, start)
    lane = lax.broadcasted_iota(jnp.int32, (tiles * TILE, TILE), 1)
    for j in range(tiles):
        i = min(tiles, j + SPAN + 1)
        tall = (i - j) * TILE
        below = slice(j * TILE, i * TILE)
        column = lane[:tall] + j * TILE
        allowed = (column <= row[below]) & (column >= start[below])
        mask[j, :tall, :] = jnp.where(allowed, 1.0, 0.0)


def add_rows(total, j, tiles, value):
    end = min(tiles, j + SPAN + 1)
    begun = min(tiles, j + SPAN) if j else 0
    if begun > j:
        total[j * TILE : begun * TILE] += value[: (begun - j) * TILE]
    if end > max(begun, j):
        start = max(begun, j)
        total[start * TILE : end * TILE] = value[(start - j) * TILE :]


def attend_kernel(
    jobs, lengths, qkv, grad_own, slabs, mix_ref, inv_ref, grad_other, unit, mask, queries, values, total, *sems
):
    m = pl.program_id(0)
    group = qkv.shape[1]
    tiles = group // TILE
    pairs = mix_ref.shape[2] // 128
    lane = lax.broadcasted_iota(jnp.int32, (group, 128), 1)
    zero = jnp.zeros((), BF16)

    def swap():
        return remote(grad_own, grad_other, sems[0], sems[1], sibling())

    plan = Plan(m, lengths.shape[0], pairs, 9.5)
    plan.add([(0.0, lambda: swap().start())], lambda: swap().wait())
    add_gathers(plan, [(slabs, unit, *job) for job in jobs], sems[2:])

    @pl.when(m == 0)
    def _():
        greet(dp_peers() + [sibling()])

    fill_mask(mask, lengths, m)
    query = qkv[0, :, :128] * jnp.asarray(0.25, BF16)
    for pair in range(pairs):
        at = 256 + 128 * pair
        now = pair % 2
        for side in range(2):
            mine = lane // VD == side
            queries[now, side] = jnp.where(lane // FEAT == 2 * pair + side, query, zero)
            values[now, side, :, :128] = jnp.where(mine, qkv[0, :, at : at + 128], zero)
            values[now, side, :, 128:] = mine.astype(F32).astype(BF16)
        for j in range(tiles):
            if j == 0:
                plan.at(pair)
            i = min(tiles, j + SPAN + 1)
            tall = (i - j) * TILE
            here, below = slice(j * TILE, (j + 1) * TILE), slice(j * TILE, i * TILE)
            scores = mm(queries[now, :, below].reshape(2 * tall, 128), qkv[0, here, 128:256], NT)
            allowed = mask[j, :tall]
            weights = []
            for side in range(2):
                t = scores[side * tall : (side + 1) * tall] + 1.0
                weights.append(((t * t + 1.0) * allowed).astype(BF16))
            part = mm(jnp.concatenate(weights, 1), values[now, :, here].reshape(2 * TILE, 256))
            add_rows(total.at[now], j, tiles, part)
        inverse = 1.0 / total[now, :, 128:]
        mix_ref[0, :, 128 * pair : 128 * (pair + 1)] = (total[now, :, :128] * inverse).astype(BF16)
        turned = inverse.T
        inv_ref[0, pair, 0:1] = turned[0:1]
        inv_ref[0, pair, 1:2] = turned[VD : VD + 1]

    @pl.when(m == pl.num_programs(0) - 1)
    def _():
        plan.finish()


def whole_group(width, group):
    return pl.BlockSpec((1, group, width), lambda m: (m, 0, 0))


def lengths_spec(lengths):
    return pl.BlockSpec(lengths.shape, lambda *_: (0, 0), memory_space=pltpu.SMEM)


def attend_all(qkv, lengths, out_grad, slabs, jobs):
    micro, group, columns = qkv.shape
    dim = out_grad.shape[2]
    wide = columns - 256
    dma = pltpu.SemaphoreType.DMA
    unit = sum(job[2] for job in jobs)
    return call(
        functools.partial(attend_kernel, jobs),
        "attend",
        2,
        micro,
        [lengths_spec(lengths), whole_group(columns, group), anywhere(), anywhere()],
        [
            whole_group(wide, group),
            pl.BlockSpec((1, wide // 128, 8, group), lambda m: (m, 0, 0, 0)),
            anywhere(),
            anywhere(),
        ],
        [
            jax.ShapeDtypeStruct((micro, group, wide), BF16),
            jax.ShapeDtypeStruct((micro, wide // 128, 8, group), F32),
            jax.ShapeDtypeStruct(out_grad.shape, BF16),
            jax.ShapeDtypeStruct((dim, unit), BF16),
        ],
        [
            pltpu.VMEM((group // TILE, TILE * (SPAN + 1), TILE), F32),
            pltpu.VMEM((2, 2, group, 128), BF16),
            pltpu.VMEM((2, 2, group, 256), BF16),
            pltpu.VMEM((2, group, 256), F32),
            dma,
            dma,
        ]
        + gather_sems() * len(jobs),
        (lengths, qkv, out_grad, slabs),
    )


def attend_back_kernel(jobs, lengths, qkv, mix_ref, inv_ref, d_own, d_other, weights, *refs):
    sources, refs = refs[: len(jobs)], refs[len(jobs) :]
    (dqkv, grads), refs = refs[:2], refs[2:]
    outs, refs = refs[: len(jobs)], refs[len(jobs) :]
    (mask, queries, queries_t, keys, douts, douts_t, deltas, dv_t, dk_t, dq), refs = refs[:10], refs[10:]
    (d, dmix, grad_total, rounded, out_sem), refs = refs[:5], refs[5:]
    m = pl.program_id(0)
    group = qkv.shape[1]
    tiles = group // TILE
    pairs = mix_ref.shape[2] // 128
    lane = lax.broadcasted_iota(jnp.int32, (group, 128), 1)
    zero = jnp.zeros((), BF16)
    plan = Plan(m, lengths.shape[0], pairs, 18.0)
    add_scatters(plan, jobs, sources, outs, refs)

    @pl.when(m == 0)
    def _():
        greet(dp_peers())
        grad_total[...] = jnp.zeros_like(grad_total)

    plan.at(0)
    rows = d_own.shape[1]
    core = lax.axis_index("tensor")
    d[pl.ds(pl.multiple_of(core * rows, rows), rows)] = d_own[0]
    d[pl.ds(pl.multiple_of((1 - core) * rows, rows), rows)] = d_other[0]
    dmix[...] = mm(d[...], weights[...]).astype(BF16)
    grad_total[...] += mm(d[...], mix_ref[0], TN)
    fill_mask(mask, lengths, m)
    queries_t[...] = (qkv[0, :, :128].astype(F32) * 0.5).T.astype(BF16)
    query = qkv[0, :, :128] * jnp.asarray(0.25, BF16)
    key = qkv[0, :, 128:256] * jnp.asarray(0.5, BF16)
    for pair in range(pairs):
        now = pair % 2
        lanes = slice(128 * pair, 128 * (pair + 1))
        value = slice(256 + 128 * pair, 384 + 128 * pair)
        inverse = jnp.concatenate(
            [jnp.broadcast_to(inv_ref[0, pair, s : s + 1, :], (VD, group)) for s in range(2)], 0
        ).T
        dout_low = (dmix[:, lanes].astype(F32) * inverse).astype(BF16)
        dout = dout_low.astype(F32)
        douts_t[now] = dout.T.astype(BF16)
        product = dout * mix_ref[0, :, lanes].astype(F32)
        for side in range(2):
            mine = lane // VD == side
            head = lane // FEAT == 2 * pair + side
            queries[now, side] = jnp.where(head, query, zero)
            keys[now, side] = jnp.where(head, key, zero)
            douts[now, side] = jnp.where(mine, dout_low, zero)
            delta = jnp.sum(jnp.where(mine, product, 0.0), axis=1, keepdims=True)
            deltas[now, side] = jnp.broadcast_to(delta, (group, 128))
        for j in range(tiles):
            if j == 0 and pair:
                plan.at(pair)
            i = min(tiles, j + SPAN + 1)
            tall = (i - j) * TILE
            here, below = slice(j * TILE, (j + 1) * TILE), slice(j * TILE, i * TILE)
            scores = mm(queries[now, :, below].reshape(2 * tall, 128), qkv[0, here, 128:256], NT)
            slopes = mm(douts[now, :, below].reshape(2 * tall, 128), qkv[0, here, value], NT)
            allowed = mask[j, :tall]
            d_scores = []
            for side in range(2):
                t = scores[side * tall : (side + 1) * tall] + 1.0
                masked = t * allowed
                delta = jnp.concatenate([deltas[now, side, below]] * (TILE // 128), 1)
                d_score = ((slopes[side * tall : (side + 1) * tall] - delta) * masked).astype(BF16)
                weights = (t * masked + allowed).astype(BF16)
                mine = slice(VD * side, VD * (side + 1))
                head = slice((2 * pair + side) * FEAT, (2 * pair + side + 1) * FEAT)
                dv_t[now, mine, here] = mm(douts_t[now, mine, below], weights)
                dk_t[head, here] = mm(queries_t[head, below], d_score)
                d_scores.append(d_score)
            part = mm(jnp.concatenate(d_scores, 1), keys[now, :, here].reshape(2 * TILE, 128))
            if pair:
                dq[below] += part
            else:
                add_rows(dq, j, tiles, part)
        dqkv[0, :, value] = dv_t[now].T.astype(BF16)
    dqkv[0, :, 128:256] = dk_t[...].T.astype(BF16)
    dqkv[0, :, :128] = dq[...].astype(BF16)

    @pl.when(m == pl.num_programs(0) - 1)
    def _():
        rounded[...] = grad_total[...].astype(BF16).reshape(rounded.shape)
        write = pltpu.make_async_copy(rounded, grads, out_sem)
        write.start()
        plan.finish()
        write.wait()


def attend_back(qkv, mix, inverse, d_own, d_other, weights, lengths, sources, jobs):
    micro, group, columns = qkv.shape
    wide = columns - 256
    rows, dim = d_own.shape[1:]
    shapes, specs = scatter_outs(jobs, dim)
    grads = grad_shape(dim, wide)
    pair_rows = pltpu.VMEM((2, 2, group, 128), BF16)
    return call(
        functools.partial(attend_back_kernel, jobs),
        "attend_back",
        8,
        micro,
        [
            lengths_spec(lengths),
            whole_group(columns, group),
            whole_group(wide, group),
            pl.BlockSpec((1, wide // 128, 8, group), lambda m: (m, 0, 0, 0)),
            whole_group(dim, rows),
            whole_group(dim, rows),
            once((dim, wide)),
        ]
        + [anywhere()] * len(jobs),
        [whole_group(columns, group), anywhere()] + specs,
        [jax.ShapeDtypeStruct((micro, group, columns), BF16), grads] + shapes,
        [
            pltpu.VMEM((group // TILE, TILE * (SPAN + 1), TILE), F32),
            pair_rows,
            pltpu.VMEM((128, group), BF16),
            pair_rows,
            pair_rows,
            pltpu.VMEM((2, 128, group), BF16),
            pltpu.VMEM((2, 2, group, 128), F32),
            pltpu.VMEM((2, 128, group), F32),
            pltpu.VMEM((128, group), F32),
            pltpu.VMEM((group, 128), F32),
            pltpu.VMEM((group, dim), BF16),
            pltpu.VMEM((group, wide), BF16),
            pltpu.VMEM((dim, wide), F32),
            pltpu.VMEM(grads.shape, BF16),
            pltpu.SemaphoreType.DMA,
        ]
        + scatters_scratch(jobs, dim),
        (lengths, qkv, mix, inverse, d_own, d_other, weights, *sources),
    )


def out_kernel(
    jobs, near_job, mix_own, mix_other, x, weights, gains, slabs, resid_out, h_out, h_other, unit, near,
    parts, sent, got, h_sent, send, recv, *sems,
):
    i = pl.program_id(0)
    count, rows = got.shape[0], got.shape[1]
    per = h_other.shape[1] // rows
    plan = Plan(i, 2 * count, 1, 0.95)
    add_gathers(plan, [(slabs, unit, *job) for job in jobs], sems[3:])
    ahead = NearGather(slabs.at[:, pl.ds(*near_job)], near, *sems[:3])
    plan.add([(2.0, ahead.begin)], ahead.finish)

    def swap(k):
        return remote(sent.at[k], got.at[k], send.at[k], recv.at[k], sibling())

    def swap_h(k):
        place = h_other.at[lax.div(k, per), pl.ds(pl.multiple_of(lax.rem(k, per) * rows, rows), rows)]
        return remote(h_sent.at[k], place, send.at[count + k], recv.at[count + k], sibling())

    @pl.when(i == 0)
    def _():
        greet(dp_peers() + [sibling()])

    plan.at(0)

    @pl.when(i < count)
    def _():
        both = jnp.concatenate([mix_other[0], mix_own[0]], 0)
        part = mm(both, weights[...], NT)
        sent[i] = part[:rows].astype(BF16)
        parts[i] = part[rows:]
        swap(i).start()

    @pl.when(i >= count)
    def _():
        k = i - count
        swap(k).wait_recv()
        resid = x[0].astype(F32) + parts[k] + got[k].astype(F32)
        resid_out[0] = resid.astype(BF16)
        h = (resid * root_mean(resid) * gains[1:2]).astype(BF16)
        h_out[0] = h
        h_sent[k] = h
        swap_h(k).start()

    @pl.when(i == 2 * count - 1)
    def _():
        plan.finish()
        for k in range(count):
            swap(k).wait_send()
            swap_h(k).wait()


def out_project(mix, x, weights, gains, slabs, jobs, near_job, rows=256):
    micro, own_rows, dim = x.shape
    wide = mix.shape[2]
    per = own_rows // rows
    count = micro * per
    late = part_block(dim, per, rows, count, count - 1)
    shape = jax.ShapeDtypeStruct((micro, own_rows, dim), BF16)
    buffer = pltpu.VMEM((count, rows, dim), BF16)
    return call(
        functools.partial(out_kernel, jobs, near_job),
        "out_project",
        3,
        2 * count,
        [
            core_block(wide, per, rows, False, count - 1),
            core_block(wide, per, rows, True, count - 1),
            late,
            once((dim, wide)),
            once((8, dim)),
            anywhere(),
        ],
        [late, late, anywhere(), anywhere(), anywhere()],
        [
            shape,
            shape,
            shape,
            jax.ShapeDtypeStruct((dim, sum(job[2] for job in jobs)), BF16),
            jax.ShapeDtypeStruct((dim // 4, near_job[1]), BF16),
        ],
        [pltpu.VMEM((count, rows, dim), F32), buffer, buffer, buffer]
        + half_sems(2 * count)
        + half_sems(far_count() - 1)
        + [pltpu.SemaphoreType.DMA]
        + gather_sems() * len(jobs),
        (mix, mix, x, weights, gains, slabs),
    )


FEED_US = (5.2, 6.4, 7.2)
GATHER_AT = ((0.0, 0.0), (0.5, 26.0))
SCATTER_AT = (44.0, 59.0, 71.0, 86.0)
BACK_US = 2.4
OUT_PIECE = 512
IN_PIECE = 384


def feed_kernel(
    steps, widths, loads, cuts, jobs, h_own, h_other, g_own, g_other, unit_0, unit_1, near, slabs,
    resid, g_late, resid_end, g_end, gains, mixed_out, d_out, d_other, *refs,
):
    def take(number):
        nonlocal refs
        taken, refs = refs[:number], refs[number:]
        return taken

    chunks = len(widths)
    grads = take(chunks)
    units = take(chunks - 1)
    outs = take(len(jobs))
    slab_a, slab_b, total, h, g, hidden_s, dgu_s = take(7)
    out_own, out_other, dm_own, dm_other, dm_got, out_got, d_sent, mixed_s = take(8)
    load_sems, write_sems, send, recv, local = take(5)
    i = pl.program_id(0)
    rows = h_own.shape[1]
    per = d_other.shape[1] // rows
    weights = [(slab_a, slab_b)[chunk % 2] for chunk in range(chunks)]

    def place(ref, k):
        return ref.at[lax.div(k, per), pl.ds(pl.multiple_of(lax.rem(k, per) * rows, rows), rows)]

    def swaps(k):
        return [
            remote(dm_other.at[k], dm_got.at[k + 1], send.at[3 * k], recv.at[3 * k], sibling()),
            remote(out_other.at[k], out_got.at[k + 1], send.at[3 * k + 1], recv.at[3 * k + 1], sibling()),
        ]

    def results(k):
        return [
            remote(d_sent.at[k + 1], place(d_other, k), send.at[3 * k + 2], recv.at[3 * k + 2], sibling()),
            pltpu.make_async_copy(d_sent.at[k + 1], place(d_out, k), local.at[2 * k]),
            pltpu.make_async_copy(mixed_s.at[k + 1], place(mixed_out, k), local.at[2 * k + 1]),
        ]

    def finish_part(slot, before, resid, g_late):
        values = resid[0].astype(F32)
        mixed_s[slot] = add(values, out_own[before], out_got[slot]).astype(BF16)
        scaled = add(dm_own[before], dm_got[slot]) * gains[1:2]
        d_sent[slot] = (g_late[0].astype(F32) + norm_slope(values, scaled)).astype(BF16)

    def copies(chunk):
        made = []
        sources = loads if chunk == 0 else [(0, 0, 3 * widths[chunk])]
        for at, (source, target, columns) in enumerate(sources):
            ref = (unit_0, unit_1)[at] if chunk == 0 else units[chunk - 1]
            tall = slab_a.shape[0] // 4
            for part in range(4):
                rows_at = pl.ds(part * tall, tall)
                cut = ref.at[rows_at, pl.ds(source, columns)]
                target_at = weights[chunk].at[rows_at, pl.ds(target, columns)]
                made.append(pltpu.make_async_copy(cut, target_at, load_sems.at[chunk, at, part]))
        return made

    def writes(chunk):
        made = []
        far, low, parts, half, columns = grads[chunk].shape
        for at in range(far * low * parts):
            source = weights[chunk].at[pl.ds(at * half, half), pl.ds(0, columns)]
            target = grads[chunk].at[at // (low * parts), at // parts % low, at % parts]
            made.append(pltpu.make_async_copy(source, target, write_sems.at[chunk, at]))
        return made

    def start_all(made):
        for copy in made:
            copy.start()

    def wait_all(made):
        for copy in made:
            copy.wait()

    clock = []
    for chunk in range(chunks):
        start = clock[-2] + FEED_US[chunk - 1] if clock else 0.0
        clock += [start + FEED_US[chunk] * (step + part) for step in range(steps) for part in (0, 0.65)]
    plan = Plan(i, chunks * steps, 2, None, clock)
    for chunk in range(1, chunks):
        first, width = cuts[chunk - 1]
        gather = Gather(slabs.at[:, pl.ds(first, width)], units[chunk - 1], *take(3), near if chunk == 1 else None)
        plan.add(gather.plan_near(*GATHER_AT[chunk - 1]), lambda: None, 2 * chunk * steps - 2)
        plan.put(chunk * steps - 1, 1000.0, gather.finish)
        plan.put(chunk * steps - 1, 1001.0, lambda chunk=chunk: start_all(copies(chunk)))
    for at, (chunk, (first, width)) in enumerate(jobs):
        scatter = Scatter(grads[chunk], first, outs[at], take(SCATTER_REFS))
        plan.add(scatter.plan(SCATTER_AT[at]), scatter.finish, None, 2 * (chunk + 1) * steps + 2)
    for chunk in range(chunks - 1):
        plan.put((chunk + 1) * steps + 1, -1.0, lambda chunk=chunk: wait_all(writes(chunk)))

    @pl.when(i == 0)
    def _():
        start_all(copies(0))
        zeros = jnp.zeros(dm_got.shape[1:], BF16)
        dm_got[0] = zeros
        out_got[0] = zeros
        greet(dp_peers() + [sibling()])

    plan.at(0)
    half = jnp.asarray(0.5, BF16)
    one = jnp.asarray(1.0, BF16)
    dim = slab_a.shape[0]

    def chunk_step(chunk):
        slab, width, last = weights[chunk], widths[chunk], chunk == chunks - 1
        j = i - chunk * steps

        @pl.when(j == 0)
        def _():
            total[:, : 3 * width] = jnp.zeros((dim, 3 * width), F32)
            wait_all(copies(chunk))

        h[:rows], h[rows:] = h_other[0], h_own[0]
        g[:rows], g[rows:] = g_other[0], g_own[0]
        for at, wide in chunk_slices(width):
            both = slice(2 * at, 2 * (at + wide))
            gate_up = mm(h[...], slab[:, both]).astype(BF16)
            d_hidden = mm(g[...], slab[:, 2 * width + at : 2 * width + at + wide]).astype(BF16)
            gate, up = gate_up[:, :wide], gate_up[:, wide:]
            sigmoid = half * jnp.tanh(half * gate) + half
            silu = gate * sigmoid
            hidden_s[:, at : at + wide] = silu * up
            d_gate = d_hidden * up * (sigmoid + silu * (one - sigmoid))
            dgu_s[:, both] = jnp.concatenate([d_gate, d_hidden * silu], 1)
        for at in range(0, dim, 512):
            cut = slice(at, at + 512)
            out = mm(hidden_s[:, :width], slab[cut, 2 * width : 3 * width], NT)
            dm = mm(dgu_s[:, : 2 * width], slab[cut, : 2 * width], NT)
            for ref, value in ((out_own, out[rows:]), (out_other, out[:rows]), (dm_own, dm[rows:]), (dm_other, dm[:rows])):
                if chunk:
                    value = value + ref[j, :, cut].astype(F32)
                ref[j, :, cut] = value.astype(BF16)
        if last:
            start_all(swaps(j))

            @pl.when(j > 0)
            def _():
                for swap in swaps(j - 1):
                    swap.wait_recv()

            finish_part(j, jnp.maximum(j - 1, 0), resid, g_late)
        plan.at(1)
        total[:, : 2 * width] += mm(h[...], dgu_s[:, : 2 * width], TN)
        total[:, 2 * width : 3 * width] += mm(g[...], hidden_s[:, :width], TN)
        if last:

            @pl.when(j > 0)
            def _():
                start_all(results(j - 1))

        @pl.when(j == steps - 1)
        def _():
            slab[:, : 3 * width] = total[:, : 3 * width].astype(BF16)
            start_all(writes(chunk))
            if last:
                for swap in swaps(steps - 1):
                    swap.wait_recv()
                finish_part(steps, steps - 1, resid_end, g_end)
                start_all(results(steps - 1))
                plan.finish()
                for k in range(steps):
                    for copy in swaps(k):
                        copy.wait_send()
                    wait_all(results(k))
                wait_all(writes(chunk))

    for chunk in range(chunks):

        @pl.when((i >= chunk * steps) & (i < (chunk + 1) * steps))
        def _(chunk=chunk):
            chunk_step(chunk)


def feed(rows_in, unit_0, unit_1, near, loads, widths, slabs, cuts, jobs, resid, gains, rows=256):
    micro, own_rows, dim = rows_in[0].shape
    per = own_rows // rows
    steps = micro * per
    chunks = len(widths)

    def part_at(lag):
        def place(i):
            k = lax.rem(i, steps) if lag == 0 else jnp.clip(i - (chunks - 1) * steps - lag, 0, steps - 1)
            return lax.div(k, per), lax.rem(k, per), 0

        return pl.BlockSpec((1, rows, dim), place)

    part, late = part_at(0), part_at(1)
    end = pl.BlockSpec((1, rows, dim), lambda i: (micro - 1, per - 1, 0), pipeline_mode=pl.Buffered(1))
    shape = jax.ShapeDtypeStruct((micro, own_rows, dim), BF16)
    grads = [grad_shape(dim, 3 * width) for width in widths]
    units = [jax.ShapeDtypeStruct((dim, width), BF16) for _, width in cuts]
    shapes, specs = scatter_outs([job for _, job in jobs], dim)
    most = max(widths)
    slots, late_slots = pltpu.VMEM((steps, rows, dim), BF16), pltpu.VMEM((steps + 1, rows, dim), BF16)
    blocks = grads[0].shape[0] * grads[0].shape[1] * grads[0].shape[2]
    results = call(
        functools.partial(feed_kernel, steps, widths, loads, cuts, jobs),
        "feed",
        4,
        chunks * steps,
        [part] * 4 + [anywhere()] * 4 + [late, late, end, end, once((8, dim))],
        [anywhere()] * (3 + chunks + chunks - 1) + specs,
        [shape] * 3 + grads + units + shapes,
        [pltpu.VMEM((dim, 3 * most), BF16)] * 2
        + [
            pltpu.VMEM((dim, 3 * most), F32),
            pltpu.VMEM((2 * rows, dim), BF16),
            pltpu.VMEM((2 * rows, dim), BF16),
            pltpu.VMEM((2 * rows, most), BF16),
            pltpu.VMEM((2 * rows, 2 * most), BF16),
        ]
        + [slots] * 4
        + [late_slots] * 4
        + [pltpu.SemaphoreType.DMA((chunks, 2, 4)), pltpu.SemaphoreType.DMA((chunks, blocks))]
        + half_sems(3 * steps)
        + [pltpu.SemaphoreType.DMA((2 * steps,))]
        + gather_sems() * (chunks - 1)
        + scatters_scratch([job for _, job in jobs], dim),
        (*rows_in, unit_0, unit_1, near, slabs, resid, rows_in[2], resid, rows_in[2], gains),
    )
    return results[:3], results[3 : 3 + chunks], results[2 + 2 * chunks :]


def back_in_kernel(
    micro, feed_jobs, out_jobs, in_jobs, h, dqkv_all, dqkv, x, d_own, weights, gains, grads_last,
    w_query, w_key, w_value, slabs, *refs,
):
    jobs = out_jobs + in_jobs
    feed_count = sum(len(chunk) for chunk in feed_jobs)
    feed_grads, refs = refs[:feed_count], refs[feed_count:]
    (input_grad, gain_sums, grads), refs = refs[:3], refs[3:]
    outs, refs = refs[: len(jobs)], refs[len(jobs) :]
    (total, sent, got, send, recv, out_sem, rounded, sums, sums_got, sums_sems), refs = refs[:10], refs[10:]
    i = pl.program_id(0)
    m = lax.rem(i, micro)
    plan = Plan(i, 3 * micro, 1, BACK_US)
    split = SCATTER_REFS * len(out_jobs)
    add_scatters(plan, out_jobs, [grads_last] * len(out_jobs), outs, refs[:split])
    outs = outs[len(out_jobs) :]
    add_scatters(plan, in_jobs, [grads] * len(in_jobs), outs, refs[split:], BACK_US * micro)

    def swap(k):
        return remote(sent.at[k], got.at[k], send.at[k], recv.at[k], sibling())

    def swap_sums():
        return remote(sums, sums_got, sums_sems.at[0], sums_sems.at[1], sibling())

    @pl.when(i == 0)
    def _():
        greet(dp_peers() + [sibling()])
        total[...] = jnp.zeros_like(total)

    @pl.when(i < micro)
    def _():
        total[...] += mm(h[0], dqkv_all[0], TN)

    @pl.when(i == micro - 1)
    def _():
        rounded[...] = total[...].astype(BF16).reshape(rounded.shape)
        write = pltpu.make_async_copy(rounded, grads, out_sem)
        write.start()
        write.wait()

    plan.at(0)

    @pl.when(i >= micro)
    def _():
        part = mm(dqkv[0], weights[...], NT)

        @pl.when(i < 2 * micro)
        def _():
            sent[m] = part.astype(BF16)
            swap(m).start()

        @pl.when(i >= 2 * micro)
        def _():
            swap(m).wait_recv()
            scaled = (part + got[m].astype(F32)) * gains[0:1]
            input_grad[0] = (d_own[0].astype(F32) + norm_slope(x[0].astype(F32), scaled)).astype(BF16)

    @pl.when(i == 3 * micro - 1)
    def _():
        each = slabs.shape[0]
        sizes = [sum(wide for _, wide in chunk) for chunk in feed_jobs]
        at = slabs.shape[1] - sum(sizes)
        index = 0
        mid = jnp.zeros((each, 128), F32)
        for size, chunk in zip(sizes, feed_jobs):
            for first, wide in chunk:
                value = feed_grads[index][...].reshape(each, wide)
                for column in range(0, wide, 128):
                    if first + column < 2 * (size // 3):
                        lanes = slice(at + first + column, at + first + column + 128)
                        mid = mid + value[:, column : column + 128] * slabs[:, lanes].astype(F32)
                index += 1
            at += size
        sums[1] = mid
        plan.finish()
        near = jnp.zeros((each, 128), F32)
        at = 0
        columns = [out[...].reshape(each, out.shape[2]) for out in outs]
        columns = jnp.concatenate(columns, 1) if len(columns) > 1 else columns[0]
        for ref in (w_query, w_key, w_value):
            for column in range(0, ref.shape[1], 128):
                near = near + columns[:, at : at + 128] * ref[:, column : column + 128].astype(F32)
                at += 128
        sums[0] = near
        swap_sums().start()
        for k in range(micro):
            swap(k).wait_send()
        swap_sums().wait()
        gain_sums[...] = sums[...] + sums_got[...]


def back_in(h, dqkv, x, d_own, weights, gains, grads_last, w_in, slabs, feed_grads, feed_jobs, out_jobs, in_jobs):
    jobs = out_jobs + in_jobs
    micro, rows, dim = x.shape
    columns = dqkv.shape[2]
    each = slabs.shape[0]
    own = pl.BlockSpec((1, rows, dim), lambda i: (jnp.maximum(i - 2 * micro, 0), 0, 0))
    grads = grad_shape(dim, columns)
    shapes, specs = scatter_outs(jobs, dim)
    buffer = pltpu.VMEM((micro, rows, dim), BF16)
    sums = jax.ShapeDtypeStruct((2, each, 128), F32)

    def all_place(i):
        return jnp.minimum(i, micro - 1), 0, 0

    def place(i):
        core = lax.axis_index("tensor")
        k = jnp.maximum(i - micro, 0)
        return lax.rem(k, micro), jnp.where(k < micro, 1 - core, core), 0

    locals_ = list(w_in) + [slabs] + list(feed_grads)
    return call(
        functools.partial(back_in_kernel, micro, feed_jobs, out_jobs, in_jobs),
        "back_in",
        9,
        3 * micro,
        [
            pl.BlockSpec((1, 2 * rows, dim), all_place),
            pl.BlockSpec((1, 2 * rows, columns), all_place),
            pl.BlockSpec((1, rows, columns), place),
            own,
            own,
            once(weights.shape),
            once((8, dim)),
            anywhere(),
        ]
        + [once(a.shape) for a in locals_],
        [own, once(sums.shape), anywhere()] + specs,
        [jax.ShapeDtypeStruct((micro, rows, dim), BF16), sums, grads] + shapes,
        [pltpu.VMEM((dim, columns), F32), buffer, buffer]
        + half_sems(micro)
        + [
            pltpu.SemaphoreType.DMA,
            pltpu.VMEM(grads.shape, BF16),
            pltpu.VMEM(sums.shape, F32),
            pltpu.VMEM(sums.shape, F32),
            pltpu.SemaphoreType.DMA((2,)),
        ]
        + scatters_scratch(jobs, dim),
        (h, dqkv, dqkv, x, d_own, weights, gains, grads_last, *locals_),
    )


def finish_kernel(edges, counts, grad_in, mixed, gain_attn, gain_mlp, gain_sums, *refs):
    feed_grads, refs = refs[: counts[0]], refs[counts[0] :]
    out_grads, refs = refs[: counts[1]], refs[counts[1] :]
    in_grads, refs = refs[: counts[2]], refs[counts[2] :]
    mixed_out, grad_out, attn_out, mlp_out, q_out, k_out, v_out, out_t, gate_out, up_out, down_t = refs
    each, units = gate_out.shape
    grad_out[...] = grad_in[...].astype(F32)
    mixed_out[...] = mixed[...]

    def blocks(pieces):
        found = []
        for piece in pieces:
            for at in range(0, piece.shape[2], 128):
                found.append((piece, at))
        return found

    def copy_to(ref, at, block):
        piece, column = block
        wide = min(128, ref.shape[1] - at)
        ref[:, at : at + wide] = piece[:, :, column : column + wide].reshape(each, wide)

    @pl.when(pl.program_id(0) == 0)
    def _():
        turned = [gain_sums[k].T for k in range(2)]
        for value, gain, ref in zip(turned, (gain_attn, gain_mlp), (attn_out, mlp_out)):
            ref[...] = jnp.sum(value, axis=0, keepdims=True) / gain[...].astype(F32)
        queue = blocks(in_grads)
        for ref in (q_out, k_out, v_out):
            for at in range(0, ref.shape[1], 128):
                copy_to(ref, at, queue.pop(0))
        for at, block in zip(range(0, out_t.shape[1], 128), blocks(out_grads)):
            copy_to(out_t, at, block)
        queue = blocks(feed_grads)
        for low, high in edges:
            for start, width in chunk_slices(high - low):
                for ref in (gate_out, up_out):
                    for at in range(low + start, low + start + width, 128):
                        copy_to(ref, at, queue.pop(0))
            for at in range(low, high, 128):
                copy_to(down_t, at, queue.pop(0))


def finish(edges, grad_in, mixed, gain_attn, gain_mlp, gain_sums, feed_grads, out_grads, in_grads, widths, units):
    micro, rows, dim = mixed.shape
    each = gain_sums.shape[1]
    tile = min(rows, 256)
    block = pl.BlockSpec((1, tile, dim), lambda m, t: (m, t, 0))
    small = [gain_attn, gain_mlp, gain_sums, *feed_grads, *out_grads, *in_grads]
    shapes = [jax.ShapeDtypeStruct((1, each), F32)] * 2
    shapes += [jax.ShapeDtypeStruct((each, w), F32) for w in widths + [units] * 3]
    counts = (len(feed_grads), len(out_grads), len(in_grads))
    return call(
        functools.partial(finish_kernel, edges, counts),
        "finish",
        None,
        (micro, rows // tile),
        [block, block] + [once(a.shape) for a in small],
        [block, block] + [once(s.shape) for s in shapes],
        [jax.ShapeDtypeStruct(mixed.shape, BF16), jax.ShapeDtypeStruct(mixed.shape, F32)] + shapes,
        [],
        (grad_in, mixed, *small),
    )


def fused_body(
    inputs, gain_attn, gain_mlp, w_query, w_key, w_value, w_out, w_gate, w_up, w_down, out_grad, lengths
):
    micro, rows, dim = inputs.shape
    units = w_gate.shape[1]
    out_columns = w_out.shape[0]
    lengths = lengths[:, 0]
    gains = gain_attn.reshape(1, -1), gain_mlp.reshape(1, -1)
    w_in = (w_query, w_key, w_value)
    padded = -(-units // 128) * 128
    edges = [(max(at - CHUNK, 0), at) for at in range(padded, 0, -CHUNK)][::-1]
    wide = [3 * (high - low) for low, high in edges]

    h_in, qkv, gain_full, whole_in, slabs = project(edges, inputs, *w_in, *gains, w_gate, w_up, w_down.T, w_out.T)

    begin = [out_columns, out_columns + wide[0], out_columns + wide[0] + wide[1]]
    early = min(EARLY, wide[0])
    mix, inverse, g_other, unit_0 = attend_all(qkv, lengths, out_grad, slabs, [(0, 0, begin[0] + early)])
    resid, h_own, h_other, unit_1, near = out_project(
        mix, inputs, unit_0, gain_full, slabs, [(begin[0] + early, 0, wide[0] - early)], (begin[1], wide[1])
    )

    feed_jobs, at = [[], [], []], []
    for kernel in JOBS:
        at.append([])
        for chunk, width in kernel:
            first = sum(w for _, w in feed_jobs[chunk])
            feed_jobs[chunk].append((first, width))
            at[-1].append((chunk, (first, width)))
    loads = [(out_columns, 0, early), (0, early, wide[0] - early)]
    (mixed_out, d_own, d_other), grads_of, done = feed(
        (h_own, h_other, out_grad, g_other),
        unit_0,
        unit_1,
        near,
        loads,
        [w // 3 for w in wide],
        slabs,
        list(zip(begin[1:], wide[1:])),
        at[0],
        resid,
        gain_full,
    )
    found = dict(zip(at[0], done))
    sources, jobs = [grads_of[chunk] for chunk, _ in at[1]], [job for _, job in at[1]]
    dqkv, grads_out, *done = attend_back(qkv, mix, inverse, d_own, d_other, unit_0, lengths, sources, jobs)
    found |= dict(zip(at[1], done))
    feed_grads = [found[key] for key in sorted(found)]
    out_jobs, in_jobs = pieces_of(out_columns, OUT_PIECE), pieces_of(qkv.shape[2], IN_PIECE)
    input_grad, gain_sums, _, *done = back_in(
        h_in, dqkv, inputs, d_own, whole_in, gain_full, grads_out, w_in, slabs, feed_grads, feed_jobs, out_jobs, in_jobs
    )
    out_grads, in_grads = done[: len(out_jobs)], done[len(out_jobs) :]
    widths = [w.shape[1] for w in w_in] + [out_columns]
    mixed_out, input_grad, attn_grad, mlp_grad, grad_query, grad_key, grad_value, out_t, gate, up, down_t = finish(
        edges, input_grad, mixed_out, *gains, gain_sums, feed_grads, out_grads, in_grads, widths, units
    )
    return (
        mixed_out,
        input_grad,
        attn_grad[0],
        mlp_grad[0],
        grad_query,
        grad_key,
        grad_value,
        out_t.T,
        gate,
        up,
        down_t.T,
    )


def solution(mesh):
    in_specs = (
        P(None, ("dp", "tensor"), None),
        P("dp"),
        P("dp"),
        P("dp", "tensor"),
        P("dp", "tensor"),
        P("dp", "tensor"),
        P("tensor", "dp"),
        P("dp", "tensor"),
        P("dp", "tensor"),
        P("tensor", "dp"),
        P(None, ("dp", "tensor"), None),
        P(None, "dp", None),
    )
    out_specs = (
        P(None, ("dp", "tensor"), None),
        P(None, ("dp", "tensor"), None),
        P("dp"),
        P("dp"),
        P("dp", "tensor"),
        P("dp", "tensor"),
        P("dp", "tensor"),
        P("tensor", "dp"),
        P("dp", "tensor"),
        P("dp", "tensor"),
        P("tensor", "dp"),
    )
    fits = mesh.shape["tensor"] == 2 and mesh.shape["dp"] % 4 == 0
    chosen = fused_body if fits else plain_body
    return jax.shard_map(chosen, mesh=mesh, in_specs=in_specs, out_specs=out_specs, check_vma=False)
```

```python
import functools
import math

import jax
import jax.numpy as jnp
import numpy as np
from jax import lax
from jax.experimental import pallas as pl
from jax.experimental.pallas import tpu as pltpu
from jax.sharding import PartitionSpec as P

FEAT = 16
VD = 64
BLK = 512


EXACT = lax.Precision.HIGHEST


def taylor(halved):
    feature_dim = halved.shape[-1]
    upper_idx, lower_idx = np.triu_indices(feature_dim)
    flat_index = jnp.asarray(upper_idx * feature_dim + lower_idx, jnp.int32)
    factors = jnp.asarray(np.where(upper_idx == lower_idx, math.sqrt(0.5), 1.0), jnp.float32)
    outer = (halved[..., :, None] * halved[..., None, :]).reshape(
        halved.shape[:-1] + (feature_dim * feature_dim,)
    )
    second = jnp.take(outer, flat_index, axis=-1) * factors
    ones_col = jnp.ones(halved.shape[:-1] + (1,), jnp.float32)
    return jnp.concatenate([ones_col, halved, second], axis=-1)


def attend_block(carry_in, block_in):
    kv_state, totals, previous = carry_in
    queries, keys_in, values_in, doc_ids = block_in
    half_q = 0.5 * queries
    half_k = 0.5 * keys_in
    scores = jnp.einsum("rhf,chf->hrc", half_q, half_k, preferred_element_type=jnp.float32)
    places = jnp.arange(doc_ids.shape[0], dtype=jnp.int32)
    allowed = (doc_ids[:, None] == doc_ids[None, :]) & (places[None, :] <= places[:, None])
    weights = jnp.where(allowed[None], 1.0 + scores + 0.5 * scores * scores, 0.0)
    feat_q = taylor(half_q)
    feat_k = taylor(half_k)
    carried_in = (doc_ids == previous).astype(jnp.float32)
    numerator = jnp.einsum("hrc,chv->rhv", weights, values_in, precision=EXACT) + carried_in[
        :, None, None
    ] * jnp.einsum("rhf,hfv->rhv", feat_q, kv_state, precision=EXACT)
    denominator = jnp.sum(weights, axis=2).T + carried_in[:, None] * jnp.einsum(
        "rhf,hf->rh", feat_q, totals, precision=EXACT
    )
    mixed_rows = numerator / denominator[:, :, None]
    final_doc = doc_ids[-1]
    staying = (doc_ids == final_doc).astype(jnp.float32)[:, None, None] * feat_k
    joined = (final_doc == previous).astype(jnp.float32)
    kv_state = jnp.einsum("rhf,rhv->hfv", staying, values_in, precision=EXACT) + joined * kv_state
    totals = jnp.sum(staying, axis=0) + joined * totals
    return ((kv_state, totals, final_doc), mixed_rows)


def attend(queries, keys_in, values_in, doc_ids):
    row_total, head_count, feature_dim = queries.shape
    value_dim = values_in.shape[2]
    block_count = row_total // BLK
    feature_total = 1 + feature_dim + feature_dim * (feature_dim + 1) // 2
    initial = (
        jnp.zeros((head_count, feature_total, value_dim), jnp.float32),
        jnp.zeros((head_count, feature_total), jnp.float32),
        jnp.array(-1, jnp.int32),
    )
    pieces = (
        queries.reshape(block_count, BLK, head_count, feature_dim),
        keys_in.reshape(block_count, BLK, head_count, feature_dim),
        values_in.reshape(block_count, BLK, head_count, value_dim),
        doc_ids.reshape(block_count, BLK),
    )
    last_carry, mixed_rows = lax.scan(jax.checkpoint(attend_block), initial, pieces)
    return mixed_rows.reshape(row_total, head_count * value_dim)


def document_ids(lengths_row, row_total):
    doc_ends = jnp.cumsum(lengths_row)
    places = jnp.arange(row_total, dtype=jnp.int32)
    return jnp.sum((places[:, None] >= doc_ends[None, :]).astype(jnp.int32), axis=1)


def rows_product(left, right):
    return lax.dot_general(
        left, right, (((0,), (0,)), ((), ())), preferred_element_type=jnp.float32
    )


def back_product(left, right):
    return lax.dot_general(
        left, right, (((1,), (1,)), ((), ())), preferred_element_type=jnp.float32
    )


def norm_back(grad_normed, normed, inverse, gain_full):
    scaled = grad_normed * gain_full
    return inverse * (scaled - normed * jnp.mean(scaled * normed, axis=-1, keepdims=True))


def row_slice(matrix, first_row, row_count):
    return lax.dynamic_slice_in_dim(matrix, first_row, row_count, 0)


def inverse_root(values):
    return lax.rsqrt(jnp.mean(values * values, axis=-1, keepdims=True) + 1e-05)


def fetch_weights(gain_attn, gain_mlp, w_query, w_key, w_value, w_out, w_gate, w_up, w_down):
    row_parts = (
        lax.all_gather(w_query, "dp", axis=0, tiled=True),
        lax.all_gather(w_key, "dp", axis=0, tiled=True),
        lax.all_gather(w_value, "dp", axis=0, tiled=True),
        lax.all_gather(w_gate, "dp", axis=0, tiled=True),
        lax.all_gather(w_up, "dp", axis=0, tiled=True),
        lax.all_gather(gain_attn, "dp", axis=0, tiled=True),
        lax.all_gather(gain_mlp, "dp", axis=0, tiled=True),
    )
    col_parts = (
        lax.all_gather(w_out, "dp", axis=1, tiled=True),
        lax.all_gather(w_down, "dp", axis=1, tiled=True),
    )
    return tuple(row_parts) + tuple(col_parts)


def plain_body(
    inputs,
    gain_attn,
    gain_mlp,
    w_query,
    w_key,
    w_value,
    w_out,
    w_gate,
    w_up,
    w_down,
    out_grad,
    lengths,
):
    micro_count = inputs.shape[0]
    shard_rows = inputs.shape[1]
    model_dim = inputs.shape[2]
    group_rows = shard_rows * lax.axis_size("tensor")
    local_heads = w_query.shape[1] // FEAT
    grad_query_sum = jnp.zeros((model_dim, w_query.shape[1]), jnp.float32)
    grad_key_sum = jnp.zeros((model_dim, w_key.shape[1]), jnp.float32)
    grad_value_sum = jnp.zeros((model_dim, w_value.shape[1]), jnp.float32)
    grad_gate_sum = jnp.zeros((model_dim, w_gate.shape[1]), jnp.float32)
    grad_up_sum = jnp.zeros((model_dim, w_up.shape[1]), jnp.float32)
    grad_out_sum = jnp.zeros((w_out.shape[0], model_dim), jnp.float32)
    grad_down_sum = jnp.zeros((w_down.shape[0], model_dim), jnp.float32)
    gain_attn_sum = jnp.zeros((model_dim,), jnp.float32)
    gain_mlp_sum = jnp.zeros((model_dim,), jnp.float32)
    outputs = []
    input_grads = []
    for micro_step in range(micro_count):
        (
            full_query,
            full_key,
            full_value,
            full_gate,
            full_up,
            full_gain_attn,
            full_gain_mlp,
            full_out,
            full_down,
        ) = fetch_weights(gain_attn, gain_mlp, w_query, w_key, w_value, w_out, w_gate, w_up, w_down)
        gain_in = full_gain_attn.astype(jnp.float32)
        gain_mid = full_gain_mlp.astype(jnp.float32)
        doc_ids = document_ids(lengths[micro_step, 0], group_rows)
        values = inputs[micro_step].astype(jnp.float32)
        inverse_in = inverse_root(values)
        normed_in = values * inverse_in
        gathered_in = lax.all_gather(
            (normed_in * gain_in).astype(jnp.bfloat16), "tensor", axis=0, tiled=True
        )
        query_low = jnp.dot(gathered_in, full_query, preferred_element_type=jnp.float32).astype(
            jnp.bfloat16
        )
        key_low = jnp.dot(gathered_in, full_key, preferred_element_type=jnp.float32).astype(
            jnp.bfloat16
        )
        value_low = jnp.dot(gathered_in, full_value, preferred_element_type=jnp.float32).astype(
            jnp.bfloat16
        )
        query_full = query_low.astype(jnp.float32).reshape(group_rows, local_heads, FEAT)
        key_full = key_low.astype(jnp.float32).reshape(group_rows, local_heads, FEAT)
        value_full = value_low.astype(jnp.float32).reshape(group_rows, local_heads, VD)

        def local_attend(query_arg, key_arg, value_arg):
            return attend(query_arg, key_arg, value_arg, doc_ids)

        mixed_full, pullback = jax.vjp(local_attend, query_full, key_full, value_full)
        mixed_low = mixed_full.astype(jnp.bfloat16)
        residual = values + lax.psum_scatter(
            jnp.dot(
                row_slice(mixed_low, jnp.int32(0), shard_rows * lax.axis_size("tensor")),
                full_out,
                preferred_element_type=jnp.float32,
            ),
            "tensor",
            scatter_dimension=0,
            tiled=True,
        )
        inverse_mid = inverse_root(residual)
        normed_mid = residual * inverse_mid
        gathered_mid = lax.all_gather(
            (normed_mid * gain_mid).astype(jnp.bfloat16), "tensor", axis=0, tiled=True
        )
        gate_pre = jnp.dot(gathered_mid, full_gate, preferred_element_type=jnp.float32)
        up_pre = jnp.dot(gathered_mid, full_up, preferred_element_type=jnp.float32)
        sigmoid_gate = jax.nn.sigmoid(gate_pre)
        silu_gate = gate_pre * sigmoid_gate
        hidden = (silu_gate * up_pre).astype(jnp.bfloat16)
        mlp_part = lax.psum_scatter(
            jnp.dot(
                row_slice(hidden, jnp.int32(0), shard_rows * lax.axis_size("tensor")),
                full_down,
                preferred_element_type=jnp.float32,
            ).astype(jnp.bfloat16),
            "tensor",
            scatter_dimension=0,
            tiled=True,
        ).astype(jnp.float32)
        outputs.append((residual + mlp_part).astype(jnp.bfloat16))
        cotangent = out_grad[micro_step]
        gathered_grad = lax.all_gather(cotangent, "tensor", axis=0, tiled=True)
        grad_down_sum += rows_product(hidden, gathered_grad)
        grad_hidden = back_product(gathered_grad, full_down)
        grad_gate_low = (
            grad_hidden * up_pre * sigmoid_gate * (1.0 + gate_pre * (1.0 - sigmoid_gate))
        ).astype(jnp.bfloat16)
        grad_up_low = (grad_hidden * silu_gate).astype(jnp.bfloat16)
        grad_gate_sum += rows_product(gathered_mid, grad_gate_low)
        grad_up_sum += rows_product(gathered_mid, grad_up_low)
        first_row = jnp.int32(0)
        grad_mid = lax.psum_scatter(
            back_product(
                row_slice(grad_gate_low, first_row, shard_rows * lax.axis_size("tensor")), full_gate
            )
            + back_product(
                row_slice(grad_up_low, first_row, shard_rows * lax.axis_size("tensor")), full_up
            ),
            "tensor",
            scatter_dimension=0,
            tiled=True,
        )
        gain_mlp_sum += jnp.sum(grad_mid * normed_mid, axis=0)
        grad_resid = cotangent.astype(jnp.float32) + norm_back(
            grad_mid, normed_mid, inverse_mid, gain_mid
        )
        gathered_resid = lax.all_gather(
            grad_resid.astype(jnp.bfloat16), "tensor", axis=0, tiled=True
        )
        grad_out_sum += rows_product(mixed_low, gathered_resid)
        grad_mixed = back_product(gathered_resid, full_out).astype(jnp.bfloat16).astype(jnp.float32)
        grad_query_full, grad_key_full, grad_value_full = pullback(grad_mixed)
        grad_query_low = grad_query_full.reshape(group_rows, -1).astype(jnp.bfloat16)
        grad_key_low = grad_key_full.reshape(group_rows, -1).astype(jnp.bfloat16)
        grad_value_low = grad_value_full.reshape(group_rows, -1).astype(jnp.bfloat16)
        grad_query_sum += rows_product(gathered_in, grad_query_low)
        grad_key_sum += rows_product(gathered_in, grad_key_low)
        grad_value_sum += rows_product(gathered_in, grad_value_low)
        attn_first_row = jnp.int32(0)
        grad_in = lax.psum_scatter(
            (
                back_product(
                    row_slice(grad_query_low, attn_first_row, shard_rows * lax.axis_size("tensor")),
                    full_query,
                )
                + back_product(
                    row_slice(grad_key_low, attn_first_row, shard_rows * lax.axis_size("tensor")),
                    full_key,
                )
                + back_product(
                    row_slice(grad_value_low, attn_first_row, shard_rows * lax.axis_size("tensor")),
                    full_value,
                )
            ).astype(jnp.bfloat16),
            "tensor",
            scatter_dimension=0,
            tiled=True,
        ).astype(jnp.float32)
        gain_attn_sum += jnp.sum(grad_in * normed_in, axis=0)
        input_grads.append(grad_resid + norm_back(grad_in, normed_in, inverse_in, gain_in))
    row_grads = (
        lax.psum_scatter(
            grad_query_sum.astype(jnp.bfloat16), "dp", scatter_dimension=0, tiled=True
        ).astype(jnp.float32),
        lax.psum_scatter(
            grad_key_sum.astype(jnp.bfloat16), "dp", scatter_dimension=0, tiled=True
        ).astype(jnp.float32),
        lax.psum_scatter(
            grad_value_sum.astype(jnp.bfloat16), "dp", scatter_dimension=0, tiled=True
        ).astype(jnp.float32),
        lax.psum_scatter(
            grad_gate_sum.astype(jnp.bfloat16), "dp", scatter_dimension=0, tiled=True
        ).astype(jnp.float32),
        lax.psum_scatter(
            grad_up_sum.astype(jnp.bfloat16), "dp", scatter_dimension=0, tiled=True
        ).astype(jnp.float32),
        lax.psum_scatter(
            gain_attn_sum.astype(jnp.bfloat16), "dp", scatter_dimension=0, tiled=True
        ).astype(jnp.float32),
        lax.psum_scatter(
            gain_mlp_sum.astype(jnp.bfloat16), "dp", scatter_dimension=0, tiled=True
        ).astype(jnp.float32),
    )
    col_grads = (
        lax.psum_scatter(
            grad_out_sum.astype(jnp.bfloat16), "dp", scatter_dimension=1, tiled=True
        ).astype(jnp.float32),
        lax.psum_scatter(
            grad_down_sum.astype(jnp.bfloat16), "dp", scatter_dimension=1, tiled=True
        ).astype(jnp.float32),
    )
    gain_grads = lax.psum((row_grads[5], row_grads[6]), "tensor")
    return (
        jnp.stack(outputs, 0),
        jnp.stack(input_grads, 0),
        gain_grads[0],
        gain_grads[1],
        row_grads[0],
        row_grads[1],
        row_grads[2],
        col_grads[0],
        row_grads[3],
        row_grads[4],
        col_grads[1],
    )


F32 = jnp.float32
BF16 = jnp.bfloat16
NN = (((1,), (0,)), ((), ()))
NT = (((1,), (1,)), ((), ()))
TN = (((0,), (0,)), ((), ()))
TILE = 256
SPAN = 2
CHUNK = 512
EARLY = 640
AHEAD = 768
JOBS = (((0, 768), (0, 384), (1, 768)), ((1, 768), (2, 768), (2, 384), (2, 384)))
RATE = 0.019
VMEM_BYTES = 62 << 20
MESH = pl.DeviceIdType.MESH


def mm(left, right, dims=NN):
    return lax.dot_general(left, right, dims, preferred_element_type=F32)


def params(number=None):
    if number is None:
        return pltpu.CompilerParams(vmem_limit_bytes=VMEM_BYTES)
    return pltpu.CompilerParams(vmem_limit_bytes=VMEM_BYTES, collective_id=number, has_side_effects=True)


def anywhere():
    return pl.BlockSpec(memory_space=pl.ANY)


def once(shape):
    return pl.BlockSpec(shape, lambda *_: (0,) * len(shape), pipeline_mode=pl.Buffered(1))


def far_count():
    return lax.axis_size("dp") // 4


def dp_peer(bits):
    return {"dp": lax.axis_index("dp") ^ bits}


def sibling():
    return {"tensor": 1 - lax.axis_index("tensor")}


def dp_peers():
    return [dp_peer(1), dp_peer(2)] + [dp_peer(4 * k) for k in range(1, far_count())]


def greet(peers):
    barrier = pltpu.get_barrier_semaphore()
    for peer in peers:
        pl.semaphore_signal(barrier, inc=1, device_id=peer, device_id_type=MESH)
    pl.semaphore_wait(barrier, len(peers))


def remote(source, target, send, recv, peer):
    return pltpu.make_async_remote_copy(
        src_ref=source, dst_ref=target, send_sem=send, recv_sem=recv, device_id=peer, device_id_type=MESH
    )


def gather_sems():
    count = 7 * far_count() - 1
    return [pltpu.SemaphoreType.DMA((count,)), pltpu.SemaphoreType.DMA((count,)), pltpu.SemaphoreType.DMA]


class Gather:

    def __init__(self, source, whole, send, recv, local=None, near=None):
        self.source, self.whole, self.send, self.recv, self.local = source, whole, send, recv, local
        self.near = near
        self.me = lax.axis_index("dp")
        self.far = far_count()
        self.each = whole.shape[0] // lax.axis_size("dp")
        self.half = self.each // 2

    def block(self, bits):
        start = pl.multiple_of((self.me ^ bits) * self.each, self.each)
        return self.whole.at[pl.ds(start, self.each)]

    def piece(self, bits, part):
        start = pl.multiple_of((self.me ^ bits) * self.each + part * self.half, self.half)
        return self.whole.at[pl.ds(start, self.half)]


    def along(self, k):
        return k - 1, self.source, self.block(0), 4 * k, self.block(4 * k)

    def first(self, k, part, bit):
        index = self.far - 1 + 4 * k + 2 * part + bit - 1
        if self.near is not None:
            source = near_block(self.near, k, part * self.half, self.half)
        elif k == 0:
            source = self.source.at[pl.ds(part * self.half, self.half)]
        else:
            source = self.piece(4 * k, part)
        return index, source, self.piece(4 * k, part), bit, self.piece(4 * k + bit, part)

    def second(self, k, part):
        index = 5 * self.far - 1 + 2 * k + part
        source = self.piece(4 * k + 2 - part, part)
        return index, source, source, 1 + part, self.piece(4 * k + 3, part)

    def outgoing(self, transfer):
        index, source, target, bits, _ = transfer
        return remote(source, target, self.send.at[index], self.recv.at[index], dp_peer(bits))

    def start(self, transfer):
        self.outgoing(transfer).start()

    def sent(self, transfer):
        self.outgoing(transfer).wait_send()

    def arrived(self, transfer):
        index, _, _, bits, landing = transfer
        remote(landing, landing, self.send.at[index], self.recv.at[index], dp_peer(bits)).wait_recv()

    def kept(self):
        if self.near is None:
            return [pltpu.make_async_copy(self.source, self.block(0), self.local)]
        sems = [self.local] + [self.recv.at[k - 1] for k in range(1, self.far)]
        return [
            pltpu.make_async_copy(near_block(self.near, k, 0, self.each), self.block(4 * k), sems[k])
            for k in range(self.far)
        ]

    def pass_on(self, k):
        for part, bit in ((0, 2), (1, 1), (0, 1), (1, 2)):
            self.start(self.first(k, part, bit))

    def begin_far(self):
        if self.local is not None:
            for copy in self.kept():
                copy.start()
        if self.near is None:
            for k in range(1, self.far):
                self.start(self.along(k))

    def begin(self):
        self.begin_far()
        self.pass_on(0)

    def spread(self, k):
        if self.near is None:
            self.arrived(self.along(k))
        self.pass_on(k)

    def turn(self, k):
        self.arrived(self.first(k, 0, 2))
        self.start(self.second(k, 0))
        self.arrived(self.first(k, 1, 1))
        self.start(self.second(k, 1))

    def finish(self):
        for k in range(self.far):
            self.arrived(self.first(k, 0, 1))
            self.arrived(self.first(k, 1, 2))
            for part in range(2):
                self.arrived(self.second(k, part))
        if self.near is None:
            for k in range(1, self.far):
                self.sent(self.along(k))
        for k in range(self.far):
            for part in range(2):
                for bit in (1, 2):
                    self.sent(self.first(k, part, bit))
                self.sent(self.second(k, part))
        if self.local is not None:
            for copy in self.kept():
                copy.wait()

    def plan(self, start):
        along = RATE * self.whole.shape[1]
        far = 2 * along / 3
        events = [(start, self.begin)]
        for k in range(1, self.far):
            at = start + 1.0 + far * (0.4 + 0.6 * k / (self.far - 1))
            events.append((at, functools.partial(self.spread, k)))
        for k in range(self.far):
            at = start + 2.0 + far * (0.4 + 0.6 * k / (self.far - 1)) + along / 4
            events.append((at, functools.partial(self.turn, k)))
        return events


    def plan_near(self, far_start, start):
        along = RATE * self.whole.shape[1]
        events = [(far_start, self.begin_far)]
        events += [(start, functools.partial(self.pass_on, 0))]
        events += [(start + 0.001 * k, functools.partial(self.spread, k)) for k in range(1, self.far)]
        for k in range(self.far):
            events.append((start + 2.0 + along * (k + 1) / 6, functools.partial(self.turn, k)))
        return events


def near_block(near, k, first, rows):
    each = near.shape[0] // far_count()
    start = (lax.div(lax.axis_index("dp"), 4) ^ k) * each + first
    return near.at[pl.ds(pl.multiple_of(start, rows), rows)]


class NearGather:

    def __init__(self, source, near, send, recv, local):
        self.source, self.near, self.send, self.recv, self.local = source, near, send, recv, local
        self.each = source.shape[0]

    def copies(self):
        mine = near_block(self.near, 0, 0, self.each)
        made = [pltpu.make_async_copy(self.source, mine, self.local)]
        for k in range(1, far_count()):
            made.append(remote(self.source, mine, self.send.at[k - 1], self.recv.at[k - 1], dp_peer(4 * k)))
        return made

    def begin(self):
        for copy in self.copies():
            copy.start()

    def finish(self):
        for k in range(1, far_count()):
            landing = near_block(self.near, k, 0, self.each)
            remote(landing, landing, self.send.at[k - 1], self.recv.at[k - 1], dp_peer(4 * k)).wait_recv()
        for copy in self.copies()[1:]:
            copy.wait_send()
        self.copies()[0].wait()


class Plan:

    def __init__(self, step, steps, places, step_us, clock=None):
        self.step, self.steps, self.places = step, steps, places
        self.clock = clock or [at * step_us / places for at in range(steps * places)]
        self.events = {}
        self.tail = []
        self.ends = []

    def add(self, events, end, latest=None, earliest=0):
        for at, (time, action) in enumerate(events):
            index = sum(tick < time for tick in self.clock) if at else sum(tick <= time for tick in self.clock) - 1
            index = max(index, earliest)
            if latest is not None:
                index = min(index, latest)
            if index < self.steps * self.places:
                self.events.setdefault(divmod(index, self.places), []).append((time, action))
            else:
                self.tail.append((time, action))
        self.ends.append(end)

    def put(self, step, time, action):
        self.events.setdefault((step, 0), []).append((time, action))

    def at(self, place):
        for key in sorted(self.events):
            if key[1] == place:

                @pl.when(self.step == key[0])
                def _(actions=sorted(self.events[key], key=lambda event: event[0])):
                    for _, action in actions:
                        action()

    def finish(self):
        for _, action in sorted(self.tail, key=lambda event: event[0]):
            action()
        for end in self.ends:
            end()


def add_gathers(plan, jobs, refs, start=0.0):
    for at, (source, whole, first, target, width) in enumerate(jobs):
        gather = Gather(
            source.at[:, pl.ds(first, width)], whole.at[:, pl.ds(target, width)], *refs[3 * at : 3 * at + 3]
        )
        plan.add(gather.plan(start), gather.finish)
        start += RATE * width


def pieces_of(width, most):
    return [(at, min(most, width - at)) for at in range(0, width, most)]


def scatter_scratch(columns, dim):
    far = far_count()
    half = dim // lax.axis_size("dp") // 2
    part = pltpu.VMEM((far, half, columns), BF16)
    return [part] * 8 + [
        pltpu.VMEM((far, 2, half, columns), BF16),
        pltpu.VMEM((far - 1, 2, half, columns), BF16),
        pltpu.SemaphoreType.DMA((5 + far,)),
        pltpu.SemaphoreType.DMA((5 + far,)),
        pltpu.SemaphoreType.DMA((3,)),
    ]


SCATTER_REFS = 13


class Scatter:
    def __init__(self, grads, first, out, refs):
        (
            self.mine_y, self.mine_x, self.got_dy, self.got_dx, self.got_x, self.got_y, self.got_y2, self.got_x2,
            self.mine, self.got_far, self.send, self.recv, self.local,
        ) = refs
        self.grads, self.out = grads, out
        self.columns = pl.ds(first, self.mine.shape[3])
        me = lax.axis_index("dp")
        self.far = far_count()
        self.low, self.high = lax.rem(me, 4), lax.div(me, 4)

    def copy(self, index, source, target, bits):
        return remote(source, target, self.send.at[index], self.recv.at[index], dp_peer(bits))

    def share(self, bits, part):
        return self.grads.at[:, self.low ^ bits, part, :, self.columns]

    def from_grads(self):
        return [
            self.copy(0, self.share(3, 0), self.got_dy, 1),
            self.copy(1, self.share(3, 1), self.got_dx, 2),
            self.copy(2, self.share(1, 0), self.got_x, 1),
            self.copy(3, self.share(2, 1), self.got_y, 2),
        ]

    def added(self):
        return [self.copy(4, self.mine_y, self.got_y2, 2), self.copy(5, self.mine_x, self.got_x2, 1)]

    def along(self):
        return [
            self.copy(5 + k, self.mine.at[self.high ^ k], self.got_far.at[k - 1], 4 * k) for k in range(1, self.far)
        ]

    def loads(self):
        own = self.grads.at[:, self.low, :, :, self.columns]
        return [
            pltpu.make_async_copy(self.share(2, 0), self.mine_y, self.local.at[0]),
            pltpu.make_async_copy(self.share(1, 1), self.mine_x, self.local.at[1]),
            pltpu.make_async_copy(own, self.mine, self.local.at[2]),
        ]

    def begin(self):
        for copy in self.from_grads() + self.loads():
            copy.start()

    def second(self):
        loads, got, added = self.loads(), self.from_grads(), self.added()
        loads[0].wait()
        got[0].wait_recv()
        self.mine_y[...] = add(self.mine_y[...], self.got_dy[...]).astype(BF16)
        added[0].start()
        loads[1].wait()
        got[1].wait_recv()
        self.mine_x[...] = add(self.mine_x[...], self.got_dx[...]).astype(BF16)
        added[1].start()

    def third(self):
        got, added = self.from_grads(), self.added()
        self.loads()[2].wait()
        got[2].wait_recv()
        added[0].wait_recv()
        self.mine[:, 0] = add(self.mine[:, 0], self.got_x[...], self.got_y2[...]).astype(BF16)
        got[3].wait_recv()
        added[1].wait_recv()
        self.mine[:, 1] = add(self.mine[:, 1], self.got_y[...], self.got_x2[...]).astype(BF16)
        for copy in self.along():
            copy.start()

    def finish(self):
        for copy in self.along():
            copy.wait_recv()
        self.out[...] = add(self.mine[self.high], *[self.got_far[k] for k in range(self.far - 1)])
        for copy in self.from_grads() + self.added() + self.along():
            copy.wait_send()


    def plan(self, start):
        along = RATE * self.mine.shape[3]
        times = (start, start + 1.5 + 2 * along / 3, start + 3 + along)
        return list(zip(times, (self.begin, self.second, self.third)))


def scatters_scratch(jobs, dim):
    scratch = []
    for _, width in jobs:
        scratch += scatter_scratch(width, dim)
    return scratch


def scatter_outs(jobs, dim):
    half = dim // lax.axis_size("dp") // 2
    shapes = [jax.ShapeDtypeStruct((2, half, width), F32) for _, width in jobs]
    return shapes, [once(shape.shape) for shape in shapes]


def add_scatters(plan, jobs, sources, outs, refs, start=0.0):
    for at, (first, width) in enumerate(jobs):
        scatter = Scatter(sources[at], first, outs[at], refs[SCATTER_REFS * at : SCATTER_REFS * (at + 1)])
        plan.add(scatter.plan(start), scatter.finish)
        start += RATE * width


def grad_shape(dim, columns):
    return jax.ShapeDtypeStruct((far_count(), 4, 2, dim // lax.axis_size("dp") // 2, columns), BF16)


def add(*terms):
    total = terms[0].astype(F32)
    for term in terms[1:]:
        total = total + term.astype(F32)
    return total


def call(kernel, name, number, steps, in_specs, out_specs, out_shape, scratch, operands):
    return pl.pallas_call(
        kernel,
        grid=steps if isinstance(steps, tuple) else (steps,),
        in_specs=in_specs,
        out_specs=out_specs,
        out_shape=out_shape,
        scratch_shapes=scratch,
        compiler_params=params(number),
        name=name,
    )(*operands)


def spread_gains(slab, column):
    dim = slab.shape[0]
    blocks = lax.axis_size("dp")
    each = dim // blocks
    lane_block = lax.broadcasted_iota(jnp.int32, (blocks, dim), 1) // each
    block = lax.broadcasted_iota(jnp.int32, (blocks, dim), 0)
    rows = []
    for which in range(2):
        picked = jnp.concatenate(
            [slab[each * b : each * b + 16, column : column + 128].astype(F32)[which : which + 1] for b in range(blocks)], 0
        )
        tiled = jnp.concatenate([picked] * (dim // 128), 1)
        rows.append(jnp.sum(jnp.where(lane_block == block, tiled, 0.0), axis=0, keepdims=True))
    return jnp.concatenate(rows + [jnp.zeros((6, dim), F32)], 0)


def part_block(width, per, rows, lag=0, last=None):
    def place(i):
        i = i - lag if last is None else jnp.clip(i - lag, 0, last)
        return lax.div(i, per), lax.rem(i, per), 0

    return pl.BlockSpec((1, rows, width), place)


def core_block(width, per, rows, other, last=None):
    def place(i):
        if last is not None:
            i = jnp.minimum(i, last)
        core = lax.axis_index("tensor")
        return lax.div(i, per), (1 - core if other else core) * per + lax.rem(i, per), 0

    return pl.BlockSpec((1, rows, width), place)


def root_mean(values):
    return lax.rsqrt(jnp.mean(values * values, axis=-1, keepdims=True) + 1e-05)


def norm_slope(values, scaled):
    inverse = root_mean(values)
    normed = values * inverse
    return inverse * (scaled - normed * jnp.mean(scaled * normed, axis=-1, keepdims=True))


def half_sems(count):
    return [pltpu.SemaphoreType.DMA((count,)), pltpu.SemaphoreType.DMA((count,))]


def chunk_slices(width):
    return [(at, min(256, width - at)) for at in range(0, width, 256)]


def build_slabs(edges, gate, up, down_t, out_t, slabs):
    at = out_t.shape[1]
    slabs[:, :at] = out_t[...]
    units = gate.shape[1]

    def place(ref, low, high):
        nonlocal at
        end = min(high, units)
        slabs[:, at : at + end - low] = ref[:, low:end]
        if end < high:
            slabs[:, at + end - low : at + high - low] = jnp.zeros((slabs.shape[0], high - end), BF16)
        at += high - low

    for low, high in edges:
        for start, width in chunk_slices(high - low):
            place(gate, low + start, low + start + width)
            place(up, low + start, low + start + width)
        place(down_t, low, high)


def project_kernel(
    edges, inputs, w_query, w_key, w_value, gain_attn, gain_mlp, gate, up, down_t, out_t,
    h_out, qkv_out, gain_out, whole_in, slabs, x_own, x_other, h_all, qkv_all, slab, gain_slab,
    local, swap_send, swap_recv, *sems,
):
    micro, rows, _ = x_own.shape
    each = w_query.shape[0]
    core = lax.axis_index("tensor")
    parts = 2 * micro

    def load(m):
        return pltpu.make_async_copy(inputs.at[m], x_own.at[m], local.at[m])

    def swap(m):
        return remote(inputs.at[m], x_other.at[m], swap_send.at[m], swap_recv.at[m], sibling())

    def place(t):
        first = pl.multiple_of((core if t < micro else 1 - core) * rows, rows)
        return t % micro, pl.ds(first, rows)

    def store_h(t):
        return pltpu.make_async_copy(h_all.at[t], h_out.at[place(t)], local.at[micro + t])

    def store_qkv(t):
        return pltpu.make_async_copy(qkv_all.at[t], qkv_out.at[place(t)], local.at[micro + parts + t])

    def keep():
        return pltpu.make_async_copy(slab, whole_in, local.at[micro + 2 * parts])

    def norm(t):
        x = (x_own if t < micro else x_other)[t % micro].astype(F32)
        h_all[t] = (x * root_mean(x) * gain_out[0:1]).astype(BF16)
        store_h(t).start()

    for m in range(micro):
        load(m).start()
    mine = pl.ds(pl.multiple_of(lax.axis_index("dp") * each, each), each)
    at = 0
    for ref in (w_query, w_key, w_value):
        slab[mine, at : at + ref.shape[1]] = ref[...]
        at += ref.shape[1]
    both = jnp.concatenate([gain_attn[...], gain_mlp[...]], 0).astype(F32)
    both = jnp.concatenate([both, both], 1)
    gain_slab[mine] = jnp.concatenate([both, jnp.zeros((each - 2, both.shape[1]), F32)], 0).astype(BF16)
    greet(dp_peers() + [sibling()])
    gains = Gather(gain_slab.at[mine], gain_slab, *sems[:2])
    weights = Gather(slab.at[mine], slab, *sems[2:])
    gains.begin()
    weights.begin()
    for m in range(micro):
        swap(m).start()
    build_slabs(edges, gate, up, down_t, out_t, slabs)
    for k in range(1, gains.far):
        gains.spread(k)
    for k in range(gains.far):
        gains.turn(k)
    gains.finish()
    gain_out[...] = spread_gains(gain_slab, 0)
    duties = [functools.partial(weights.spread, k) for k in range(1, weights.far)]
    duties += [functools.partial(weights.turn, k) for k in range(weights.far)]
    for t in range(parts):
        if t < micro:
            load(t).wait()
        else:
            swap(t - micro).wait()
        norm(t)
        if duties:
            duties.pop(0)()
    for duty in duties:
        duty()
    weights.finish()
    keep().start()
    for t in range(parts):
        qkv_all[t] = mm(h_all[t], slab[...]).astype(BF16)
        store_qkv(t).start()
    for t in range(parts):
        store_h(t).wait()
        store_qkv(t).wait()
    keep().wait()


def project(edges, inputs, w_query, w_key, w_value, gain_attn, gain_mlp, w_gate, w_up, down_t, out_t):
    micro, rows, dim = inputs.shape
    each = w_query.shape[0]
    columns = w_query.shape[1] + w_key.shape[1] + w_value.shape[1]
    all_columns = out_t.shape[1] + 3 * edges[-1][1]
    locals_ = (w_query, w_key, w_value, gain_attn, gain_mlp, w_gate, w_up, down_t, out_t)
    return call(
        functools.partial(project_kernel, edges),
        "project",
        1,
        1,
        [anywhere()] + [once(a.shape) for a in locals_],
        [anywhere(), anywhere(), once((8, dim)), anywhere(), once((each, all_columns))],
        [
            jax.ShapeDtypeStruct((micro, 2 * rows, dim), BF16),
            jax.ShapeDtypeStruct((micro, 2 * rows, columns), BF16),
            jax.ShapeDtypeStruct((8, dim), F32),
            jax.ShapeDtypeStruct((dim, columns), BF16),
            jax.ShapeDtypeStruct((each, all_columns), BF16),
        ],
        [
            pltpu.VMEM((micro, rows, dim), BF16),
            pltpu.VMEM((micro, rows, dim), BF16),
            pltpu.VMEM((2 * micro, rows, dim), BF16),
            pltpu.VMEM((2 * micro, rows, columns), BF16),
            pltpu.VMEM((dim, columns), BF16),
            pltpu.VMEM((dim, 128), BF16),
            pltpu.SemaphoreType.DMA((5 * micro + 1,)),
        ]
        + half_sems(micro)
        + gather_sems()[:2]
        + gather_sems()[:2],
        (inputs, *locals_),
    )


def fill_mask(mask, lengths, micro_step):
    tiles = mask.shape[0]
    row = lax.broadcasted_iota(jnp.int32, (tiles * TILE, TILE), 0)
    start = jnp.zeros_like(row)
    end = 0
    for d in range(lengths.shape[1]):
        end = end + lengths[micro_step, d]
        start = jnp.where(row >= end, end, start)
    lane = lax.broadcasted_iota(jnp.int32, (tiles * TILE, TILE), 1)
    for j in range(tiles):
        i = min(tiles, j + SPAN + 1)
        tall = (i - j) * TILE
        below = slice(j * TILE, i * TILE)
        column = lane[:tall] + j * TILE
        allowed = (column <= row[below]) & (column >= start[below])
        mask[j, :tall, :] = jnp.where(allowed, 1.0, 0.0)


def add_rows(total, j, tiles, value):
    end = min(tiles, j + SPAN + 1)
    begun = min(tiles, j + SPAN) if j else 0
    if begun > j:
        total[j * TILE : begun * TILE] += value[: (begun - j) * TILE]
    if end > max(begun, j):
        start = max(begun, j)
        total[start * TILE : end * TILE] = value[(start - j) * TILE :]


def attend_kernel(
    jobs, near_job, lengths, qkv, grad_own, slabs, mix_ref, inv_ref, grad_other, unit, near,
    mask, queries, values, total, *sems,
):
    m = pl.program_id(0)
    group = qkv.shape[1]
    tiles = group // TILE
    pairs = mix_ref.shape[2] // 128
    lane = lax.broadcasted_iota(jnp.int32, (group, 128), 1)
    zero = jnp.zeros((), BF16)

    def swap():
        return remote(grad_own, grad_other, sems[0], sems[1], sibling())

    plan = Plan(m, lengths.shape[0], pairs, 9.5)
    plan.add([(0.0, lambda: swap().start())], lambda: swap().wait())
    add_gathers(plan, [(slabs, unit, *job) for job in jobs], sems[5:])
    ahead = NearGather(slabs.at[:, pl.ds(*near_job)], near, *sems[2:5])
    plan.add([(12.0, ahead.begin)], ahead.finish)

    @pl.when(m == 0)
    def _():
        greet(dp_peers() + [sibling()])

    fill_mask(mask, lengths, m)
    query = qkv[0, :, :128] * jnp.asarray(0.25, BF16)
    for pair in range(pairs):
        at = 256 + 128 * pair
        now = pair % 2
        for side in range(2):
            mine = lane // VD == side
            queries[now, side] = jnp.where(lane // FEAT == 2 * pair + side, query, zero)
            values[now, side, :, :128] = jnp.where(mine, qkv[0, :, at : at + 128], zero)
            values[now, side, :, 128:] = mine.astype(F32).astype(BF16)
        for j in range(tiles):
            if j == 0:
                plan.at(pair)
            i = min(tiles, j + SPAN + 1)
            tall = (i - j) * TILE
            here, below = slice(j * TILE, (j + 1) * TILE), slice(j * TILE, i * TILE)
            scores = mm(queries[now, :, below].reshape(2 * tall, 128), qkv[0, here, 128:256], NT)
            allowed = mask[j, :tall]
            weights = []
            for side in range(2):
                t = scores[side * tall : (side + 1) * tall] + 1.0
                weights.append(((t * t + 1.0) * allowed).astype(BF16))
            part = mm(jnp.concatenate(weights, 1), values[now, :, here].reshape(2 * TILE, 256))
            add_rows(total.at[now], j, tiles, part)
        inverse = 1.0 / total[now, :, 128:]
        mix_ref[0, :, 128 * pair : 128 * (pair + 1)] = (total[now, :, :128] * inverse).astype(BF16)
        turned = inverse.T
        inv_ref[0, pair, 0:1] = turned[0:1]
        inv_ref[0, pair, 1:2] = turned[VD : VD + 1]

    @pl.when(m == pl.num_programs(0) - 1)
    def _():
        plan.finish()


def whole_group(width, group):
    return pl.BlockSpec((1, group, width), lambda m: (m, 0, 0))


def lengths_spec(lengths):
    return pl.BlockSpec(lengths.shape, lambda *_: (0, 0), memory_space=pltpu.SMEM)


def attend_all(qkv, lengths, out_grad, slabs, jobs, near_job):
    micro, group, columns = qkv.shape
    dim = out_grad.shape[2]
    wide = columns - 256
    dma = pltpu.SemaphoreType.DMA
    unit = sum(job[2] for job in jobs)
    return call(
        functools.partial(attend_kernel, jobs, near_job),
        "attend",
        2,
        micro,
        [lengths_spec(lengths), whole_group(columns, group), anywhere(), anywhere()],
        [
            whole_group(wide, group),
            pl.BlockSpec((1, wide // 128, 8, group), lambda m: (m, 0, 0, 0)),
            anywhere(),
            anywhere(),
            anywhere(),
        ],
        [
            jax.ShapeDtypeStruct((micro, group, wide), BF16),
            jax.ShapeDtypeStruct((micro, wide // 128, 8, group), F32),
            jax.ShapeDtypeStruct(out_grad.shape, BF16),
            jax.ShapeDtypeStruct((dim, unit), BF16),
            jax.ShapeDtypeStruct((dim // 4, near_job[1]), BF16),
        ],
        [
            pltpu.VMEM((group // TILE, TILE * (SPAN + 1), TILE), F32),
            pltpu.VMEM((2, 2, group, 128), BF16),
            pltpu.VMEM((2, 2, group, 256), BF16),
            pltpu.VMEM((2, group, 256), F32),
            dma,
            dma,
        ]
        + half_sems(far_count() - 1)
        + [dma]
        + gather_sems() * len(jobs),
        (lengths, qkv, out_grad, slabs),
    )


def attend_back_kernel(jobs, lengths, qkv, mix_ref, inv_ref, d_own, d_other, weights, *refs):
    sources, refs = refs[: len(jobs)], refs[len(jobs) :]
    (dqkv, grads), refs = refs[:2], refs[2:]
    outs, refs = refs[: len(jobs)], refs[len(jobs) :]
    (mask, queries, queries_t, keys, douts, douts_t, deltas, dv_t, dk_t, dq), refs = refs[:10], refs[10:]
    (d, dmix, grad_total, rounded, out_sem), refs = refs[:5], refs[5:]
    m = pl.program_id(0)
    group = qkv.shape[1]
    tiles = group // TILE
    pairs = mix_ref.shape[2] // 128
    lane = lax.broadcasted_iota(jnp.int32, (group, 128), 1)
    zero = jnp.zeros((), BF16)
    plan = Plan(m, lengths.shape[0], 2 * pairs, 18.0)
    add_scatters(plan, jobs, sources, outs, refs)

    @pl.when(m == 0)
    def _():
        greet(dp_peers())
        grad_total[...] = jnp.zeros_like(grad_total)

    plan.at(0)
    rows = d_own.shape[1]
    core = lax.axis_index("tensor")
    d[pl.ds(pl.multiple_of(core * rows, rows), rows)] = d_own[0]
    d[pl.ds(pl.multiple_of((1 - core) * rows, rows), rows)] = d_other[0]
    dmix[...] = mm(d[...], weights[...]).astype(BF16)
    grad_total[...] += mm(d[...], mix_ref[0], TN)
    fill_mask(mask, lengths, m)
    queries_t[...] = (qkv[0, :, :128].astype(F32) * 0.5).T.astype(BF16)
    query = qkv[0, :, :128] * jnp.asarray(0.25, BF16)
    key = qkv[0, :, 128:256] * jnp.asarray(0.5, BF16)
    for pair in range(pairs):
        now = pair % 2
        lanes = slice(128 * pair, 128 * (pair + 1))
        value = slice(256 + 128 * pair, 384 + 128 * pair)
        inverse = jnp.concatenate(
            [jnp.broadcast_to(inv_ref[0, pair, s : s + 1, :], (VD, group)) for s in range(2)], 0
        ).T
        dout_low = (dmix[:, lanes].astype(F32) * inverse).astype(BF16)
        dout = dout_low.astype(F32)
        douts_t[now] = dout.T.astype(BF16)
        product = dout * mix_ref[0, :, lanes].astype(F32)
        for side in range(2):
            mine = lane // VD == side
            head = lane // FEAT == 2 * pair + side
            queries[now, side] = jnp.where(head, query, zero)
            keys[now, side] = jnp.where(head, key, zero)
            douts[now, side] = jnp.where(mine, dout_low, zero)
            delta = jnp.sum(jnp.where(mine, product, 0.0), axis=1, keepdims=True)
            deltas[now, side] = jnp.broadcast_to(delta, (group, 128))
        for j in range(tiles):
            if j % 2 == 0 and pair + j:
                plan.at(2 * pair + j // 2)
            i = min(tiles, j + SPAN + 1)
            tall = (i - j) * TILE
            here, below = slice(j * TILE, (j + 1) * TILE), slice(j * TILE, i * TILE)
            scores = mm(queries[now, :, below].reshape(2 * tall, 128), qkv[0, here, 128:256], NT)
            slopes = mm(douts[now, :, below].reshape(2 * tall, 128), qkv[0, here, value], NT)
            allowed = mask[j, :tall]
            d_scores = []
            for side in range(2):
                t = scores[side * tall : (side + 1) * tall] + 1.0
                masked = t * allowed
                delta = jnp.concatenate([deltas[now, side, below]] * (TILE // 128), 1)
                d_score = ((slopes[side * tall : (side + 1) * tall] - delta) * masked).astype(BF16)
                weights = (t * masked + allowed).astype(BF16)
                mine = slice(VD * side, VD * (side + 1))
                head = slice((2 * pair + side) * FEAT, (2 * pair + side + 1) * FEAT)
                dv_t[now, mine, here] = mm(douts_t[now, mine, below], weights)
                dk_t[head, here] = mm(queries_t[head, below], d_score)
                d_scores.append(d_score)
            part = mm(jnp.concatenate(d_scores, 1), keys[now, :, here].reshape(2 * TILE, 128))
            if pair:
                dq[below] += part
            else:
                add_rows(dq, j, tiles, part)
        dqkv[0, :, value] = dv_t[now].T.astype(BF16)
    dqkv[0, :, 128:256] = dk_t[...].T.astype(BF16)
    dqkv[0, :, :128] = dq[...].astype(BF16)

    @pl.when(m == pl.num_programs(0) - 1)
    def _():
        rounded[...] = grad_total[...].astype(BF16).reshape(rounded.shape)
        write = pltpu.make_async_copy(rounded, grads, out_sem)
        write.start()
        plan.finish()
        write.wait()


def attend_back(qkv, mix, inverse, d_own, d_other, weights, lengths, sources, jobs):
    micro, group, columns = qkv.shape
    wide = columns - 256
    rows, dim = d_own.shape[1:]
    shapes, specs = scatter_outs(jobs, dim)
    grads = grad_shape(dim, wide)
    pair_rows = pltpu.VMEM((2, 2, group, 128), BF16)
    return call(
        functools.partial(attend_back_kernel, jobs),
        "attend_back",
        8,
        micro,
        [
            lengths_spec(lengths),
            whole_group(columns, group),
            whole_group(wide, group),
            pl.BlockSpec((1, wide // 128, 8, group), lambda m: (m, 0, 0, 0)),
            whole_group(dim, rows),
            whole_group(dim, rows),
            once((dim, wide)),
        ]
        + [anywhere()] * len(jobs),
        [whole_group(columns, group), anywhere()] + specs,
        [jax.ShapeDtypeStruct((micro, group, columns), BF16), grads] + shapes,
        [
            pltpu.VMEM((group // TILE, TILE * (SPAN + 1), TILE), F32),
            pair_rows,
            pltpu.VMEM((128, group), BF16),
            pair_rows,
            pair_rows,
            pltpu.VMEM((2, 128, group), BF16),
            pltpu.VMEM((2, 2, group, 128), F32),
            pltpu.VMEM((2, 128, group), F32),
            pltpu.VMEM((128, group), F32),
            pltpu.VMEM((group, 128), F32),
            pltpu.VMEM((group, dim), BF16),
            pltpu.VMEM((group, wide), BF16),
            pltpu.VMEM((dim, wide), F32),
            pltpu.VMEM(grads.shape, BF16),
            pltpu.SemaphoreType.DMA,
        ]
        + scatters_scratch(jobs, dim),
        (lengths, qkv, mix, inverse, d_own, d_other, weights, *sources),
    )


def out_kernel(
    jobs, near_job, mix_own, mix_other, x, weights, gains, slabs, resid_out, h_out, h_other, unit, near,
    parts, sent, got, h_sent, send, recv, *sems,
):
    i = pl.program_id(0)
    count, rows = got.shape[0], got.shape[1]
    per = h_other.shape[1] // rows
    plan = Plan(i, 2 * count, 1, 0.95)
    add_gathers(plan, [(slabs, unit, *job) for job in jobs], sems[3:])
    ahead = NearGather(slabs.at[:, pl.ds(*near_job)], near, *sems[:3])
    plan.add([(2.0, ahead.begin)], ahead.finish)

    def swap(k):
        return remote(sent.at[k], got.at[k], send.at[k], recv.at[k], sibling())

    def swap_h(k):
        place = h_other.at[lax.div(k, per), pl.ds(pl.multiple_of(lax.rem(k, per) * rows, rows), rows)]
        return remote(h_sent.at[k], place, send.at[count + k], recv.at[count + k], sibling())

    @pl.when(i == 0)
    def _():
        greet(dp_peers() + [sibling()])

    plan.at(0)

    @pl.when(i < count)
    def _():
        both = jnp.concatenate([mix_other[0], mix_own[0]], 0)
        part = mm(both, weights[...], NT)
        sent[i] = part[:rows].astype(BF16)
        parts[i] = part[rows:]
        swap(i).start()

    @pl.when(i >= count)
    def _():
        k = i - count
        swap(k).wait_recv()
        resid = x[0].astype(F32) + parts[k] + got[k].astype(F32)
        resid_out[0] = resid.astype(BF16)
        h = (resid * root_mean(resid) * gains[1:2]).astype(BF16)
        h_out[0] = h
        h_sent[k] = h
        swap_h(k).start()

    @pl.when(i == 2 * count - 1)
    def _():
        plan.finish()
        for k in range(count):
            swap(k).wait_send()
            swap_h(k).wait()


def out_project(mix, x, weights, gains, slabs, jobs, near_job, rows=256):
    micro, own_rows, dim = x.shape
    wide = mix.shape[2]
    per = own_rows // rows
    count = micro * per
    late = part_block(dim, per, rows, count, count - 1)
    shape = jax.ShapeDtypeStruct((micro, own_rows, dim), BF16)
    buffer = pltpu.VMEM((count, rows, dim), BF16)
    return call(
        functools.partial(out_kernel, jobs, near_job),
        "out_project",
        3,
        2 * count,
        [
            core_block(wide, per, rows, False, count - 1),
            core_block(wide, per, rows, True, count - 1),
            late,
            once((dim, wide)),
            once((8, dim)),
            anywhere(),
        ],
        [late, late, anywhere(), anywhere(), anywhere()],
        [
            shape,
            shape,
            shape,
            jax.ShapeDtypeStruct((dim, sum(job[2] for job in jobs)), BF16),
            jax.ShapeDtypeStruct((dim // 4, near_job[1]), BF16),
        ],
        [pltpu.VMEM((count, rows, dim), F32), buffer, buffer, buffer]
        + half_sems(2 * count)
        + half_sems(far_count() - 1)
        + [pltpu.SemaphoreType.DMA]
        + gather_sems() * len(jobs),
        (mix, mix, x, weights, gains, slabs),
    )


FEED_US = (5.2, 6.4, 7.2)
GATHER_AT = ((0.0, 0.0), (0.0, 8.0), (0.5, 26.0))
SCATTER_AT = (44.0, 59.0, 71.0, 86.0)
BACK_US = 2.4
OUT_PIECE = 512
IN_PIECE = 384


def feed_kernel(
    steps, widths, loads, cuts, jobs, h_own, h_other, g_own, g_other, unit_0, unit_1, near_a, near_b, slabs,
    resid, g_late, resid_end, g_end, gains, mixed_out, d_out, d_other, *refs,
):
    def take(number):
        nonlocal refs
        taken, refs = refs[:number], refs[number:]
        return taken

    chunks = len(widths)
    grads = take(chunks)
    units = take(chunks - 1)
    outs = take(len(jobs))
    slab_a, slab_b, total, h, g, hidden_s, dgu_s = take(7)
    out_own, out_other, dm_own, dm_other, dm_got, out_got, d_sent, mixed_s = take(8)
    load_sems, write_sems, send, recv, local = take(5)
    i = pl.program_id(0)
    rows = h_own.shape[1]
    per = d_other.shape[1] // rows
    weights = [(slab_a, slab_b)[chunk % 2] for chunk in range(chunks)]

    def place(ref, k):
        return ref.at[lax.div(k, per), pl.ds(pl.multiple_of(lax.rem(k, per) * rows, rows), rows)]

    def swaps(k):
        return [
            remote(dm_other.at[k], dm_got.at[k + 1], send.at[3 * k], recv.at[3 * k], sibling()),
            remote(out_other.at[k], out_got.at[k + 1], send.at[3 * k + 1], recv.at[3 * k + 1], sibling()),
        ]

    def results(k):
        return [
            remote(d_sent.at[k + 1], place(d_other, k), send.at[3 * k + 2], recv.at[3 * k + 2], sibling()),
            pltpu.make_async_copy(d_sent.at[k + 1], place(d_out, k), local.at[2 * k]),
            pltpu.make_async_copy(mixed_s.at[k + 1], place(mixed_out, k), local.at[2 * k + 1]),
        ]

    def finish_part(slot, before, resid, g_late):
        values = resid[0].astype(F32)
        mixed_s[slot] = add(values, out_own[before], out_got[slot]).astype(BF16)
        scaled = add(dm_own[before], dm_got[slot]) * gains[1:2]
        d_sent[slot] = (g_late[0].astype(F32) + norm_slope(values, scaled)).astype(BF16)

    def copies(chunk):
        made = []
        sources = loads if chunk == 0 else [(0, 0, 3 * widths[chunk])]
        for at, (source, target, columns) in enumerate(sources):
            ref = (unit_0, unit_1)[at] if chunk == 0 else units[chunk - 1]
            tall = slab_a.shape[0] // 4
            for part in range(4):
                rows_at = pl.ds(part * tall, tall)
                cut = ref.at[rows_at, pl.ds(source, columns)]
                target_at = weights[chunk].at[rows_at, pl.ds(target, columns)]
                made.append(pltpu.make_async_copy(cut, target_at, load_sems.at[chunk, at, part]))
        return made

    def writes(chunk):
        made = []
        far, low, parts, half, columns = grads[chunk].shape
        for at in range(far * low * parts):
            source = weights[chunk].at[pl.ds(at * half, half), pl.ds(0, columns)]
            target = grads[chunk].at[at // (low * parts), at // parts % low, at % parts]
            made.append(pltpu.make_async_copy(source, target, write_sems.at[chunk, at]))
        return made

    def start_all(made):
        for copy in made:
            copy.start()

    def wait_all(made):
        for copy in made:
            copy.wait()

    clock = []
    for chunk in range(chunks):
        start = clock[-2] + FEED_US[chunk - 1] if clock else 0.0
        clock += [start + FEED_US[chunk] * (step + part) for step in range(steps) for part in (0, 0.65)]
    plan = Plan(i, chunks * steps, 2, None, clock)
    for chunk in range(1, chunks):
        first, width = cuts[chunk - 1]
        whole = units[chunk - 1]
        if chunk == 1:
            part = near_a.shape[1]
            parts = [(0, part, near_a, GATHER_AT[0]), (part, width - part, near_b, GATHER_AT[1])]
        else:
            parts = [(0, width, None, GATHER_AT[2])]
        for at, wide, near, times in parts:
            source = slabs.at[:, pl.ds(first + at, wide)]
            gather = Gather(source, whole.at[:, pl.ds(at, wide)], *take(3), near)
            plan.add(gather.plan_near(*times), lambda: None, 2 * chunk * steps - 2)
            plan.put(chunk * steps - 1, 1000.0, gather.finish)
        plan.put(chunk * steps - 1, 1001.0, lambda chunk=chunk: start_all(copies(chunk)))
    for at, (chunk, (first, width)) in enumerate(jobs):
        scatter = Scatter(grads[chunk], first, outs[at], take(SCATTER_REFS))
        plan.add(scatter.plan(SCATTER_AT[at]), scatter.finish, None, 2 * (chunk + 1) * steps + 2)
    for chunk in range(chunks - 1):
        plan.put((chunk + 1) * steps + 1, -1.0, lambda chunk=chunk: wait_all(writes(chunk)))

    @pl.when(i == 0)
    def _():
        start_all(copies(0))
        zeros = jnp.zeros(dm_got.shape[1:], BF16)
        dm_got[0] = zeros
        out_got[0] = zeros
        greet(dp_peers() + [sibling()])

    plan.at(0)
    half = jnp.asarray(0.5, BF16)
    one = jnp.asarray(1.0, BF16)
    dim = slab_a.shape[0]

    def chunk_step(chunk):
        slab, width, last = weights[chunk], widths[chunk], chunk == chunks - 1
        j = i - chunk * steps

        @pl.when(j == 0)
        def _():
            total[:, : 3 * width] = jnp.zeros((dim, 3 * width), F32)
            wait_all(copies(chunk))

        h[:rows], h[rows:] = h_other[0], h_own[0]
        g[:rows], g[rows:] = g_other[0], g_own[0]
        for at, wide in chunk_slices(width):
            both = slice(2 * at, 2 * (at + wide))
            gate_up = mm(h[...], slab[:, both]).astype(BF16)
            d_hidden = mm(g[...], slab[:, 2 * width + at : 2 * width + at + wide]).astype(BF16)
            gate, up = gate_up[:, :wide], gate_up[:, wide:]
            sigmoid = half * jnp.tanh(half * gate) + half
            silu = gate * sigmoid
            hidden_s[:, at : at + wide] = silu * up
            d_gate = d_hidden * up * (sigmoid + silu * (one - sigmoid))
            dgu_s[:, both] = jnp.concatenate([d_gate, d_hidden * silu], 1)
        for at in range(0, dim, 512):
            cut = slice(at, at + 512)
            out = mm(hidden_s[:, :width], slab[cut, 2 * width : 3 * width], NT)
            dm = mm(dgu_s[:, : 2 * width], slab[cut, : 2 * width], NT)
            for ref, value in ((out_own, out[rows:]), (out_other, out[:rows]), (dm_own, dm[rows:]), (dm_other, dm[:rows])):
                if chunk:
                    value = value + ref[j, :, cut].astype(F32)
                ref[j, :, cut] = value.astype(BF16)
        if last:
            start_all(swaps(j))

            @pl.when(j > 0)
            def _():
                for swap in swaps(j - 1):
                    swap.wait_recv()

            finish_part(j, jnp.maximum(j - 1, 0), resid, g_late)
        plan.at(1)
        total[:, : 2 * width] += mm(h[...], dgu_s[:, : 2 * width], TN)
        total[:, 2 * width : 3 * width] += mm(g[...], hidden_s[:, :width], TN)
        if last:

            @pl.when(j > 0)
            def _():
                start_all(results(j - 1))

        @pl.when(j == steps - 1)
        def _():
            slab[:, : 3 * width] = total[:, : 3 * width].astype(BF16)
            start_all(writes(chunk))
            if last:
                for swap in swaps(steps - 1):
                    swap.wait_recv()
                finish_part(steps, steps - 1, resid_end, g_end)
                start_all(results(steps - 1))
                plan.finish()
                for k in range(steps):
                    for copy in swaps(k):
                        copy.wait_send()
                    wait_all(results(k))
                wait_all(writes(chunk))

    for chunk in range(chunks):

        @pl.when((i >= chunk * steps) & (i < (chunk + 1) * steps))
        def _(chunk=chunk):
            chunk_step(chunk)


def feed(rows_in, unit_0, unit_1, near_a, near_b, loads, widths, slabs, cuts, jobs, resid, gains, rows=256):
    micro, own_rows, dim = rows_in[0].shape
    per = own_rows // rows
    steps = micro * per
    chunks = len(widths)

    def part_at(lag):
        def place(i):
            k = lax.rem(i, steps) if lag == 0 else jnp.clip(i - (chunks - 1) * steps - lag, 0, steps - 1)
            return lax.div(k, per), lax.rem(k, per), 0

        return pl.BlockSpec((1, rows, dim), place)

    part, late = part_at(0), part_at(1)
    end = pl.BlockSpec((1, rows, dim), lambda i: (micro - 1, per - 1, 0), pipeline_mode=pl.Buffered(1))
    shape = jax.ShapeDtypeStruct((micro, own_rows, dim), BF16)
    grads = [grad_shape(dim, 3 * width) for width in widths]
    units = [jax.ShapeDtypeStruct((dim, width), BF16) for _, width in cuts]
    shapes, specs = scatter_outs([job for _, job in jobs], dim)
    most = max(widths)
    slots, late_slots = pltpu.VMEM((steps, rows, dim), BF16), pltpu.VMEM((steps + 1, rows, dim), BF16)
    blocks = grads[0].shape[0] * grads[0].shape[1] * grads[0].shape[2]
    results = call(
        functools.partial(feed_kernel, steps, widths, loads, cuts, jobs),
        "feed",
        4,
        chunks * steps,
        [part] * 4 + [anywhere()] * 5 + [late, late, end, end, once((8, dim))],
        [anywhere()] * (3 + chunks + chunks - 1) + specs,
        [shape] * 3 + grads + units + shapes,
        [pltpu.VMEM((dim, 3 * most), BF16)] * 2
        + [
            pltpu.VMEM((dim, 3 * most), F32),
            pltpu.VMEM((2 * rows, dim), BF16),
            pltpu.VMEM((2 * rows, dim), BF16),
            pltpu.VMEM((2 * rows, most), BF16),
            pltpu.VMEM((2 * rows, 2 * most), BF16),
        ]
        + [slots] * 4
        + [late_slots] * 4
        + [pltpu.SemaphoreType.DMA((chunks, 2, 4)), pltpu.SemaphoreType.DMA((chunks, blocks))]
        + half_sems(3 * steps)
        + [pltpu.SemaphoreType.DMA((2 * steps,))]
        + gather_sems() * chunks
        + scatters_scratch([job for _, job in jobs], dim),
        (*rows_in, unit_0, unit_1, near_a, near_b, slabs, resid, rows_in[2], resid, rows_in[2], gains),
    )
    return results[:3], results[3 : 3 + chunks], results[2 + 2 * chunks :]


def back_in_kernel(
    micro, feed_jobs, out_jobs, in_jobs, h, dqkv_all, dqkv, x, d_own, weights, gains, grads_last,
    w_query, w_key, w_value, slabs, *refs,
):
    jobs = out_jobs + in_jobs
    feed_count = sum(len(chunk) for chunk in feed_jobs)
    feed_grads, refs = refs[:feed_count], refs[feed_count:]
    (input_grad, gain_sums, grads), refs = refs[:3], refs[3:]
    outs, refs = refs[: len(jobs)], refs[len(jobs) :]
    (total, sent, got, send, recv, out_sem, rounded, sums, sums_got, sums_sems), refs = refs[:10], refs[10:]
    i = pl.program_id(0)
    m = lax.rem(i, micro)
    plan = Plan(i, 3 * micro, 1, BACK_US)
    split = SCATTER_REFS * len(out_jobs)
    add_scatters(plan, out_jobs, [grads_last] * len(out_jobs), outs, refs[:split])
    outs = outs[len(out_jobs) :]
    add_scatters(plan, in_jobs, [grads] * len(in_jobs), outs, refs[split:], BACK_US * micro)

    def swap(k):
        return remote(sent.at[k], got.at[k], send.at[k], recv.at[k], sibling())

    def swap_sums():
        return remote(sums, sums_got, sums_sems.at[0], sums_sems.at[1], sibling())

    @pl.when(i == 0)
    def _():
        greet(dp_peers() + [sibling()])
        total[...] = jnp.zeros_like(total)

    @pl.when(i < micro)
    def _():
        total[...] += mm(h[0], dqkv_all[0], TN)

    @pl.when(i == micro - 1)
    def _():
        rounded[...] = total[...].astype(BF16).reshape(rounded.shape)
        write = pltpu.make_async_copy(rounded, grads, out_sem)
        write.start()
        write.wait()

    plan.at(0)

    @pl.when(i >= micro)
    def _():
        part = mm(dqkv[0], weights[...], NT)

        @pl.when(i < 2 * micro)
        def _():
            sent[m] = part.astype(BF16)
            swap(m).start()

        @pl.when(i >= 2 * micro)
        def _():
            swap(m).wait_recv()
            scaled = (part + got[m].astype(F32)) * gains[0:1]
            input_grad[0] = (d_own[0].astype(F32) + norm_slope(x[0].astype(F32), scaled)).astype(BF16)

    @pl.when(i == 3 * micro - 1)
    def _():
        each = slabs.shape[0]
        sizes = [sum(wide for _, wide in chunk) for chunk in feed_jobs]
        at = slabs.shape[1] - sum(sizes)
        index = 0
        mid = jnp.zeros((each, 128), F32)
        for size, chunk in zip(sizes, feed_jobs):
            for first, wide in chunk:
                value = feed_grads[index][...].reshape(each, wide)
                for column in range(0, wide, 128):
                    if first + column < 2 * (size // 3):
                        lanes = slice(at + first + column, at + first + column + 128)
                        mid = mid + value[:, column : column + 128] * slabs[:, lanes].astype(F32)
                index += 1
            at += size
        sums[1] = mid
        plan.finish()
        near = jnp.zeros((each, 128), F32)
        at = 0
        columns = [out[...].reshape(each, out.shape[2]) for out in outs]
        columns = jnp.concatenate(columns, 1) if len(columns) > 1 else columns[0]
        for ref in (w_query, w_key, w_value):
            for column in range(0, ref.shape[1], 128):
                near = near + columns[:, at : at + 128] * ref[:, column : column + 128].astype(F32)
                at += 128
        sums[0] = near
        swap_sums().start()
        for k in range(micro):
            swap(k).wait_send()
        swap_sums().wait()
        gain_sums[...] = sums[...] + sums_got[...]


def back_in(h, dqkv, x, d_own, weights, gains, grads_last, w_in, slabs, feed_grads, feed_jobs, out_jobs, in_jobs):
    jobs = out_jobs + in_jobs
    micro, rows, dim = x.shape
    columns = dqkv.shape[2]
    each = slabs.shape[0]
    own = pl.BlockSpec((1, rows, dim), lambda i: (jnp.maximum(i - 2 * micro, 0), 0, 0))
    grads = grad_shape(dim, columns)
    shapes, specs = scatter_outs(jobs, dim)
    buffer = pltpu.VMEM((micro, rows, dim), BF16)
    sums = jax.ShapeDtypeStruct((2, each, 128), F32)

    def all_place(i):
        return jnp.minimum(i, micro - 1), 0, 0

    def place(i):
        core = lax.axis_index("tensor")
        k = jnp.maximum(i - micro, 0)
        return lax.rem(k, micro), jnp.where(k < micro, 1 - core, core), 0

    locals_ = list(w_in) + [slabs] + list(feed_grads)
    return call(
        functools.partial(back_in_kernel, micro, feed_jobs, out_jobs, in_jobs),
        "back_in",
        9,
        3 * micro,
        [
            pl.BlockSpec((1, 2 * rows, dim), all_place),
            pl.BlockSpec((1, 2 * rows, columns), all_place),
            pl.BlockSpec((1, rows, columns), place),
            own,
            own,
            once(weights.shape),
            once((8, dim)),
            anywhere(),
        ]
        + [once(a.shape) for a in locals_],
        [own, once(sums.shape), anywhere()] + specs,
        [jax.ShapeDtypeStruct((micro, rows, dim), BF16), sums, grads] + shapes,
        [pltpu.VMEM((dim, columns), F32), buffer, buffer]
        + half_sems(micro)
        + [
            pltpu.SemaphoreType.DMA,
            pltpu.VMEM(grads.shape, BF16),
            pltpu.VMEM(sums.shape, F32),
            pltpu.VMEM(sums.shape, F32),
            pltpu.SemaphoreType.DMA((2,)),
        ]
        + scatters_scratch(jobs, dim),
        (h, dqkv, dqkv, x, d_own, weights, gains, grads_last, *locals_),
    )


def finish_kernel(edges, counts, grad_in, mixed, gain_attn, gain_mlp, gain_sums, *refs):
    feed_grads, refs = refs[: counts[0]], refs[counts[0] :]
    out_grads, refs = refs[: counts[1]], refs[counts[1] :]
    in_grads, refs = refs[: counts[2]], refs[counts[2] :]
    mixed_out, grad_out, attn_out, mlp_out, q_out, k_out, v_out, out_t, gate_out, up_out, down_t = refs
    each, units = gate_out.shape
    grad_out[...] = grad_in[...].astype(F32)
    mixed_out[...] = mixed[...]

    def blocks(pieces):
        found = []
        for piece in pieces:
            for at in range(0, piece.shape[2], 128):
                found.append((piece, at))
        return found

    def copy_to(ref, at, block):
        piece, column = block
        wide = min(128, ref.shape[1] - at)
        ref[:, at : at + wide] = piece[:, :, column : column + wide].reshape(each, wide)

    @pl.when(pl.program_id(0) == 0)
    def _():
        turned = [gain_sums[k].T for k in range(2)]
        for value, gain, ref in zip(turned, (gain_attn, gain_mlp), (attn_out, mlp_out)):
            ref[...] = jnp.sum(value, axis=0, keepdims=True) / gain[...].astype(F32)
        queue = blocks(in_grads)
        for ref in (q_out, k_out, v_out):
            for at in range(0, ref.shape[1], 128):
                copy_to(ref, at, queue.pop(0))
        for at, block in zip(range(0, out_t.shape[1], 128), blocks(out_grads)):
            copy_to(out_t, at, block)
        queue = blocks(feed_grads)
        for low, high in edges:
            for start, width in chunk_slices(high - low):
                for ref in (gate_out, up_out):
                    for at in range(low + start, low + start + width, 128):
                        copy_to(ref, at, queue.pop(0))
            for at in range(low, high, 128):
                copy_to(down_t, at, queue.pop(0))


def finish(edges, grad_in, mixed, gain_attn, gain_mlp, gain_sums, feed_grads, out_grads, in_grads, widths, units):
    micro, rows, dim = mixed.shape
    each = gain_sums.shape[1]
    tile = min(rows, 512)
    block = pl.BlockSpec((1, tile, dim), lambda m, t: (m, t, 0))
    small = [gain_attn, gain_mlp, gain_sums, *feed_grads, *out_grads, *in_grads]
    shapes = [jax.ShapeDtypeStruct((1, each), F32)] * 2
    shapes += [jax.ShapeDtypeStruct((each, w), F32) for w in widths + [units] * 3]
    counts = (len(feed_grads), len(out_grads), len(in_grads))
    return call(
        functools.partial(finish_kernel, edges, counts),
        "finish",
        None,
        (micro, rows // tile),
        [block, block] + [once(a.shape) for a in small],
        [block, block] + [once(s.shape) for s in shapes],
        [jax.ShapeDtypeStruct(mixed.shape, BF16), jax.ShapeDtypeStruct(mixed.shape, F32)] + shapes,
        [],
        (grad_in, mixed, *small),
    )


def fused_body(
    inputs, gain_attn, gain_mlp, w_query, w_key, w_value, w_out, w_gate, w_up, w_down, out_grad, lengths
):
    micro, rows, dim = inputs.shape
    units = w_gate.shape[1]
    out_columns = w_out.shape[0]
    lengths = lengths[:, 0]
    gains = gain_attn.reshape(1, -1), gain_mlp.reshape(1, -1)
    w_in = (w_query, w_key, w_value)
    padded = -(-units // 128) * 128
    edges = [(max(at - CHUNK, 0), at) for at in range(padded, 0, -CHUNK)][::-1]
    wide = [3 * (high - low) for low, high in edges]

    h_in, qkv, gain_full, whole_in, slabs = project(edges, inputs, *w_in, *gains, w_gate, w_up, w_down.T, w_out.T)

    begin = [out_columns, out_columns + wide[0], out_columns + wide[0] + wide[1]]
    early = min(EARLY, wide[0])
    ahead = min(AHEAD, wide[1] - 128)
    mix, inverse, g_other, unit_0, near_a = attend_all(
        qkv, lengths, out_grad, slabs, [(0, 0, begin[0] + early)], (begin[1], ahead)
    )
    resid, h_own, h_other, unit_1, near_b = out_project(
        mix, inputs, unit_0, gain_full, slabs, [(begin[0] + early, 0, wide[0] - early)], (begin[1] + ahead, wide[1] - ahead)
    )

    feed_jobs, at = [[], [], []], []
    for kernel in JOBS:
        at.append([])
        for chunk, width in kernel:
            first = sum(w for _, w in feed_jobs[chunk])
            feed_jobs[chunk].append((first, width))
            at[-1].append((chunk, (first, width)))
    loads = [(out_columns, 0, early), (0, early, wide[0] - early)]
    (mixed_out, d_own, d_other), grads_of, done = feed(
        (h_own, h_other, out_grad, g_other),
        unit_0,
        unit_1,
        near_a,
        near_b,
        loads,
        [w // 3 for w in wide],
        slabs,
        list(zip(begin[1:], wide[1:])),
        at[0],
        resid,
        gain_full,
    )
    found = dict(zip(at[0], done))
    sources, jobs = [grads_of[chunk] for chunk, _ in at[1]], [job for _, job in at[1]]
    dqkv, grads_out, *done = attend_back(qkv, mix, inverse, d_own, d_other, unit_0, lengths, sources, jobs)
    found |= dict(zip(at[1], done))
    feed_grads = [found[key] for key in sorted(found)]
    out_jobs, in_jobs = pieces_of(out_columns, OUT_PIECE), pieces_of(qkv.shape[2], IN_PIECE)
    input_grad, gain_sums, _, *done = back_in(
        h_in, dqkv, inputs, d_own, whole_in, gain_full, grads_out, w_in, slabs, feed_grads, feed_jobs, out_jobs, in_jobs
    )
    out_grads, in_grads = done[: len(out_jobs)], done[len(out_jobs) :]
    widths = [w.shape[1] for w in w_in] + [out_columns]
    mixed_out, input_grad, attn_grad, mlp_grad, grad_query, grad_key, grad_value, out_t, gate, up, down_t = finish(
        edges, input_grad, mixed_out, *gains, gain_sums, feed_grads, out_grads, in_grads, widths, units
    )
    return (
        mixed_out,
        input_grad,
        attn_grad[0],
        mlp_grad[0],
        grad_query,
        grad_key,
        grad_value,
        out_t.T,
        gate,
        up,
        down_t.T,
    )


def solution(mesh):
    in_specs = (
        P(None, ("dp", "tensor"), None),
        P("dp"),
        P("dp"),
        P("dp", "tensor"),
        P("dp", "tensor"),
        P("dp", "tensor"),
        P("tensor", "dp"),
        P("dp", "tensor"),
        P("dp", "tensor"),
        P("tensor", "dp"),
        P(None, ("dp", "tensor"), None),
        P(None, "dp", None),
    )
    out_specs = (
        P(None, ("dp", "tensor"), None),
        P(None, ("dp", "tensor"), None),
        P("dp"),
        P("dp"),
        P("dp", "tensor"),
        P("dp", "tensor"),
        P("dp", "tensor"),
        P("tensor", "dp"),
        P("dp", "tensor"),
        P("dp", "tensor"),
        P("tensor", "dp"),
    )
    fits = mesh.shape["tensor"] == 2 and mesh.shape["dp"] % 4 == 0
    chosen = fused_body if fits else plain_body
    return jax.shard_map(chosen, mesh=mesh, in_specs=in_specs, out_specs=out_specs, check_vma=False)
```

```python
import functools
import math

import jax
import jax.numpy as jnp
import numpy as np
from jax import lax
from jax.experimental import pallas as pl
from jax.experimental.pallas import tpu as pltpu
from jax.sharding import PartitionSpec as P

FEAT = 16
VD = 64
BLK = 512


EXACT = lax.Precision.HIGHEST


def taylor(halved):
    feature_dim = halved.shape[-1]
    upper_idx, lower_idx = np.triu_indices(feature_dim)
    flat_index = jnp.asarray(upper_idx * feature_dim + lower_idx, jnp.int32)
    factors = jnp.asarray(np.where(upper_idx == lower_idx, math.sqrt(0.5), 1.0), jnp.float32)
    outer = (halved[..., :, None] * halved[..., None, :]).reshape(
        halved.shape[:-1] + (feature_dim * feature_dim,)
    )
    second = jnp.take(outer, flat_index, axis=-1) * factors
    ones_col = jnp.ones(halved.shape[:-1] + (1,), jnp.float32)
    return jnp.concatenate([ones_col, halved, second], axis=-1)


def attend_block(carry_in, block_in):
    kv_state, totals, previous = carry_in
    queries, keys_in, values_in, doc_ids = block_in
    half_q = 0.5 * queries
    half_k = 0.5 * keys_in
    scores = jnp.einsum("rhf,chf->hrc", half_q, half_k, preferred_element_type=jnp.float32)
    places = jnp.arange(doc_ids.shape[0], dtype=jnp.int32)
    allowed = (doc_ids[:, None] == doc_ids[None, :]) & (places[None, :] <= places[:, None])
    weights = jnp.where(allowed[None], 1.0 + scores + 0.5 * scores * scores, 0.0)
    feat_q = taylor(half_q)
    feat_k = taylor(half_k)
    carried_in = (doc_ids == previous).astype(jnp.float32)
    numerator = jnp.einsum("hrc,chv->rhv", weights, values_in, precision=EXACT) + carried_in[
        :, None, None
    ] * jnp.einsum("rhf,hfv->rhv", feat_q, kv_state, precision=EXACT)
    denominator = jnp.sum(weights, axis=2).T + carried_in[:, None] * jnp.einsum(
        "rhf,hf->rh", feat_q, totals, precision=EXACT
    )
    mixed_rows = numerator / denominator[:, :, None]
    final_doc = doc_ids[-1]
    staying = (doc_ids == final_doc).astype(jnp.float32)[:, None, None] * feat_k
    joined = (final_doc == previous).astype(jnp.float32)
    kv_state = jnp.einsum("rhf,rhv->hfv", staying, values_in, precision=EXACT) + joined * kv_state
    totals = jnp.sum(staying, axis=0) + joined * totals
    return ((kv_state, totals, final_doc), mixed_rows)


def attend(queries, keys_in, values_in, doc_ids):
    row_total, head_count, feature_dim = queries.shape
    value_dim = values_in.shape[2]
    block_count = row_total // BLK
    feature_total = 1 + feature_dim + feature_dim * (feature_dim + 1) // 2
    initial = (
        jnp.zeros((head_count, feature_total, value_dim), jnp.float32),
        jnp.zeros((head_count, feature_total), jnp.float32),
        jnp.array(-1, jnp.int32),
    )
    pieces = (
        queries.reshape(block_count, BLK, head_count, feature_dim),
        keys_in.reshape(block_count, BLK, head_count, feature_dim),
        values_in.reshape(block_count, BLK, head_count, value_dim),
        doc_ids.reshape(block_count, BLK),
    )
    last_carry, mixed_rows = lax.scan(jax.checkpoint(attend_block), initial, pieces)
    return mixed_rows.reshape(row_total, head_count * value_dim)


def document_ids(lengths_row, row_total):
    doc_ends = jnp.cumsum(lengths_row)
    places = jnp.arange(row_total, dtype=jnp.int32)
    return jnp.sum((places[:, None] >= doc_ends[None, :]).astype(jnp.int32), axis=1)


def rows_product(left, right):
    return lax.dot_general(
        left, right, (((0,), (0,)), ((), ())), preferred_element_type=jnp.float32
    )


def back_product(left, right):
    return lax.dot_general(
        left, right, (((1,), (1,)), ((), ())), preferred_element_type=jnp.float32
    )


def norm_back(grad_normed, normed, inverse, gain_full):
    scaled = grad_normed * gain_full
    return inverse * (scaled - normed * jnp.mean(scaled * normed, axis=-1, keepdims=True))


def row_slice(matrix, first_row, row_count):
    return lax.dynamic_slice_in_dim(matrix, first_row, row_count, 0)


def inverse_root(values):
    return lax.rsqrt(jnp.mean(values * values, axis=-1, keepdims=True) + 1e-05)


def fetch_weights(gain_attn, gain_mlp, w_query, w_key, w_value, w_out, w_gate, w_up, w_down):
    row_parts = (
        lax.all_gather(w_query, "dp", axis=0, tiled=True),
        lax.all_gather(w_key, "dp", axis=0, tiled=True),
        lax.all_gather(w_value, "dp", axis=0, tiled=True),
        lax.all_gather(w_gate, "dp", axis=0, tiled=True),
        lax.all_gather(w_up, "dp", axis=0, tiled=True),
        lax.all_gather(gain_attn, "dp", axis=0, tiled=True),
        lax.all_gather(gain_mlp, "dp", axis=0, tiled=True),
    )
    col_parts = (
        lax.all_gather(w_out, "dp", axis=1, tiled=True),
        lax.all_gather(w_down, "dp", axis=1, tiled=True),
    )
    return tuple(row_parts) + tuple(col_parts)


def plain_body(
    inputs,
    gain_attn,
    gain_mlp,
    w_query,
    w_key,
    w_value,
    w_out,
    w_gate,
    w_up,
    w_down,
    out_grad,
    lengths,
):
    micro_count = inputs.shape[0]
    shard_rows = inputs.shape[1]
    model_dim = inputs.shape[2]
    group_rows = shard_rows * lax.axis_size("tensor")
    local_heads = w_query.shape[1] // FEAT
    grad_query_sum = jnp.zeros((model_dim, w_query.shape[1]), jnp.float32)
    grad_key_sum = jnp.zeros((model_dim, w_key.shape[1]), jnp.float32)
    grad_value_sum = jnp.zeros((model_dim, w_value.shape[1]), jnp.float32)
    grad_gate_sum = jnp.zeros((model_dim, w_gate.shape[1]), jnp.float32)
    grad_up_sum = jnp.zeros((model_dim, w_up.shape[1]), jnp.float32)
    grad_out_sum = jnp.zeros((w_out.shape[0], model_dim), jnp.float32)
    grad_down_sum = jnp.zeros((w_down.shape[0], model_dim), jnp.float32)
    gain_attn_sum = jnp.zeros((model_dim,), jnp.float32)
    gain_mlp_sum = jnp.zeros((model_dim,), jnp.float32)
    outputs = []
    input_grads = []
    for micro_step in range(micro_count):
        (
            full_query,
            full_key,
            full_value,
            full_gate,
            full_up,
            full_gain_attn,
            full_gain_mlp,
            full_out,
            full_down,
        ) = fetch_weights(gain_attn, gain_mlp, w_query, w_key, w_value, w_out, w_gate, w_up, w_down)
        gain_in = full_gain_attn.astype(jnp.float32)
        gain_mid = full_gain_mlp.astype(jnp.float32)
        doc_ids = document_ids(lengths[micro_step, 0], group_rows)
        values = inputs[micro_step].astype(jnp.float32)
        inverse_in = inverse_root(values)
        normed_in = values * inverse_in
        gathered_in = lax.all_gather(
            (normed_in * gain_in).astype(jnp.bfloat16), "tensor", axis=0, tiled=True
        )
        query_low = jnp.dot(gathered_in, full_query, preferred_element_type=jnp.float32).astype(
            jnp.bfloat16
        )
        key_low = jnp.dot(gathered_in, full_key, preferred_element_type=jnp.float32).astype(
            jnp.bfloat16
        )
        value_low = jnp.dot(gathered_in, full_value, preferred_element_type=jnp.float32).astype(
            jnp.bfloat16
        )
        query_full = query_low.astype(jnp.float32).reshape(group_rows, local_heads, FEAT)
        key_full = key_low.astype(jnp.float32).reshape(group_rows, local_heads, FEAT)
        value_full = value_low.astype(jnp.float32).reshape(group_rows, local_heads, VD)

        def local_attend(query_arg, key_arg, value_arg):
            return attend(query_arg, key_arg, value_arg, doc_ids)

        mixed_full, pullback = jax.vjp(local_attend, query_full, key_full, value_full)
        mixed_low = mixed_full.astype(jnp.bfloat16)
        residual = values + lax.psum_scatter(
            jnp.dot(
                row_slice(mixed_low, jnp.int32(0), shard_rows * lax.axis_size("tensor")),
                full_out,
                preferred_element_type=jnp.float32,
            ),
            "tensor",
            scatter_dimension=0,
            tiled=True,
        )
        inverse_mid = inverse_root(residual)
        normed_mid = residual * inverse_mid
        gathered_mid = lax.all_gather(
            (normed_mid * gain_mid).astype(jnp.bfloat16), "tensor", axis=0, tiled=True
        )
        gate_pre = jnp.dot(gathered_mid, full_gate, preferred_element_type=jnp.float32)
        up_pre = jnp.dot(gathered_mid, full_up, preferred_element_type=jnp.float32)
        sigmoid_gate = jax.nn.sigmoid(gate_pre)
        silu_gate = gate_pre * sigmoid_gate
        hidden = (silu_gate * up_pre).astype(jnp.bfloat16)
        mlp_part = lax.psum_scatter(
            jnp.dot(
                row_slice(hidden, jnp.int32(0), shard_rows * lax.axis_size("tensor")),
                full_down,
                preferred_element_type=jnp.float32,
            ).astype(jnp.bfloat16),
            "tensor",
            scatter_dimension=0,
            tiled=True,
        ).astype(jnp.float32)
        outputs.append((residual + mlp_part).astype(jnp.bfloat16))
        cotangent = out_grad[micro_step]
        gathered_grad = lax.all_gather(cotangent, "tensor", axis=0, tiled=True)
        grad_down_sum += rows_product(hidden, gathered_grad)
        grad_hidden = back_product(gathered_grad, full_down)
        grad_gate_low = (
            grad_hidden * up_pre * sigmoid_gate * (1.0 + gate_pre * (1.0 - sigmoid_gate))
        ).astype(jnp.bfloat16)
        grad_up_low = (grad_hidden * silu_gate).astype(jnp.bfloat16)
        grad_gate_sum += rows_product(gathered_mid, grad_gate_low)
        grad_up_sum += rows_product(gathered_mid, grad_up_low)
        first_row = jnp.int32(0)
        grad_mid = lax.psum_scatter(
            back_product(
                row_slice(grad_gate_low, first_row, shard_rows * lax.axis_size("tensor")), full_gate
            )
            + back_product(
                row_slice(grad_up_low, first_row, shard_rows * lax.axis_size("tensor")), full_up
            ),
            "tensor",
            scatter_dimension=0,
            tiled=True,
        )
        gain_mlp_sum += jnp.sum(grad_mid * normed_mid, axis=0)
        grad_resid = cotangent.astype(jnp.float32) + norm_back(
            grad_mid, normed_mid, inverse_mid, gain_mid
        )
        gathered_resid = lax.all_gather(
            grad_resid.astype(jnp.bfloat16), "tensor", axis=0, tiled=True
        )
        grad_out_sum += rows_product(mixed_low, gathered_resid)
        grad_mixed = back_product(gathered_resid, full_out).astype(jnp.bfloat16).astype(jnp.float32)
        grad_query_full, grad_key_full, grad_value_full = pullback(grad_mixed)
        grad_query_low = grad_query_full.reshape(group_rows, -1).astype(jnp.bfloat16)
        grad_key_low = grad_key_full.reshape(group_rows, -1).astype(jnp.bfloat16)
        grad_value_low = grad_value_full.reshape(group_rows, -1).astype(jnp.bfloat16)
        grad_query_sum += rows_product(gathered_in, grad_query_low)
        grad_key_sum += rows_product(gathered_in, grad_key_low)
        grad_value_sum += rows_product(gathered_in, grad_value_low)
        attn_first_row = jnp.int32(0)
        grad_in = lax.psum_scatter(
            (
                back_product(
                    row_slice(grad_query_low, attn_first_row, shard_rows * lax.axis_size("tensor")),
                    full_query,
                )
                + back_product(
                    row_slice(grad_key_low, attn_first_row, shard_rows * lax.axis_size("tensor")),
                    full_key,
                )
                + back_product(
                    row_slice(grad_value_low, attn_first_row, shard_rows * lax.axis_size("tensor")),
                    full_value,
                )
            ).astype(jnp.bfloat16),
            "tensor",
            scatter_dimension=0,
            tiled=True,
        ).astype(jnp.float32)
        gain_attn_sum += jnp.sum(grad_in * normed_in, axis=0)
        input_grads.append(grad_resid + norm_back(grad_in, normed_in, inverse_in, gain_in))
    row_grads = (
        lax.psum_scatter(
            grad_query_sum.astype(jnp.bfloat16), "dp", scatter_dimension=0, tiled=True
        ).astype(jnp.float32),
        lax.psum_scatter(
            grad_key_sum.astype(jnp.bfloat16), "dp", scatter_dimension=0, tiled=True
        ).astype(jnp.float32),
        lax.psum_scatter(
            grad_value_sum.astype(jnp.bfloat16), "dp", scatter_dimension=0, tiled=True
        ).astype(jnp.float32),
        lax.psum_scatter(
            grad_gate_sum.astype(jnp.bfloat16), "dp", scatter_dimension=0, tiled=True
        ).astype(jnp.float32),
        lax.psum_scatter(
            grad_up_sum.astype(jnp.bfloat16), "dp", scatter_dimension=0, tiled=True
        ).astype(jnp.float32),
        lax.psum_scatter(
            gain_attn_sum.astype(jnp.bfloat16), "dp", scatter_dimension=0, tiled=True
        ).astype(jnp.float32),
        lax.psum_scatter(
            gain_mlp_sum.astype(jnp.bfloat16), "dp", scatter_dimension=0, tiled=True
        ).astype(jnp.float32),
    )
    col_grads = (
        lax.psum_scatter(
            grad_out_sum.astype(jnp.bfloat16), "dp", scatter_dimension=1, tiled=True
        ).astype(jnp.float32),
        lax.psum_scatter(
            grad_down_sum.astype(jnp.bfloat16), "dp", scatter_dimension=1, tiled=True
        ).astype(jnp.float32),
    )
    gain_grads = lax.psum((row_grads[5], row_grads[6]), "tensor")
    return (
        jnp.stack(outputs, 0),
        jnp.stack(input_grads, 0),
        gain_grads[0],
        gain_grads[1],
        row_grads[0],
        row_grads[1],
        row_grads[2],
        col_grads[0],
        row_grads[3],
        row_grads[4],
        col_grads[1],
    )


F32 = jnp.float32
BF16 = jnp.bfloat16
NN = (((1,), (0,)), ((), ()))
NT = (((1,), (1,)), ((), ()))
TN = (((0,), (0,)), ((), ()))
TILE = 256
SPAN = 2
CHUNK = 512
EARLY = 640
AHEAD = 768
JOBS = (((0, 768), (0, 384), (1, 768)), ((1, 768), (2, 768), (2, 384), (2, 384)))
RATE = 0.019
VMEM_BYTES = 62 << 20
MESH = pl.DeviceIdType.MESH


def mm(left, right, dims=NN):
    return lax.dot_general(left, right, dims, preferred_element_type=F32)


def params(number=None):
    if number is None:
        return pltpu.CompilerParams(vmem_limit_bytes=VMEM_BYTES)
    return pltpu.CompilerParams(vmem_limit_bytes=VMEM_BYTES, collective_id=number, has_side_effects=True)


def anywhere():
    return pl.BlockSpec(memory_space=pl.ANY)


def once(shape):
    return pl.BlockSpec(shape, lambda *_: (0,) * len(shape), pipeline_mode=pl.Buffered(1))


def far_count():
    return lax.axis_size("dp") // 4


def dp_peer(bits):
    return {"dp": lax.axis_index("dp") ^ bits}


def sibling():
    return {"tensor": 1 - lax.axis_index("tensor")}


def dp_peers():
    return [dp_peer(1), dp_peer(2)] + [dp_peer(4 * k) for k in range(1, far_count())]


def greet(peers):
    barrier = pltpu.get_barrier_semaphore()
    for peer in peers:
        pl.semaphore_signal(barrier, inc=1, device_id=peer, device_id_type=MESH)
    pl.semaphore_wait(barrier, len(peers))


def remote(source, target, send, recv, peer):
    return pltpu.make_async_remote_copy(
        src_ref=source, dst_ref=target, send_sem=send, recv_sem=recv, device_id=peer, device_id_type=MESH
    )


def gather_sems():
    count = 7 * far_count() - 1
    return [pltpu.SemaphoreType.DMA((count,)), pltpu.SemaphoreType.DMA((count,)), pltpu.SemaphoreType.DMA]


class Gather:

    def __init__(self, source, whole, send, recv, local=None, near=None):
        self.source, self.whole, self.send, self.recv, self.local = source, whole, send, recv, local
        self.near = near
        self.me = lax.axis_index("dp")
        self.far = far_count()
        self.each = whole.shape[0] // lax.axis_size("dp")
        self.half = self.each // 2

    def block(self, bits):
        start = pl.multiple_of((self.me ^ bits) * self.each, self.each)
        return self.whole.at[pl.ds(start, self.each)]

    def piece(self, bits, part):
        start = pl.multiple_of((self.me ^ bits) * self.each + part * self.half, self.half)
        return self.whole.at[pl.ds(start, self.half)]


    def along(self, k):
        return k - 1, self.source, self.block(0), 4 * k, self.block(4 * k)

    def first(self, k, part, bit):
        index = self.far - 1 + 4 * k + 2 * part + bit - 1
        if self.near is not None:
            source = near_block(self.near, k, part * self.half, self.half)
        elif k == 0:
            source = self.source.at[pl.ds(part * self.half, self.half)]
        else:
            source = self.piece(4 * k, part)
        return index, source, self.piece(4 * k, part), bit, self.piece(4 * k + bit, part)

    def second(self, k, part):
        index = 5 * self.far - 1 + 2 * k + part
        source = self.piece(4 * k + 2 - part, part)
        return index, source, source, 1 + part, self.piece(4 * k + 3, part)

    def outgoing(self, transfer):
        index, source, target, bits, _ = transfer
        return remote(source, target, self.send.at[index], self.recv.at[index], dp_peer(bits))

    def start(self, transfer):
        self.outgoing(transfer).start()

    def sent(self, transfer):
        self.outgoing(transfer).wait_send()

    def arrived(self, transfer):
        index, _, _, bits, landing = transfer
        remote(landing, landing, self.send.at[index], self.recv.at[index], dp_peer(bits)).wait_recv()

    def kept(self):
        if self.near is None:
            return [pltpu.make_async_copy(self.source, self.block(0), self.local)]
        sems = [self.local] + [self.recv.at[k - 1] for k in range(1, self.far)]
        return [
            pltpu.make_async_copy(near_block(self.near, k, 0, self.each), self.block(4 * k), sems[k])
            for k in range(self.far)
        ]

    def pass_on(self, k):
        for part, bit in ((0, 2), (1, 1), (0, 1), (1, 2)):
            self.start(self.first(k, part, bit))

    def begin_far(self):
        if self.local is not None:
            for copy in self.kept():
                copy.start()
        if self.near is None:
            for k in range(1, self.far):
                self.start(self.along(k))

    def begin(self):
        self.begin_far()
        self.pass_on(0)

    def spread(self, k):
        if self.near is None:
            self.arrived(self.along(k))
        self.pass_on(k)

    def turn(self, k):
        self.arrived(self.first(k, 0, 2))
        self.start(self.second(k, 0))
        self.arrived(self.first(k, 1, 1))
        self.start(self.second(k, 1))

    def finish(self):
        for k in range(self.far):
            self.arrived(self.first(k, 0, 1))
            self.arrived(self.first(k, 1, 2))
            for part in range(2):
                self.arrived(self.second(k, part))
        if self.near is None:
            for k in range(1, self.far):
                self.sent(self.along(k))
        for k in range(self.far):
            for part in range(2):
                for bit in (1, 2):
                    self.sent(self.first(k, part, bit))
                self.sent(self.second(k, part))
        if self.local is not None:
            for copy in self.kept():
                copy.wait()

    def plan(self, start):
        along = RATE * self.whole.shape[1]
        far = 2 * along / 3
        events = [(start, self.begin)]
        for k in range(1, self.far):
            at = start + 1.0 + far * (0.4 + 0.6 * k / (self.far - 1))
            events.append((at, functools.partial(self.spread, k)))
        for k in range(self.far):
            at = start + 2.0 + far * (0.4 + 0.6 * k / (self.far - 1)) + along / 4
            events.append((at, functools.partial(self.turn, k)))
        return events


    def plan_near(self, far_start, start):
        along = RATE * self.whole.shape[1]
        events = [(far_start, self.begin_far)]
        events += [(start, functools.partial(self.pass_on, 0))]
        events += [(start + 0.001 * k, functools.partial(self.spread, k)) for k in range(1, self.far)]
        for k in range(self.far):
            events.append((start + 2.0 + along * (k + 1) / 6, functools.partial(self.turn, k)))
        return events


def near_block(near, k, first, rows):
    each = near.shape[0] // far_count()
    start = (lax.div(lax.axis_index("dp"), 4) ^ k) * each + first
    return near.at[pl.ds(pl.multiple_of(start, rows), rows)]


class NearGather:

    def __init__(self, source, near, send, recv, local):
        self.source, self.near, self.send, self.recv, self.local = source, near, send, recv, local
        self.each = source.shape[0]

    def copies(self):
        mine = near_block(self.near, 0, 0, self.each)
        made = [pltpu.make_async_copy(self.source, mine, self.local)]
        for k in range(1, far_count()):
            made.append(remote(self.source, mine, self.send.at[k - 1], self.recv.at[k - 1], dp_peer(4 * k)))
        return made

    def begin(self):
        for copy in self.copies():
            copy.start()

    def finish(self):
        for k in range(1, far_count()):
            landing = near_block(self.near, k, 0, self.each)
            remote(landing, landing, self.send.at[k - 1], self.recv.at[k - 1], dp_peer(4 * k)).wait_recv()
        for copy in self.copies()[1:]:
            copy.wait_send()
        self.copies()[0].wait()


class Plan:

    def __init__(self, step, steps, places, step_us, clock=None):
        self.step, self.steps, self.places = step, steps, places
        self.clock = clock or [at * step_us / places for at in range(steps * places)]
        self.events = {}
        self.tail = []
        self.ends = []

    def add(self, events, end, latest=None, earliest=0):
        for at, (time, action) in enumerate(events):
            index = sum(tick < time for tick in self.clock) if at else sum(tick <= time for tick in self.clock) - 1
            index = max(index, earliest)
            if latest is not None:
                index = min(index, latest)
            if index < self.steps * self.places:
                self.events.setdefault(divmod(index, self.places), []).append((time, action))
            else:
                self.tail.append((time, action))
        self.ends.append(end)

    def put(self, step, time, action):
        self.events.setdefault((step, 0), []).append((time, action))

    def at(self, place):
        for key in sorted(self.events):
            if key[1] == place:

                @pl.when(self.step == key[0])
                def _(actions=sorted(self.events[key], key=lambda event: event[0])):
                    for _, action in actions:
                        action()

    def finish(self):
        for _, action in sorted(self.tail, key=lambda event: event[0]):
            action()
        for end in self.ends:
            end()


def add_gathers(plan, jobs, refs, start=0.0):
    for at, (source, whole, first, target, width) in enumerate(jobs):
        gather = Gather(
            source.at[:, pl.ds(first, width)], whole.at[:, pl.ds(target, width)], *refs[3 * at : 3 * at + 3]
        )
        plan.add(gather.plan(start), gather.finish)
        start += RATE * width


def pieces_of(width, most):
    return [(at, min(most, width - at)) for at in range(0, width, most)]


def scatter_scratch(columns, dim):
    far = far_count()
    half = dim // lax.axis_size("dp") // 2
    part = pltpu.VMEM((far, half, columns), BF16)
    return [part] * 8 + [
        pltpu.VMEM((far, 2, half, columns), BF16),
        pltpu.VMEM((far - 1, 2, half, columns), BF16),
        pltpu.SemaphoreType.DMA((5 + far,)),
        pltpu.SemaphoreType.DMA((5 + far,)),
        pltpu.SemaphoreType.DMA((3,)),
    ]


SCATTER_REFS = 13


class Scatter:
    def __init__(self, grads, first, out, refs):
        (
            self.mine_y, self.mine_x, self.got_dy, self.got_dx, self.got_x, self.got_y, self.got_y2, self.got_x2,
            self.mine, self.got_far, self.send, self.recv, self.local,
        ) = refs
        self.grads, self.out = grads, out
        self.columns = pl.ds(first, self.mine.shape[3])
        me = lax.axis_index("dp")
        self.far = far_count()
        self.low, self.high = lax.rem(me, 4), lax.div(me, 4)

    def copy(self, index, source, target, bits):
        return remote(source, target, self.send.at[index], self.recv.at[index], dp_peer(bits))

    def share(self, bits, part):
        return self.grads.at[:, self.low ^ bits, part, :, self.columns]

    def from_grads(self):
        return [
            self.copy(0, self.share(3, 0), self.got_dy, 1),
            self.copy(1, self.share(3, 1), self.got_dx, 2),
            self.copy(2, self.share(1, 0), self.got_x, 1),
            self.copy(3, self.share(2, 1), self.got_y, 2),
        ]

    def added(self):
        return [self.copy(4, self.mine_y, self.got_y2, 2), self.copy(5, self.mine_x, self.got_x2, 1)]

    def along(self):
        return [
            self.copy(5 + k, self.mine.at[self.high ^ k], self.got_far.at[k - 1], 4 * k) for k in range(1, self.far)
        ]

    def loads(self):
        own = self.grads.at[:, self.low, :, :, self.columns]
        return [
            pltpu.make_async_copy(self.share(2, 0), self.mine_y, self.local.at[0]),
            pltpu.make_async_copy(self.share(1, 1), self.mine_x, self.local.at[1]),
            pltpu.make_async_copy(own, self.mine, self.local.at[2]),
        ]

    def begin(self):
        for copy in self.from_grads() + self.loads():
            copy.start()

    def second(self):
        loads, got, added = self.loads(), self.from_grads(), self.added()
        loads[0].wait()
        got[0].wait_recv()
        self.mine_y[...] = add(self.mine_y[...], self.got_dy[...]).astype(BF16)
        added[0].start()
        loads[1].wait()
        got[1].wait_recv()
        self.mine_x[...] = add(self.mine_x[...], self.got_dx[...]).astype(BF16)
        added[1].start()

    def third(self):
        got, added = self.from_grads(), self.added()
        self.loads()[2].wait()
        got[2].wait_recv()
        added[0].wait_recv()
        self.mine[:, 0] = add(self.mine[:, 0], self.got_x[...], self.got_y2[...]).astype(BF16)
        got[3].wait_recv()
        added[1].wait_recv()
        self.mine[:, 1] = add(self.mine[:, 1], self.got_y[...], self.got_x2[...]).astype(BF16)
        for copy in self.along():
            copy.start()

    def finish(self):
        for copy in self.along():
            copy.wait_recv()
        self.out[...] = add(self.mine[self.high], *[self.got_far[k] for k in range(self.far - 1)])
        for copy in self.from_grads() + self.added() + self.along():
            copy.wait_send()


    def plan(self, start):
        along = RATE * self.mine.shape[3]
        times = (start, start + 2.5 + 2 * along / 3, start + 5 + along)
        return list(zip(times, (self.begin, self.second, self.third)))


def scatters_scratch(jobs, dim):
    scratch = []
    for _, width in jobs:
        scratch += scatter_scratch(width, dim)
    return scratch


def scatter_outs(jobs, dim):
    half = dim // lax.axis_size("dp") // 2
    shapes = [jax.ShapeDtypeStruct((2, half, width), F32) for _, width in jobs]
    return shapes, [once(shape.shape) for shape in shapes]


def add_scatters(plan, jobs, sources, outs, refs, start=0.0):
    for at, (first, width) in enumerate(jobs):
        scatter = Scatter(sources[at], first, outs[at], refs[SCATTER_REFS * at : SCATTER_REFS * (at + 1)])
        plan.add(scatter.plan(start), scatter.finish)
        start += RATE * width


def grad_shape(dim, columns):
    return jax.ShapeDtypeStruct((far_count(), 4, 2, dim // lax.axis_size("dp") // 2, columns), BF16)


def add(*terms):
    total = terms[0].astype(F32)
    for term in terms[1:]:
        total = total + term.astype(F32)
    return total


def call(kernel, name, number, steps, in_specs, out_specs, out_shape, scratch, operands):
    return pl.pallas_call(
        kernel,
        grid=steps if isinstance(steps, tuple) else (steps,),
        in_specs=in_specs,
        out_specs=out_specs,
        out_shape=out_shape,
        scratch_shapes=scratch,
        compiler_params=params(number),
        name=name,
    )(*operands)


def spread_gains(slab, column):
    dim = slab.shape[0]
    blocks = lax.axis_size("dp")
    each = dim // blocks
    lane_block = lax.broadcasted_iota(jnp.int32, (blocks, dim), 1) // each
    block = lax.broadcasted_iota(jnp.int32, (blocks, dim), 0)
    rows = []
    for which in range(2):
        picked = jnp.concatenate(
            [slab[each * b : each * b + 16, column : column + 128].astype(F32)[which : which + 1] for b in range(blocks)], 0
        )
        tiled = jnp.concatenate([picked] * (dim // 128), 1)
        rows.append(jnp.sum(jnp.where(lane_block == block, tiled, 0.0), axis=0, keepdims=True))
    return jnp.concatenate(rows + [jnp.zeros((6, dim), F32)], 0)


def part_block(width, per, rows, lag=0, last=None):
    def place(i):
        i = i - lag if last is None else jnp.clip(i - lag, 0, last)
        return lax.div(i, per), lax.rem(i, per), 0

    return pl.BlockSpec((1, rows, width), place)


def core_block(width, per, rows, other, last=None):
    def place(i):
        if last is not None:
            i = jnp.minimum(i, last)
        core = lax.axis_index("tensor")
        return lax.div(i, per), (1 - core if other else core) * per + lax.rem(i, per), 0

    return pl.BlockSpec((1, rows, width), place)


def root_mean(values):
    return lax.rsqrt(jnp.mean(values * values, axis=-1, keepdims=True) + 1e-05)


def norm_slope(values, scaled):
    inverse = root_mean(values)
    normed = values * inverse
    return inverse * (scaled - normed * jnp.mean(scaled * normed, axis=-1, keepdims=True))


def half_sems(count):
    return [pltpu.SemaphoreType.DMA((count,)), pltpu.SemaphoreType.DMA((count,))]


def chunk_slices(width):
    return [(at, min(256, width - at)) for at in range(0, width, 256)]


def build_slabs(edges, gate, up, down_t, out_t, slabs):
    at = out_t.shape[1]
    slabs[:, :at] = out_t[...]
    units = gate.shape[1]

    def place(ref, low, high):
        nonlocal at
        end = min(high, units)
        slabs[:, at : at + end - low] = ref[:, low:end]
        if end < high:
            slabs[:, at + end - low : at + high - low] = jnp.zeros((slabs.shape[0], high - end), BF16)
        at += high - low

    for low, high in edges:
        for start, width in chunk_slices(high - low):
            place(gate, low + start, low + start + width)
            place(up, low + start, low + start + width)
        place(down_t, low, high)


def project_kernel(
    edges, inputs, w_query, w_key, w_value, gain_attn, gain_mlp, gate, up, down_t, out_t,
    h_out, qkv_out, gain_out, whole_in, slabs, x_own, x_other, h_all, qkv_all, slab, gain_slab,
    local, swap_send, swap_recv, *sems,
):
    micro, rows, _ = x_own.shape
    each = w_query.shape[0]
    core = lax.axis_index("tensor")
    parts = 2 * micro

    def load(m):
        return pltpu.make_async_copy(inputs.at[m], x_own.at[m], local.at[m])

    def swap(m):
        return remote(inputs.at[m], x_other.at[m], swap_send.at[m], swap_recv.at[m], sibling())

    def place(t):
        first = pl.multiple_of((core if t < micro else 1 - core) * rows, rows)
        return t % micro, pl.ds(first, rows)

    def store_h(t):
        return pltpu.make_async_copy(h_all.at[t], h_out.at[place(t)], local.at[micro + t])

    def store_qkv(t):
        return pltpu.make_async_copy(qkv_all.at[t], qkv_out.at[place(t)], local.at[micro + parts + t])

    def keep():
        return pltpu.make_async_copy(slab, whole_in, local.at[micro + 2 * parts])

    def norm(t):
        x = (x_own if t < micro else x_other)[t % micro].astype(F32)
        h_all[t] = (x * root_mean(x) * gain_out[0:1]).astype(BF16)
        store_h(t).start()

    for m in range(micro):
        load(m).start()
    mine = pl.ds(pl.multiple_of(lax.axis_index("dp") * each, each), each)
    at = 0
    for ref in (w_query, w_key, w_value):
        slab[mine, at : at + ref.shape[1]] = ref[...]
        at += ref.shape[1]
    both = jnp.concatenate([gain_attn[...], gain_mlp[...]], 0).astype(F32)
    both = jnp.concatenate([both, both], 1)
    gain_slab[mine] = jnp.concatenate([both, jnp.zeros((each - 2, both.shape[1]), F32)], 0).astype(BF16)
    greet(dp_peers() + [sibling()])
    gains = Gather(gain_slab.at[mine], gain_slab, *sems[:2])
    weights = Gather(slab.at[mine], slab, *sems[2:])
    gains.begin()
    weights.begin()
    for m in range(micro):
        swap(m).start()
    build_slabs(edges, gate, up, down_t, out_t, slabs)
    for k in range(1, gains.far):
        gains.spread(k)
    for k in range(gains.far):
        gains.turn(k)
    gains.finish()
    gain_out[...] = spread_gains(gain_slab, 0)
    duties = [functools.partial(weights.spread, k) for k in range(1, weights.far)]
    duties += [functools.partial(weights.turn, k) for k in range(weights.far)]
    for t in range(parts):
        if t < micro:
            load(t).wait()
        else:
            swap(t - micro).wait()
        norm(t)
        if duties:
            duties.pop(0)()
    for duty in duties:
        duty()
    weights.finish()
    keep().start()
    for t in range(parts):
        qkv_all[t] = mm(h_all[t], slab[...]).astype(BF16)
        store_qkv(t).start()
    for t in range(parts):
        store_h(t).wait()
        store_qkv(t).wait()
    keep().wait()


def project(edges, inputs, w_query, w_key, w_value, gain_attn, gain_mlp, w_gate, w_up, down_t, out_t):
    micro, rows, dim = inputs.shape
    each = w_query.shape[0]
    columns = w_query.shape[1] + w_key.shape[1] + w_value.shape[1]
    all_columns = out_t.shape[1] + 3 * edges[-1][1]
    locals_ = (w_query, w_key, w_value, gain_attn, gain_mlp, w_gate, w_up, down_t, out_t)
    return call(
        functools.partial(project_kernel, edges),
        "project",
        1,
        1,
        [anywhere()] + [once(a.shape) for a in locals_],
        [anywhere(), anywhere(), once((8, dim)), anywhere(), once((each, all_columns))],
        [
            jax.ShapeDtypeStruct((micro, 2 * rows, dim), BF16),
            jax.ShapeDtypeStruct((micro, 2 * rows, columns), BF16),
            jax.ShapeDtypeStruct((8, dim), F32),
            jax.ShapeDtypeStruct((dim, columns), BF16),
            jax.ShapeDtypeStruct((each, all_columns), BF16),
        ],
        [
            pltpu.VMEM((micro, rows, dim), BF16),
            pltpu.VMEM((micro, rows, dim), BF16),
            pltpu.VMEM((2 * micro, rows, dim), BF16),
            pltpu.VMEM((2 * micro, rows, columns), BF16),
            pltpu.VMEM((dim, columns), BF16),
            pltpu.VMEM((dim, 128), BF16),
            pltpu.SemaphoreType.DMA((5 * micro + 1,)),
        ]
        + half_sems(micro)
        + gather_sems()[:2]
        + gather_sems()[:2],
        (inputs, *locals_),
    )


def fill_mask(mask, lengths, micro_step):
    tiles = mask.shape[0]
    row = lax.broadcasted_iota(jnp.int32, (tiles * TILE, TILE), 0)
    start = jnp.zeros_like(row)
    end = 0
    for d in range(lengths.shape[1]):
        end = end + lengths[micro_step, d]
        start = jnp.where(row >= end, end, start)
    lane = lax.broadcasted_iota(jnp.int32, (tiles * TILE, TILE), 1)
    for j in range(tiles):
        i = min(tiles, j + SPAN + 1)
        tall = (i - j) * TILE
        below = slice(j * TILE, i * TILE)
        column = lane[:tall] + j * TILE
        allowed = (column <= row[below]) & (column >= start[below])
        mask[j, :tall, :] = jnp.where(allowed, 1.0, 0.0)


def add_rows(total, j, tiles, value):
    end = min(tiles, j + SPAN + 1)
    begun = min(tiles, j + SPAN) if j else 0
    if begun > j:
        total[j * TILE : begun * TILE] += value[: (begun - j) * TILE]
    if end > max(begun, j):
        start = max(begun, j)
        total[start * TILE : end * TILE] = value[(start - j) * TILE :]


def attend_kernel(
    jobs, near_job, lengths, qkv, grad_own, slabs, mix_ref, inv_ref, grad_other, unit, near,
    mask, queries, values, total, *sems,
):
    m = pl.program_id(0)
    group = qkv.shape[1]
    tiles = group // TILE
    pairs = mix_ref.shape[2] // 128
    lane = lax.broadcasted_iota(jnp.int32, (group, 128), 1)
    zero = jnp.zeros((), BF16)

    def swap():
        return remote(grad_own, grad_other, sems[0], sems[1], sibling())

    plan = Plan(m, lengths.shape[0], pairs, 9.5)
    plan.add([(0.0, lambda: swap().start())], lambda: swap().wait())
    add_gathers(plan, [(slabs, unit, *job) for job in jobs], sems[5:])
    ahead = NearGather(slabs.at[:, pl.ds(*near_job)], near, *sems[2:5])
    plan.add([(12.0, ahead.begin)], ahead.finish)

    @pl.when(m == 0)
    def _():
        greet(dp_peers() + [sibling()])

    fill_mask(mask, lengths, m)
    query = qkv[0, :, :128] * jnp.asarray(0.25, BF16)
    for pair in range(pairs):
        at = 256 + 128 * pair
        now = pair % 2
        for side in range(2):
            mine = lane // VD == side
            queries[now, side] = jnp.where(lane // FEAT == 2 * pair + side, query, zero)
            values[now, side, :, :128] = jnp.where(mine, qkv[0, :, at : at + 128], zero)
            values[now, side, :, 128:] = mine.astype(F32).astype(BF16)
        for j in range(tiles):
            if j == 0:
                plan.at(pair)
            i = min(tiles, j + SPAN + 1)
            tall = (i - j) * TILE
            here, below = slice(j * TILE, (j + 1) * TILE), slice(j * TILE, i * TILE)
            scores = mm(queries[now, :, below].reshape(2 * tall, 128), qkv[0, here, 128:256], NT)
            allowed = mask[j, :tall]
            weights = []
            for side in range(2):
                t = scores[side * tall : (side + 1) * tall] + 1.0
                weights.append(((t * t + 1.0) * allowed).astype(BF16))
            part = mm(jnp.concatenate(weights, 1), values[now, :, here].reshape(2 * TILE, 256))
            add_rows(total.at[now], j, tiles, part)
        inverse = 1.0 / total[now, :, 128:]
        mix_ref[0, :, 128 * pair : 128 * (pair + 1)] = (total[now, :, :128] * inverse).astype(BF16)
        turned = inverse.T
        inv_ref[0, pair, 0:1] = turned[0:1]
        inv_ref[0, pair, 1:2] = turned[VD : VD + 1]

    @pl.when(m == pl.num_programs(0) - 1)
    def _():
        plan.finish()


def whole_group(width, group):
    return pl.BlockSpec((1, group, width), lambda m: (m, 0, 0))


def lengths_spec(lengths):
    return pl.BlockSpec(lengths.shape, lambda *_: (0, 0), memory_space=pltpu.SMEM)


def attend_all(qkv, lengths, out_grad, slabs, jobs, near_job):
    micro, group, columns = qkv.shape
    dim = out_grad.shape[2]
    wide = columns - 256
    dma = pltpu.SemaphoreType.DMA
    unit = sum(job[2] for job in jobs)
    return call(
        functools.partial(attend_kernel, jobs, near_job),
        "attend",
        2,
        micro,
        [lengths_spec(lengths), whole_group(columns, group), anywhere(), anywhere()],
        [
            whole_group(wide, group),
            pl.BlockSpec((1, wide // 128, 8, group), lambda m: (m, 0, 0, 0)),
            anywhere(),
            anywhere(),
            anywhere(),
        ],
        [
            jax.ShapeDtypeStruct((micro, group, wide), BF16),
            jax.ShapeDtypeStruct((micro, wide // 128, 8, group), F32),
            jax.ShapeDtypeStruct(out_grad.shape, BF16),
            jax.ShapeDtypeStruct((dim, unit), BF16),
            jax.ShapeDtypeStruct((dim // 4, near_job[1]), BF16),
        ],
        [
            pltpu.VMEM((group // TILE, TILE * (SPAN + 1), TILE), F32),
            pltpu.VMEM((2, 2, group, 128), BF16),
            pltpu.VMEM((2, 2, group, 256), BF16),
            pltpu.VMEM((2, group, 256), F32),
            dma,
            dma,
        ]
        + half_sems(far_count() - 1)
        + [dma]
        + gather_sems() * len(jobs),
        (lengths, qkv, out_grad, slabs),
    )


def attend_back_kernel(jobs, lengths, qkv, mix_ref, inv_ref, d_own, d_other, weights, *refs):
    sources, refs = refs[: len(jobs)], refs[len(jobs) :]
    (dqkv, grads), refs = refs[:2], refs[2:]
    outs, refs = refs[: len(jobs)], refs[len(jobs) :]
    (mask, queries, queries_t, keys, douts, douts_t, deltas, dv_t, dk_t, dq), refs = refs[:10], refs[10:]
    (d, dmix, grad_total, rounded, out_sem), refs = refs[:5], refs[5:]
    m = pl.program_id(0)
    group = qkv.shape[1]
    tiles = group // TILE
    pairs = mix_ref.shape[2] // 128
    lane = lax.broadcasted_iota(jnp.int32, (group, 128), 1)
    zero = jnp.zeros((), BF16)
    plan = Plan(m, lengths.shape[0], 2 * pairs, 18.0)
    add_scatters(plan, jobs, sources, outs, refs)

    @pl.when(m == 0)
    def _():
        greet(dp_peers())
        grad_total[...] = jnp.zeros_like(grad_total)

    plan.at(0)
    rows = d_own.shape[1]
    core = lax.axis_index("tensor")
    d[pl.ds(pl.multiple_of(core * rows, rows), rows)] = d_own[0]
    d[pl.ds(pl.multiple_of((1 - core) * rows, rows), rows)] = d_other[0]
    dmix[...] = mm(d[...], weights[...]).astype(BF16)
    grad_total[...] += mm(d[...], mix_ref[0], TN)
    fill_mask(mask, lengths, m)
    queries_t[...] = (qkv[0, :, :128].astype(F32) * 0.5).T.astype(BF16)
    query = qkv[0, :, :128] * jnp.asarray(0.25, BF16)
    key = qkv[0, :, 128:256] * jnp.asarray(0.5, BF16)
    for pair in range(pairs):
        now = pair % 2
        lanes = slice(128 * pair, 128 * (pair + 1))
        value = slice(256 + 128 * pair, 384 + 128 * pair)
        inverse = jnp.concatenate(
            [jnp.broadcast_to(inv_ref[0, pair, s : s + 1, :], (VD, group)) for s in range(2)], 0
        ).T
        dout_low = (dmix[:, lanes].astype(F32) * inverse).astype(BF16)
        dout = dout_low.astype(F32)
        douts_t[now] = dout.T.astype(BF16)
        product = dout * mix_ref[0, :, lanes].astype(F32)
        for side in range(2):
            mine = lane // VD == side
            head = lane // FEAT == 2 * pair + side
            queries[now, side] = jnp.where(head, query, zero)
            keys[now, side] = jnp.where(head, key, zero)
            douts[now, side] = jnp.where(mine, dout_low, zero)
            delta = jnp.sum(jnp.where(mine, product, 0.0), axis=1, keepdims=True)
            deltas[now, side] = jnp.broadcast_to(delta, (group, 128))
        for j in range(tiles):
            if j % 2 == 0 and pair + j:
                plan.at(2 * pair + j // 2)
            i = min(tiles, j + SPAN + 1)
            tall = (i - j) * TILE
            here, below = slice(j * TILE, (j + 1) * TILE), slice(j * TILE, i * TILE)
            scores = mm(queries[now, :, below].reshape(2 * tall, 128), qkv[0, here, 128:256], NT)
            slopes = mm(douts[now, :, below].reshape(2 * tall, 128), qkv[0, here, value], NT)
            allowed = mask[j, :tall]
            d_scores = []
            for side in range(2):
                t = scores[side * tall : (side + 1) * tall] + 1.0
                masked = t * allowed
                delta = jnp.concatenate([deltas[now, side, below]] * (TILE // 128), 1)
                d_score = ((slopes[side * tall : (side + 1) * tall] - delta) * masked).astype(BF16)
                weights = (t * masked + allowed).astype(BF16)
                mine = slice(VD * side, VD * (side + 1))
                head = slice((2 * pair + side) * FEAT, (2 * pair + side + 1) * FEAT)
                dv_t[now, mine, here] = mm(douts_t[now, mine, below], weights)
                dk_t[head, here] = mm(queries_t[head, below], d_score)
                d_scores.append(d_score)
            part = mm(jnp.concatenate(d_scores, 1), keys[now, :, here].reshape(2 * TILE, 128))
            if pair:
                dq[below] += part
            else:
                add_rows(dq, j, tiles, part)
        dqkv[0, :, value] = dv_t[now].T.astype(BF16)
    dqkv[0, :, 128:256] = dk_t[...].T.astype(BF16)
    dqkv[0, :, :128] = dq[...].astype(BF16)

    @pl.when(m == pl.num_programs(0) - 1)
    def _():
        rounded[...] = grad_total[...].astype(BF16).reshape(rounded.shape)
        write = pltpu.make_async_copy(rounded, grads, out_sem)
        write.start()
        plan.finish()
        write.wait()


def attend_back(qkv, mix, inverse, d_own, d_other, weights, lengths, sources, jobs):
    micro, group, columns = qkv.shape
    wide = columns - 256
    rows, dim = d_own.shape[1:]
    shapes, specs = scatter_outs(jobs, dim)
    grads = grad_shape(dim, wide)
    pair_rows = pltpu.VMEM((2, 2, group, 128), BF16)
    return call(
        functools.partial(attend_back_kernel, jobs),
        "attend_back",
        8,
        micro,
        [
            lengths_spec(lengths),
            whole_group(columns, group),
            whole_group(wide, group),
            pl.BlockSpec((1, wide // 128, 8, group), lambda m: (m, 0, 0, 0)),
            whole_group(dim, rows),
            whole_group(dim, rows),
            once((dim, wide)),
        ]
        + [anywhere()] * len(jobs),
        [whole_group(columns, group), anywhere()] + specs,
        [jax.ShapeDtypeStruct((micro, group, columns), BF16), grads] + shapes,
        [
            pltpu.VMEM((group // TILE, TILE * (SPAN + 1), TILE), F32),
            pair_rows,
            pltpu.VMEM((128, group), BF16),
            pair_rows,
            pair_rows,
            pltpu.VMEM((2, 128, group), BF16),
            pltpu.VMEM((2, 2, group, 128), F32),
            pltpu.VMEM((2, 128, group), F32),
            pltpu.VMEM((128, group), F32),
            pltpu.VMEM((group, 128), F32),
            pltpu.VMEM((group, dim), BF16),
            pltpu.VMEM((group, wide), BF16),
            pltpu.VMEM((dim, wide), F32),
            pltpu.VMEM(grads.shape, BF16),
            pltpu.SemaphoreType.DMA,
        ]
        + scatters_scratch(jobs, dim),
        (lengths, qkv, mix, inverse, d_own, d_other, weights, *sources),
    )


def out_kernel(
    jobs, near_job, mix_own, mix_other, x, weights, gains, slabs, resid_out, h_out, h_other, unit, near,
    parts, sent, got, h_sent, send, recv, *sems,
):
    i = pl.program_id(0)
    count, rows = got.shape[0], got.shape[1]
    per = h_other.shape[1] // rows
    plan = Plan(i, 2 * count, 1, 0.95)
    add_gathers(plan, [(slabs, unit, *job) for job in jobs], sems[3:])
    ahead = NearGather(slabs.at[:, pl.ds(*near_job)], near, *sems[:3])
    plan.add([(2.0, ahead.begin)], ahead.finish)

    def swap(k):
        return remote(sent.at[k], got.at[k], send.at[k], recv.at[k], sibling())

    def swap_h(k):
        place = h_other.at[lax.div(k, per), pl.ds(pl.multiple_of(lax.rem(k, per) * rows, rows), rows)]
        return remote(h_sent.at[k], place, send.at[count + k], recv.at[count + k], sibling())

    @pl.when(i == 0)
    def _():
        greet(dp_peers() + [sibling()])

    plan.at(0)

    @pl.when(i < count)
    def _():
        both = jnp.concatenate([mix_other[0], mix_own[0]], 0)
        part = mm(both, weights[...], NT)
        sent[i] = part[:rows].astype(BF16)
        parts[i] = part[rows:]
        swap(i).start()

    @pl.when(i >= count)
    def _():
        k = i - count
        swap(k).wait_recv()
        resid = x[0].astype(F32) + parts[k] + got[k].astype(F32)
        resid_out[0] = resid.astype(BF16)
        h = (resid * root_mean(resid) * gains[1:2]).astype(BF16)
        h_out[0] = h
        h_sent[k] = h
        swap_h(k).start()

    @pl.when(i == 2 * count - 1)
    def _():
        plan.finish()
        for k in range(count):
            swap(k).wait_send()
            swap_h(k).wait()


def out_project(mix, x, weights, gains, slabs, jobs, near_job, rows=256):
    micro, own_rows, dim = x.shape
    wide = mix.shape[2]
    per = own_rows // rows
    count = micro * per
    late = part_block(dim, per, rows, count, count - 1)
    shape = jax.ShapeDtypeStruct((micro, own_rows, dim), BF16)
    buffer = pltpu.VMEM((count, rows, dim), BF16)
    return call(
        functools.partial(out_kernel, jobs, near_job),
        "out_project",
        3,
        2 * count,
        [
            core_block(wide, per, rows, False, count - 1),
            core_block(wide, per, rows, True, count - 1),
            late,
            once((dim, wide)),
            once((8, dim)),
            anywhere(),
        ],
        [late, late, anywhere(), anywhere(), anywhere()],
        [
            shape,
            shape,
            shape,
            jax.ShapeDtypeStruct((dim, sum(job[2] for job in jobs)), BF16),
            jax.ShapeDtypeStruct((dim // 4, near_job[1]), BF16),
        ],
        [pltpu.VMEM((count, rows, dim), F32), buffer, buffer, buffer]
        + half_sems(2 * count)
        + half_sems(far_count() - 1)
        + [pltpu.SemaphoreType.DMA]
        + gather_sems() * len(jobs),
        (mix, mix, x, weights, gains, slabs),
    )


FEED_US = (5.2, 6.4, 7.2)
GATHER_AT = ((0.0, 0.0), (0.0, 8.0), (0.5, 26.0))
SCATTER_AT = (52.0, 67.0, 79.0, 90.0)
BACK_US = 2.4
OUT_PIECE = 512
IN_PIECE = 384


def feed_kernel(
    steps, widths, loads, cuts, jobs, h_own, h_other, g_own, g_other, unit_0, unit_1, near_a, near_b, slabs,
    resid, g_late, resid_end, g_end, gains, mixed_out, d_out, d_other, *refs,
):
    def take(number):
        nonlocal refs
        taken, refs = refs[:number], refs[number:]
        return taken

    chunks = len(widths)
    grads = take(chunks)
    units = take(chunks - 1)
    outs = take(len(jobs))
    slab_a, slab_b, total, h, g, hidden_s, dgu_s = take(7)
    out_own, out_other, dm_own, dm_other, dm_got, out_got, d_sent, mixed_s = take(8)
    load_sems, write_sems, send, recv, local = take(5)
    i = pl.program_id(0)
    rows = h_own.shape[1]
    per = d_other.shape[1] // rows
    weights = [(slab_a, slab_b)[chunk % 2] for chunk in range(chunks)]

    def place(ref, k):
        return ref.at[lax.div(k, per), pl.ds(pl.multiple_of(lax.rem(k, per) * rows, rows), rows)]

    def swaps(k):
        return [
            remote(dm_other.at[k], dm_got.at[k + 1], send.at[3 * k], recv.at[3 * k], sibling()),
            remote(out_other.at[k], out_got.at[k + 1], send.at[3 * k + 1], recv.at[3 * k + 1], sibling()),
        ]

    def results(k):
        return [
            remote(d_sent.at[k + 1], place(d_other, k), send.at[3 * k + 2], recv.at[3 * k + 2], sibling()),
            pltpu.make_async_copy(d_sent.at[k + 1], place(d_out, k), local.at[2 * k]),
            pltpu.make_async_copy(mixed_s.at[k + 1], place(mixed_out, k), local.at[2 * k + 1]),
        ]

    def finish_part(slot, before, resid, g_late):
        values = resid[0].astype(F32)
        mixed_s[slot] = add(values, out_own[before], out_got[slot]).astype(BF16)
        scaled = add(dm_own[before], dm_got[slot]) * gains[1:2]
        d_sent[slot] = (g_late[0].astype(F32) + norm_slope(values, scaled)).astype(BF16)

    def copies(chunk):
        made = []
        sources = loads if chunk == 0 else [(0, 0, 3 * widths[chunk])]
        for at, (source, target, columns) in enumerate(sources):
            ref = (unit_0, unit_1)[at] if chunk == 0 else units[chunk - 1]
            tall = slab_a.shape[0] // 4
            for part in range(4):
                rows_at = pl.ds(part * tall, tall)
                cut = ref.at[rows_at, pl.ds(source, columns)]
                target_at = weights[chunk].at[rows_at, pl.ds(target, columns)]
                made.append(pltpu.make_async_copy(cut, target_at, load_sems.at[chunk, at, part]))
        return made

    def writes(chunk):
        made = []
        far, low, parts, half, columns = grads[chunk].shape
        for at in range(far * low * parts):
            source = weights[chunk].at[pl.ds(at * half, half), pl.ds(0, columns)]
            target = grads[chunk].at[at // (low * parts), at // parts % low, at % parts]
            made.append(pltpu.make_async_copy(source, target, write_sems.at[chunk, at]))
        return made

    def start_all(made):
        for copy in made:
            copy.start()

    def wait_all(made):
        for copy in made:
            copy.wait()

    clock = []
    for chunk in range(chunks):
        start = clock[-2] + FEED_US[chunk - 1] if clock else 0.0
        clock += [start + FEED_US[chunk] * (step + part) for step in range(steps) for part in (0, 0.65)]
    plan = Plan(i, chunks * steps, 2, None, clock)
    for chunk in range(1, chunks):
        first, width = cuts[chunk - 1]
        whole = units[chunk - 1]
        if chunk == 1:
            part = near_a.shape[1]
            parts = [(0, part, near_a, GATHER_AT[0]), (part, width - part, near_b, GATHER_AT[1])]
        else:
            parts = [(0, width, None, GATHER_AT[2])]
        for at, wide, near, times in parts:
            source = slabs.at[:, pl.ds(first + at, wide)]
            gather = Gather(source, whole.at[:, pl.ds(at, wide)], *take(3), near)
            plan.add(gather.plan_near(*times), lambda: None, 2 * chunk * steps - 2)
            plan.put(chunk * steps - 1, 1000.0, gather.finish)
        plan.put(chunk * steps - 1, 1001.0, lambda chunk=chunk: start_all(copies(chunk)))
    for at, (chunk, (first, width)) in enumerate(jobs):
        scatter = Scatter(grads[chunk], first, outs[at], take(SCATTER_REFS))
        plan.add(scatter.plan(SCATTER_AT[at]), scatter.finish, None, 2 * (chunk + 1) * steps + 2)
    for chunk in range(chunks - 1):
        plan.put((chunk + 1) * steps + 1, -1.0, lambda chunk=chunk: wait_all(writes(chunk)))

    @pl.when(i == 0)
    def _():
        start_all(copies(0))
        zeros = jnp.zeros(dm_got.shape[1:], BF16)
        dm_got[0] = zeros
        out_got[0] = zeros
        greet(dp_peers() + [sibling()])

    plan.at(0)
    half = jnp.asarray(0.5, BF16)
    one = jnp.asarray(1.0, BF16)
    dim = slab_a.shape[0]

    def chunk_step(chunk):
        slab, width, last = weights[chunk], widths[chunk], chunk == chunks - 1
        j = i - chunk * steps

        @pl.when(j == 0)
        def _():
            total[:, : 3 * width] = jnp.zeros((dim, 3 * width), F32)
            wait_all(copies(chunk))

        h[:rows], h[rows:] = h_other[0], h_own[0]
        g[:rows], g[rows:] = g_other[0], g_own[0]
        for at, wide in chunk_slices(width):
            both = slice(2 * at, 2 * (at + wide))
            gate_up = mm(h[...], slab[:, both]).astype(BF16)
            d_hidden = mm(g[...], slab[:, 2 * width + at : 2 * width + at + wide]).astype(BF16)
            gate, up = gate_up[:, :wide], gate_up[:, wide:]
            sigmoid = half * jnp.tanh(half * gate) + half
            silu = gate * sigmoid
            hidden_s[:, at : at + wide] = silu * up
            d_gate = d_hidden * up * (sigmoid + silu * (one - sigmoid))
            dgu_s[:, both] = jnp.concatenate([d_gate, d_hidden * silu], 1)
        for at in range(0, dim, 512):
            cut = slice(at, at + 512)
            out = mm(hidden_s[:, :width], slab[cut, 2 * width : 3 * width], NT)
            dm = mm(dgu_s[:, : 2 * width], slab[cut, : 2 * width], NT)
            for ref, value in ((out_own, out[rows:]), (out_other, out[:rows]), (dm_own, dm[rows:]), (dm_other, dm[:rows])):
                if chunk:
                    value = value + ref[j, :, cut].astype(F32)
                ref[j, :, cut] = value.astype(BF16)
        if last:
            start_all(swaps(j))

            @pl.when(j > 0)
            def _():
                for swap in swaps(j - 1):
                    swap.wait_recv()

            finish_part(j, jnp.maximum(j - 1, 0), resid, g_late)
        plan.at(1)
        total[:, : 2 * width] += mm(h[...], dgu_s[:, : 2 * width], TN)
        total[:, 2 * width : 3 * width] += mm(g[...], hidden_s[:, :width], TN)
        if last:

            @pl.when(j > 0)
            def _():
                start_all(results(j - 1))

        @pl.when(j == steps - 1)
        def _():
            slab[:, : 3 * width] = total[:, : 3 * width].astype(BF16)
            start_all(writes(chunk))
            if last:
                for swap in swaps(steps - 1):
                    swap.wait_recv()
                finish_part(steps, steps - 1, resid_end, g_end)
                start_all(results(steps - 1))
                plan.finish()
                for k in range(steps):
                    for copy in swaps(k):
                        copy.wait_send()
                    wait_all(results(k))
                wait_all(writes(chunk))

    for chunk in range(chunks):

        @pl.when((i >= chunk * steps) & (i < (chunk + 1) * steps))
        def _(chunk=chunk):
            chunk_step(chunk)


def feed(rows_in, unit_0, unit_1, near_a, near_b, loads, widths, slabs, cuts, jobs, resid, gains, rows=256):
    micro, own_rows, dim = rows_in[0].shape
    per = own_rows // rows
    steps = micro * per
    chunks = len(widths)

    def part_at(lag):
        def place(i):
            k = lax.rem(i, steps) if lag == 0 else jnp.clip(i - (chunks - 1) * steps - lag, 0, steps - 1)
            return lax.div(k, per), lax.rem(k, per), 0

        return pl.BlockSpec((1, rows, dim), place)

    part, late = part_at(0), part_at(1)
    end = pl.BlockSpec((1, rows, dim), lambda i: (micro - 1, per - 1, 0), pipeline_mode=pl.Buffered(1))
    shape = jax.ShapeDtypeStruct((micro, own_rows, dim), BF16)
    grads = [grad_shape(dim, 3 * width) for width in widths]
    units = [jax.ShapeDtypeStruct((dim, width), BF16) for _, width in cuts]
    shapes, specs = scatter_outs([job for _, job in jobs], dim)
    most = max(widths)
    slots, late_slots = pltpu.VMEM((steps, rows, dim), BF16), pltpu.VMEM((steps + 1, rows, dim), BF16)
    blocks = grads[0].shape[0] * grads[0].shape[1] * grads[0].shape[2]
    results = call(
        functools.partial(feed_kernel, steps, widths, loads, cuts, jobs),
        "feed",
        4,
        chunks * steps,
        [part] * 4 + [anywhere()] * 5 + [late, late, end, end, once((8, dim))],
        [anywhere()] * (3 + chunks + chunks - 1) + specs,
        [shape] * 3 + grads + units + shapes,
        [pltpu.VMEM((dim, 3 * most), BF16)] * 2
        + [
            pltpu.VMEM((dim, 3 * most), F32),
            pltpu.VMEM((2 * rows, dim), BF16),
            pltpu.VMEM((2 * rows, dim), BF16),
            pltpu.VMEM((2 * rows, most), BF16),
            pltpu.VMEM((2 * rows, 2 * most), BF16),
        ]
        + [slots] * 4
        + [late_slots] * 4
        + [pltpu.SemaphoreType.DMA((chunks, 2, 4)), pltpu.SemaphoreType.DMA((chunks, blocks))]
        + half_sems(3 * steps)
        + [pltpu.SemaphoreType.DMA((2 * steps,))]
        + gather_sems() * chunks
        + scatters_scratch([job for _, job in jobs], dim),
        (*rows_in, unit_0, unit_1, near_a, near_b, slabs, resid, rows_in[2], resid, rows_in[2], gains),
    )
    return results[:3], results[3 : 3 + chunks], results[2 + 2 * chunks :]


def back_in_kernel(
    micro, feed_jobs, out_jobs, in_jobs, h, dqkv_all, dqkv, x, d_own, weights, gains, grads_last,
    w_query, w_key, w_value, slabs, *refs,
):
    jobs = out_jobs + in_jobs
    feed_count = sum(len(chunk) for chunk in feed_jobs)
    feed_grads, refs = refs[:feed_count], refs[feed_count:]
    (input_grad, gain_sums, grads), refs = refs[:3], refs[3:]
    outs, refs = refs[: len(jobs)], refs[len(jobs) :]
    (total, sent, got, send, recv, out_sem, rounded, sums, sums_got, sums_sems), refs = refs[:10], refs[10:]
    i = pl.program_id(0)
    m = lax.rem(i, micro)
    plan = Plan(i, 3 * micro, 1, BACK_US)
    split = SCATTER_REFS * len(out_jobs)
    add_scatters(plan, out_jobs, [grads_last] * len(out_jobs), outs, refs[:split])
    outs = outs[len(out_jobs) :]
    add_scatters(plan, in_jobs, [grads] * len(in_jobs), outs, refs[split:], BACK_US * micro)

    def swap(k):
        return remote(sent.at[k], got.at[k], send.at[k], recv.at[k], sibling())

    def swap_sums():
        return remote(sums, sums_got, sums_sems.at[0], sums_sems.at[1], sibling())

    @pl.when(i == 0)
    def _():
        greet(dp_peers() + [sibling()])
        total[...] = jnp.zeros_like(total)

    @pl.when(i < micro)
    def _():
        total[...] += mm(h[0], dqkv_all[0], TN)

    @pl.when(i == micro - 1)
    def _():
        rounded[...] = total[...].astype(BF16).reshape(rounded.shape)
        write = pltpu.make_async_copy(rounded, grads, out_sem)
        write.start()
        write.wait()

    plan.at(0)

    @pl.when(i >= micro)
    def _():
        part = mm(dqkv[0], weights[...], NT)

        @pl.when(i < 2 * micro)
        def _():
            sent[m] = part.astype(BF16)
            swap(m).start()

        @pl.when(i >= 2 * micro)
        def _():
            swap(m).wait_recv()
            scaled = (part + got[m].astype(F32)) * gains[0:1]
            input_grad[0] = (d_own[0].astype(F32) + norm_slope(x[0].astype(F32), scaled)).astype(BF16)

    @pl.when(i == 3 * micro - 1)
    def _():
        each = slabs.shape[0]
        sizes = [sum(wide for _, wide in chunk) for chunk in feed_jobs]
        at = slabs.shape[1] - sum(sizes)
        index = 0
        mid = jnp.zeros((each, 128), F32)
        for size, chunk in zip(sizes, feed_jobs):
            for first, wide in chunk:
                value = feed_grads[index][...].reshape(each, wide)
                for column in range(0, wide, 128):
                    if first + column < 2 * (size // 3):
                        lanes = slice(at + first + column, at + first + column + 128)
                        mid = mid + value[:, column : column + 128] * slabs[:, lanes].astype(F32)
                index += 1
            at += size
        sums[1] = mid
        plan.finish()
        near = jnp.zeros((each, 128), F32)
        at = 0
        columns = [out[...].reshape(each, out.shape[2]) for out in outs]
        columns = jnp.concatenate(columns, 1) if len(columns) > 1 else columns[0]
        for ref in (w_query, w_key, w_value):
            for column in range(0, ref.shape[1], 128):
                near = near + columns[:, at : at + 128] * ref[:, column : column + 128].astype(F32)
                at += 128
        sums[0] = near
        swap_sums().start()
        for k in range(micro):
            swap(k).wait_send()
        swap_sums().wait()
        gain_sums[...] = sums[...] + sums_got[...]


def back_in(h, dqkv, x, d_own, weights, gains, grads_last, w_in, slabs, feed_grads, feed_jobs, out_jobs, in_jobs):
    jobs = out_jobs + in_jobs
    micro, rows, dim = x.shape
    columns = dqkv.shape[2]
    each = slabs.shape[0]
    own = pl.BlockSpec((1, rows, dim), lambda i: (jnp.maximum(i - 2 * micro, 0), 0, 0))
    grads = grad_shape(dim, columns)
    shapes, specs = scatter_outs(jobs, dim)
    buffer = pltpu.VMEM((micro, rows, dim), BF16)
    sums = jax.ShapeDtypeStruct((2, each, 128), F32)

    def all_place(i):
        return jnp.minimum(i, micro - 1), 0, 0

    def place(i):
        core = lax.axis_index("tensor")
        k = jnp.maximum(i - micro, 0)
        return lax.rem(k, micro), jnp.where(k < micro, 1 - core, core), 0

    locals_ = list(w_in) + [slabs] + list(feed_grads)
    return call(
        functools.partial(back_in_kernel, micro, feed_jobs, out_jobs, in_jobs),
        "back_in",
        9,
        3 * micro,
        [
            pl.BlockSpec((1, 2 * rows, dim), all_place),
            pl.BlockSpec((1, 2 * rows, columns), all_place),
            pl.BlockSpec((1, rows, columns), place),
            own,
            own,
            once(weights.shape),
            once((8, dim)),
            anywhere(),
        ]
        + [once(a.shape) for a in locals_],
        [own, once(sums.shape), anywhere()] + specs,
        [jax.ShapeDtypeStruct((micro, rows, dim), BF16), sums, grads] + shapes,
        [pltpu.VMEM((dim, columns), F32), buffer, buffer]
        + half_sems(micro)
        + [
            pltpu.SemaphoreType.DMA,
            pltpu.VMEM(grads.shape, BF16),
            pltpu.VMEM(sums.shape, F32),
            pltpu.VMEM(sums.shape, F32),
            pltpu.SemaphoreType.DMA((2,)),
        ]
        + scatters_scratch(jobs, dim),
        (h, dqkv, dqkv, x, d_own, weights, gains, grads_last, *locals_),
    )


def finish_kernel(edges, counts, grad_in, mixed, gain_attn, gain_mlp, gain_sums, *refs):
    feed_grads, refs = refs[: counts[0]], refs[counts[0] :]
    out_grads, refs = refs[: counts[1]], refs[counts[1] :]
    in_grads, refs = refs[: counts[2]], refs[counts[2] :]
    mixed_out, grad_out, attn_out, mlp_out, q_out, k_out, v_out, out_t, gate_out, up_out, down_t = refs
    each, units = gate_out.shape
    grad_out[...] = grad_in[...].astype(F32)
    mixed_out[...] = mixed[...]

    def blocks(pieces):
        found = []
        for piece in pieces:
            for at in range(0, piece.shape[2], 128):
                found.append((piece, at))
        return found

    def copy_to(ref, at, block):
        piece, column = block
        wide = min(128, ref.shape[1] - at)
        ref[:, at : at + wide] = piece[:, :, column : column + wide].reshape(each, wide)

    @pl.when(pl.program_id(0) == 0)
    def _():
        turned = [gain_sums[k].T for k in range(2)]
        for value, gain, ref in zip(turned, (gain_attn, gain_mlp), (attn_out, mlp_out)):
            ref[...] = jnp.sum(value, axis=0, keepdims=True) / gain[...].astype(F32)
        queue = blocks(in_grads)
        for ref in (q_out, k_out, v_out):
            for at in range(0, ref.shape[1], 128):
                copy_to(ref, at, queue.pop(0))
        for at, block in zip(range(0, out_t.shape[1], 128), blocks(out_grads)):
            copy_to(out_t, at, block)
        queue = blocks(feed_grads)
        for low, high in edges:
            for start, width in chunk_slices(high - low):
                for ref in (gate_out, up_out):
                    for at in range(low + start, low + start + width, 128):
                        copy_to(ref, at, queue.pop(0))
            for at in range(low, high, 128):
                copy_to(down_t, at, queue.pop(0))


def finish(edges, grad_in, mixed, gain_attn, gain_mlp, gain_sums, feed_grads, out_grads, in_grads, widths, units):
    micro, rows, dim = mixed.shape
    each = gain_sums.shape[1]
    tile = min(rows, 512)
    block = pl.BlockSpec((1, tile, dim), lambda m, t: (m, t, 0))
    small = [gain_attn, gain_mlp, gain_sums, *feed_grads, *out_grads, *in_grads]
    shapes = [jax.ShapeDtypeStruct((1, each), F32)] * 2
    shapes += [jax.ShapeDtypeStruct((each, w), F32) for w in widths + [units] * 3]
    counts = (len(feed_grads), len(out_grads), len(in_grads))
    return call(
        functools.partial(finish_kernel, edges, counts),
        "finish",
        None,
        (micro, rows // tile),
        [block, block] + [once(a.shape) for a in small],
        [block, block] + [once(s.shape) for s in shapes],
        [jax.ShapeDtypeStruct(mixed.shape, BF16), jax.ShapeDtypeStruct(mixed.shape, F32)] + shapes,
        [],
        (grad_in, mixed, *small),
    )


def fused_body(
    inputs, gain_attn, gain_mlp, w_query, w_key, w_value, w_out, w_gate, w_up, w_down, out_grad, lengths
):
    micro, rows, dim = inputs.shape
    units = w_gate.shape[1]
    out_columns = w_out.shape[0]
    lengths = lengths[:, 0]
    gains = gain_attn.reshape(1, -1), gain_mlp.reshape(1, -1)
    w_in = (w_query, w_key, w_value)
    padded = -(-units // 128) * 128
    edges = [(max(at - CHUNK, 0), at) for at in range(padded, 0, -CHUNK)][::-1]
    wide = [3 * (high - low) for low, high in edges]

    h_in, qkv, gain_full, whole_in, slabs = project(edges, inputs, *w_in, *gains, w_gate, w_up, w_down.T, w_out.T)

    begin = [out_columns, out_columns + wide[0], out_columns + wide[0] + wide[1]]
    early = min(EARLY, wide[0])
    ahead = min(AHEAD, wide[1] - 128)
    mix, inverse, g_other, unit_0, near_a = attend_all(
        qkv, lengths, out_grad, slabs, [(0, 0, begin[0] + early)], (begin[1], ahead)
    )
    resid, h_own, h_other, unit_1, near_b = out_project(
        mix, inputs, unit_0, gain_full, slabs, [(begin[0] + early, 0, wide[0] - early)], (begin[1] + ahead, wide[1] - ahead)
    )

    feed_jobs, at = [[], [], []], []
    for kernel in JOBS:
        at.append([])
        for chunk, width in kernel:
            first = sum(w for _, w in feed_jobs[chunk])
            feed_jobs[chunk].append((first, width))
            at[-1].append((chunk, (first, width)))
    loads = [(out_columns, 0, early), (0, early, wide[0] - early)]
    (mixed_out, d_own, d_other), grads_of, done = feed(
        (h_own, h_other, out_grad, g_other),
        unit_0,
        unit_1,
        near_a,
        near_b,
        loads,
        [w // 3 for w in wide],
        slabs,
        list(zip(begin[1:], wide[1:])),
        at[0],
        resid,
        gain_full,
    )
    found = dict(zip(at[0], done))
    sources, jobs = [grads_of[chunk] for chunk, _ in at[1]], [job for _, job in at[1]]
    dqkv, grads_out, *done = attend_back(qkv, mix, inverse, d_own, d_other, unit_0, lengths, sources, jobs)
    found |= dict(zip(at[1], done))
    feed_grads = [found[key] for key in sorted(found)]
    out_jobs, in_jobs = pieces_of(out_columns, OUT_PIECE), pieces_of(qkv.shape[2], IN_PIECE)
    input_grad, gain_sums, _, *done = back_in(
        h_in, dqkv, inputs, d_own, whole_in, gain_full, grads_out, w_in, slabs, feed_grads, feed_jobs, out_jobs, in_jobs
    )
    out_grads, in_grads = done[: len(out_jobs)], done[len(out_jobs) :]
    widths = [w.shape[1] for w in w_in] + [out_columns]
    mixed_out, input_grad, attn_grad, mlp_grad, grad_query, grad_key, grad_value, out_t, gate, up, down_t = finish(
        edges, input_grad, mixed_out, *gains, gain_sums, feed_grads, out_grads, in_grads, widths, units
    )
    return (
        mixed_out,
        input_grad,
        attn_grad[0],
        mlp_grad[0],
        grad_query,
        grad_key,
        grad_value,
        out_t.T,
        gate,
        up,
        down_t.T,
    )


def solution(mesh):
    in_specs = (
        P(None, ("dp", "tensor"), None),
        P("dp"),
        P("dp"),
        P("dp", "tensor"),
        P("dp", "tensor"),
        P("dp", "tensor"),
        P("tensor", "dp"),
        P("dp", "tensor"),
        P("dp", "tensor"),
        P("tensor", "dp"),
        P(None, ("dp", "tensor"), None),
        P(None, "dp", None),
    )
    out_specs = (
        P(None, ("dp", "tensor"), None),
        P(None, ("dp", "tensor"), None),
        P("dp"),
        P("dp"),
        P("dp", "tensor"),
        P("dp", "tensor"),
        P("dp", "tensor"),
        P("tensor", "dp"),
        P("dp", "tensor"),
        P("dp", "tensor"),
        P("tensor", "dp"),
    )
    fits = mesh.shape["tensor"] == 2 and mesh.shape["dp"] % 4 == 0
    chosen = fused_body if fits else plain_body
    return jax.shard_map(chosen, mesh=mesh, in_specs=in_specs, out_specs=out_specs, check_vma=False)
```
